32 devices in a mesh: dp: 2 (over x), context: 4 (over z), expert: 4 (over y, core).
Axes of the slice: x: 2, y: 2, z: 4, core: 2. Of those that a mesh axis runs over, the one named last changes fastest.
Arguments:
- packed_in: bfloat16 [8, 1024, 1536], P(('dp', 'expert'), 'context'), may hold values from -6 to 6
- routes: int32 [8, 1024, 4], P(('dp', 'expert'), 'context'), may hold values from 0 to 7, all different within a row; in each aligned block of 256 rows (0 to 255, 256 to 511, ..., all dimensions but the last counted through in order) at most 192 rows name the same one
- gates: float32 [8, 1024, 4], P(('dp', 'expert'), 'context'), may hold values from 0.1 to 0.4
- doc_starts: int32 [8, 6], P(('dp', 'expert')), may hold values from 0 to 1023, as said below
- attn_gain: float32 [1536], replicated, may hold values from 0.5 to 1.5
- w_qkv: bfloat16 [1536, 2048], replicated, may hold values from -0.15625 to 0.15625
- w_out: bfloat16 [1536, 1536], replicated, may hold values from -2.5 to 2.5
- ffn_gain: float32 [1536], replicated, may hold values from 0.5 to 1.5
- expert_gate_up: bfloat16 [8, 1536, 1536], P('expert'), may hold values from -0.15625 to 0.15625
- expert_down: bfloat16 [8, 768, 1536], P('expert'), may hold values from -0.875 to 0.875
- cotangent: bfloat16 [8, 1024, 1536], P(('dp', 'expert'), 'context'), may hold values from -6 to 6
Outputs:
- packed_out: bfloat16 [8, 1024, 1536], P(('dp', 'expert'), 'context')
- packed_grad: float32 [8, 1024, 1536], P(('dp', 'expert'), 'context')
- attn_gain_grad: float32 [1536], P('context')
- qkv_grad: float32 [1536, 2048], P('context')
- out_proj_grad: float32 [1536, 1536], P('context')
- ffn_gain_grad: float32 [1536], P('context')
- gate_up_grad: float32 [8, 1536, 1536], P('expert', 'context')
- down_grad: float32 [8, 768, 1536], P('expert', 'context')
The draws below stay inside these ranges and needn't reach their ends.
Inputs may be any that keep to these rules, and one draw needn't show every extreme that they name: `routes`: each token names 4 different experts; among the 256 tokens of one device (aligned blocks along a pack) no expert is named more than 192 times. `doc_starts`: each row holds the first positions of the 6 documents of one pack, strictly increasing, the first 0; a document runs to the next start or to the pack's end.
All inputs are finite; a program needn't handle non-finite values.
Results may differ from the reference program's by a relative error of at most 0.025.
Values may be sent and summed in bfloat16 or wider, within the bound.
A program may use at most 192 MiB of HBM per device.

```python
import math
import jax
import jax.numpy as jnp
import numpy as np
from jax import lax

D = 1536
QUERY_HEADS = 12
KEY_VALUE_HEADS = 2
HEAD_SIZE = 128
FF = 768
TOP = 4
DOCS = 6
TOK_DEV = 256
PACKS = 8
PACK_TOKENS = 1024
EXPERTS = 8
CAP = 192
QKV = 2048
QB = 512


def draw_doc_starts(key, part):
    key = jax.random.fold_in(key, 11)
    first_key, offset_key, length_key = jax.random.split(key, 3)
    first_long = jax.random.randint(first_key, (PACKS, 1), 0, DOCS)
    second_long = (first_long + jax.random.randint(offset_key, (PACKS, 1), 1, DOCS)) % DOCS
    short_lengths = jax.random.randint(length_key, (PACKS, DOCS), 1, TOK_DEV // DOCS + 1)
    doc_ids = jnp.arange(DOCS, dtype=jnp.int32)[None, :]
    is_first = doc_ids == first_long
    is_second = doc_ids == second_long
    short_lengths = jnp.where(is_first | is_second, 0, short_lengths)
    remaining = PACK_TOKENS - jnp.sum(short_lengths, axis=1, keepdims=True)
    first_length = jnp.minimum(remaining - 1, jnp.maximum(4096, (remaining + 1) // 2))
    second_length = remaining - first_length
    lengths = jnp.where(is_first, first_length, jnp.where(is_second, second_length, short_lengths))
    return (jnp.cumsum(lengths, axis=1) - lengths).astype(jnp.int32)


def level_of(rng, shape, shards, least, largest):
    level = 1.0
    for dim, parts in shards:
        heights = jax.random.uniform(jax.random.fold_in(jax.random.fold_in(rng, 6), dim), (parts,), jnp.float32, least / len(shards), largest / len(shards))
        level = level * jnp.repeat(jnp.exp(heights), shape[dim] // parts).reshape((-1,) + (1,) * (len(shape) - 1 - dim))
    return level


def shared_out(stream_key, own, number, rows, number_of, top, most, skew):
    order = jax.random.permutation(stream_key, number_of)
    packed, usual = portions_of(number_of, rows * top, most, skew, True), portions_of(number_of, rows * top, most, skew, False)
    places = jnp.arange(number_of)

    def named(sizes, turn):
        used = int((sizes > 0).sum())
        fixed = max(1, used // 4)
        shifted = fixed + (places - fixed + turn * (used - fixed)) % max(1, number_of - fixed)
        return jnp.zeros((number_of,), jnp.int32).at[order[jnp.where(places < fixed, places, shifted)]].set(jnp.asarray(sizes, jnp.int32))

    sizes = jnp.where(number % 4 == 0, named(packed, number // 4), named(usual, number - number // 4 - 1))
    mixed = jax.random.permutation(jax.random.fold_in(own, 3), number_of)
    donor, receiver = mixed[0:number_of // 2 * 2:2], mixed[1:number_of // 2 * 2:2]
    slack = jnp.minimum(sizes[donor] - 1, most - sizes[receiver]) // 2
    slack = jnp.where((donor == order[0]) | (receiver == order[0]) | (sizes[receiver] == 0), 0, jnp.maximum(slack, 0))
    shifted = jax.random.randint(jax.random.fold_in(own, 4), (number_of // 2,), 0, 1 << 20) % (slack + 1)
    sizes = sizes.at[donor].add(-shifted).at[receiver].add(shifted)
    items = jnp.searchsorted(jnp.cumsum(sizes), jnp.arange(rows * top), side="right").astype(jnp.int32)
    listing = items.reshape(top, rows).T
    listing = listing[jax.random.permutation(jax.random.fold_in(own, 1), rows)]
    turn = jax.random.randint(jax.random.fold_in(own, 2), (rows, 1), 0, top)
    return jnp.take_along_axis(listing, (jnp.arange(top)[None, :] + turn) % top, axis=1)


def portions_of(amount, total, bound, skew, full):
    weights = [(1 << 20) // math.isqrt(standing ** skew) + 1 for standing in range(1, amount + 1)]
    largest = bound if full else min(bound, max(-(-total // amount), total * weights[0] // sum(weights)))
    least = 1 if total - largest >= amount - 1 else 0
    holding, surplus = [largest] + [least] * (amount - 1), total - largest - least * (amount - 1)
    while surplus > 0:
        candidates = [i for i in range(1, amount) if holding[i] < largest] or [i for i in range(1, amount) if holding[i] < bound]
        pool, left = sum([weights[i] for i in candidates]), surplus
        for i in candidates:
            addition = min(bound - holding[i], max(1, left * weights[i] // pool), surplus)
            holding[i] = holding[i] + addition
            surplus = surplus - addition
    return np.array(holding)


def bell_draw(key, dims, deviation, most, pieces=(), held_as=jnp.bfloat16):
    drawn = jax.random.normal(key, dims, jnp.float32) * deviation
    if len(pieces) > 0:
        drawn = level_of(key, dims, pieces, -0.22, 0.18) * drawn
    return jnp.clip(drawn, min=-most, max=most).astype(held_as)


def setup_inputs(seed: int = 0) -> dict:
    seeds = jax.random.split(jax.random.key(seed), 12)
    packed_in = bell_draw(seeds[0], (PACKS, PACK_TOKENS, D), 1.0, 6.0, ((0, 8), (1, 4)))
    routes_keys = jax.random.split(jax.random.fold_in(seeds[1], 1), PACKS * PACK_TOKENS // TOK_DEV)
    routes_turns = jax.random.permutation(jax.random.fold_in(seeds[1], 3), PACKS * PACK_TOKENS // TOK_DEV)
    routes = jax.vmap(lambda own, number: shared_out(jax.random.fold_in(seeds[1], 2), own, number, TOK_DEV, EXPERTS, TOP, CAP, 1))(routes_keys, routes_turns).reshape((PACKS, PACK_TOKENS, TOP))
    gates = jnp.clip(jnp.exp(math.log(0.4) - 1.3862944 * jax.random.uniform(seeds[2], (PACKS, PACK_TOKENS, TOP), jnp.float32) ** level_of(seeds[2], (PACKS, PACK_TOKENS, TOP), ((0, 8), (1, 4)), -0.2, 0.2)), 0.1, 0.4)
    doc_starts = draw_doc_starts(jax.random.fold_in(seeds[11], 71), 0)
    attn_gain = jnp.clip(1.0 + 0.1 * jax.random.normal(seeds[4], (D,), jnp.float32), 0.5, 1.5)
    w_qkv = bell_draw(seeds[5], (D, QKV), D ** -0.5, 0.15625)
    w_out = bell_draw(seeds[6], (QUERY_HEADS * HEAD_SIZE, D), (max(1, 4 * D // PACK_TOKENS)) ** -0.5, 2.5)
    ffn_gain = jnp.clip(1.0 + 0.1 * jax.random.normal(seeds[7], (D,), jnp.float32), 0.5, 1.5)
    expert_gate_up = bell_draw(seeds[8], (EXPERTS, D, 2 * FF), D ** -0.5, 0.15625, ((0, 4),))
    expert_down = bell_draw(seeds[9], (EXPERTS, FF, D), (FF // 16) ** -0.5, 0.875, ((0, 4),))
    cotangent = bell_draw(seeds[10], (PACKS, PACK_TOKENS, D), 1.0, 6.0, ((0, 8), (1, 4)))
    return {"packed_in": packed_in, "routes": routes, "gates": gates, "doc_starts": doc_starts, "attn_gain": attn_gain, "w_qkv": w_qkv, "w_out": w_out, "ffn_gain": ffn_gain, "expert_gate_up": expert_gate_up, "expert_down": expert_down, "cotangent": cotangent}


epsilon = 1e-06
rope_base = 10000.0
negative_huge = -1e+30
highest = lax.Precision.HIGHEST

@jax.custom_vjp
def lower_bound(v):
    return lax.optimization_barrier(v.astype(jnp.bfloat16)).astype(jnp.float32)

@jax.custom_vjp
def low_back(v):
    return v

def low_keep(v):
    return (lower_bound(v), None)

def low_pass(kept, grad):
    return (grad,)

def back_keep(v):
    return (v, None)

def back_low(kept, grad):
    return (lower_bound(grad),)
lower_bound.defvjp(low_keep, low_pass)
low_back.defvjp(back_keep, back_low)

def smooth_gate(preact):
    return jax.nn.gelu(preact, approximate=True)

def norm_rows(values, gain):
    inverse = lax.rsqrt(lax.optimization_barrier(jnp.mean(values * values, axis=-1, keepdims=True)) + epsilon)
    return values * inverse * gain

def doc_begins(positions, starts):
    return lax.optimization_barrier(jnp.max(jnp.where(starts[None, :] <= positions[:, None], starts[None, :], 0), axis=1)).astype(jnp.int32)

def rope_tables(offsets, half_dim):
    frequency = rope_base ** (-(jnp.arange(half_dim, dtype=jnp.float32) * 2.0 / (2.0 * half_dim)))
    angles = offsets.astype(jnp.float32)[:, None] * frequency[None, :]
    return (jnp.cos(angles), jnp.sin(angles))

def apply_rotary(values, cosine_table, sine_values):
    half_dim = cosine_table.shape[1]
    first = values[..., :half_dim]
    second = values[..., half_dim:]
    cosine_wide = cosine_table[:, None, :]
    sine_wide = sine_values[:, None, :]
    return jnp.concatenate([first * cosine_wide - second * sine_wide, second * cosine_wide + first * sine_wide], axis=-1)

def attention(query_matrix, key_matrix, value_matrix, positions, begins):
    scaling = HEAD_SIZE ** (-0.5)

    def one_block(block_index):
        first_row = (block_index * QB).astype(jnp.int32)
        query_block = lax.dynamic_slice_in_dim(query_matrix, first_row, QB, 0)
        query_pos = lax.dynamic_slice_in_dim(positions, first_row, QB, 0)
        query_begin = lax.dynamic_slice_in_dim(begins, first_row, QB, 0)
        scores = low_back(jnp.einsum('qgha,kga->ghqk', query_block, key_matrix, precision=highest) * scaling)
        allowed = (positions[None, :] <= query_pos[:, None]) & (positions[None, :] >= query_begin[:, None])
        probs = jax.nn.softmax(jnp.where(allowed, scores, negative_huge), axis=-1)
        return jnp.einsum('ghqk,kga->qgha', lower_bound(probs), value_matrix, precision=highest)
    blocks = lax.map(jax.checkpoint(one_block), jnp.arange(PACK_TOKENS // QB, dtype=jnp.int32))
    return blocks.reshape(PACK_TOKENS, QUERY_HEADS * HEAD_SIZE)

def layer(tokens, weights, routes, gates, starts):
    attn_gain, w_qkv, w_out, ffn_gain, gate_up_all, down_all = weights
    positions = jnp.arange(PACK_TOKENS, dtype=jnp.int32)
    begins = doc_begins(positions, starts)
    cosine_table, sine_values = rope_tables(positions - begins, HEAD_SIZE // 2)
    query_width = QUERY_HEADS * HEAD_SIZE
    key_value_width = KEY_VALUE_HEADS * HEAD_SIZE
    projected_rows = low_back(jnp.dot(lower_bound(norm_rows(tokens, attn_gain)), w_qkv, precision=highest))
    query_matrix = lower_bound(apply_rotary(projected_rows[:, :query_width].reshape(PACK_TOKENS, QUERY_HEADS, HEAD_SIZE), cosine_table, sine_values))
    query_matrix = query_matrix.reshape(PACK_TOKENS, KEY_VALUE_HEADS, QUERY_HEADS // KEY_VALUE_HEADS, HEAD_SIZE)
    key_matrix = lower_bound(apply_rotary(projected_rows[:, query_width:query_width + key_value_width].reshape(PACK_TOKENS, KEY_VALUE_HEADS, HEAD_SIZE), cosine_table, sine_values))
    value_matrix = lower_bound(projected_rows[:, query_width + key_value_width:].reshape(PACK_TOKENS, KEY_VALUE_HEADS, HEAD_SIZE))
    attended = lower_bound(low_back(attention(query_matrix, key_matrix, value_matrix, positions, begins)))
    residual = tokens + low_back(jnp.dot(attended, w_out, precision=highest))
    normed = lower_bound(norm_rows(residual, ffn_gain))
    mixture = jnp.zeros_like(residual)
    for expert in range(EXPERTS):
        dispatched = low_back(normed)
        gate_up = low_back(jnp.dot(dispatched, gate_up_all[expert], precision=highest))
        hidden = lower_bound(smooth_gate(gate_up[:, :FF]) * gate_up[:, FF:])
        produced = lower_bound(low_back(jnp.dot(hidden, down_all[expert], precision=highest)))
        share = lax.optimization_barrier(jnp.sum(jnp.where(routes == expert, gates, 0.0), axis=1))
        mixture = mixture + share[:, None] * produced
    return residual + mixture

def reference(packed_in, routes, gates, doc_starts, attn_gain, w_qkv, w_out, ffn_gain, expert_gate_up, expert_down, cotangent):
    weights = (attn_gain, w_qkv.astype(jnp.float32), w_out.astype(jnp.float32), ffn_gain, expert_gate_up.astype(jnp.float32), expert_down.astype(jnp.float32))

    def per_pack(grad_sums, inputs):
        tokens, pack_routes, pack_gates, starts, upstream = inputs

        def forward(token_values, weight_values):
            return layer(token_values, weight_values, pack_routes, pack_gates, starts)
        result, pullback = jax.vjp(forward, tokens.astype(jnp.float32), weights)
        token_grad, weight_grads = pullback(upstream.astype(jnp.float32))
        grad_sums = jax.tree.map(jnp.add, grad_sums, weight_grads)
        return (grad_sums, (result.astype(jnp.bfloat16), token_grad))
    zero_sums = jax.tree.map(jnp.zeros_like, weights)
    grad_sums, outputs = lax.scan(per_pack, zero_sums, (packed_in, routes, gates, doc_starts, cotangent))
    return (outputs[0], outputs[1], grad_sums[0], grad_sums[1], grad_sums[2], grad_sums[3], grad_sums[4], grad_sums[5])
```

```python
import jax
import jax.numpy as jnp
from jax import lax
from jax.experimental import pallas as pl
from jax.experimental.pallas import tpu as pltpu
from jax.sharding import PartitionSpec as P

D = 1536
QUERY_HEADS = 12
KEY_VALUE_HEADS = 2
HEAD_SIZE = 128
FF = 768
TOP = 4
CAP = 192


epsilon = 1e-06
rope_base = 10000.0
negative_huge = -1e30


def smooth_gate(preact):
    return jax.nn.gelu(preact, approximate=True)


def norm_rows(values, gain):
    inverse = lax.rsqrt(jnp.mean(values * values, axis=-1, keepdims=True) + epsilon)
    return (values * inverse * gain, inverse)


def norm_back(values, inverse, gain, upstream):
    scaled = upstream * gain
    inner = jnp.mean(scaled * values, axis=-1, keepdims=True)
    grad_in = inverse * scaled - values * inverse * inverse * inverse * inner
    grad_gain = jnp.sum(upstream * values * inverse, axis=0)
    return (grad_in, grad_gain)


def doc_begins(positions, starts):
    return jnp.max(jnp.where(starts[None, :] <= positions[:, None], starts[None, :], 0), axis=1)


def rope_tables(offsets, half_dim):
    frequency = rope_base ** (-(jnp.arange(half_dim, dtype=jnp.float32) * 2.0 / (2.0 * half_dim)))
    angles = offsets.astype(jnp.float32)[:, None] * frequency[None, :]
    return (jnp.cos(angles), jnp.sin(angles))


def apply_rotary(values, cosine_table, sine_values, forward):
    half_dim = cosine_table.shape[1]
    first = values[..., :half_dim]
    second = values[..., half_dim:]
    cosine_wide = cosine_table[:, None, :]
    sine_wide = sine_values[:, None, :]
    if forward:
        return jnp.concatenate(
            [first * cosine_wide - second * sine_wide, second * cosine_wide + first * sine_wide],
            axis=-1,
        )
    return jnp.concatenate(
        [first * cosine_wide + second * sine_wide, second * cosine_wide - first * sine_wide],
        axis=-1,
    )


def fold_keys(
    folded, key_matrix, value_matrix, key_start, query_matrix, positions, begins, scaling
):
    running_max, denominator, weighted = folded
    row_count = key_matrix.shape[0]
    key_pos = key_start + jnp.arange(row_count, dtype=jnp.int32)
    allowed = (key_pos[None, :] <= positions[:, None]) & (key_pos[None, :] >= begins[:, None])
    scores = (
        jnp.einsum("qgha,kga->ghqk", query_matrix, key_matrix, preferred_element_type=jnp.float32)
        * scaling
    )
    masked = jnp.where(allowed, scores, negative_huge)
    new_max = jnp.maximum(running_max, jnp.max(masked, axis=-1))
    weights = jnp.where(allowed, jnp.exp(scores - new_max[..., None]), 0.0)
    shrink = jnp.exp(running_max - new_max)
    denominator = denominator * shrink + jnp.sum(weights, axis=-1)
    weighted = weighted * shrink[..., None] + jnp.einsum(
        "ghqk,kga->ghqa",
        weights.astype(jnp.bfloat16),
        value_matrix,
        preferred_element_type=jnp.float32,
    )
    return (new_max, denominator, weighted)


def attend_back(
    query_matrix,
    output_gradient,
    logsum,
    delta,
    positions,
    begins,
    key_matrix,
    value_matrix,
    key_start,
    scaling,
):
    row_count = key_matrix.shape[0]
    key_pos = key_start + jnp.arange(row_count, dtype=jnp.int32)
    allowed = (key_pos[None, :] <= positions[:, None]) & (key_pos[None, :] >= begins[:, None])
    scores = (
        jnp.einsum("qgha,kga->ghqk", query_matrix, key_matrix, preferred_element_type=jnp.float32)
        * scaling
    )
    probs = jnp.where(allowed, jnp.exp(scores - logsum[..., None]), 0.0)
    grad_probs = jnp.einsum(
        "ghqa,kga->ghqk", output_gradient, value_matrix, preferred_element_type=jnp.float32
    )
    grad_scores = (probs * (grad_probs - delta[..., None])).astype(jnp.bfloat16)
    grad_query = (
        jnp.einsum("ghqk,kga->ghqa", grad_scores, key_matrix, preferred_element_type=jnp.float32)
        * scaling
    )
    grad_key = (
        jnp.einsum("ghqk,qgha->kga", grad_scores, query_matrix, preferred_element_type=jnp.float32)
        * scaling
    )
    grad_value = jnp.einsum(
        "ghqk,ghqa->kga",
        probs.astype(jnp.bfloat16),
        output_gradient,
        preferred_element_type=jnp.float32,
    )
    return (grad_query, grad_key, grad_value)


def body(
    packed_in,
    routes,
    gates,
    doc_starts,
    attn_gain,
    w_qkv,
    w_out,
    ffn_gain,
    expert_gate_up,
    expert_down,
    cotangent,
):
    tokens = packed_in[0].astype(jnp.float32)
    token_count = tokens.shape[0]
    query_groups = QUERY_HEADS // KEY_VALUE_HEADS
    query_width = QUERY_HEADS * HEAD_SIZE
    key_value_width = KEY_VALUE_HEADS * HEAD_SIZE
    scaling = HEAD_SIZE ** (-0.5)
    contexts = lax.axis_size("context")
    own_index = lax.axis_index("context")
    positions = own_index * token_count + jnp.arange(token_count, dtype=jnp.int32)
    last_pos = own_index * token_count + token_count - 1
    begins = doc_begins(positions, doc_starts[0])
    cosine_table, sine_values = rope_tables(positions - begins, HEAD_SIZE // 2)
    normed_a, inverse_a = norm_rows(tokens, attn_gain)
    normed_ab = normed_a.astype(jnp.bfloat16)
    projected_rows = jnp.dot(normed_ab, w_qkv, preferred_element_type=jnp.float32)
    query_matrix = apply_rotary(
        projected_rows[:, :query_width].reshape(token_count, QUERY_HEADS, HEAD_SIZE),
        cosine_table,
        sine_values,
        True,
    )
    query_matrix = query_matrix.astype(jnp.bfloat16).reshape(
        token_count, KEY_VALUE_HEADS, query_groups, HEAD_SIZE
    )
    key_matrix = apply_rotary(
        projected_rows[:, query_width : query_width + key_value_width].reshape(
            token_count, KEY_VALUE_HEADS, HEAD_SIZE
        ),
        cosine_table,
        sine_values,
        True,
    )
    key_matrix = key_matrix.astype(jnp.bfloat16)
    value_matrix = (
        projected_rows[:, query_width + key_value_width :]
        .reshape(token_count, KEY_VALUE_HEADS, HEAD_SIZE)
        .astype(jnp.bfloat16)
    )
    query_layout = (KEY_VALUE_HEADS, query_groups, token_count, HEAD_SIZE)
    start_state = (
        jnp.full((KEY_VALUE_HEADS, query_groups, token_count), negative_huge, jnp.float32),
        jnp.zeros((KEY_VALUE_HEADS, query_groups, token_count), jnp.float32),
        jnp.zeros(query_layout, jnp.float32),
    )
    part_keys = lax.all_gather(key_matrix, "context", axis=0, tiled=True)
    part_values = lax.all_gather(value_matrix, "context", axis=0, tiled=True)
    row_count = part_keys.shape[0]
    width = 512 if row_count > 1024 and row_count % 512 == 0 else row_count

    def inner_step(block_index, state_now):
        offset = block_index * width
        block_keys = lax.dynamic_slice_in_dim(part_keys, block_index * width, width, 0)
        block_values = lax.dynamic_slice_in_dim(part_values, block_index * width, width, 0)

        def update(state_in):
            return fold_keys(
                state_in, block_keys, block_values, offset, query_matrix, positions, begins, scaling
            )

        def unchanged(state_in):
            return state_in

        return lax.cond(offset <= last_pos, update, unchanged, state_now)

    running_max, denominator, weighted = lax.fori_loop(
        0, row_count // width, inner_step, start_state
    )
    attended = weighted / denominator[..., None]
    logsum = running_max + jnp.log(denominator)
    merged_b = (
        jnp.transpose(attended, (2, 0, 1, 3)).reshape(token_count, query_width).astype(jnp.bfloat16)
    )
    residual = tokens + jnp.dot(merged_b, w_out, preferred_element_type=jnp.float32)
    normed_f, inverse_f = norm_rows(residual, ffn_gain)
    normed_fb = normed_f.astype(jnp.bfloat16)
    local_experts = expert_gate_up.shape[0]
    expert_devices = lax.axis_size("expert")
    expert_total = local_experts * expert_devices
    chosen = routes[0].reshape(-1)
    onehot = (chosen[:, None] == jnp.arange(expert_total, dtype=jnp.int32)[None, :]).astype(
        jnp.int32
    )
    slots = jnp.sum((jnp.cumsum(onehot, axis=0) - onehot) * onehot, axis=1)
    repeated = jnp.repeat(normed_fb, TOP, axis=0)
    outgoing = jnp.zeros((expert_total, CAP, D), jnp.bfloat16).at[chosen, slots].set(repeated)
    outgoing = outgoing.reshape(expert_devices, local_experts, CAP, D)
    arrived_rows = lax.all_to_all(outgoing, "expert", split_axis=0, concat_axis=0, tiled=True)
    gate_up_rows = jnp.einsum(
        "sjcd,jdf->sjcf", arrived_rows, expert_gate_up, preferred_element_type=jnp.float32
    )
    hidden = (smooth_gate(gate_up_rows[..., :FF]) * gate_up_rows[..., FF:]).astype(jnp.bfloat16)
    produced = jnp.einsum("sjcf,jfd->sjcd", hidden, expert_down, preferred_element_type=jnp.float32)
    returned_rows = lax.all_to_all(
        produced.astype(jnp.bfloat16), "expert", split_axis=0, concat_axis=0, tiled=True
    )
    picked = (
        returned_rows.reshape(expert_total, CAP, D)[chosen, slots]
        .astype(jnp.float32)
        .reshape(token_count, TOP, D)
    )
    gate_values = gates[0]
    mixture = jnp.sum(gate_values[..., None] * picked, axis=1)
    packed_out = (residual + mixture).astype(jnp.bfloat16)
    upstream = cotangent[0].astype(jnp.float32)
    grad_mix = (
        (gate_values[..., None] * upstream[:, None, :])
        .astype(jnp.bfloat16)
        .reshape(token_count * TOP, D)
    )
    grad_send = jnp.zeros((expert_total, CAP, D), jnp.bfloat16).at[chosen, slots].set(grad_mix)
    grad_send = grad_send.reshape(expert_devices, local_experts, CAP, D)
    grad_arrived = lax.all_to_all(grad_send, "expert", split_axis=0, concat_axis=0, tiled=True)
    gate_part = gate_up_rows[..., :FF]
    up_part = gate_up_rows[..., FF:]
    activated, gelu_back = jax.vjp(smooth_gate, gate_part)
    hidden_b = (activated * up_part).astype(jnp.bfloat16)
    grad_hidden = jnp.einsum(
        "sjcd,jfd->sjcf", grad_arrived, expert_down, preferred_element_type=jnp.float32
    )
    down_grad = jnp.einsum(
        "sjcf,sjcd->jfd", hidden_b, grad_arrived, preferred_element_type=jnp.float32
    )
    grad_gate = gelu_back(grad_hidden * up_part)[0]
    grad_gu = jnp.concatenate([grad_gate, grad_hidden * activated], axis=-1).astype(jnp.bfloat16)
    gate_up_grad = jnp.einsum(
        "sjcd,sjcf->jdf", arrived_rows, grad_gu, preferred_element_type=jnp.float32
    )
    grad_rows = jnp.einsum(
        "sjcf,jdf->sjcd", grad_gu, expert_gate_up, preferred_element_type=jnp.float32
    )
    grad_back = lax.all_to_all(
        grad_rows.astype(jnp.bfloat16), "expert", split_axis=0, concat_axis=0, tiled=True
    )
    grad_picked = grad_back.reshape(expert_total, CAP, D)[chosen, slots].astype(jnp.float32)
    grad_normed_f = jnp.sum(grad_picked.reshape(token_count, TOP, D), axis=1)
    grad_resid_part, ffn_gain_grad = norm_back(residual, inverse_f, ffn_gain, grad_normed_f)
    grad_residual = upstream + grad_resid_part
    grad_branch = grad_residual.astype(jnp.bfloat16)
    out_proj_grad = jnp.einsum(
        "td,tf->df", merged_b, grad_branch, preferred_element_type=jnp.float32
    )
    merged_gradient = jnp.einsum(
        "tf,df->td", grad_branch, w_out, preferred_element_type=jnp.float32
    ).astype(jnp.bfloat16)
    output_gradient = jnp.transpose(
        merged_gradient.reshape(token_count, KEY_VALUE_HEADS, query_groups, HEAD_SIZE), (1, 2, 0, 3)
    )
    delta = jnp.sum(output_gradient.astype(jnp.float32) * attended, axis=-1)

    def block_back(part_keys, part_values, key_start):

        def compute(operands):
            return attend_back(
                query_matrix,
                output_gradient,
                logsum,
                delta,
                positions,
                begins,
                operands[0],
                operands[1],
                key_start,
                scaling,
            )

        def nothing(operands):
            return (
                jnp.zeros(query_layout, jnp.float32),
                jnp.zeros(operands[0].shape, jnp.float32),
                jnp.zeros(operands[1].shape, jnp.float32),
            )

        return lax.cond(key_start <= last_pos, compute, nothing, (part_keys, part_values))

    grad_query = jnp.zeros(query_layout, jnp.float32)
    complete_keys, whole_values = (
        lax.all_gather(key_matrix, "context", axis=0, tiled=True),
        lax.all_gather(value_matrix, "context", axis=0, tiled=True),
    )
    block_span = 2 * token_count

    def block_turn(turn_index, block_state):
        keys_grad_all, values_grad_all, query_sum = block_state
        offset = turn_index * block_span
        add_query, add_key, add_value = block_back(
            lax.dynamic_slice_in_dim(complete_keys, offset, block_span, 0),
            lax.dynamic_slice_in_dim(whole_values, offset, block_span, 0),
            offset,
        )
        keys_grad_all = lax.dynamic_update_slice_in_dim(keys_grad_all, add_key, offset, 0)
        values_grad_all = lax.dynamic_update_slice_in_dim(values_grad_all, add_value, offset, 0)
        return (keys_grad_all, values_grad_all, query_sum + add_query)

    zero_filled = jnp.zeros((complete_keys.shape[0], KEY_VALUE_HEADS, HEAD_SIZE), jnp.float32)
    finished = lax.fori_loop(0, contexts // 2, block_turn, (zero_filled, zero_filled, grad_query))
    grad_keys, grad_values = (
        lax.psum_scatter(
            finished[0].astype(jnp.bfloat16), "context", scatter_dimension=0, tiled=True
        ).astype(jnp.float32),
        lax.psum_scatter(
            finished[1].astype(jnp.bfloat16), "context", scatter_dimension=0, tiled=True
        ).astype(jnp.float32),
    )
    grad_query = finished[2]
    grad_q_rows = apply_rotary(
        jnp.transpose(grad_query, (2, 0, 1, 3)).reshape(token_count, QUERY_HEADS, HEAD_SIZE),
        cosine_table,
        sine_values,
        False,
    )
    grad_k_rows = apply_rotary(grad_keys, cosine_table, sine_values, False)
    grad_projected = jnp.concatenate(
        [
            grad_q_rows.reshape(token_count, query_width),
            grad_k_rows.reshape(token_count, key_value_width),
            grad_values.reshape(token_count, key_value_width),
        ],
        axis=-1,
    ).astype(jnp.bfloat16)
    qkv_grad = jnp.einsum(
        "td,tf->df", normed_ab, grad_projected, preferred_element_type=jnp.float32
    )
    grad_normed_a = jnp.einsum(
        "tf,df->td", grad_projected, w_qkv, preferred_element_type=jnp.float32
    )
    grad_in_part, attn_gain_grad = norm_back(tokens, inverse_a, attn_gain, grad_normed_a)
    packed_grad = grad_residual + grad_in_part
    summed = (
        lax.psum_scatter(
            attn_gain_grad.astype(jnp.bfloat16), "context", scatter_dimension=0, tiled=True
        ).astype(jnp.float32),
        lax.psum_scatter(
            qkv_grad.astype(jnp.bfloat16), "context", scatter_dimension=0, tiled=True
        ).astype(jnp.float32),
        lax.psum_scatter(
            out_proj_grad.astype(jnp.bfloat16), "context", scatter_dimension=0, tiled=True
        ).astype(jnp.float32),
        lax.psum_scatter(
            ffn_gain_grad.astype(jnp.bfloat16), "context", scatter_dimension=0, tiled=True
        ).astype(jnp.float32),
        lax.psum_scatter(
            gate_up_grad.astype(jnp.bfloat16), "context", scatter_dimension=1, tiled=True
        ).astype(jnp.float32),
        lax.psum_scatter(
            down_grad.astype(jnp.bfloat16), "context", scatter_dimension=1, tiled=True
        ).astype(jnp.float32),
    )
    dense_rows = (summed[0], summed[1], summed[2], summed[3])
    expert_sums = (
        lax.psum(summed[4].astype(jnp.bfloat16), "dp").astype(jnp.float32),
        lax.psum(summed[5].astype(jnp.bfloat16), "dp").astype(jnp.float32),
    )
    shared = (
        lax.psum(dense_rows[0].astype(jnp.bfloat16), ("dp", "expert")).astype(jnp.float32),
        lax.psum(dense_rows[1].astype(jnp.bfloat16), ("dp", "expert")).astype(jnp.float32),
        lax.psum(dense_rows[2].astype(jnp.bfloat16), ("dp", "expert")).astype(jnp.float32),
        lax.psum(dense_rows[3].astype(jnp.bfloat16), ("dp", "expert")).astype(jnp.float32),
    )
    return (
        packed_out[None],
        packed_grad[None],
        shared[0],
        shared[1],
        shared[2],
        shared[3],
        expert_sums[0],
        expert_sums[1],
    )


MESH = pl.DeviceIdType.MESH
BF = jnp.bfloat16
F32 = jnp.float32
NN = (((1,), (0,)), ((), ()))
NT = (((1,), (1,)), ((), ()))
TN = (((0,), (0,)), ((), ()))


def matmul(left, right, dims=NN):
    return lax.dot_general(left, right, dims, preferred_element_type=F32)


def flip(axis, bit):
    index = lax.axis_index(axis)
    return {axis: index + bit - 2 * bit * ((index // bit) % 2)}


def greet(peers):
    barrier = pltpu.get_barrier_semaphore()
    for peer in peers:
        pl.semaphore_signal(barrier, inc=1, device_id=peer, device_id_type=MESH)
    pl.semaphore_wait(barrier, len(peers))


def remote(src, dst, send_sem, recv_sem, peer):
    return pltpu.make_async_remote_copy(
        src_ref=src,
        dst_ref=dst,
        send_sem=send_sem,
        recv_sem=recv_sem,
        device_id=peer,
        device_id_type=MESH,
    )


def other(axis, distance):
    size = lax.axis_size(axis)
    return {axis: lax.rem(lax.axis_index(axis) + distance, size)}


def mate(code):
    expert = lax.axis_index("expert")
    for bit in (1, 2):
        if code & bit:
            expert = expert + bit - 2 * bit * ((expert // bit) % 2)
    return {**flip("dp", 1), "expert": expert} if code & 4 else {"expert": expert}


class GroupGather:
    def __init__(self, own, held, sems, rows):
        half = rows // 2
        self.x, self.y, self.core = flip("dp", 1), flip("expert", 2), flip("expert", 1)

        def part(which, index, amount=1):
            return held.at[pl.ds(which * 2 * rows + index * half, amount * half)]

        def link(number, src, dst, peer):
            return remote(src, dst, sems.at[0, number], sems.at[1, number], peer)

        first, second = own.at[pl.ds(0, half)], own.at[pl.ds(half, half)]
        self.links = [
            link(0, first, part(1, 0), self.x),
            link(1, second, part(1, 1), self.y),
            link(2, first, part(2, 0), self.y),
            link(3, second, part(2, 1), self.x),
            link(4, part(1, 0), part(3, 0), self.y),
            link(5, part(1, 1), part(3, 1), self.x),
        ]
        self.cores = [link(6, own, part(0, 2, 2), self.core)]
        for which in range(1, 4):
            self.cores.append(
                link(6 + which, part(which, 0, 2), part(which, 2, 2), self.core)
            )

    def start(self):
        self.cores[0].start()
        for link in self.links[:4]:
            link.start()

    def forward(self, which):
        for link in self.links[2 * which - 2 : 2 * which]:
            link.wait_recv()
        if which == 1:
            for link in self.links[4:]:
                link.start()
        self.cores[which].start()

    def arrived(self, which):
        self.cores[which].wait_recv()

    def finish(self):
        for link in self.links + self.cores:
            link.wait_send()


GATHER_SEMS = pltpu.SemaphoreType.DMA((2, 10))


def rotate(values, cosine, sine):
    return values * cosine + pltpu.roll(values, values.shape[1] // 2, 1) * sine


def attention_kernel(
    x_ref,
    share_ref,
    begin_ref,
    cos_ref,
    sin_ref,
    attn_gain_ref,
    ffn_gain_ref,
    c_ref,
    w_qkv_ref,
    w_out_ref,
    h1_ref,
    q_ref,
    att_ref,
    logsum_ref,
    merged_ref,
    residual_ref,
    h2_ref,
    kv_ref,
    c_all_ref,
    share_all_ref,
    w_qkv,
    w_out,
    kv,
    accumulated,
    top,
    total,
    bias,
    load_sems,
    kv_sems,
    share_sems,
    gather_sems,
):
    contexts = lax.axis_size("context")
    me = lax.axis_index("context")
    rows = x_ref.shape[0]
    query_width = QUERY_HEADS * HEAD_SIZE
    heads = QUERY_HEADS // KEY_VALUE_HEADS
    scaling = HEAD_SIZE ** (-0.5)

    loads = [
        pltpu.make_async_copy(
            w_qkv_ref.at[:, query_width:], w_qkv.at[:, query_width:], load_sems.at[0]
        ),
        pltpu.make_async_copy(
            w_qkv_ref.at[:, :query_width], w_qkv.at[:, :query_width], load_sems.at[1]
        ),
        pltpu.make_async_copy(w_out_ref, w_out, load_sems.at[2]),
        pltpu.make_async_copy(c_ref, c_all_ref.at[pl.ds(0, rows)], load_sems.at[3]),
        pltpu.make_async_copy(share_ref, share_all_ref.at[0], load_sems.at[4]),
    ]
    for load in loads:
        load.start()

    mates = [mate(code) for code in range(1, 8)]
    greet([other("context", step) for step in range(1, contexts)] + mates)

    gather = GroupGather(c_ref, c_all_ref, gather_sems, rows)
    gather.start()
    shares = [
        remote(
            share_ref,
            share_all_ref.at[1 + index],
            share_sems.at[0, index],
            share_sems.at[1, index],
            mate,
        )
        for index, mate in enumerate(mates)
    ]
    for share in shares:
        share.start()

    x = x_ref[...].astype(F32)
    inverse = lax.rsqrt(jnp.mean(x * x, axis=-1, keepdims=True) + epsilon)
    h1_ref[...] = (x * inverse * attn_gain_ref[...]).astype(BF)

    loads[0].wait()
    projected = matmul(h1_ref[...], w_qkv[:, query_width:])
    for head in range(KEY_VALUE_HEADS):
        lanes = slice(head * HEAD_SIZE, (head + 1) * HEAD_SIZE)
        kv[me, :, lanes] = rotate(projected[:, lanes], cos_ref[...], sin_ref[...]).astype(BF)
    kv[me, :, KEY_VALUE_HEADS * HEAD_SIZE :] = projected[:, KEY_VALUE_HEADS * HEAD_SIZE :].astype(
        BF
    )

    def kv_copy(step):
        return remote(
            kv.at[me],
            kv.at[me],
            kv_sems.at[0, step],
            kv_sems.at[1, step],
            {"context": lax.rem(me + step, contexts)},
        )

    for step in range(1, contexts):

        @pl.when(me + step < contexts)
        def _():
            kv_copy(step).start()

    loads[1].wait()
    chunk = 4 * HEAD_SIZE
    for offset in range(0, query_width, chunk):
        projected = matmul(h1_ref[...], w_qkv[:, offset : offset + chunk])
        for head in range(chunk // HEAD_SIZE):
            lanes = slice(head * HEAD_SIZE, (head + 1) * HEAD_SIZE)
            q_ref[offset // HEAD_SIZE + head] = rotate(
                projected[:, lanes], cos_ref[...], sin_ref[...]
            ).astype(BF)

    top[...] = jnp.full_like(top, negative_huge)
    total[...] = jnp.zeros_like(total)
    accumulated[...] = jnp.zeros_like(accumulated)
    query_pos = me * rows + lax.broadcasted_iota(jnp.int32, (rows, rows), 1)
    begin_row = begin_ref[...]

    def fold(block):
        key_pos = block * rows + lax.broadcasted_iota(jnp.int32, (rows, rows), 0)
        allowed = (key_pos <= query_pos) & (key_pos >= begin_row)
        bias[...] = jnp.where(allowed, 0.0, negative_huge)
        for head in range(QUERY_HEADS):
            group = head // heads
            keys = kv[block, :, group * HEAD_SIZE : (group + 1) * HEAD_SIZE]
            values = kv[
                block,
                :,
                (KEY_VALUE_HEADS + group) * HEAD_SIZE : (KEY_VALUE_HEADS + group + 1) * HEAD_SIZE,
            ]
            scores = matmul(keys, q_ref[head], NT) * scaling + bias[...]
            old = top[head : head + 1]
            new = jnp.maximum(old, jnp.max(scores, axis=0, keepdims=True))
            weights = jnp.exp(scores - new)
            shrink = jnp.exp(old - new)
            top[head : head + 1] = new
            total[head : head + 1] = total[head : head + 1] * shrink + jnp.sum(
                weights, axis=0, keepdims=True
            )
            accumulated[head] = accumulated[head] * shrink + matmul(
                values, weights.astype(BF), TN
            )

    fold(me)

    def earlier(step, carry):
        kv_arrival(step).wait_recv()
        fold(me - step)
        return carry

    def kv_arrival(step):
        return remote(
            kv.at[me],
            kv.at[lax.rem(me - step + contexts, contexts)],
            kv_sems.at[0, step],
            kv_sems.at[1, step],
            {"context": lax.rem(me + step, contexts)},
        )

    gather.forward(1)
    lax.fori_loop(1, me + 1, earlier, 0)
    gather.forward(2)

    loads[2].wait()
    for head in range(QUERY_HEADS):
        attended = accumulated[head] / total[head : head + 1]
        att_ref[head] = attended
        merged_ref[:, head * HEAD_SIZE : (head + 1) * HEAD_SIZE] = attended.T.astype(BF)
    logsum_ref[...] = jnp.where(total[...] > 0, top[...] + jnp.log(total[...]), 0.0)
    residual = x_ref[...].astype(F32) + matmul(merged_ref[...], w_out[...])
    residual_ref[...] = residual
    inverse = lax.rsqrt(jnp.mean(residual * residual, axis=-1, keepdims=True) + epsilon)
    h2_ref[...] = (residual * inverse * ffn_gain_ref[...]).astype(BF)

    def keep(block, carry):
        copy = pltpu.make_async_copy(kv.at[block], kv_ref.at[block], load_sems.at[5])
        copy.start()
        copy.wait()
        return carry

    lax.fori_loop(0, me + 1, keep, 0)
    gather.forward(3)
    for which in range(4):
        gather.arrived(which)
    gather.finish()
    for share in shares:
        share.wait()
    loads[3].wait()
    loads[4].wait()
    for step in range(1, contexts):

        @pl.when(me + step < contexts)
        def _():
            kv_copy(step).wait_send()


VM = pl.BlockSpec(memory_space=pltpu.VMEM)
ANY = pl.BlockSpec(memory_space=pl.ANY)


def attention_forward(
    x, share, begins, cosine, sine, attn_gain, ffn_gain, cotangent, w_qkv, w_out
):
    rows = x.shape[0]
    contexts = lax.axis_size("context")
    group = lax.axis_size("dp") * lax.axis_size("expert")
    kv_width = 2 * KEY_VALUE_HEADS * HEAD_SIZE
    padded = -(-QUERY_HEADS // 8) * 8
    shape = jax.ShapeDtypeStruct
    return pl.pallas_call(
        attention_kernel,
        out_shape=[
            shape((rows, D), BF),
            shape((QUERY_HEADS, rows, HEAD_SIZE), BF),
            shape((QUERY_HEADS, HEAD_SIZE, rows), F32),
            shape((padded, rows), F32),
            shape((rows, D), BF),
            shape((rows, D), F32),
            shape((rows, D), BF),
            shape((contexts, rows, kv_width), BF),
            shape((group * rows, D), BF),
            shape((group,) + share.shape, F32),
        ],
        in_specs=[VM] * 7 + [ANY] * 3,
        out_specs=[VM] * 7 + [ANY] * 3,
        scratch_shapes=[
            pltpu.VMEM(w_qkv.shape, BF),
            pltpu.VMEM(w_out.shape, BF),
            pltpu.VMEM((contexts, rows, kv_width), BF),
            pltpu.VMEM((QUERY_HEADS, HEAD_SIZE, rows), F32),
            pltpu.VMEM((padded, rows), F32),
            pltpu.VMEM((padded, rows), F32),
            pltpu.VMEM((rows, rows), F32),
            pltpu.SemaphoreType.DMA((6,)),
            pltpu.SemaphoreType.DMA((2, contexts)),
            pltpu.SemaphoreType.DMA((2, group - 1)),
            GATHER_SEMS,
        ],
        compiler_params=pltpu.CompilerParams(
            collective_id=0, has_side_effects=True, vmem_limit_bytes=56 << 20
        ),
        cost_estimate=pl.CostEstimate(
            flops=2 * rows * D * 4096, bytes_accessed=30 << 20, transcendentals=rows * rows * 12
        ),
    )(x, share, begins, cosine, sine, attn_gain, ffn_gain, cotangent, w_qkv, w_out)


def prepare(routes, gates, doc_starts, rows, expert_total):
    positions = lax.axis_index("context") * rows + jnp.arange(rows, dtype=jnp.int32)
    begins = doc_begins(positions, doc_starts[0])
    cosine, sine = rope_tables(positions - begins, HEAD_SIZE // 2)
    cosine = jnp.concatenate([cosine, cosine], axis=1)
    sine = jnp.concatenate([-sine, sine], axis=1)
    named = routes[0][None] == jnp.arange(expert_total, dtype=jnp.int32)[:, None, None]
    share = jnp.sum(jnp.where(named, gates[0][None], 0.0), axis=2)
    return begins[None, :], cosine, sine, share


SLOT_CODES = ((0, 0, 1, 1), (4, 2, 5, 3), (2, 4, 3, 5), (6, 6, 7, 7))


def gelu_parts(gate):
    slope = 0.7978845608
    bend = 0.044715
    square = gate * gate
    tanh = jnp.tanh(slope * gate * (1.0 + bend * square))
    half = 0.5 * (1.0 + tanh)
    grad = half + 0.5 * slope * gate * (1.0 - tanh * tanh) * (1.0 + 3.0 * bend * square)
    return gate * half, grad


def experts_kernel(
    h2_ref,
    share_ref,
    c_all_ref,
    gate_up_ref,
    down_ref,
    h2_all_ref,
    dgu_ref,
    hidden_ref,
    du_ref,
    w_gu,
    w_down,
    h2_all,
    c_all,
    dhid,
    gu,
    hidden,
    dgu,
    du,
    share,
    load_sems,
    out_sems,
    gather_sems,
):
    rows = h2_ref.shape[0]
    half = rows // 2
    two = 2 * rows
    dp = lax.axis_index("dp")
    loads = [
        pltpu.make_async_copy(down_ref.at[dp], w_down, load_sems.at[0]),
        pltpu.make_async_copy(c_all_ref, c_all, load_sems.at[1]),
        pltpu.make_async_copy(gate_up_ref.at[dp], w_gu, load_sems.at[2]),
    ]
    for load in loads:
        load.start()
    greet([flip("dp", 1), flip("expert", 2), flip("expert", 1)])
    gather = GroupGather(h2_ref, h2_all, gather_sems, rows)
    gather.start()
    h2_all[0:rows] = h2_ref[...]

    expert = lax.axis_index("expert") * lax.axis_size("dp") + dp
    columns = []
    for code in range(8):
        turned = share_ref[code].T
        mine = lax.broadcasted_iota(jnp.int32, turned.shape, 1) == expert
        columns.append(jnp.sum(jnp.where(mine, turned, 0.0), axis=1, keepdims=True))
    for which, codes in enumerate(SLOT_CODES):
        for index, code in enumerate(codes):
            part = (index % 2) * half
            share[pl.ds(which * two + index * half, half), :] = columns[code][part : part + half]

    loads[0].wait()
    loads[1].wait()
    for which in range(4):
        span = slice(which * two, (which + 1) * two)
        dhid[span] = matmul(c_all[span], w_down[...], NT)
    loads[2].wait()

    outs = []

    def out(number, src, dst, span):
        copy = pltpu.make_async_copy(src.at[span], dst.at[span], out_sems.at[number])
        copy.start()
        outs.append(copy)

    for which in range(4):
        span = slice(which * two, (which + 1) * two)
        place = pl.ds(which * two, two)
        if which > 1:
            gather.forward(which)
        gather.arrived(which)
        out(4 * which, h2_all, h2_all_ref, place)
        gu[...] = matmul(h2_all[span], w_gu[...])

        def activate(step, carry):
            near = pl.ds(pl.multiple_of(step * half, half), half)
            far = pl.ds(pl.multiple_of(which * two + step * half, half), half)
            up = gu[near, FF:]
            activated, grad = gelu_parts(gu[near, :FF])
            scale = share[far, :]
            upstream = dhid[far, :] * scale
            hidden[far, :] = (activated * up * scale).astype(BF)
            dgu[far, :FF] = (upstream * up * grad).astype(BF)
            dgu[far, FF:] = (upstream * activated).astype(BF)
            return carry

        lax.fori_loop(0, 4, activate, 0)
        if which == 0:
            gather.forward(1)
        out(4 * which + 1, dgu, dgu_ref, place)
        out(4 * which + 2, hidden, hidden_ref, place)
        du[span] = matmul(dgu[span], w_gu[...], NT).astype(BF)
        out(4 * which + 3, du, du_ref, place)
    gather.finish()
    for copy in outs:
        copy.wait()


def experts(h2, share_all, c_all, gate_up, down):
    rows = h2.shape[0]
    total = 8 * rows
    shape = jax.ShapeDtypeStruct
    return pl.pallas_call(
        experts_kernel,
        out_shape=[
            shape((total, D), BF),
            shape((total, 2 * FF), BF),
            shape((total, FF), BF),
            shape((total, D), BF),
        ],
        in_specs=[VM] * 2 + [ANY] * 3,
        out_specs=[ANY] * 4,
        scratch_shapes=[
            pltpu.VMEM(gate_up.shape[1:], BF),
            pltpu.VMEM(down.shape[1:], BF),
            pltpu.VMEM((total, D), BF),
            pltpu.VMEM((total, D), BF),
            pltpu.VMEM((total, FF), F32),
            pltpu.VMEM((2 * rows, 2 * FF), F32),
            pltpu.VMEM((total, FF), BF),
            pltpu.VMEM((total, 2 * FF), BF),
            pltpu.VMEM((total, D), BF),
            pltpu.VMEM((total, 1), F32),
            pltpu.SemaphoreType.DMA((3,)),
            pltpu.SemaphoreType.DMA((16,)),
            GATHER_SEMS,
        ],
        compiler_params=pltpu.CompilerParams(
            collective_id=1, has_side_effects=True, vmem_limit_bytes=60 << 20
        ),
        cost_estimate=pl.CostEstimate(
            flops=2 * total * D * FF * 5, bytes_accessed=50 << 20, transcendentals=total * FF
        ),
    )(h2, share_all, c_all, gate_up, down)


def fast_body(
    packed_in,
    routes,
    gates,
    doc_starts,
    attn_gain,
    w_qkv,
    w_out,
    ffn_gain,
    expert_gate_up,
    expert_down,
    cotangent,
):
    tokens = packed_in[0].astype(F32)
    rows = tokens.shape[0]
    heads = QUERY_HEADS // KEY_VALUE_HEADS
    query_width = QUERY_HEADS * HEAD_SIZE
    key_value_width = KEY_VALUE_HEADS * HEAD_SIZE
    scaling = HEAD_SIZE ** (-0.5)
    contexts = lax.axis_size("context")
    dp = lax.axis_index("dp")
    own = dp * lax.axis_size("expert") + lax.axis_index("expert")
    begins, cosine, sine, share = prepare(routes, gates, doc_starts, rows, 8)
    (h1, query, att, logsum, merged, residual, h2, kv, c_all, share_all) = attention_forward(
        packed_in[0],
        share,
        begins,
        cosine,
        sine,
        attn_gain[None],
        ffn_gain[None],
        cotangent[0],
        w_qkv,
        w_out,
    )
    h2_all, dgu, hidden, du = experts(h2, share_all, c_all, expert_gate_up, expert_down)
    down_grad = matmul(hidden, c_all, TN)
    gate_up_grad = matmul(h2_all, dgu, TN)
    y = matmul(hidden, lax.dynamic_index_in_dim(expert_down, dp, 0, False)).astype(BF)

    def home(values):
        half = rows // 2
        parts = values.reshape(16, half, D)
        halves = {}
        for which, codes in enumerate(SLOT_CODES):
            for index, code in enumerate(codes):
                halves[code, index % 2] = parts[4 * which + index]
        stacked = jnp.stack(
            [jnp.concatenate([halves[code, 0], halves[code, 1]]) for code in range(8)]
        )
        placed = stacked[jnp.arange(8) ^ own].reshape(8 * rows, D)
        return lax.psum_scatter(placed, ("dp", "expert"), scatter_dimension=0, tiled=True)

    packed_out = (residual + home(y).astype(F32)).astype(BF)
    upstream = cotangent[0].astype(F32)
    inverse_f = lax.rsqrt(jnp.mean(residual * residual, axis=-1, keepdims=True) + epsilon)
    grad_part, ffn_gain_grad = norm_back(residual, inverse_f, ffn_gain, home(du).astype(F32))
    grad_residual = upstream + grad_part
    grad_branch = grad_residual.astype(BF)
    out_proj_grad = matmul(merged, grad_branch, TN)
    merged_gradient = matmul(grad_branch, w_out, NT).astype(BF)
    output_gradient = jnp.transpose(
        merged_gradient.reshape(rows, KEY_VALUE_HEADS, heads, HEAD_SIZE), (1, 2, 0, 3)
    )
    att = jnp.transpose(att, (0, 2, 1)).reshape(KEY_VALUE_HEADS, heads, rows, HEAD_SIZE)
    delta = jnp.sum(output_gradient.astype(F32) * att, axis=-1)
    logsum = logsum[:QUERY_HEADS].reshape(KEY_VALUE_HEADS, heads, rows)
    query = jnp.transpose(
        query.reshape(KEY_VALUE_HEADS, heads, rows, HEAD_SIZE), (2, 0, 1, 3)
    )
    known = jnp.arange(contexts) <= lax.axis_index("context")
    kv = jnp.where(known[:, None, None], kv, 0).reshape(contexts * rows, -1)
    keys = kv[:, :key_value_width].reshape(-1, KEY_VALUE_HEADS, HEAD_SIZE)
    values = kv[:, key_value_width:].reshape(-1, KEY_VALUE_HEADS, HEAD_SIZE)
    positions = lax.axis_index("context") * rows + jnp.arange(rows, dtype=jnp.int32)
    grad_query, grad_key, grad_value = attend_back(
        query,
        output_gradient,
        logsum,
        delta,
        positions,
        begins[0],
        keys,
        values,
        0,
        scaling,
    )
    both = jnp.concatenate([grad_key, grad_value], axis=1).astype(BF)
    both = lax.psum_scatter(both, "context", scatter_dimension=0, tiled=True).astype(F32)
    half_cos, half_sin = cosine[:, : HEAD_SIZE // 2], sine[:, HEAD_SIZE // 2 :]
    grad_q_rows = apply_rotary(
        jnp.transpose(grad_query, (2, 0, 1, 3)).reshape(rows, QUERY_HEADS, HEAD_SIZE),
        half_cos,
        half_sin,
        False,
    )
    grad_k_rows = apply_rotary(both[:, :KEY_VALUE_HEADS], half_cos, half_sin, False)
    grad_projected = jnp.concatenate(
        [
            grad_q_rows.reshape(rows, query_width),
            grad_k_rows.reshape(rows, key_value_width),
            both[:, KEY_VALUE_HEADS:].reshape(rows, key_value_width),
        ],
        axis=-1,
    ).astype(BF)
    qkv_grad = matmul(h1, grad_projected, TN)
    inverse_a = lax.rsqrt(jnp.mean(tokens * tokens, axis=-1, keepdims=True) + epsilon)
    grad_part, attn_gain_grad = norm_back(
        tokens, inverse_a, attn_gain, matmul(grad_projected, w_qkv, NT)
    )
    packed_grad = grad_residual + grad_part

    def scattered(values, axes):
        part = lax.psum_scatter(values.astype(BF), "context", scatter_dimension=0, tiled=True)
        return part if axes is None else lax.psum(part, axes).astype(F32)

    dense = ("dp", "expert")
    gate_up_own, down_own = scattered(gate_up_grad, None), scattered(down_grad, None)
    gate_up_both = lax.all_gather(gate_up_own, "dp", axis=0).astype(F32)
    down_both = lax.all_gather(down_own, "dp", axis=0).astype(F32)
    return (
        packed_out[None],
        packed_grad[None],
        scattered(attn_gain_grad, dense),
        scattered(qkv_grad, dense),
        scattered(out_proj_grad, dense),
        scattered(ffn_gain_grad, dense),
        gate_up_both,
        down_both,
    )


def fits(mesh):
    sizes = mesh.shape
    contexts = sizes["context"]
    return (
        sizes["dp"] == 2
        and sizes["expert"] == 4
        and D % (contexts * 128) == 0
        and FF % (contexts * 64) == 0
    )


def solution(mesh):
    chosen_body = fast_body if fits(mesh) else body
    placed = (
        P(("dp", "expert"), "context", None),
        P(("dp", "expert"), "context", None),
        P(("dp", "expert"), "context", None),
        P(("dp", "expert"), None),
        P(),
        P(),
        P(),
        P(),
        P("expert", None, None),
        P("expert", None, None),
        P(("dp", "expert"), "context", None),
    )
    return jax.shard_map(
        chosen_body,
        mesh=mesh,
        in_specs=placed,
        out_specs=(
            P(("dp", "expert"), "context", None),
            P(("dp", "expert"), "context", None),
            P("context"),
            P("context", None),
            P("context", None),
            P("context"),
            P("expert", "context", None),
            P("expert", "context", None),
        ),
        check_vma=False,
    )
```

```python
import jax
import jax.numpy as jnp
from jax import lax
from jax.experimental import pallas as pl
from jax.experimental.pallas import tpu as pltpu
from jax.sharding import PartitionSpec as P

D = 1536
QUERY_HEADS = 12
KEY_VALUE_HEADS = 2
HEAD_SIZE = 128
FF = 768
TOP = 4
CAP = 192


epsilon = 1e-06
rope_base = 10000.0
negative_huge = -1e30


def smooth_gate(preact):
    return jax.nn.gelu(preact, approximate=True)


def norm_rows(values, gain):
    inverse = lax.rsqrt(jnp.mean(values * values, axis=-1, keepdims=True) + epsilon)
    return (values * inverse * gain, inverse)


def norm_back(values, inverse, gain, upstream):
    scaled = upstream * gain
    inner = jnp.mean(scaled * values, axis=-1, keepdims=True)
    grad_in = inverse * scaled - values * inverse * inverse * inverse * inner
    grad_gain = jnp.sum(upstream * values * inverse, axis=0)
    return (grad_in, grad_gain)


def doc_begins(positions, starts):
    return jnp.max(jnp.where(starts[None, :] <= positions[:, None], starts[None, :], 0), axis=1)


def rope_tables(offsets, half_dim):
    frequency = rope_base ** (-(jnp.arange(half_dim, dtype=jnp.float32) * 2.0 / (2.0 * half_dim)))
    angles = offsets.astype(jnp.float32)[:, None] * frequency[None, :]
    return (jnp.cos(angles), jnp.sin(angles))


def apply_rotary(values, cosine_table, sine_values, forward):
    half_dim = cosine_table.shape[1]
    first = values[..., :half_dim]
    second = values[..., half_dim:]
    cosine_wide = cosine_table[:, None, :]
    sine_wide = sine_values[:, None, :]
    if forward:
        return jnp.concatenate(
            [first * cosine_wide - second * sine_wide, second * cosine_wide + first * sine_wide],
            axis=-1,
        )
    return jnp.concatenate(
        [first * cosine_wide + second * sine_wide, second * cosine_wide - first * sine_wide],
        axis=-1,
    )


def fold_keys(
    folded, key_matrix, value_matrix, key_start, query_matrix, positions, begins, scaling
):
    running_max, denominator, weighted = folded
    row_count = key_matrix.shape[0]
    key_pos = key_start + jnp.arange(row_count, dtype=jnp.int32)
    allowed = (key_pos[None, :] <= positions[:, None]) & (key_pos[None, :] >= begins[:, None])
    scores = (
        jnp.einsum("qgha,kga->ghqk", query_matrix, key_matrix, preferred_element_type=jnp.float32)
        * scaling
    )
    masked = jnp.where(allowed, scores, negative_huge)
    new_max = jnp.maximum(running_max, jnp.max(masked, axis=-1))
    weights = jnp.where(allowed, jnp.exp(scores - new_max[..., None]), 0.0)
    shrink = jnp.exp(running_max - new_max)
    denominator = denominator * shrink + jnp.sum(weights, axis=-1)
    weighted = weighted * shrink[..., None] + jnp.einsum(
        "ghqk,kga->ghqa",
        weights.astype(jnp.bfloat16),
        value_matrix,
        preferred_element_type=jnp.float32,
    )
    return (new_max, denominator, weighted)


def attend_back(
    query_matrix,
    output_gradient,
    logsum,
    delta,
    positions,
    begins,
    key_matrix,
    value_matrix,
    key_start,
    scaling,
):
    row_count = key_matrix.shape[0]
    key_pos = key_start + jnp.arange(row_count, dtype=jnp.int32)
    allowed = (key_pos[None, :] <= positions[:, None]) & (key_pos[None, :] >= begins[:, None])
    scores = (
        jnp.einsum("qgha,kga->ghqk", query_matrix, key_matrix, preferred_element_type=jnp.float32)
        * scaling
    )
    probs = jnp.where(allowed, jnp.exp(scores - logsum[..., None]), 0.0)
    grad_probs = jnp.einsum(
        "ghqa,kga->ghqk", output_gradient, value_matrix, preferred_element_type=jnp.float32
    )
    grad_scores = (probs * (grad_probs - delta[..., None])).astype(jnp.bfloat16)
    grad_query = (
        jnp.einsum("ghqk,kga->ghqa", grad_scores, key_matrix, preferred_element_type=jnp.float32)
        * scaling
    )
    grad_key = (
        jnp.einsum("ghqk,qgha->kga", grad_scores, query_matrix, preferred_element_type=jnp.float32)
        * scaling
    )
    grad_value = jnp.einsum(
        "ghqk,ghqa->kga",
        probs.astype(jnp.bfloat16),
        output_gradient,
        preferred_element_type=jnp.float32,
    )
    return (grad_query, grad_key, grad_value)


def body(
    packed_in,
    routes,
    gates,
    doc_starts,
    attn_gain,
    w_qkv,
    w_out,
    ffn_gain,
    expert_gate_up,
    expert_down,
    cotangent,
):
    tokens = packed_in[0].astype(jnp.float32)
    token_count = tokens.shape[0]
    query_groups = QUERY_HEADS // KEY_VALUE_HEADS
    query_width = QUERY_HEADS * HEAD_SIZE
    key_value_width = KEY_VALUE_HEADS * HEAD_SIZE
    scaling = HEAD_SIZE ** (-0.5)
    contexts = lax.axis_size("context")
    own_index = lax.axis_index("context")
    positions = own_index * token_count + jnp.arange(token_count, dtype=jnp.int32)
    last_pos = own_index * token_count + token_count - 1
    begins = doc_begins(positions, doc_starts[0])
    cosine_table, sine_values = rope_tables(positions - begins, HEAD_SIZE // 2)
    normed_a, inverse_a = norm_rows(tokens, attn_gain)
    normed_ab = normed_a.astype(jnp.bfloat16)
    projected_rows = jnp.dot(normed_ab, w_qkv, preferred_element_type=jnp.float32)
    query_matrix = apply_rotary(
        projected_rows[:, :query_width].reshape(token_count, QUERY_HEADS, HEAD_SIZE),
        cosine_table,
        sine_values,
        True,
    )
    query_matrix = query_matrix.astype(jnp.bfloat16).reshape(
        token_count, KEY_VALUE_HEADS, query_groups, HEAD_SIZE
    )
    key_matrix = apply_rotary(
        projected_rows[:, query_width : query_width + key_value_width].reshape(
            token_count, KEY_VALUE_HEADS, HEAD_SIZE
        ),
        cosine_table,
        sine_values,
        True,
    )
    key_matrix = key_matrix.astype(jnp.bfloat16)
    value_matrix = (
        projected_rows[:, query_width + key_value_width :]
        .reshape(token_count, KEY_VALUE_HEADS, HEAD_SIZE)
        .astype(jnp.bfloat16)
    )
    query_layout = (KEY_VALUE_HEADS, query_groups, token_count, HEAD_SIZE)
    start_state = (
        jnp.full((KEY_VALUE_HEADS, query_groups, token_count), negative_huge, jnp.float32),
        jnp.zeros((KEY_VALUE_HEADS, query_groups, token_count), jnp.float32),
        jnp.zeros(query_layout, jnp.float32),
    )
    part_keys = lax.all_gather(key_matrix, "context", axis=0, tiled=True)
    part_values = lax.all_gather(value_matrix, "context", axis=0, tiled=True)
    row_count = part_keys.shape[0]
    width = 512 if row_count > 1024 and row_count % 512 == 0 else row_count

    def inner_step(block_index, state_now):
        offset = block_index * width
        block_keys = lax.dynamic_slice_in_dim(part_keys, block_index * width, width, 0)
        block_values = lax.dynamic_slice_in_dim(part_values, block_index * width, width, 0)

        def update(state_in):
            return fold_keys(
                state_in, block_keys, block_values, offset, query_matrix, positions, begins, scaling
            )

        def unchanged(state_in):
            return state_in

        return lax.cond(offset <= last_pos, update, unchanged, state_now)

    running_max, denominator, weighted = lax.fori_loop(
        0, row_count // width, inner_step, start_state
    )
    attended = weighted / denominator[..., None]
    logsum = running_max + jnp.log(denominator)
    merged_b = (
        jnp.transpose(attended, (2, 0, 1, 3)).reshape(token_count, query_width).astype(jnp.bfloat16)
    )
    residual = tokens + jnp.dot(merged_b, w_out, preferred_element_type=jnp.float32)
    normed_f, inverse_f = norm_rows(residual, ffn_gain)
    normed_fb = normed_f.astype(jnp.bfloat16)
    local_experts = expert_gate_up.shape[0]
    expert_devices = lax.axis_size("expert")
    expert_total = local_experts * expert_devices
    chosen = routes[0].reshape(-1)
    onehot = (chosen[:, None] == jnp.arange(expert_total, dtype=jnp.int32)[None, :]).astype(
        jnp.int32
    )
    slots = jnp.sum((jnp.cumsum(onehot, axis=0) - onehot) * onehot, axis=1)
    repeated = jnp.repeat(normed_fb, TOP, axis=0)
    outgoing = jnp.zeros((expert_total, CAP, D), jnp.bfloat16).at[chosen, slots].set(repeated)
    outgoing = outgoing.reshape(expert_devices, local_experts, CAP, D)
    arrived_rows = lax.all_to_all(outgoing, "expert", split_axis=0, concat_axis=0, tiled=True)
    gate_up_rows = jnp.einsum(
        "sjcd,jdf->sjcf", arrived_rows, expert_gate_up, preferred_element_type=jnp.float32
    )
    hidden = (smooth_gate(gate_up_rows[..., :FF]) * gate_up_rows[..., FF:]).astype(jnp.bfloat16)
    produced = jnp.einsum("sjcf,jfd->sjcd", hidden, expert_down, preferred_element_type=jnp.float32)
    returned_rows = lax.all_to_all(
        produced.astype(jnp.bfloat16), "expert", split_axis=0, concat_axis=0, tiled=True
    )
    picked = (
        returned_rows.reshape(expert_total, CAP, D)[chosen, slots]
        .astype(jnp.float32)
        .reshape(token_count, TOP, D)
    )
    gate_values = gates[0]
    mixture = jnp.sum(gate_values[..., None] * picked, axis=1)
    packed_out = (residual + mixture).astype(jnp.bfloat16)
    upstream = cotangent[0].astype(jnp.float32)
    grad_mix = (
        (gate_values[..., None] * upstream[:, None, :])
        .astype(jnp.bfloat16)
        .reshape(token_count * TOP, D)
    )
    grad_send = jnp.zeros((expert_total, CAP, D), jnp.bfloat16).at[chosen, slots].set(grad_mix)
    grad_send = grad_send.reshape(expert_devices, local_experts, CAP, D)
    grad_arrived = lax.all_to_all(grad_send, "expert", split_axis=0, concat_axis=0, tiled=True)
    gate_part = gate_up_rows[..., :FF]
    up_part = gate_up_rows[..., FF:]
    activated, gelu_back = jax.vjp(smooth_gate, gate_part)
    hidden_b = (activated * up_part).astype(jnp.bfloat16)
    grad_hidden = jnp.einsum(
        "sjcd,jfd->sjcf", grad_arrived, expert_down, preferred_element_type=jnp.float32
    )
    down_grad = jnp.einsum(
        "sjcf,sjcd->jfd", hidden_b, grad_arrived, preferred_element_type=jnp.float32
    )
    grad_gate = gelu_back(grad_hidden * up_part)[0]
    grad_gu = jnp.concatenate([grad_gate, grad_hidden * activated], axis=-1).astype(jnp.bfloat16)
    gate_up_grad = jnp.einsum(
        "sjcd,sjcf->jdf", arrived_rows, grad_gu, preferred_element_type=jnp.float32
    )
    grad_rows = jnp.einsum(
        "sjcf,jdf->sjcd", grad_gu, expert_gate_up, preferred_element_type=jnp.float32
    )
    grad_back = lax.all_to_all(
        grad_rows.astype(jnp.bfloat16), "expert", split_axis=0, concat_axis=0, tiled=True
    )
    grad_picked = grad_back.reshape(expert_total, CAP, D)[chosen, slots].astype(jnp.float32)
    grad_normed_f = jnp.sum(grad_picked.reshape(token_count, TOP, D), axis=1)
    grad_resid_part, ffn_gain_grad = norm_back(residual, inverse_f, ffn_gain, grad_normed_f)
    grad_residual = upstream + grad_resid_part
    grad_branch = grad_residual.astype(jnp.bfloat16)
    out_proj_grad = jnp.einsum(
        "td,tf->df", merged_b, grad_branch, preferred_element_type=jnp.float32
    )
    merged_gradient = jnp.einsum(
        "tf,df->td", grad_branch, w_out, preferred_element_type=jnp.float32
    ).astype(jnp.bfloat16)
    output_gradient = jnp.transpose(
        merged_gradient.reshape(token_count, KEY_VALUE_HEADS, query_groups, HEAD_SIZE), (1, 2, 0, 3)
    )
    delta = jnp.sum(output_gradient.astype(jnp.float32) * attended, axis=-1)

    def block_back(part_keys, part_values, key_start):

        def compute(operands):
            return attend_back(
                query_matrix,
                output_gradient,
                logsum,
                delta,
                positions,
                begins,
                operands[0],
                operands[1],
                key_start,
                scaling,
            )

        def nothing(operands):
            return (
                jnp.zeros(query_layout, jnp.float32),
                jnp.zeros(operands[0].shape, jnp.float32),
                jnp.zeros(operands[1].shape, jnp.float32),
            )

        return lax.cond(key_start <= last_pos, compute, nothing, (part_keys, part_values))

    grad_query = jnp.zeros(query_layout, jnp.float32)
    complete_keys, whole_values = (
        lax.all_gather(key_matrix, "context", axis=0, tiled=True),
        lax.all_gather(value_matrix, "context", axis=0, tiled=True),
    )
    block_span = 2 * token_count

    def block_turn(turn_index, block_state):
        keys_grad_all, values_grad_all, query_sum = block_state
        offset = turn_index * block_span
        add_query, add_key, add_value = block_back(
            lax.dynamic_slice_in_dim(complete_keys, offset, block_span, 0),
            lax.dynamic_slice_in_dim(whole_values, offset, block_span, 0),
            offset,
        )
        keys_grad_all = lax.dynamic_update_slice_in_dim(keys_grad_all, add_key, offset, 0)
        values_grad_all = lax.dynamic_update_slice_in_dim(values_grad_all, add_value, offset, 0)
        return (keys_grad_all, values_grad_all, query_sum + add_query)

    zero_filled = jnp.zeros((complete_keys.shape[0], KEY_VALUE_HEADS, HEAD_SIZE), jnp.float32)
    finished = lax.fori_loop(0, contexts // 2, block_turn, (zero_filled, zero_filled, grad_query))
    grad_keys, grad_values = (
        lax.psum_scatter(
            finished[0].astype(jnp.bfloat16), "context", scatter_dimension=0, tiled=True
        ).astype(jnp.float32),
        lax.psum_scatter(
            finished[1].astype(jnp.bfloat16), "context", scatter_dimension=0, tiled=True
        ).astype(jnp.float32),
    )
    grad_query = finished[2]
    grad_q_rows = apply_rotary(
        jnp.transpose(grad_query, (2, 0, 1, 3)).reshape(token_count, QUERY_HEADS, HEAD_SIZE),
        cosine_table,
        sine_values,
        False,
    )
    grad_k_rows = apply_rotary(grad_keys, cosine_table, sine_values, False)
    grad_projected = jnp.concatenate(
        [
            grad_q_rows.reshape(token_count, query_width),
            grad_k_rows.reshape(token_count, key_value_width),
            grad_values.reshape(token_count, key_value_width),
        ],
        axis=-1,
    ).astype(jnp.bfloat16)
    qkv_grad = jnp.einsum(
        "td,tf->df", normed_ab, grad_projected, preferred_element_type=jnp.float32
    )
    grad_normed_a = jnp.einsum(
        "tf,df->td", grad_projected, w_qkv, preferred_element_type=jnp.float32
    )
    grad_in_part, attn_gain_grad = norm_back(tokens, inverse_a, attn_gain, grad_normed_a)
    packed_grad = grad_residual + grad_in_part
    summed = (
        lax.psum_scatter(
            attn_gain_grad.astype(jnp.bfloat16), "context", scatter_dimension=0, tiled=True
        ).astype(jnp.float32),
        lax.psum_scatter(
            qkv_grad.astype(jnp.bfloat16), "context", scatter_dimension=0, tiled=True
        ).astype(jnp.float32),
        lax.psum_scatter(
            out_proj_grad.astype(jnp.bfloat16), "context", scatter_dimension=0, tiled=True
        ).astype(jnp.float32),
        lax.psum_scatter(
            ffn_gain_grad.astype(jnp.bfloat16), "context", scatter_dimension=0, tiled=True
        ).astype(jnp.float32),
        lax.psum_scatter(
            gate_up_grad.astype(jnp.bfloat16), "context", scatter_dimension=1, tiled=True
        ).astype(jnp.float32),
        lax.psum_scatter(
            down_grad.astype(jnp.bfloat16), "context", scatter_dimension=1, tiled=True
        ).astype(jnp.float32),
    )
    dense_rows = (summed[0], summed[1], summed[2], summed[3])
    expert_sums = (
        lax.psum(summed[4].astype(jnp.bfloat16), "dp").astype(jnp.float32),
        lax.psum(summed[5].astype(jnp.bfloat16), "dp").astype(jnp.float32),
    )
    shared = (
        lax.psum(dense_rows[0].astype(jnp.bfloat16), ("dp", "expert")).astype(jnp.float32),
        lax.psum(dense_rows[1].astype(jnp.bfloat16), ("dp", "expert")).astype(jnp.float32),
        lax.psum(dense_rows[2].astype(jnp.bfloat16), ("dp", "expert")).astype(jnp.float32),
        lax.psum(dense_rows[3].astype(jnp.bfloat16), ("dp", "expert")).astype(jnp.float32),
    )
    return (
        packed_out[None],
        packed_grad[None],
        shared[0],
        shared[1],
        shared[2],
        shared[3],
        expert_sums[0],
        expert_sums[1],
    )


MESH = pl.DeviceIdType.MESH
BF = jnp.bfloat16
F32 = jnp.float32
NN = (((1,), (0,)), ((), ()))
NT = (((1,), (1,)), ((), ()))
TN = (((0,), (0,)), ((), ()))


def matmul(left, right, dims=NN):
    return lax.dot_general(left, right, dims, preferred_element_type=F32)


def flip(axis, bit):
    index = lax.axis_index(axis)
    return {axis: index + bit - 2 * bit * ((index // bit) % 2)}


def greet(peers):
    barrier = pltpu.get_barrier_semaphore()
    for peer in peers:
        pl.semaphore_signal(barrier, inc=1, device_id=peer, device_id_type=MESH)
    pl.semaphore_wait(barrier, len(peers))


def remote(src, dst, send_sem, recv_sem, peer):
    return pltpu.make_async_remote_copy(
        src_ref=src,
        dst_ref=dst,
        send_sem=send_sem,
        recv_sem=recv_sem,
        device_id=peer,
        device_id_type=MESH,
    )


def other(axis, distance):
    size = lax.axis_size(axis)
    return {axis: lax.rem(lax.axis_index(axis) + distance, size)}


def mate(code):
    expert = lax.axis_index("expert")
    for bit in (1, 2):
        if code & bit:
            expert = expert + bit - 2 * bit * ((expert // bit) % 2)
    return {**flip("dp", 1), "expert": expert} if code & 4 else {"expert": expert}


class GroupGather:
    def __init__(self, own, held, sems, rows):
        half = rows // 2
        self.x, self.y, self.core = flip("dp", 1), flip("expert", 2), flip("expert", 1)

        def part(which, index, amount=1):
            return held.at[pl.ds(which * 2 * rows + index * half, amount * half)]

        def link(number, src, dst, peer):
            return remote(src, dst, sems.at[0, number], sems.at[1, number], peer)

        first, second = own.at[pl.ds(0, half)], own.at[pl.ds(half, half)]
        self.links = [
            link(0, first, part(1, 0), self.x),
            link(1, second, part(1, 1), self.y),
            link(2, first, part(2, 0), self.y),
            link(3, second, part(2, 1), self.x),
            link(4, part(1, 0), part(3, 0), self.y),
            link(5, part(1, 1), part(3, 1), self.x),
        ]
        self.cores = [link(6, own, part(0, 2, 2), self.core)]
        for which in range(1, 4):
            self.cores.append(
                link(6 + which, part(which, 0, 2), part(which, 2, 2), self.core)
            )

    def start(self):
        self.cores[0].start()
        for link in self.links[:4]:
            link.start()

    def forward(self, which):
        for link in self.links[2 * which - 2 : 2 * which]:
            link.wait_recv()
        if which == 1:
            for link in self.links[4:]:
                link.start()
        self.cores[which].start()

    def arrived(self, which):
        self.cores[which].wait_recv()

    def finish(self):
        for link in self.links + self.cores:
            link.wait_send()


GATHER_SEMS = pltpu.SemaphoreType.DMA((2, 10))


def rotate(values, cosine, sine):
    return values * cosine + pltpu.roll(values, values.shape[1] // 2, 1) * sine


def attention_kernel(
    x_ref,
    share_ref,
    begin_ref,
    cos_ref,
    sin_ref,
    attn_gain_ref,
    ffn_gain_ref,
    c_ref,
    w_qkv_ref,
    w_out_ref,
    h1_ref,
    q_ref,
    att_ref,
    logsum_ref,
    merged_ref,
    residual_ref,
    h2_ref,
    kv_ref,
    c_all_ref,
    share_all_ref,
    w_qkv,
    w_out,
    kv,
    accumulated,
    top,
    total,
    bias,
    load_sems,
    kv_sems,
    share_sems,
    gather_sems,
):
    contexts = lax.axis_size("context")
    me = lax.axis_index("context")
    rows = x_ref.shape[0]
    query_width = QUERY_HEADS * HEAD_SIZE
    heads = QUERY_HEADS // KEY_VALUE_HEADS
    scaling = HEAD_SIZE ** (-0.5)

    loads = [
        pltpu.make_async_copy(
            w_qkv_ref.at[:, query_width:], w_qkv.at[:, query_width:], load_sems.at[0]
        ),
        pltpu.make_async_copy(
            w_qkv_ref.at[:, :query_width], w_qkv.at[:, :query_width], load_sems.at[1]
        ),
        pltpu.make_async_copy(w_out_ref, w_out, load_sems.at[2]),
        pltpu.make_async_copy(c_ref, c_all_ref.at[pl.ds(0, rows)], load_sems.at[3]),
        pltpu.make_async_copy(share_ref, share_all_ref.at[0], load_sems.at[4]),
    ]
    for load in loads:
        load.start()

    mates = [mate(code) for code in range(1, 8)]
    greet([other("context", step) for step in range(1, contexts)] + mates)

    gather = GroupGather(c_ref, c_all_ref, gather_sems, rows)
    gather.start()
    shares = [
        remote(
            share_ref,
            share_all_ref.at[1 + index],
            share_sems.at[0, index],
            share_sems.at[1, index],
            mate,
        )
        for index, mate in enumerate(mates)
    ]
    for share in shares:
        share.start()

    x = x_ref[...].astype(F32)
    inverse = lax.rsqrt(jnp.mean(x * x, axis=-1, keepdims=True) + epsilon)
    h1_ref[...] = (x * inverse * attn_gain_ref[...]).astype(BF)

    loads[0].wait()
    projected = matmul(h1_ref[...], w_qkv[:, query_width:])
    for head in range(KEY_VALUE_HEADS):
        lanes = slice(head * HEAD_SIZE, (head + 1) * HEAD_SIZE)
        kv[me, :, lanes] = rotate(projected[:, lanes], cos_ref[...], sin_ref[...]).astype(BF)
    kv[me, :, KEY_VALUE_HEADS * HEAD_SIZE :] = projected[:, KEY_VALUE_HEADS * HEAD_SIZE :].astype(
        BF
    )

    def kv_copy(step):
        return remote(
            kv.at[me],
            kv.at[me],
            kv_sems.at[0, step],
            kv_sems.at[1, step],
            {"context": lax.rem(me + step, contexts)},
        )

    for step in range(1, contexts):

        @pl.when(me + step < contexts)
        def _():
            kv_copy(step).start()

    loads[1].wait()
    chunk = 4 * HEAD_SIZE
    for offset in range(0, query_width, chunk):
        projected = matmul(h1_ref[...], w_qkv[:, offset : offset + chunk])
        for head in range(chunk // HEAD_SIZE):
            lanes = slice(head * HEAD_SIZE, (head + 1) * HEAD_SIZE)
            q_ref[offset // HEAD_SIZE + head] = rotate(
                projected[:, lanes], cos_ref[...], sin_ref[...]
            ).astype(BF)

    top[...] = jnp.full_like(top, negative_huge)
    total[...] = jnp.zeros_like(total)
    accumulated[...] = jnp.zeros_like(accumulated)
    query_pos = me * rows + lax.broadcasted_iota(jnp.int32, (rows, rows), 1)
    begin_row = begin_ref[...]

    def fold(block):
        key_pos = block * rows + lax.broadcasted_iota(jnp.int32, (rows, rows), 0)
        allowed = (key_pos <= query_pos) & (key_pos >= begin_row)
        bias[...] = jnp.where(allowed, 0.0, negative_huge)
        for head in range(QUERY_HEADS):
            group = head // heads
            keys = kv[block, :, group * HEAD_SIZE : (group + 1) * HEAD_SIZE]
            values = kv[
                block,
                :,
                (KEY_VALUE_HEADS + group) * HEAD_SIZE : (KEY_VALUE_HEADS + group + 1) * HEAD_SIZE,
            ]
            scores = matmul(keys, q_ref[head], NT) * scaling + bias[...]
            old = top[head : head + 1]
            new = jnp.maximum(old, jnp.max(scores, axis=0, keepdims=True))
            weights = jnp.exp(scores - new)
            shrink = jnp.exp(old - new)
            top[head : head + 1] = new
            total[head : head + 1] = total[head : head + 1] * shrink + jnp.sum(
                weights, axis=0, keepdims=True
            )
            accumulated[head] = accumulated[head] * shrink + matmul(
                values, weights.astype(BF), TN
            )

    fold(me)

    def earlier(step, carry):
        kv_arrival(step).wait_recv()
        fold(me - step)
        return carry

    def kv_arrival(step):
        return remote(
            kv.at[me],
            kv.at[lax.rem(me - step + contexts, contexts)],
            kv_sems.at[0, step],
            kv_sems.at[1, step],
            {"context": lax.rem(me + step, contexts)},
        )

    gather.forward(1)
    lax.fori_loop(1, me + 1, earlier, 0)
    gather.forward(2)

    loads[2].wait()
    for head in range(QUERY_HEADS):
        attended = accumulated[head] / total[head : head + 1]
        att_ref[head] = attended
        merged_ref[:, head * HEAD_SIZE : (head + 1) * HEAD_SIZE] = attended.T.astype(BF)
    logsum_ref[...] = jnp.where(total[...] > 0, top[...] + jnp.log(total[...]), 0.0)
    residual = x_ref[...].astype(F32) + matmul(merged_ref[...], w_out[...])
    residual_ref[...] = residual
    inverse = lax.rsqrt(jnp.mean(residual * residual, axis=-1, keepdims=True) + epsilon)
    h2_ref[...] = (residual * inverse * ffn_gain_ref[...]).astype(BF)

    def keep(block, carry):
        copy = pltpu.make_async_copy(kv.at[block], kv_ref.at[block], load_sems.at[5])
        copy.start()
        copy.wait()
        return carry

    lax.fori_loop(0, me + 1, keep, 0)
    gather.forward(3)
    for which in range(4):
        gather.arrived(which)
    gather.finish()
    for share in shares:
        share.wait()
    loads[3].wait()
    loads[4].wait()
    for step in range(1, contexts):

        @pl.when(me + step < contexts)
        def _():
            kv_copy(step).wait_send()


VM = pl.BlockSpec(memory_space=pltpu.VMEM)
ANY = pl.BlockSpec(memory_space=pl.ANY)


def attention_forward(
    x, share, begins, cosine, sine, attn_gain, ffn_gain, cotangent, w_qkv, w_out
):
    rows = x.shape[0]
    contexts = lax.axis_size("context")
    group = lax.axis_size("dp") * lax.axis_size("expert")
    kv_width = 2 * KEY_VALUE_HEADS * HEAD_SIZE
    padded = -(-QUERY_HEADS // 8) * 8
    shape = jax.ShapeDtypeStruct
    return pl.pallas_call(
        attention_kernel,
        out_shape=[
            shape((rows, D), BF),
            shape((QUERY_HEADS, rows, HEAD_SIZE), BF),
            shape((QUERY_HEADS, HEAD_SIZE, rows), F32),
            shape((padded, rows), F32),
            shape((rows, D), BF),
            shape((rows, D), F32),
            shape((rows, D), BF),
            shape((contexts, rows, kv_width), BF),
            shape((group * rows, D), BF),
            shape((group,) + share.shape, F32),
        ],
        in_specs=[VM] * 7 + [ANY] * 3,
        out_specs=[VM] * 7 + [ANY] * 3,
        scratch_shapes=[
            pltpu.VMEM(w_qkv.shape, BF),
            pltpu.VMEM(w_out.shape, BF),
            pltpu.VMEM((contexts, rows, kv_width), BF),
            pltpu.VMEM((QUERY_HEADS, HEAD_SIZE, rows), F32),
            pltpu.VMEM((padded, rows), F32),
            pltpu.VMEM((padded, rows), F32),
            pltpu.VMEM((rows, rows), F32),
            pltpu.SemaphoreType.DMA((6,)),
            pltpu.SemaphoreType.DMA((2, contexts)),
            pltpu.SemaphoreType.DMA((2, group - 1)),
            GATHER_SEMS,
        ],
        compiler_params=pltpu.CompilerParams(
            collective_id=0, has_side_effects=True, vmem_limit_bytes=56 << 20
        ),
        cost_estimate=pl.CostEstimate(
            flops=2 * rows * D * 4096, bytes_accessed=30 << 20, transcendentals=rows * rows * 12
        ),
    )(x, share, begins, cosine, sine, attn_gain, ffn_gain, cotangent, w_qkv, w_out)


def prepare(routes, gates, doc_starts, rows, expert_total):
    positions = lax.axis_index("context") * rows + jnp.arange(rows, dtype=jnp.int32)
    begins = doc_begins(positions, doc_starts[0])
    cosine, sine = rope_tables(positions - begins, HEAD_SIZE // 2)
    cosine = jnp.concatenate([cosine, cosine], axis=1)
    sine = jnp.concatenate([-sine, sine], axis=1)
    named = routes[0][None] == jnp.arange(expert_total, dtype=jnp.int32)[:, None, None]
    share = jnp.sum(jnp.where(named, gates[0][None], 0.0), axis=2)
    return begins[None, :], cosine, sine, share


SLOT_CODES = ((0, 0, 1, 1), (4, 2, 5, 3), (2, 4, 3, 5), (6, 6, 7, 7))


def gelu_parts(gate):
    slope = 0.7978845608
    bend = 0.044715
    square = gate * gate
    tanh = jnp.tanh(slope * gate * (1.0 + bend * square))
    half = 0.5 * (1.0 + tanh)
    grad = half + 0.5 * slope * gate * (1.0 - tanh * tanh) * (1.0 + 3.0 * bend * square)
    return gate * half, grad


def experts_kernel(
    h2_ref,
    share_ref,
    c_all_ref,
    gate_up_ref,
    down_ref,
    h2_all_ref,
    dgu_ref,
    hidden_ref,
    du_ref,
    w_gu,
    w_down,
    h2_all,
    c_all,
    dhid,
    gu,
    hidden,
    dgu,
    du,
    share,
    load_sems,
    out_sems,
    gather_sems,
):
    rows = h2_ref.shape[0]
    half = rows // 2
    two = 2 * rows
    dp = lax.axis_index("dp")
    loads = [
        pltpu.make_async_copy(down_ref.at[dp], w_down, load_sems.at[0]),
        pltpu.make_async_copy(c_all_ref, c_all, load_sems.at[1]),
        pltpu.make_async_copy(gate_up_ref.at[dp], w_gu, load_sems.at[2]),
    ]
    for load in loads:
        load.start()
    greet([flip("dp", 1), flip("expert", 2), flip("expert", 1)])
    gather = GroupGather(h2_ref, h2_all, gather_sems, rows)
    gather.start()
    h2_all[0:rows] = h2_ref[...]

    expert = lax.axis_index("expert") * lax.axis_size("dp") + dp
    columns = []
    for code in range(8):
        turned = share_ref[code].T
        mine = lax.broadcasted_iota(jnp.int32, turned.shape, 1) == expert
        columns.append(jnp.sum(jnp.where(mine, turned, 0.0), axis=1, keepdims=True))
    for which, codes in enumerate(SLOT_CODES):
        for index, code in enumerate(codes):
            part = (index % 2) * half
            share[pl.ds(which * two + index * half, half), :] = columns[code][part : part + half]

    loads[0].wait()
    loads[1].wait()
    for which in range(4):
        span = slice(which * two, (which + 1) * two)
        dhid[span] = matmul(c_all[span], w_down[...], NT)
    loads[2].wait()

    outs = []

    def out(number, src, dst, span):
        copy = pltpu.make_async_copy(src.at[span], dst.at[span], out_sems.at[number])
        copy.start()
        outs.append(copy)

    for which in range(4):
        span = slice(which * two, (which + 1) * two)
        place = pl.ds(which * two, two)
        if which > 1:
            gather.forward(which)
        gather.arrived(which)
        out(4 * which, h2_all, h2_all_ref, place)
        gu[...] = matmul(h2_all[span], w_gu[...])

        def activate(step, carry):
            near = pl.ds(pl.multiple_of(step * half, half), half)
            far = pl.ds(pl.multiple_of(which * two + step * half, half), half)
            up = gu[near, FF:]
            activated, grad = gelu_parts(gu[near, :FF])
            scale = share[far, :]
            upstream = dhid[far, :] * scale
            hidden[far, :] = (activated * up * scale).astype(BF)
            dgu[far, :FF] = (upstream * up * grad).astype(BF)
            dgu[far, FF:] = (upstream * activated).astype(BF)
            return carry

        lax.fori_loop(0, 4, activate, 0)
        if which == 0:
            gather.forward(1)
        out(4 * which + 1, dgu, dgu_ref, place)
        out(4 * which + 2, hidden, hidden_ref, place)
        du[span] = matmul(dgu[span], w_gu[...], NT).astype(BF)
        out(4 * which + 3, du, du_ref, place)
    gather.finish()
    for copy in outs:
        copy.wait()


def experts(h2, share_all, c_all, gate_up, down):
    rows = h2.shape[0]
    total = 8 * rows
    shape = jax.ShapeDtypeStruct
    return pl.pallas_call(
        experts_kernel,
        out_shape=[
            shape((total, D), BF),
            shape((total, 2 * FF), BF),
            shape((total, FF), BF),
            shape((total, D), BF),
        ],
        in_specs=[VM] * 2 + [ANY] * 3,
        out_specs=[ANY] * 4,
        scratch_shapes=[
            pltpu.VMEM(gate_up.shape[1:], BF),
            pltpu.VMEM(down.shape[1:], BF),
            pltpu.VMEM((total, D), BF),
            pltpu.VMEM((total, D), BF),
            pltpu.VMEM((total, FF), F32),
            pltpu.VMEM((2 * rows, 2 * FF), F32),
            pltpu.VMEM((total, FF), BF),
            pltpu.VMEM((total, 2 * FF), BF),
            pltpu.VMEM((total, D), BF),
            pltpu.VMEM((total, 1), F32),
            pltpu.SemaphoreType.DMA((3,)),
            pltpu.SemaphoreType.DMA((16,)),
            GATHER_SEMS,
        ],
        compiler_params=pltpu.CompilerParams(
            collective_id=1, has_side_effects=True, vmem_limit_bytes=60 << 20
        ),
        cost_estimate=pl.CostEstimate(
            flops=2 * total * D * FF * 5, bytes_accessed=50 << 20, transcendentals=total * FF
        ),
    )(h2, share_all, c_all, gate_up, down)


class GroupReturn:
    def __init__(self, source, own, near, second, third, sems, rows):
        self.rows, self.half = rows, rows // 2
        self.own, self.near, self.second, self.third = own, near, second, third
        x, y, core = flip("dp", 1), flip("expert", 2), flip("expert", 1)

        def link(number, src, dst, peer):
            return remote(src, dst, sems.at[0, number], sems.at[1, number], peer)

        def part(which, index):
            return own.at[which, pl.ds(index * self.half, self.half)]

        self.loads = []
        self.cores = []
        for which in range(4):
            begin = which * 2 * rows
            self.loads.append(
                pltpu.make_async_copy(
                    source.at[pl.ds(begin, rows)], own.at[which], sems.at[0, 10 + which]
                )
            )
            self.cores.append(
                link(6 + which, source.at[pl.ds(begin + rows, rows)], near.at[which], core)
            )
        self.links = [
            link(0, part(1, 0), third.at[0], x),
            link(1, part(1, 1), third.at[1], y),
            link(2, part(2, 0), third.at[2], y),
            link(3, part(2, 1), third.at[3], x),
            link(4, part(3, 0), second.at[0], y),
            link(5, part(3, 1), second.at[1], x),
        ]

    def start(self):
        for which in (3, 2, 1, 0):
            self.cores[which].start()
            self.loads[which].start()

    def fold(self, which, more=()):
        self.loads[which].wait()
        self.cores[which].wait_recv()
        for index in range(2):
            span = slice(index * self.half, (index + 1) * self.half)
            value = self.own[which, span].astype(F32) + self.near[which, span].astype(F32)
            for extra in more:
                value = value + extra[index].astype(F32)
            self.own[which, span] = value.astype(BF)

    def far(self):
        self.fold(3)
        for link in self.links[4:]:
            link.start()
        self.fold(2)
        for link in self.links[2:4]:
            link.start()

    def middle(self):
        for link in self.links[4:]:
            link.wait_recv()
        self.fold(1, (self.second,))
        for link in self.links[:2]:
            link.start()

    def total(self, index):
        span = slice(index * self.half, (index + 1) * self.half)
        value = self.own[0, span].astype(F32) + self.near[0, span].astype(F32)
        return value + self.third[index].astype(F32) + self.third[2 + index].astype(F32)

    def settle(self):
        self.loads[0].wait()
        self.cores[0].wait_recv()
        for link in self.links[:4]:
            link.wait_recv()
        for link in self.links + self.cores:
            link.wait_send()

    @staticmethod
    def scratch(rows):
        return [
            pltpu.VMEM((4, rows, D), BF),
            pltpu.VMEM((4, rows, D), BF),
            pltpu.VMEM((2, rows // 2, D), BF),
            pltpu.VMEM((4, rows // 2, D), BF),
            pltpu.SemaphoreType.DMA((2, 14)),
        ]


def turned(axis, code):
    index = lax.axis_index(axis)
    bit = 1
    while bit <= code:
        if code & bit:
            index = index + bit - 2 * bit * ((index // bit) % 2)
        bit *= 2
    return index


def weights_kernel(
    h2_all_ref,
    dgu_ref,
    hidden_ref,
    c_all_ref,
    du_ref,
    down_ref,
    dh2_ref,
    gu_part_ref,
    down_part_ref,
    gu_in_ref,
    down_in_ref,
    y_ref,
    h2_all,
    dgu,
    hidden,
    c_all,
    w_down,
    gu_part,
    down_part,
    y,
    load_sems,
    out_sems,
    z_sems,
    own,
    near,
    second,
    third,
    return_sems,
):
    rows = dh2_ref.shape[0]
    slice_rows = gu_part.shape[1]
    down_rows = down_part.shape[1] // 2
    loads = [
        pltpu.make_async_copy(h2_all_ref, h2_all, load_sems.at[0]),
        pltpu.make_async_copy(dgu_ref, dgu, load_sems.at[1]),
        pltpu.make_async_copy(hidden_ref, hidden, load_sems.at[2]),
        pltpu.make_async_copy(c_all_ref, c_all, load_sems.at[3]),
        pltpu.make_async_copy(down_ref.at[lax.axis_index("dp")], w_down, load_sems.at[4]),
    ]
    for load in loads:
        load.start()
    z = flip("context", 1)
    greet([flip("dp", 1), flip("expert", 2), flip("expert", 1), z])
    back = GroupReturn(du_ref, own, near, second, third, return_sems, rows)
    back.start()
    outs = []

    def out(number, src, dst):
        copy = pltpu.make_async_copy(src, dst, out_sems.at[number])
        copy.start()
        outs.append(copy)

    def gate_up_slice(code):
        lanes = pl.ds(pl.multiple_of(turned("context", code) * slice_rows, 128), slice_rows)
        gu_part[code] = matmul(h2_all[:, lanes], dgu[...], TN).astype(BF)

    def down_pair(pair):
        first = turned("context", 2 * pair) // 2
        lanes = pl.ds(pl.multiple_of(first * 2 * down_rows, 128), 2 * down_rows)
        down_part[pair] = matmul(hidden[:, lanes], c_all[...], TN).astype(BF)

    loads[0].wait()
    loads[1].wait()
    gate_up_slice(3)
    sends = [remote(gu_part.at[3], gu_in_ref, z_sems.at[0, 0], z_sems.at[1, 0], z)]
    sends[0].start()
    loads[2].wait()
    loads[3].wait()
    down_pair(1)
    back.far()
    place = pl.ds(
        pl.multiple_of(lax.rem(turned("context", 3), 2) * down_rows, 16), down_rows
    )
    sends.append(
        remote(down_part.at[1, place], down_in_ref, z_sems.at[0, 1], z_sems.at[1, 1], z)
    )
    sends[1].start()
    gate_up_slice(1)
    out(0, gu_part.at[1], gu_part_ref.at[1])
    down_pair(0)
    out(1, down_part, down_part_ref)
    back.middle()
    gate_up_slice(2)
    out(2, gu_part.at[2], gu_part_ref.at[2])
    gate_up_slice(0)
    out(3, gu_part.at[0], gu_part_ref.at[0])
    loads[4].wait()
    for which in range(4):
        span = pl.ds(which * 2 * rows, 2 * rows)
        y[span] = matmul(hidden[span], w_down[...]).astype(BF)
        out(4 + which, y.at[span], y_ref.at[span])
    back.settle()
    for index in range(2):
        dh2_ref[index * rows // 2 : (index + 1) * rows // 2] = back.total(index)
    for copy in outs + sends:
        copy.wait()


def expert_weights(h2_all, dgu, hidden, c_all, du, down):
    total = h2_all.shape[0]
    rows = total // 8
    contexts = lax.axis_size("context")
    slice_rows, down_rows = D // contexts, FF // contexts
    shape = jax.ShapeDtypeStruct
    gu_shape, down_shape = (contexts, slice_rows, 2 * FF), (contexts // 2, 2 * down_rows, D)
    return pl.pallas_call(
        weights_kernel,
        out_shape=[
            shape((rows, D), F32),
            shape(gu_shape, BF),
            shape(down_shape, BF),
            shape(gu_shape[1:], BF),
            shape((down_rows, D), BF),
            shape((total, D), BF),
        ],
        in_specs=[ANY] * 6,
        out_specs=[VM] + [ANY] * 5,
        scratch_shapes=[
            pltpu.VMEM((total, D), BF),
            pltpu.VMEM((total, 2 * FF), BF),
            pltpu.VMEM((total, FF), BF),
            pltpu.VMEM((total, D), BF),
            pltpu.VMEM(down.shape[1:], BF),
            pltpu.VMEM(gu_shape, BF),
            pltpu.VMEM(down_shape, BF),
            pltpu.VMEM((total, D), BF),
            pltpu.SemaphoreType.DMA((5,)),
            pltpu.SemaphoreType.DMA((8,)),
            pltpu.SemaphoreType.DMA((2, 2)),
        ]
        + GroupReturn.scratch(rows),
        compiler_params=pltpu.CompilerParams(
            collective_id=2, has_side_effects=True, vmem_limit_bytes=60 << 20
        ),
        cost_estimate=pl.CostEstimate(
            flops=2 * total * D * FF * 4, bytes_accessed=50 << 20, transcendentals=0
        ),
    )(h2_all, dgu, hidden, c_all, du, down)


def unrotate(values, cosine, sine):
    return values * cosine - pltpu.roll(values, values.shape[1] // 2, 1) * sine


def norm_pull(values, gain, upstream):
    inverse = lax.rsqrt(jnp.mean(values * values, axis=-1, keepdims=True) + epsilon)
    scaled = upstream * gain
    inner = jnp.mean(scaled * values, axis=-1, keepdims=True)
    grad_in = inverse * scaled - values * (inverse * inverse * inverse * inner)
    return grad_in, jnp.sum(upstream * (values * inverse), axis=0, keepdims=True)


def backward_kernel(
    dh2_ref,
    residual_ref,
    c_ref,
    merged_ref,
    att_ref,
    logsum_ref,
    q_ref,
    h1_ref,
    x_ref,
    attn_gain_ref,
    ffn_gain_ref,
    begin_ref,
    cos_ref,
    sin_ref,
    kv_ref,
    w_qkv_ref,
    w_out_ref,
    y_ref,
    gu_part_ref,
    down_part_ref,
    packed_out_ref,
    packed_grad_ref,
    gains_ref,
    out_proj_ref,
    qkv_grad_ref,
    gu_in_ref,
    down_in_ref,
    w_qkv,
    w_out,
    kv,
    dres,
    dbranch,
    datt,
    delta,
    bias,
    dq,
    dkv_sum,
    dkv_out,
    dkv_in,
    dqkv,
    load_sems,
    kv_sems,
    z_sems,
    dkv_sems,
    own,
    near,
    second,
    third,
    return_sems,
):
    rows = x_ref.shape[0]
    half = rows // 2
    contexts = lax.axis_size("context")
    me = lax.axis_index("context")
    query_width = QUERY_HEADS * HEAD_SIZE
    key_width = KEY_VALUE_HEADS * HEAD_SIZE
    heads = QUERY_HEADS // KEY_VALUE_HEADS
    scaling = HEAD_SIZE ** (-0.5)
    down_rows = down_in_ref.shape[0]

    load_out = pltpu.make_async_copy(w_out_ref, w_out, load_sems.at[0])
    load_out.start()

    def load_kv(block):
        return pltpu.make_async_copy(kv_ref.at[block], kv.at[block], kv_sems.at[block])

    def begin_load(block, carry):
        load_kv(block).start()
        return carry

    def end_load(block, carry):
        load_kv(block).wait()
        return carry

    lax.fori_loop(0, me + 1, begin_load, 0)
    load_qkv = pltpu.make_async_copy(w_qkv_ref, w_qkv, load_sems.at[1])
    load_qkv.start()
    z = flip("context", 1)
    greet(
        [flip("dp", 1), flip("expert", 2), flip("expert", 1)]
        + [other("context", step) for step in range(1, contexts)]
    )
    place = pl.ds(
        pl.multiple_of(lax.rem(turned("context", 1), 2) * down_rows, 16), down_rows
    )
    sends = [
        remote(gu_part_ref.at[1], gu_in_ref, z_sems.at[0, 0], z_sems.at[1, 0], z),
        remote(down_part_ref.at[0, place], down_in_ref, z_sems.at[0, 1], z_sems.at[1, 1], z),
    ]
    for send in sends:
        send.start()
    back = GroupReturn(y_ref, own, near, second, third, return_sems, rows)
    back.start()

    grad_part, gain_grad = norm_pull(residual_ref[...], ffn_gain_ref[...], dh2_ref[...])
    gains_ref[...] = jnp.zeros_like(gains_ref)
    gains_ref[1:2] = gain_grad
    dres[...] = c_ref[...].astype(F32) + grad_part
    dbranch[...] = dres[...].astype(BF)
    load_out.wait()
    datt[...] = matmul(dbranch[...], w_out[...], NT).astype(BF)
    delta[...] = jnp.zeros_like(delta)
    for head in range(QUERY_HEADS):
        lanes = slice(head * HEAD_SIZE, (head + 1) * HEAD_SIZE)
        turned_grad = datt[:, lanes].astype(F32).T
        delta[head : head + 1] = jnp.sum(turned_grad * att_ref[head], axis=0, keepdims=True)
    back.far()

    lax.fori_loop(0, me + 1, end_load, 0)
    query_pos = me * rows + lax.broadcasted_iota(jnp.int32, (rows, rows), 1)
    dq[...] = jnp.zeros_like(dq)

    def pull(block):
        key_pos = block * rows + lax.broadcasted_iota(jnp.int32, (rows, rows), 0)
        allowed = (key_pos <= query_pos) & (key_pos >= begin_ref[...])
        bias[...] = jnp.where(allowed, 0.0, negative_huge)
        dkv_sum[...] = jnp.zeros_like(dkv_sum)
        for head in range(QUERY_HEADS):
            group = head // heads
            key_lanes = slice(group * HEAD_SIZE, (group + 1) * HEAD_SIZE)
            value_lanes = slice(key_width + group * HEAD_SIZE, key_width + (group + 1) * HEAD_SIZE)
            keys = kv[block, :, key_lanes]
            values = kv[block, :, value_lanes]
            upstream = datt[:, head * HEAD_SIZE : (head + 1) * HEAD_SIZE]
            scores = matmul(keys, q_ref[head], NT) * scaling + bias[...]
            probs = jnp.exp(scores - logsum_ref[head : head + 1])
            dprobs = matmul(values, upstream, NT)
            dscores = (probs * (dprobs - delta[head : head + 1])).astype(BF)
            dkv_sum[:, value_lanes] += matmul(probs.astype(BF), upstream)
            dkv_sum[:, key_lanes] += matmul(dscores, q_ref[head])
            dq[head] += matmul(keys, dscores, TN)

    def dkv_copy(step):
        return remote(
            dkv_out.at[step],
            dkv_in.at[step],
            dkv_sems.at[0, step],
            dkv_sems.at[1, step],
            {"context": lax.rem(me - step + contexts, contexts)},
        )

    def earlier(turn, carry):
        step = me - turn
        pull(turn)
        dkv_out[step] = dkv_sum[...].astype(BF)
        dkv_copy(step).start()
        return carry

    lax.fori_loop(0, me, earlier, 0)
    pull(me)
    back.middle()

    for head in range(QUERY_HEADS):
        lanes = slice(head * HEAD_SIZE, (head + 1) * HEAD_SIZE)
        dqkv[:, lanes] = unrotate(dq[head].T * scaling, cos_ref[...], sin_ref[...]).astype(BF)
    for offset in range(0, query_width, 512):
        lanes = slice(offset, offset + 512)
        qkv_grad_ref[:, lanes] = matmul(h1_ref[...], dqkv[:, lanes], TN).astype(BF)
        out_proj_ref[:, lanes] = matmul(merged_ref[...], dbranch[:, lanes], TN).astype(BF)

    def later(step, carry):
        dkv_copy(step).wait_recv()
        dkv_sum[...] += dkv_in[step].astype(F32)
        return carry

    lax.fori_loop(1, contexts - me, later, 0)
    for head in range(KEY_VALUE_HEADS):
        lanes = slice(head * HEAD_SIZE, (head + 1) * HEAD_SIZE)
        place = slice(query_width + head * HEAD_SIZE, query_width + (head + 1) * HEAD_SIZE)
        dqkv[:, place] = unrotate(
            dkv_sum[:, lanes] * scaling, cos_ref[...], sin_ref[...]
        ).astype(BF)
    dqkv[:, query_width + key_width :] = dkv_sum[:, key_width:].astype(BF)
    qkv_grad_ref[:, query_width:] = matmul(h1_ref[...], dqkv[:, query_width:], TN).astype(BF)
    load_qkv.wait()
    grad_part, gain_grad = norm_pull(
        x_ref[...].astype(F32), attn_gain_ref[...], matmul(dqkv[...], w_qkv[...], NT)
    )
    gains_ref[0:1] = gain_grad
    packed_grad_ref[...] = dres[...] + grad_part

    back.settle()
    for index in range(2):
        span = slice(index * half, (index + 1) * half)
        packed_out_ref[span] = (residual_ref[span] + back.total(index)).astype(BF)

    def sent(step, carry):
        dkv_copy(step).wait_send()
        return carry

    lax.fori_loop(1, me + 1, sent, 0)
    for send in sends:
        send.wait()


def attention_backward(
    dh2,
    residual,
    cotangent,
    merged,
    att,
    logsum,
    query,
    h1,
    x,
    attn_gain,
    ffn_gain,
    begins,
    cosine,
    sine,
    kv,
    w_qkv,
    w_out,
    y,
    gu_part,
    down_part,
):
    rows = x.shape[0]
    contexts = lax.axis_size("context")
    kv_width = 2 * KEY_VALUE_HEADS * HEAD_SIZE
    shape = jax.ShapeDtypeStruct
    return pl.pallas_call(
        backward_kernel,
        out_shape=[
            shape((rows, D), BF),
            shape((rows, D), F32),
            shape((8, D), F32),
            shape(w_out.shape, BF),
            shape(w_qkv.shape, BF),
            shape(gu_part.shape[1:], BF),
            shape((down_part.shape[1] // 2, D), BF),
        ],
        in_specs=[VM] * 14 + [ANY] * 6,
        out_specs=[VM] * 5 + [ANY] * 2,
        scratch_shapes=[
            pltpu.VMEM(w_qkv.shape, BF),
            pltpu.VMEM(w_out.shape, BF),
            pltpu.VMEM(kv.shape, BF),
            pltpu.VMEM((rows, D), F32),
            pltpu.VMEM((rows, D), BF),
            pltpu.VMEM((rows, D), BF),
            pltpu.VMEM(logsum.shape, F32),
            pltpu.VMEM((rows, rows), F32),
            pltpu.VMEM((QUERY_HEADS, HEAD_SIZE, rows), F32),
            pltpu.VMEM((rows, kv_width), F32),
            pltpu.VMEM((contexts, rows, kv_width), BF),
            pltpu.VMEM((contexts, rows, kv_width), BF),
            pltpu.VMEM((rows, w_qkv.shape[1]), BF),
            pltpu.SemaphoreType.DMA((2,)),
            pltpu.SemaphoreType.DMA((contexts,)),
            pltpu.SemaphoreType.DMA((2, 2)),
            pltpu.SemaphoreType.DMA((2, contexts)),
        ]
        + GroupReturn.scratch(rows),
        compiler_params=pltpu.CompilerParams(
            collective_id=3, has_side_effects=True, vmem_limit_bytes=60 << 20
        ),
        cost_estimate=pl.CostEstimate(
            flops=2 * rows * D * 8000, bytes_accessed=40 << 20, transcendentals=rows * rows * 48
        ),
    )(
        dh2,
        residual,
        cotangent,
        merged,
        att,
        logsum,
        query,
        h1,
        x,
        attn_gain,
        ffn_gain,
        begins,
        cosine,
        sine,
        kv,
        w_qkv,
        w_out,
        y,
        gu_part,
        down_part,
    )


def bit_of(axis, bit):
    return lax.rem(lax.axis_index(axis) // bit, 2)


class DenseReduce:
    def __init__(self, part, keep, near, first, second, third, fourth, out, sems):
        self.part, self.keep, self.near, self.first = part, keep, near, first
        self.second, self.third, self.fourth, self.out = second, third, fourth, out
        self.sems = sems
        self.count = 0
        self.width = part.shape[2] // 2
        self.rows = part.shape[1] // 8
        self.x, self.y, self.core = flip("dp", 1), flip("expert", 2), flip("expert", 1)
        self.xb, self.yb, self.cb = bit_of("dp", 1), bit_of("expert", 2), bit_of("expert", 1)
        self.flows = (
            (self.y, self.yb, self.x, self.xb),
            (self.x, self.xb, self.y, self.yb),
        )
        self.pending = []

    def link(self, src, dst, peer):
        number = self.count
        self.count += 1
        copy = remote(src, dst, self.sems.at[0, number], self.sems.at[1, number], peer)
        copy.start()
        self.pending.append(copy)
        return copy

    def lanes(self, flow):
        return slice(flow * self.width, (flow + 1) * self.width)

    def span(self, bit, size, base=0):
        return pl.ds(pl.multiple_of(base + bit * size, 16), size)

    def start(self):
        size = 4 * self.rows
        self.load = pltpu.make_async_copy(
            self.part.at[:, self.span(self.cb, size)], self.keep, self.sems.at[0, 16]
        )
        self.load.start()
        self.copies = [
            self.link(self.part.at[:, self.span(1 - self.cb, size)], self.near, self.core)
        ]

    def after_core(self):
        self.load.wait()
        self.copies[0].wait_recv()
        slices = self.part.shape[0]
        for index in range(slices):
            value = self.near[index].astype(F32) + self.keep[index].astype(F32)
            self.near[index] = value.astype(BF)
        size = 2 * self.rows
        self.copies = [
            self.link(
                self.near.at[:, self.span(1 - bit, size), self.lanes(flow)],
                self.first.at[flow],
                peer,
            )
            for flow, (peer, bit, _, _) in enumerate(self.flows)
        ]

    def after_first(self):
        size = 2 * self.rows
        copies = []
        for flow, (_, bit, peer, later_bit) in enumerate(self.flows):
            self.copies[flow].wait_recv()
            for index in range(self.part.shape[0]):
                value = self.near[index, self.span(bit, size), self.lanes(flow)].astype(F32)
                value = value + self.first[flow, index].astype(F32)
                self.first[flow, index] = value.astype(BF)
            copies.append(
                self.link(
                    self.first.at[flow, :, self.span(1 - later_bit, self.rows)],
                    self.second.at[flow],
                    peer,
                )
            )
        self.copies = copies

    def after_second(self):
        peer, bit = flip("context", 1), bit_of("context", 1)
        copies = []
        for flow, (_, _, _, later_bit) in enumerate(self.flows):
            self.copies[flow].wait_recv()
            for index in range(self.part.shape[0]):
                value = self.first[flow, index, self.span(later_bit, self.rows)].astype(F32)
                place = (flow, index)
                self.second[place] = (value + self.second[place].astype(F32)).astype(BF)
            for high in range(2):
                copies.append(
                    self.link(
                        self.second.at[flow, 2 * high + 1 - bit],
                        self.third.at[flow, high],
                        peer,
                    )
                )
        self.copies = copies

    def after_third(self):
        bit = bit_of("context", 1)
        peer, later_bit = flip("context", 2), bit_of("context", 2)
        copies = []
        for flow in range(2):
            for high in range(2):
                self.copies[2 * flow + high].wait_recv()
                value = self.second[flow, 2 * high + bit].astype(F32)
                value = value + self.third[flow, high].astype(F32)
                self.third[flow, high] = value.astype(BF)
            copies.append(
                self.link(self.third.at[flow, 1 - later_bit], self.fourth.at[flow], peer)
            )
        self.copies = copies

    def place(self, flow, cuts):
        _, bit, _, later_bit = self.flows[flow]
        base = self.cb * 4 * self.rows + bit * 2 * self.rows
        if cuts:
            return pl.ds(pl.multiple_of(base, 16), 2 * self.rows)
        return pl.ds(pl.multiple_of(base + later_bit * self.rows, 16), self.rows)

    def after_fourth(self):
        bit = bit_of("context", 2)
        copies = []
        for flow, (_, _, peer, _) in enumerate(self.flows):
            self.copies[flow].wait_recv()
            value = self.third[flow, bit].astype(F32) + self.fourth[flow].astype(F32)
            rows, lanes = self.place(flow, 0), self.lanes(flow)
            self.out[rows, lanes] = value.astype(BF)
            copies.append(self.link(self.out.at[rows, lanes], self.out.at[rows, lanes], peer))
        self.copies = copies

    def spread(self):
        copies = []
        for flow, (peer, _, _, _) in enumerate(self.flows):
            self.copies[flow].wait_recv()
            rows, lanes = self.place(flow, 1), self.lanes(flow)
            copies.append(self.link(self.out.at[rows, lanes], self.out.at[rows, lanes], peer))
        self.copies = copies

    def last(self):
        for copy in self.copies:
            copy.wait_recv()
        rows = self.span(self.cb, 4 * self.rows)
        self.copies = [self.link(self.out.at[rows], self.out.at[rows], self.core)]

    def finish(self):
        self.copies[0].wait_recv()
        for copy in self.pending:
            copy.wait_send()

    @staticmethod
    def scratch(contexts, rows, width):
        quarter = rows // 8
        return [
            pltpu.VMEM((contexts, 4 * quarter, width), BF),
            pltpu.VMEM((contexts, 4 * quarter, width), BF),
            pltpu.VMEM((2, contexts, 2 * quarter, width // 2), BF),
            pltpu.VMEM((2, contexts, quarter, width // 2), BF),
            pltpu.VMEM((2, contexts // 2, quarter, width // 2), BF),
            pltpu.VMEM((2, quarter, width // 2), BF),
            pltpu.SemaphoreType.DMA((2, 17)),
        ]


def finish_kernel(
    gains_ref,
    gu_part_ref,
    down_part_ref,
    gu_far_ref,
    down_far_ref,
    gu_near_ref,
    down_near_ref,
    out_proj_ref,
    qkv_grad_ref,
    gains_out_ref,
    out_proj_out_ref,
    qkv_grad_out_ref,
    weights_out_ref,
    part,
    arrived,
    passed,
    gains_in,
    load_sems,
    z_sems,
    x_sems,
    gain_sems,
    *dense_scratch,
):
    slice_rows = gu_far_ref.shape[0]
    down_rows = down_far_ref.shape[0]
    dp = lax.axis_index("dp")
    x, z_far = flip("dp", 1), flip("context", 2)

    def down_place(code):
        return pl.ds(
            pl.multiple_of(lax.rem(turned("context", code), 2) * down_rows, 16), down_rows
        )

    gu_span, down_span = pl.ds(0, slice_rows), pl.ds(slice_rows, down_rows)
    loads = []
    for index, (code, gu_in, down_in) in enumerate(
        ((2, gu_far_ref, down_far_ref), (0, gu_near_ref, down_near_ref))
    ):
        for number, (src, dst) in enumerate(
            (
                (gu_part_ref.at[code], part.at[index, gu_span]),
                (down_part_ref.at[code // 2, down_place(code)], part.at[index, down_span]),
                (gu_in, arrived.at[index, gu_span]),
                (down_in, arrived.at[index, down_span]),
            )
        ):
            loads.append(pltpu.make_async_copy(src, dst, load_sems.at[4 * index + number]))
    for load in loads:
        load.start()

    exchange = [
        flip("expert", 1),
        flip("expert", 2),
        flip("dp", 1),
        flip("context", 1),
        flip("context", 2),
    ]
    greet(exchange)

    middle = len(dense_scratch) // 2
    qkv_scratch, out_scratch = dense_scratch[:middle], dense_scratch[middle:]
    qkv = DenseReduce(qkv_grad_ref, *qkv_scratch[:-1], qkv_grad_out_ref, qkv_scratch[-1])
    out = DenseReduce(out_proj_ref, *out_scratch[:-1], out_proj_out_ref, out_scratch[-1])
    dense = (out, qkv)
    for array in dense:
        array.start()

    gains_out_ref[...] = gains_ref[...]
    gain_copies = []

    def gain_start(step):
        copy = remote(
            gains_out_ref,
            gains_in.at[step],
            gain_sems.at[0, step],
            gain_sems.at[1, step],
            exchange[step],
        )
        copy.start()
        gain_copies.append(copy)

    def gain_add(step):
        gain_copies[step].wait()
        gains_out_ref[...] += gains_in[step]

    gain_start(0)
    for load in loads:
        load.wait()
    chunk = down_rows
    chunks = (slice_rows + down_rows) // chunk
    z_copies, x_copies = [], []
    for index in range(chunks):
        span = pl.ds(index * chunk, chunk)
        value = part[0, span].astype(F32) + arrived[0, span].astype(F32)
        part[0, span] = value.astype(BF)
        copy = remote(
            part.at[0, span], passed.at[span], z_sems.at[0, index], z_sems.at[1, index], z_far
        )
        copy.start()
        z_copies.append(copy)

    def experts_out(index):
        z_copies[index].wait_recv()
        span = pl.ds(index * chunk, chunk)
        value = part[1, span].astype(F32) + arrived[1, span].astype(F32)
        weights_out_ref[dp, span] = (value + passed[span].astype(F32)).astype(BF)
        copy = remote(
            weights_out_ref.at[dp, span],
            weights_out_ref.at[dp, span],
            x_sems.at[0, index],
            x_sems.at[1, index],
            x,
        )
        copy.start()
        x_copies.append(copy)

    gain_add(0)
    gain_start(1)
    for array in dense:
        array.after_core()
    gain_add(1)
    gain_start(2)
    for array in dense:
        array.after_first()
    gain_add(2)
    gain_start(3)
    for index in range(chunks):
        experts_out(index)
    gain_add(3)
    gain_start(4)
    for array in dense:
        array.after_second()
    gain_add(4)
    for array in dense:
        array.after_third()
    for array in dense:
        array.after_fourth()
    for array in dense:
        array.spread()
    for array in dense:
        array.last()
    for array in dense:
        array.finish()
    for copy in z_copies:
        copy.wait_send()
    for copy in x_copies:
        copy.wait()


def finish(gains, gu_part, down_part, gu_far, down_far, gu_near, down_near, out_proj, qkv_grad):
    contexts = lax.axis_size("context")
    slice_rows, down_rows = gu_far.shape[0], down_far.shape[0]
    total = slice_rows + down_rows
    shape = jax.ShapeDtypeStruct
    out_proj = out_proj.reshape(contexts, slice_rows, -1)
    qkv_grad = qkv_grad.reshape(contexts, slice_rows, -1)
    return pl.pallas_call(
        finish_kernel,
        out_shape=[
            shape(gains.shape, F32),
            shape(out_proj.shape[1:], BF),
            shape(qkv_grad.shape[1:], BF),
            shape((2, total, D), BF),
        ],
        in_specs=[VM] + [ANY] * 8,
        out_specs=[VM] * 4,
        scratch_shapes=[
            pltpu.VMEM((2, total, D), BF),
            pltpu.VMEM((2, total, D), BF),
            pltpu.VMEM((total, D), BF),
            pltpu.VMEM((5,) + gains.shape, F32),
            pltpu.SemaphoreType.DMA((8,)),
            pltpu.SemaphoreType.DMA((2, total // down_rows)),
            pltpu.SemaphoreType.DMA((2, total // down_rows)),
            pltpu.SemaphoreType.DMA((2, 5)),
        ]
        + DenseReduce.scratch(contexts, slice_rows, qkv_grad.shape[2])
        + DenseReduce.scratch(contexts, slice_rows, out_proj.shape[2]),
        compiler_params=pltpu.CompilerParams(
            collective_id=4, has_side_effects=True, vmem_limit_bytes=60 << 20
        ),
        cost_estimate=pl.CostEstimate(flops=0, bytes_accessed=40 << 20, transcendentals=0),
    )(gains, gu_part, down_part, gu_far, down_far, gu_near, down_near, out_proj, qkv_grad)


def fast_body(
    packed_in,
    routes,
    gates,
    doc_starts,
    attn_gain,
    w_qkv,
    w_out,
    ffn_gain,
    expert_gate_up,
    expert_down,
    cotangent,
):
    x, c = packed_in[0], cotangent[0]
    rows = x.shape[0]
    contexts = lax.axis_size("context")
    expert_total = expert_gate_up.shape[0] * lax.axis_size("expert")
    attn_gain, ffn_gain = attn_gain[None], ffn_gain[None]
    begins, cosine, sine, share = prepare(routes, gates, doc_starts, rows, expert_total)
    (h1, query, att, logsum, merged, residual, h2, kv, c_all, share_all) = attention_forward(
        x, share, begins, cosine, sine, attn_gain, ffn_gain, c, w_qkv, w_out
    )
    h2_all, dgu, hidden, du = experts(h2, share_all, c_all, expert_gate_up, expert_down)
    dh2, gu_part, down_part, gu_far, down_far, y = expert_weights(
        h2_all, dgu, hidden, c_all, du, expert_down
    )
    packed_out, packed_grad, gains, out_proj, qkv_grad, gu_near, down_near = attention_backward(
        dh2,
        residual,
        c,
        merged,
        att,
        logsum,
        query,
        h1,
        x,
        attn_gain,
        ffn_gain,
        begins,
        cosine,
        sine,
        kv,
        w_qkv,
        w_out,
        y,
        gu_part,
        down_part,
    )
    gains, out_proj, qkv_grad, weights = finish(
        gains, gu_part, down_part, gu_far, down_far, gu_near, down_near, out_proj, qkv_grad
    )
    slice_rows = D // contexts
    gains = lax.dynamic_slice_in_dim(gains, lax.axis_index("context") * slice_rows, slice_rows, 1)
    return (
        packed_out[None],
        packed_grad[None],
        gains[0],
        qkv_grad.astype(F32),
        out_proj.astype(F32),
        gains[1],
        weights[:, :slice_rows].astype(F32),
        weights[:, slice_rows:].astype(F32),
    )


def fits(mesh):
    sizes = mesh.shape
    contexts = sizes["context"]
    return (
        sizes["dp"] == 2
        and sizes["expert"] == 4
        and contexts == 4
        and D % (contexts * 128) == 0
        and FF % (contexts * 64) == 0
    )


def solution(mesh):
    chosen_body = fast_body if fits(mesh) else body
    placed = (
        P(("dp", "expert"), "context", None),
        P(("dp", "expert"), "context", None),
        P(("dp", "expert"), "context", None),
        P(("dp", "expert"), None),
        P(),
        P(),
        P(),
        P(),
        P("expert", None, None),
        P("expert", None, None),
        P(("dp", "expert"), "context", None),
    )
    return jax.shard_map(
        chosen_body,
        mesh=mesh,
        in_specs=placed,
        out_specs=(
            P(("dp", "expert"), "context", None),
            P(("dp", "expert"), "context", None),
            P("context"),
            P("context", None),
            P("context", None),
            P("context"),
            P("expert", "context", None),
            P("expert", "context", None),
        ),
        check_vma=False,
    )
```

```python
import jax
import jax.numpy as jnp
from jax import lax
from jax.experimental import pallas as pl
from jax.experimental.pallas import tpu as pltpu
from jax.sharding import PartitionSpec as P

D = 1536
QUERY_HEADS = 12
KEY_VALUE_HEADS = 2
HEAD_SIZE = 128
FF = 768
TOP = 4
CAP = 192


epsilon = 1e-06
rope_base = 10000.0
negative_huge = -1e30


def smooth_gate(preact):
    return jax.nn.gelu(preact, approximate=True)


def norm_rows(values, gain):
    inverse = lax.rsqrt(jnp.mean(values * values, axis=-1, keepdims=True) + epsilon)
    return (values * inverse * gain, inverse)


def norm_back(values, inverse, gain, upstream):
    scaled = upstream * gain
    inner = jnp.mean(scaled * values, axis=-1, keepdims=True)
    grad_in = inverse * scaled - values * inverse * inverse * inverse * inner
    grad_gain = jnp.sum(upstream * values * inverse, axis=0)
    return (grad_in, grad_gain)


def doc_begins(positions, starts):
    return jnp.max(jnp.where(starts[None, :] <= positions[:, None], starts[None, :], 0), axis=1)


def rope_tables(offsets, half_dim):
    frequency = rope_base ** (-(jnp.arange(half_dim, dtype=jnp.float32) * 2.0 / (2.0 * half_dim)))
    angles = offsets.astype(jnp.float32)[:, None] * frequency[None, :]
    return (jnp.cos(angles), jnp.sin(angles))


def apply_rotary(values, cosine_table, sine_values, forward):
    half_dim = cosine_table.shape[1]
    first = values[..., :half_dim]
    second = values[..., half_dim:]
    cosine_wide = cosine_table[:, None, :]
    sine_wide = sine_values[:, None, :]
    if forward:
        return jnp.concatenate(
            [first * cosine_wide - second * sine_wide, second * cosine_wide + first * sine_wide],
            axis=-1,
        )
    return jnp.concatenate(
        [first * cosine_wide + second * sine_wide, second * cosine_wide - first * sine_wide],
        axis=-1,
    )


def fold_keys(
    folded, key_matrix, value_matrix, key_start, query_matrix, positions, begins, scaling
):
    running_max, denominator, weighted = folded
    row_count = key_matrix.shape[0]
    key_pos = key_start + jnp.arange(row_count, dtype=jnp.int32)
    allowed = (key_pos[None, :] <= positions[:, None]) & (key_pos[None, :] >= begins[:, None])
    scores = (
        jnp.einsum("qgha,kga->ghqk", query_matrix, key_matrix, preferred_element_type=jnp.float32)
        * scaling
    )
    masked = jnp.where(allowed, scores, negative_huge)
    new_max = jnp.maximum(running_max, jnp.max(masked, axis=-1))
    weights = jnp.where(allowed, jnp.exp(scores - new_max[..., None]), 0.0)
    shrink = jnp.exp(running_max - new_max)
    denominator = denominator * shrink + jnp.sum(weights, axis=-1)
    weighted = weighted * shrink[..., None] + jnp.einsum(
        "ghqk,kga->ghqa",
        weights.astype(jnp.bfloat16),
        value_matrix,
        preferred_element_type=jnp.float32,
    )
    return (new_max, denominator, weighted)


def attend_back(
    query_matrix,
    output_gradient,
    logsum,
    delta,
    positions,
    begins,
    key_matrix,
    value_matrix,
    key_start,
    scaling,
):
    row_count = key_matrix.shape[0]
    key_pos = key_start + jnp.arange(row_count, dtype=jnp.int32)
    allowed = (key_pos[None, :] <= positions[:, None]) & (key_pos[None, :] >= begins[:, None])
    scores = (
        jnp.einsum("qgha,kga->ghqk", query_matrix, key_matrix, preferred_element_type=jnp.float32)
        * scaling
    )
    probs = jnp.where(allowed, jnp.exp(scores - logsum[..., None]), 0.0)
    grad_probs = jnp.einsum(
        "ghqa,kga->ghqk", output_gradient, value_matrix, preferred_element_type=jnp.float32
    )
    grad_scores = (probs * (grad_probs - delta[..., None])).astype(jnp.bfloat16)
    grad_query = (
        jnp.einsum("ghqk,kga->ghqa", grad_scores, key_matrix, preferred_element_type=jnp.float32)
        * scaling
    )
    grad_key = (
        jnp.einsum("ghqk,qgha->kga", grad_scores, query_matrix, preferred_element_type=jnp.float32)
        * scaling
    )
    grad_value = jnp.einsum(
        "ghqk,ghqa->kga",
        probs.astype(jnp.bfloat16),
        output_gradient,
        preferred_element_type=jnp.float32,
    )
    return (grad_query, grad_key, grad_value)


def body(
    packed_in,
    routes,
    gates,
    doc_starts,
    attn_gain,
    w_qkv,
    w_out,
    ffn_gain,
    expert_gate_up,
    expert_down,
    cotangent,
):
    tokens = packed_in[0].astype(jnp.float32)
    token_count = tokens.shape[0]
    query_groups = QUERY_HEADS // KEY_VALUE_HEADS
    query_width = QUERY_HEADS * HEAD_SIZE
    key_value_width = KEY_VALUE_HEADS * HEAD_SIZE
    scaling = HEAD_SIZE ** (-0.5)
    contexts = lax.axis_size("context")
    own_index = lax.axis_index("context")
    positions = own_index * token_count + jnp.arange(token_count, dtype=jnp.int32)
    last_pos = own_index * token_count + token_count - 1
    begins = doc_begins(positions, doc_starts[0])
    cosine_table, sine_values = rope_tables(positions - begins, HEAD_SIZE // 2)
    normed_a, inverse_a = norm_rows(tokens, attn_gain)
    normed_ab = normed_a.astype(jnp.bfloat16)
    projected_rows = jnp.dot(normed_ab, w_qkv, preferred_element_type=jnp.float32)
    query_matrix = apply_rotary(
        projected_rows[:, :query_width].reshape(token_count, QUERY_HEADS, HEAD_SIZE),
        cosine_table,
        sine_values,
        True,
    )
    query_matrix = query_matrix.astype(jnp.bfloat16).reshape(
        token_count, KEY_VALUE_HEADS, query_groups, HEAD_SIZE
    )
    key_matrix = apply_rotary(
        projected_rows[:, query_width : query_width + key_value_width].reshape(
            token_count, KEY_VALUE_HEADS, HEAD_SIZE
        ),
        cosine_table,
        sine_values,
        True,
    )
    key_matrix = key_matrix.astype(jnp.bfloat16)
    value_matrix = (
        projected_rows[:, query_width + key_value_width :]
        .reshape(token_count, KEY_VALUE_HEADS, HEAD_SIZE)
        .astype(jnp.bfloat16)
    )
    query_layout = (KEY_VALUE_HEADS, query_groups, token_count, HEAD_SIZE)
    start_state = (
        jnp.full((KEY_VALUE_HEADS, query_groups, token_count), negative_huge, jnp.float32),
        jnp.zeros((KEY_VALUE_HEADS, query_groups, token_count), jnp.float32),
        jnp.zeros(query_layout, jnp.float32),
    )
    part_keys = lax.all_gather(key_matrix, "context", axis=0, tiled=True)
    part_values = lax.all_gather(value_matrix, "context", axis=0, tiled=True)
    row_count = part_keys.shape[0]
    width = 512 if row_count > 1024 and row_count % 512 == 0 else row_count

    def inner_step(block_index, state_now):
        offset = block_index * width
        block_keys = lax.dynamic_slice_in_dim(part_keys, block_index * width, width, 0)
        block_values = lax.dynamic_slice_in_dim(part_values, block_index * width, width, 0)

        def update(state_in):
            return fold_keys(
                state_in, block_keys, block_values, offset, query_matrix, positions, begins, scaling
            )

        def unchanged(state_in):
            return state_in

        return lax.cond(offset <= last_pos, update, unchanged, state_now)

    running_max, denominator, weighted = lax.fori_loop(
        0, row_count // width, inner_step, start_state
    )
    attended = weighted / denominator[..., None]
    logsum = running_max + jnp.log(denominator)
    merged_b = (
        jnp.transpose(attended, (2, 0, 1, 3)).reshape(token_count, query_width).astype(jnp.bfloat16)
    )
    residual = tokens + jnp.dot(merged_b, w_out, preferred_element_type=jnp.float32)
    normed_f, inverse_f = norm_rows(residual, ffn_gain)
    normed_fb = normed_f.astype(jnp.bfloat16)
    local_experts = expert_gate_up.shape[0]
    expert_devices = lax.axis_size("expert")
    expert_total = local_experts * expert_devices
    chosen = routes[0].reshape(-1)
    onehot = (chosen[:, None] == jnp.arange(expert_total, dtype=jnp.int32)[None, :]).astype(
        jnp.int32
    )
    slots = jnp.sum((jnp.cumsum(onehot, axis=0) - onehot) * onehot, axis=1)
    repeated = jnp.repeat(normed_fb, TOP, axis=0)
    outgoing = jnp.zeros((expert_total, CAP, D), jnp.bfloat16).at[chosen, slots].set(repeated)
    outgoing = outgoing.reshape(expert_devices, local_experts, CAP, D)
    arrived_rows = lax.all_to_all(outgoing, "expert", split_axis=0, concat_axis=0, tiled=True)
    gate_up_rows = jnp.einsum(
        "sjcd,jdf->sjcf", arrived_rows, expert_gate_up, preferred_element_type=jnp.float32
    )
    hidden = (smooth_gate(gate_up_rows[..., :FF]) * gate_up_rows[..., FF:]).astype(jnp.bfloat16)
    produced = jnp.einsum("sjcf,jfd->sjcd", hidden, expert_down, preferred_element_type=jnp.float32)
    returned_rows = lax.all_to_all(
        produced.astype(jnp.bfloat16), "expert", split_axis=0, concat_axis=0, tiled=True
    )
    picked = (
        returned_rows.reshape(expert_total, CAP, D)[chosen, slots]
        .astype(jnp.float32)
        .reshape(token_count, TOP, D)
    )
    gate_values = gates[0]
    mixture = jnp.sum(gate_values[..., None] * picked, axis=1)
    packed_out = (residual + mixture).astype(jnp.bfloat16)
    upstream = cotangent[0].astype(jnp.float32)
    grad_mix = (
        (gate_values[..., None] * upstream[:, None, :])
        .astype(jnp.bfloat16)
        .reshape(token_count * TOP, D)
    )
    grad_send = jnp.zeros((expert_total, CAP, D), jnp.bfloat16).at[chosen, slots].set(grad_mix)
    grad_send = grad_send.reshape(expert_devices, local_experts, CAP, D)
    grad_arrived = lax.all_to_all(grad_send, "expert", split_axis=0, concat_axis=0, tiled=True)
    gate_part = gate_up_rows[..., :FF]
    up_part = gate_up_rows[..., FF:]
    activated, gelu_back = jax.vjp(smooth_gate, gate_part)
    hidden_b = (activated * up_part).astype(jnp.bfloat16)
    grad_hidden = jnp.einsum(
        "sjcd,jfd->sjcf", grad_arrived, expert_down, preferred_element_type=jnp.float32
    )
    down_grad = jnp.einsum(
        "sjcf,sjcd->jfd", hidden_b, grad_arrived, preferred_element_type=jnp.float32
    )
    grad_gate = gelu_back(grad_hidden * up_part)[0]
    grad_gu = jnp.concatenate([grad_gate, grad_hidden * activated], axis=-1).astype(jnp.bfloat16)
    gate_up_grad = jnp.einsum(
        "sjcd,sjcf->jdf", arrived_rows, grad_gu, preferred_element_type=jnp.float32
    )
    grad_rows = jnp.einsum(
        "sjcf,jdf->sjcd", grad_gu, expert_gate_up, preferred_element_type=jnp.float32
    )
    grad_back = lax.all_to_all(
        grad_rows.astype(jnp.bfloat16), "expert", split_axis=0, concat_axis=0, tiled=True
    )
    grad_picked = grad_back.reshape(expert_total, CAP, D)[chosen, slots].astype(jnp.float32)
    grad_normed_f = jnp.sum(grad_picked.reshape(token_count, TOP, D), axis=1)
    grad_resid_part, ffn_gain_grad = norm_back(residual, inverse_f, ffn_gain, grad_normed_f)
    grad_residual = upstream + grad_resid_part
    grad_branch = grad_residual.astype(jnp.bfloat16)
    out_proj_grad = jnp.einsum(
        "td,tf->df", merged_b, grad_branch, preferred_element_type=jnp.float32
    )
    merged_gradient = jnp.einsum(
        "tf,df->td", grad_branch, w_out, preferred_element_type=jnp.float32
    ).astype(jnp.bfloat16)
    output_gradient = jnp.transpose(
        merged_gradient.reshape(token_count, KEY_VALUE_HEADS, query_groups, HEAD_SIZE), (1, 2, 0, 3)
    )
    delta = jnp.sum(output_gradient.astype(jnp.float32) * attended, axis=-1)

    def block_back(part_keys, part_values, key_start):

        def compute(operands):
            return attend_back(
                query_matrix,
                output_gradient,
                logsum,
                delta,
                positions,
                begins,
                operands[0],
                operands[1],
                key_start,
                scaling,
            )

        def nothing(operands):
            return (
                jnp.zeros(query_layout, jnp.float32),
                jnp.zeros(operands[0].shape, jnp.float32),
                jnp.zeros(operands[1].shape, jnp.float32),
            )

        return lax.cond(key_start <= last_pos, compute, nothing, (part_keys, part_values))

    grad_query = jnp.zeros(query_layout, jnp.float32)
    complete_keys, whole_values = (
        lax.all_gather(key_matrix, "context", axis=0, tiled=True),
        lax.all_gather(value_matrix, "context", axis=0, tiled=True),
    )
    block_span = 2 * token_count

    def block_turn(turn_index, block_state):
        keys_grad_all, values_grad_all, query_sum = block_state
        offset = turn_index * block_span
        add_query, add_key, add_value = block_back(
            lax.dynamic_slice_in_dim(complete_keys, offset, block_span, 0),
            lax.dynamic_slice_in_dim(whole_values, offset, block_span, 0),
            offset,
        )
        keys_grad_all = lax.dynamic_update_slice_in_dim(keys_grad_all, add_key, offset, 0)
        values_grad_all = lax.dynamic_update_slice_in_dim(values_grad_all, add_value, offset, 0)
        return (keys_grad_all, values_grad_all, query_sum + add_query)

    zero_filled = jnp.zeros((complete_keys.shape[0], KEY_VALUE_HEADS, HEAD_SIZE), jnp.float32)
    finished = lax.fori_loop(0, contexts // 2, block_turn, (zero_filled, zero_filled, grad_query))
    grad_keys, grad_values = (
        lax.psum_scatter(
            finished[0].astype(jnp.bfloat16), "context", scatter_dimension=0, tiled=True
        ).astype(jnp.float32),
        lax.psum_scatter(
            finished[1].astype(jnp.bfloat16), "context", scatter_dimension=0, tiled=True
        ).astype(jnp.float32),
    )
    grad_query = finished[2]
    grad_q_rows = apply_rotary(
        jnp.transpose(grad_query, (2, 0, 1, 3)).reshape(token_count, QUERY_HEADS, HEAD_SIZE),
        cosine_table,
        sine_values,
        False,
    )
    grad_k_rows = apply_rotary(grad_keys, cosine_table, sine_values, False)
    grad_projected = jnp.concatenate(
        [
            grad_q_rows.reshape(token_count, query_width),
            grad_k_rows.reshape(token_count, key_value_width),
            grad_values.reshape(token_count, key_value_width),
        ],
        axis=-1,
    ).astype(jnp.bfloat16)
    qkv_grad = jnp.einsum(
        "td,tf->df", normed_ab, grad_projected, preferred_element_type=jnp.float32
    )
    grad_normed_a = jnp.einsum(
        "tf,df->td", grad_projected, w_qkv, preferred_element_type=jnp.float32
    )
    grad_in_part, attn_gain_grad = norm_back(tokens, inverse_a, attn_gain, grad_normed_a)
    packed_grad = grad_residual + grad_in_part
    summed = (
        lax.psum_scatter(
            attn_gain_grad.astype(jnp.bfloat16), "context", scatter_dimension=0, tiled=True
        ).astype(jnp.float32),
        lax.psum_scatter(
            qkv_grad.astype(jnp.bfloat16), "context", scatter_dimension=0, tiled=True
        ).astype(jnp.float32),
        lax.psum_scatter(
            out_proj_grad.astype(jnp.bfloat16), "context", scatter_dimension=0, tiled=True
        ).astype(jnp.float32),
        lax.psum_scatter(
            ffn_gain_grad.astype(jnp.bfloat16), "context", scatter_dimension=0, tiled=True
        ).astype(jnp.float32),
        lax.psum_scatter(
            gate_up_grad.astype(jnp.bfloat16), "context", scatter_dimension=1, tiled=True
        ).astype(jnp.float32),
        lax.psum_scatter(
            down_grad.astype(jnp.bfloat16), "context", scatter_dimension=1, tiled=True
        ).astype(jnp.float32),
    )
    dense_rows = (summed[0], summed[1], summed[2], summed[3])
    expert_sums = (
        lax.psum(summed[4].astype(jnp.bfloat16), "dp").astype(jnp.float32),
        lax.psum(summed[5].astype(jnp.bfloat16), "dp").astype(jnp.float32),
    )
    shared = (
        lax.psum(dense_rows[0].astype(jnp.bfloat16), ("dp", "expert")).astype(jnp.float32),
        lax.psum(dense_rows[1].astype(jnp.bfloat16), ("dp", "expert")).astype(jnp.float32),
        lax.psum(dense_rows[2].astype(jnp.bfloat16), ("dp", "expert")).astype(jnp.float32),
        lax.psum(dense_rows[3].astype(jnp.bfloat16), ("dp", "expert")).astype(jnp.float32),
    )
    return (
        packed_out[None],
        packed_grad[None],
        shared[0],
        shared[1],
        shared[2],
        shared[3],
        expert_sums[0],
        expert_sums[1],
    )


MESH = pl.DeviceIdType.MESH
BF = jnp.bfloat16
F32 = jnp.float32
NN = (((1,), (0,)), ((), ()))
NT = (((1,), (1,)), ((), ()))
TN = (((0,), (0,)), ((), ()))


def matmul(left, right, dims=NN):
    return lax.dot_general(left, right, dims, preferred_element_type=F32)


def flip(axis, bit):
    index = lax.axis_index(axis)
    return {axis: index + bit - 2 * bit * ((index // bit) % 2)}


def greet(peers):
    barrier = pltpu.get_barrier_semaphore()
    for peer in peers:
        pl.semaphore_signal(barrier, inc=1, device_id=peer, device_id_type=MESH)
    pl.semaphore_wait(barrier, len(peers))


def remote(src, dst, send_sem, recv_sem, peer):
    return pltpu.make_async_remote_copy(
        src_ref=src,
        dst_ref=dst,
        send_sem=send_sem,
        recv_sem=recv_sem,
        device_id=peer,
        device_id_type=MESH,
    )


def other(axis, distance):
    size = lax.axis_size(axis)
    return {axis: lax.rem(lax.axis_index(axis) + distance, size)}


def mate(code):
    expert = lax.axis_index("expert")
    for bit in (1, 2):
        if code & bit:
            expert = expert + bit - 2 * bit * ((expert // bit) % 2)
    return {**flip("dp", 1), "expert": expert} if code & 4 else {"expert": expert}


class GroupGather:
    def __init__(self, own, held, sems, rows):
        half = rows // 2
        self.x, self.y, self.core = flip("dp", 1), flip("expert", 2), flip("expert", 1)

        def part(which, index, amount=1):
            return held.at[pl.ds(which * 2 * rows + index * half, amount * half)]

        def link(number, src, dst, peer):
            return remote(src, dst, sems.at[0, number], sems.at[1, number], peer)

        first, second = own.at[pl.ds(0, half)], own.at[pl.ds(half, half)]
        self.links = [
            link(0, first, part(1, 0), self.x),
            link(1, second, part(1, 1), self.y),
            link(2, first, part(2, 0), self.y),
            link(3, second, part(2, 1), self.x),
            link(4, part(1, 0), part(3, 0), self.y),
            link(5, part(1, 1), part(3, 1), self.x),
        ]
        self.cores = [link(6, own, part(0, 2, 2), self.core)]
        for which in range(1, 4):
            self.cores.append(
                link(6 + which, part(which, 0, 2), part(which, 2, 2), self.core)
            )

    def start(self):
        self.cores[0].start()
        for link in self.links[:4]:
            link.start()

    def forward(self, which):
        for link in self.links[2 * which - 2 : 2 * which]:
            link.wait_recv()
        if which == 1:
            for link in self.links[4:]:
                link.start()
        self.cores[which].start()

    def arrived(self, which):
        self.cores[which].wait_recv()

    def finish(self):
        for link in self.links + self.cores:
            link.wait_send()


GATHER_SEMS = pltpu.SemaphoreType.DMA((2, 10))


def rotate(values, cosine, sine):
    return values * cosine + pltpu.roll(values, values.shape[1] // 2, 1) * sine


def attention_kernel(
    x_ref,
    share_ref,
    begin_ref,
    cos_ref,
    sin_ref,
    attn_gain_ref,
    ffn_gain_ref,
    c_ref,
    w_qkv_ref,
    w_out_ref,
    h1_ref,
    q_ref,
    logsum_ref,
    merged_ref,
    residual_ref,
    h2_ref,
    kv_ref,
    c_all_ref,
    share_all_ref,
    w_qkv,
    w_out,
    kv,
    accumulated,
    top,
    total,
    bias,
    load_sems,
    kv_sems,
    share_sems,
    gather_sems,
):
    contexts = lax.axis_size("context")
    me = lax.axis_index("context")
    rows = x_ref.shape[0]
    query_width = QUERY_HEADS * HEAD_SIZE
    heads = QUERY_HEADS // KEY_VALUE_HEADS
    scaling = HEAD_SIZE ** (-0.5)

    loads = [
        pltpu.make_async_copy(
            w_qkv_ref.at[:, query_width:], w_qkv.at[:, query_width:], load_sems.at[0]
        ),
        pltpu.make_async_copy(
            w_qkv_ref.at[:, :query_width], w_qkv.at[:, :query_width], load_sems.at[1]
        ),
        pltpu.make_async_copy(w_out_ref, w_out, load_sems.at[2]),
        pltpu.make_async_copy(c_ref, c_all_ref.at[pl.ds(0, rows)], load_sems.at[3]),
        pltpu.make_async_copy(share_ref, share_all_ref.at[0], load_sems.at[4]),
    ]
    for load in loads:
        load.start()

    mates = [mate(code) for code in range(1, 8)]
    greet([other("context", step) for step in range(1, contexts)] + mates)

    gather = GroupGather(c_ref, c_all_ref, gather_sems, rows)
    gather.start()
    shares = [
        remote(
            share_ref,
            share_all_ref.at[1 + index],
            share_sems.at[0, index],
            share_sems.at[1, index],
            mate,
        )
        for index, mate in enumerate(mates)
    ]
    for share in shares:
        share.start()

    x = x_ref[...].astype(F32)
    inverse = lax.rsqrt(jnp.mean(x * x, axis=-1, keepdims=True) + epsilon)
    h1_ref[...] = (x * inverse * attn_gain_ref[...]).astype(BF)

    loads[0].wait()
    projected = matmul(h1_ref[...], w_qkv[:, query_width:])
    for head in range(KEY_VALUE_HEADS):
        lanes = slice(head * HEAD_SIZE, (head + 1) * HEAD_SIZE)
        kv[me, :, lanes] = rotate(projected[:, lanes], cos_ref[...], sin_ref[...]).astype(BF)
    kv[me, :, KEY_VALUE_HEADS * HEAD_SIZE :] = projected[:, KEY_VALUE_HEADS * HEAD_SIZE :].astype(
        BF
    )

    def kv_copy(step):
        return remote(
            kv.at[me],
            kv.at[me],
            kv_sems.at[0, step],
            kv_sems.at[1, step],
            {"context": lax.rem(me + step, contexts)},
        )

    for step in range(1, contexts):

        @pl.when(me + step < contexts)
        def _():
            kv_copy(step).start()

    loads[1].wait()
    chunk = 4 * HEAD_SIZE
    for offset in range(0, query_width, chunk):
        projected = matmul(h1_ref[...], w_qkv[:, offset : offset + chunk])
        for head in range(chunk // HEAD_SIZE):
            lanes = slice(head * HEAD_SIZE, (head + 1) * HEAD_SIZE)
            q_ref[offset // HEAD_SIZE + head] = rotate(
                projected[:, lanes], cos_ref[...], sin_ref[...]
            ).astype(BF)

    top[...] = jnp.full_like(top, negative_huge)
    total[...] = jnp.zeros_like(total)
    accumulated[...] = jnp.zeros_like(accumulated)
    query_pos = me * rows + lax.broadcasted_iota(jnp.int32, (rows, rows), 1)
    begin_row = begin_ref[...]

    def fold(block):
        key_pos = block * rows + lax.broadcasted_iota(jnp.int32, (rows, rows), 0)
        allowed = (key_pos <= query_pos) & (key_pos >= begin_row)
        bias[...] = jnp.where(allowed, 0.0, negative_huge)
        for head in range(QUERY_HEADS):
            group = head // heads
            keys = kv[block, :, group * HEAD_SIZE : (group + 1) * HEAD_SIZE]
            values = kv[
                block,
                :,
                (KEY_VALUE_HEADS + group) * HEAD_SIZE : (KEY_VALUE_HEADS + group + 1) * HEAD_SIZE,
            ]
            scores = matmul(keys, q_ref[head], NT) * scaling + bias[...]
            old = top[head : head + 1]
            new = jnp.maximum(old, jnp.max(scores, axis=0, keepdims=True))
            weights = jnp.exp(scores - new)
            shrink = jnp.exp(old - new)
            top[head : head + 1] = new
            total[head : head + 1] = total[head : head + 1] * shrink + jnp.sum(
                weights, axis=0, keepdims=True
            )
            accumulated[head] = accumulated[head] * shrink + matmul(
                values, weights.astype(BF), TN
            )

    fold(me)

    def earlier(step, carry):
        kv_arrival(step).wait_recv()
        fold(me - step)
        return carry

    def kv_arrival(step):
        return remote(
            kv.at[me],
            kv.at[lax.rem(me - step + contexts, contexts)],
            kv_sems.at[0, step],
            kv_sems.at[1, step],
            {"context": lax.rem(me + step, contexts)},
        )

    gather.forward(1)
    lax.fori_loop(1, me + 1, earlier, 0)
    gather.forward(2)

    loads[2].wait()
    for head in range(QUERY_HEADS):
        attended = accumulated[head] / total[head : head + 1]
        merged_ref[:, head * HEAD_SIZE : (head + 1) * HEAD_SIZE] = attended.T.astype(BF)
    logsum_ref[...] = jnp.where(total[...] > 0, top[...] + jnp.log(total[...]), 0.0)
    residual = x_ref[...].astype(F32) + matmul(merged_ref[...], w_out[...])
    residual_ref[...] = residual
    inverse = lax.rsqrt(jnp.mean(residual * residual, axis=-1, keepdims=True) + epsilon)
    h2_ref[...] = (residual * inverse * ffn_gain_ref[...]).astype(BF)

    def keep(block, carry):
        copy = pltpu.make_async_copy(kv.at[block], kv_ref.at[block], load_sems.at[5])
        copy.start()
        copy.wait()
        return carry

    lax.fori_loop(0, me + 1, keep, 0)
    gather.forward(3)
    for which in range(4):
        gather.arrived(which)
    gather.finish()
    for share in shares:
        share.wait()
    loads[3].wait()
    loads[4].wait()
    for step in range(1, contexts):

        @pl.when(me + step < contexts)
        def _():
            kv_copy(step).wait_send()


VM = pl.BlockSpec(memory_space=pltpu.VMEM)
ANY = pl.BlockSpec(memory_space=pl.ANY)


def attention_forward(
    x, share, begins, cosine, sine, attn_gain, ffn_gain, cotangent, w_qkv, w_out
):
    rows = x.shape[0]
    contexts = lax.axis_size("context")
    group = lax.axis_size("dp") * lax.axis_size("expert")
    kv_width = 2 * KEY_VALUE_HEADS * HEAD_SIZE
    padded = -(-QUERY_HEADS // 8) * 8
    shape = jax.ShapeDtypeStruct
    return pl.pallas_call(
        attention_kernel,
        out_shape=[
            shape((rows, D), BF),
            shape((QUERY_HEADS, rows, HEAD_SIZE), BF),
            shape((padded, rows), F32),
            shape((rows, D), BF),
            shape((rows, D), F32),
            shape((rows, D), BF),
            shape((contexts, rows, kv_width), BF),
            shape((group * rows, D), BF),
            shape((group,) + share.shape, F32),
        ],
        in_specs=[VM] * 7 + [ANY] * 3,
        out_specs=[VM] * 6 + [ANY] * 3,
        scratch_shapes=[
            pltpu.VMEM(w_qkv.shape, BF),
            pltpu.VMEM(w_out.shape, BF),
            pltpu.VMEM((contexts, rows, kv_width), BF),
            pltpu.VMEM((QUERY_HEADS, HEAD_SIZE, rows), F32),
            pltpu.VMEM((padded, rows), F32),
            pltpu.VMEM((padded, rows), F32),
            pltpu.VMEM((rows, rows), F32),
            pltpu.SemaphoreType.DMA((6,)),
            pltpu.SemaphoreType.DMA((2, contexts)),
            pltpu.SemaphoreType.DMA((2, group - 1)),
            GATHER_SEMS,
        ],
        compiler_params=pltpu.CompilerParams(
            collective_id=0, has_side_effects=True, vmem_limit_bytes=56 << 20
        ),
        cost_estimate=pl.CostEstimate(
            flops=2 * rows * D * 4096, bytes_accessed=30 << 20, transcendentals=rows * rows * 12
        ),
    )(x, share, begins, cosine, sine, attn_gain, ffn_gain, cotangent, w_qkv, w_out)


def prepare(routes, gates, doc_starts, rows, expert_total):
    positions = lax.axis_index("context") * rows + jnp.arange(rows, dtype=jnp.int32)
    begins = doc_begins(positions, doc_starts[0])
    cosine, sine = rope_tables(positions - begins, HEAD_SIZE // 2)
    cosine = jnp.concatenate([cosine, cosine], axis=1)
    sine = jnp.concatenate([-sine, sine], axis=1)
    named = routes[0][None] == jnp.arange(expert_total, dtype=jnp.int32)[:, None, None]
    share = jnp.sum(jnp.where(named, gates[0][None], 0.0), axis=2)
    return begins[None, :], cosine, sine, share


SLOT_CODES = ((0, 0, 1, 1), (4, 2, 5, 3), (2, 4, 3, 5), (6, 6, 7, 7))


def gelu_parts(gate):
    slope = 0.7978845608
    bend = 0.044715
    square = gate * gate
    tanh = jnp.tanh(slope * gate * (1.0 + bend * square))
    half = 0.5 * (1.0 + tanh)
    grad = half + 0.5 * slope * gate * (1.0 - tanh * tanh) * (1.0 + 3.0 * bend * square)
    return gate * half, grad


def experts_kernel(
    h2_ref,
    share_ref,
    c_all_ref,
    gate_up_ref,
    down_ref,
    h2_all_ref,
    dgu_ref,
    hidden_ref,
    du_ref,
    w_gu,
    w_down,
    h2_all,
    c_all,
    dhid,
    gu,
    hidden,
    dgu,
    du,
    share,
    load_sems,
    out_sems,
    gather_sems,
):
    rows = h2_ref.shape[0]
    half = rows // 2
    two = 2 * rows
    dp = lax.axis_index("dp")
    loads = [
        pltpu.make_async_copy(down_ref.at[dp], w_down, load_sems.at[0]),
        pltpu.make_async_copy(c_all_ref, c_all, load_sems.at[1]),
        pltpu.make_async_copy(gate_up_ref.at[dp], w_gu, load_sems.at[2]),
    ]
    for load in loads:
        load.start()
    greet([flip("dp", 1), flip("expert", 2), flip("expert", 1)])
    gather = GroupGather(h2_ref, h2_all, gather_sems, rows)
    gather.start()
    h2_all[0:rows] = h2_ref[...]

    expert = lax.axis_index("expert") * lax.axis_size("dp") + dp
    columns = []
    for code in range(8):
        turned = share_ref[code].T
        mine = lax.broadcasted_iota(jnp.int32, turned.shape, 1) == expert
        columns.append(jnp.sum(jnp.where(mine, turned, 0.0), axis=1, keepdims=True))
    for which, codes in enumerate(SLOT_CODES):
        for index, code in enumerate(codes):
            part = (index % 2) * half
            share[pl.ds(which * two + index * half, half), :] = columns[code][part : part + half]

    loads[0].wait()
    loads[1].wait()
    for which in range(4):
        span = slice(which * two, (which + 1) * two)
        dhid[span] = matmul(c_all[span], w_down[...], NT)
    loads[2].wait()

    outs = []

    def out(number, src, dst, span):
        copy = pltpu.make_async_copy(src.at[span], dst.at[span], out_sems.at[number])
        copy.start()
        outs.append(copy)

    for which in range(4):
        span = slice(which * two, (which + 1) * two)
        place = pl.ds(which * two, two)
        if which > 1:
            gather.forward(which)
        gather.arrived(which)
        out(4 * which, h2_all, h2_all_ref, place)
        gu[...] = matmul(h2_all[span], w_gu[...])

        def activate(step, carry):
            near = pl.ds(pl.multiple_of(step * half, half), half)
            far = pl.ds(pl.multiple_of(which * two + step * half, half), half)
            up = gu[near, FF:]
            activated, grad = gelu_parts(gu[near, :FF])
            scale = share[far, :]
            upstream = dhid[far, :] * scale
            hidden[far, :] = (activated * up * scale).astype(BF)
            dgu[far, :FF] = (upstream * up * grad).astype(BF)
            dgu[far, FF:] = (upstream * activated).astype(BF)
            return carry

        lax.fori_loop(0, 4, activate, 0)
        if which == 0:
            gather.forward(1)
        out(4 * which + 1, dgu, dgu_ref, place)
        out(4 * which + 2, hidden, hidden_ref, place)
        du[span] = matmul(dgu[span], w_gu[...], NT).astype(BF)
        out(4 * which + 3, du, du_ref, place)
    gather.finish()
    for copy in outs:
        copy.wait()


def experts(h2, share_all, c_all, gate_up, down):
    rows = h2.shape[0]
    total = 8 * rows
    shape = jax.ShapeDtypeStruct
    return pl.pallas_call(
        experts_kernel,
        out_shape=[
            shape((total, D), BF),
            shape((total, 2 * FF), BF),
            shape((total, FF), BF),
            shape((total, D), BF),
        ],
        in_specs=[VM] * 2 + [ANY] * 3,
        out_specs=[ANY] * 4,
        scratch_shapes=[
            pltpu.VMEM(gate_up.shape[1:], BF),
            pltpu.VMEM(down.shape[1:], BF),
            pltpu.VMEM((total, D), BF),
            pltpu.VMEM((total, D), BF),
            pltpu.VMEM((total, FF), F32),
            pltpu.VMEM((2 * rows, 2 * FF), F32),
            pltpu.VMEM((total, FF), BF),
            pltpu.VMEM((total, 2 * FF), BF),
            pltpu.VMEM((total, D), BF),
            pltpu.VMEM((total, 1), F32),
            pltpu.SemaphoreType.DMA((3,)),
            pltpu.SemaphoreType.DMA((16,)),
            GATHER_SEMS,
        ],
        compiler_params=pltpu.CompilerParams(
            collective_id=1, has_side_effects=True, vmem_limit_bytes=60 << 20
        ),
        cost_estimate=pl.CostEstimate(
            flops=2 * total * D * FF * 5, bytes_accessed=50 << 20, transcendentals=total * FF
        ),
    )(h2, share_all, c_all, gate_up, down)


class GroupReturn:
    def __init__(self, source, own, near, second, third, sems, rows):
        self.rows, self.half = rows, rows // 2
        self.own, self.near, self.second, self.third = own, near, second, third
        x, y, core = flip("dp", 1), flip("expert", 2), flip("expert", 1)

        def link(number, src, dst, peer):
            return remote(src, dst, sems.at[0, number], sems.at[1, number], peer)

        def part(which, index):
            return near.at[which, pl.ds(index * self.half, self.half)]

        self.loads = []
        self.cores = []
        for which in range(4):
            begin = which * 2 * rows
            self.loads.append(
                pltpu.make_async_copy(
                    source.at[pl.ds(begin, rows)], own.at[which % 2], sems.at[0, 10 + which]
                )
            )
            self.cores.append(
                link(6 + which, source.at[pl.ds(begin + rows, rows)], near.at[which], core)
            )
        self.links = [
            link(0, part(1, 0), third.at[0], x),
            link(1, part(1, 1), third.at[1], y),
            link(2, part(2, 0), third.at[2], y),
            link(3, part(2, 1), third.at[3], x),
            link(4, part(3, 0), second.at[0], y),
            link(5, part(3, 1), second.at[1], x),
        ]

    def start(self):
        for which in (3, 2, 1, 0):
            self.cores[which].start()
        self.loads[3].start()
        self.loads[2].start()

    def fold(self, which, more=()):
        self.loads[which].wait()
        self.cores[which].wait_recv()
        for index in range(2):
            span = slice(index * self.half, (index + 1) * self.half)
            value = self.own[which % 2, span].astype(F32) + self.near[which, span].astype(F32)
            for extra in more:
                value = value + extra[index].astype(F32)
            self.near[which, span] = value.astype(BF)
        if which > 1:
            self.loads[which - 2].start()

    def far(self):
        self.fold(3)
        for link in self.links[4:]:
            link.start()
        self.fold(2)
        for link in self.links[2:4]:
            link.start()

    def middle(self):
        for link in self.links[4:]:
            link.wait_recv()
        self.fold(1, (self.second,))
        for link in self.links[:2]:
            link.start()

    def total(self, index):
        span = slice(index * self.half, (index + 1) * self.half)
        value = self.own[0, span].astype(F32) + self.near[0, span].astype(F32)
        return value + self.third[index].astype(F32) + self.third[2 + index].astype(F32)

    def settle(self):
        self.loads[0].wait()
        self.cores[0].wait_recv()
        for link in self.links[:4]:
            link.wait_recv()
        for link in self.links + self.cores:
            link.wait_send()

    @staticmethod
    def scratch(rows):
        return [
            pltpu.VMEM((2, rows, D), BF),
            pltpu.VMEM((4, rows, D), BF),
            pltpu.VMEM((2, rows // 2, D), BF),
            pltpu.VMEM((4, rows // 2, D), BF),
            pltpu.SemaphoreType.DMA((2, 14)),
        ]


def turned(axis, code):
    index = lax.axis_index(axis)
    bit = 1
    while bit <= code:
        if code & bit:
            index = index + bit - 2 * bit * ((index // bit) % 2)
        bit *= 2
    return index


def weights_kernel(
    h2_all_ref,
    dgu_ref,
    hidden_ref,
    c_all_ref,
    du_ref,
    down_ref,
    dh2_ref,
    gu_part_ref,
    down_part_ref,
    gu_in_ref,
    down_in_ref,
    y_ref,
    h2_all,
    dgu,
    hidden,
    c_all,
    w_down,
    gu_part,
    down_part,
    y,
    load_sems,
    out_sems,
    z_sems,
    own,
    near,
    second,
    third,
    return_sems,
):
    rows = dh2_ref.shape[0]
    slice_rows = gu_part.shape[1]
    down_rows = down_part.shape[1] // 2
    loads = [
        pltpu.make_async_copy(h2_all_ref, h2_all, load_sems.at[0]),
        pltpu.make_async_copy(dgu_ref, dgu, load_sems.at[1]),
        pltpu.make_async_copy(hidden_ref, hidden, load_sems.at[2]),
        pltpu.make_async_copy(c_all_ref, c_all, load_sems.at[3]),
        pltpu.make_async_copy(down_ref.at[lax.axis_index("dp")], w_down, load_sems.at[4]),
    ]
    for load in loads:
        load.start()
    z = flip("context", 1)
    greet([flip("dp", 1), flip("expert", 2), flip("expert", 1), z])
    back = GroupReturn(du_ref, own, near, second, third, return_sems, rows)
    back.start()
    outs = []

    def out(number, src, dst):
        copy = pltpu.make_async_copy(src, dst, out_sems.at[number])
        copy.start()
        outs.append(copy)

    def gate_up_slice(code):
        lanes = pl.ds(pl.multiple_of(turned("context", code) * slice_rows, 128), slice_rows)
        gu_part[code] = matmul(h2_all[:, lanes], dgu[...], TN).astype(BF)

    def down_pair(pair):
        first = turned("context", 2 * pair) // 2
        lanes = pl.ds(pl.multiple_of(first * 2 * down_rows, 128), 2 * down_rows)
        down_part[pair] = matmul(hidden[:, lanes], c_all[...], TN).astype(BF)

    loads[0].wait()
    loads[1].wait()
    gate_up_slice(3)
    sends = [remote(gu_part.at[3], gu_in_ref, z_sems.at[0, 0], z_sems.at[1, 0], z)]
    sends[0].start()
    loads[2].wait()
    loads[3].wait()
    down_pair(1)
    back.far()
    place = pl.ds(
        pl.multiple_of(lax.rem(turned("context", 3), 2) * down_rows, 16), down_rows
    )
    sends.append(
        remote(down_part.at[1, place], down_in_ref, z_sems.at[0, 1], z_sems.at[1, 1], z)
    )
    sends[1].start()
    gate_up_slice(1)
    out(0, gu_part.at[1], gu_part_ref.at[1])
    down_pair(0)
    out(1, down_part, down_part_ref)
    back.middle()
    gate_up_slice(2)
    out(2, gu_part.at[2], gu_part_ref.at[2])
    gate_up_slice(0)
    out(3, gu_part.at[0], gu_part_ref.at[0])
    loads[4].wait()
    for which in range(4):
        span = pl.ds(which * 2 * rows, 2 * rows)
        y[span] = matmul(hidden[span], w_down[...]).astype(BF)
        out(4 + which, y.at[span], y_ref.at[span])
    back.settle()
    for index in range(2):
        dh2_ref[index * rows // 2 : (index + 1) * rows // 2] = back.total(index)
    for copy in outs + sends:
        copy.wait()


def expert_weights(h2_all, dgu, hidden, c_all, du, down):
    total = h2_all.shape[0]
    rows = total // 8
    contexts = lax.axis_size("context")
    slice_rows, down_rows = D // contexts, FF // contexts
    shape = jax.ShapeDtypeStruct
    gu_shape, down_shape = (contexts, slice_rows, 2 * FF), (contexts // 2, 2 * down_rows, D)
    return pl.pallas_call(
        weights_kernel,
        out_shape=[
            shape((rows, D), F32),
            shape(gu_shape, BF),
            shape(down_shape, BF),
            shape(gu_shape[1:], BF),
            shape((down_rows, D), BF),
            shape((total, D), BF),
        ],
        in_specs=[ANY] * 6,
        out_specs=[VM] + [ANY] * 5,
        scratch_shapes=[
            pltpu.VMEM((total, D), BF),
            pltpu.VMEM((total, 2 * FF), BF),
            pltpu.VMEM((total, FF), BF),
            pltpu.VMEM((total, D), BF),
            pltpu.VMEM(down.shape[1:], BF),
            pltpu.VMEM(gu_shape, BF),
            pltpu.VMEM(down_shape, BF),
            pltpu.VMEM((total, D), BF),
            pltpu.SemaphoreType.DMA((5,)),
            pltpu.SemaphoreType.DMA((8,)),
            pltpu.SemaphoreType.DMA((2, 2)),
        ]
        + GroupReturn.scratch(rows),
        compiler_params=pltpu.CompilerParams(
            collective_id=2, has_side_effects=True, vmem_limit_bytes=60 << 20
        ),
        cost_estimate=pl.CostEstimate(
            flops=2 * total * D * FF * 4, bytes_accessed=50 << 20, transcendentals=0
        ),
    )(h2_all, dgu, hidden, c_all, du, down)


def bit_of(axis, bit):
    return lax.rem(lax.axis_index(axis) // bit, 2)


class DenseReduce:
    def __init__(self, part, near, first, second, third, fourth, out, lanes, sems):
        self.part, self.near, self.first, self.second = part, near, first, second
        self.third, self.fourth, self.out, self.lanes = third, fourth, out, lanes
        self.sems = sems
        self.rows = part.shape[1] // 8
        self.slices = part.shape[0]
        self.x, self.y, self.core = flip("dp", 1), flip("expert", 2), flip("expert", 1)
        self.xb, self.yb, self.cb = bit_of("dp", 1), bit_of("expert", 2), bit_of("expert", 1)
        self.pending = []
        self.released = 0

    def send(self, src, dst, peer, amount=1):
        number = len(self.pending)
        copy = remote(src, dst, self.sems.at[0, number], self.sems.at[1, number], peer)
        copy.start()
        self.pending.append(copy)
        self.waited = number + 1 - amount

    def wait(self):
        for copy in self.pending[self.waited :]:
            copy.wait_recv()

    def span(self, bit, size, base=0):
        return pl.ds(pl.multiple_of(base + bit * size, 16), size)

    def start(self):
        size = 4 * self.rows
        self.send(self.part.at[:, self.span(1 - self.cb, size)], self.near, self.core)

    def release(self):
        self.pending[0].wait_send()
        self.released = 1

    def after_core(self):
        self.wait()
        size = 4 * self.rows
        for index in range(self.slices):
            value = self.part[index, self.span(self.cb, size)].astype(F32)
            self.near[index] = (value + self.near[index].astype(F32)).astype(BF)
        size = 2 * self.rows
        self.send(self.near.at[:, self.span(1 - self.yb, size)], self.first, self.y)

    def after_y(self):
        self.wait()
        size = 2 * self.rows
        for index in range(self.slices):
            value = self.near[index, self.span(self.yb, size)].astype(F32)
            self.first[index] = (value + self.first[index].astype(F32)).astype(BF)
        self.send(self.first.at[:, self.span(1 - self.xb, self.rows)], self.second, self.x)

    def after_x(self):
        self.wait()
        for index in range(self.slices):
            value = self.first[index, self.span(self.xb, self.rows)].astype(F32)
            self.second[index] = (value + self.second[index].astype(F32)).astype(BF)
        bit = bit_of("context", 1)
        for index in range(2):
            source = self.second.at[2 * index + 1 - bit]
            self.send(source, self.third.at[index], flip("context", 1), index + 1)

    def after_near_z(self):
        self.wait()
        bit = bit_of("context", 1)
        for index in range(2):
            value = self.second[2 * index + bit].astype(F32) + self.third[index].astype(F32)
            self.third[index] = value.astype(BF)
        bit = bit_of("context", 2)
        self.send(self.third.at[1 - bit], self.fourth, flip("context", 2))

    def held(self, cuts):
        sizes = (1, 2, 4)
        base = self.cb * 4 * self.rows
        if cuts < 2:
            base = base + self.yb * 2 * self.rows
        if cuts < 1:
            base = base + self.xb * self.rows
        rows = pl.ds(pl.multiple_of(base, 16), sizes[cuts] * self.rows)
        return self.out.at[rows, self.lanes]

    def after_far_z(self):
        self.wait()
        value = self.third[bit_of("context", 2)].astype(F32) + self.fourth[...].astype(F32)
        place = self.held(0)
        place[...] = value.astype(BF)
        self.send(place, place, self.x)

    def return_y(self):
        self.wait()
        self.send(self.held(1), self.held(1), self.y)

    def return_core(self):
        self.wait()
        self.send(self.held(2), self.held(2), self.core)

    def finish(self):
        self.wait()
        for copy in self.pending[self.released :]:
            copy.wait_send()

    @staticmethod
    def scratch(contexts, rows, width):
        least = rows // 8
        return [
            pltpu.VMEM((contexts, 4 * least, width), BF),
            pltpu.VMEM((contexts, 2 * least, width), BF),
            pltpu.VMEM((contexts, least, width), BF),
            pltpu.VMEM((2, least, width), BF),
            pltpu.VMEM((least, width), BF),
            pltpu.SemaphoreType.DMA((2, 9)),
        ]


def unrotate(values, cosine, sine):
    return values * cosine - pltpu.roll(values, values.shape[1] // 2, 1) * sine


def norm_pull(values, gain, upstream):
    inverse = lax.rsqrt(jnp.mean(values * values, axis=-1, keepdims=True) + epsilon)
    scaled = upstream * gain
    inner = jnp.mean(scaled * values, axis=-1, keepdims=True)
    grad_in = inverse * scaled - values * (inverse * inverse * inverse * inner)
    return grad_in, jnp.sum(upstream * (values * inverse), axis=0, keepdims=True)


def backward_kernel(
    dh2_ref,
    residual_ref,
    c_ref,
    merged_ref,
    logsum_ref,
    q_ref,
    h1_ref,
    x_ref,
    attn_gain_ref,
    ffn_gain_ref,
    begin_ref,
    cos_ref,
    sin_ref,
    kv_ref,
    w_qkv_ref,
    w_out_ref,
    y_ref,
    gu_part_ref,
    down_part_ref,
    gu_far_ref,
    down_far_ref,
    packed_out_ref,
    packed_grad_ref,
    gains_ref,
    out_proj_ref,
    qkv_grad_ref,
    weights_ref,
    w_dense,
    w_kv,
    kv,
    dres,
    dbranch,
    datt,
    delta,
    bias,
    dq,
    dkv_sum,
    dkv_out,
    dkv_in,
    dqkv,
    dense,
    dense_kv,
    stage_a,
    stage_b,
    near_in,
    far_in,
    gains_in,
    load_sems,
    kv_sems,
    dkv_sems,
    near_sems,
    far_sems,
    x_sems,
    gain_sems,
    *others,
):
    rows = x_ref.shape[0]
    half = rows // 2
    contexts = lax.axis_size("context")
    me = lax.axis_index("context")
    dp = lax.axis_index("dp")
    query_width = QUERY_HEADS * HEAD_SIZE
    key_width = KEY_VALUE_HEADS * HEAD_SIZE
    heads = QUERY_HEADS // KEY_VALUE_HEADS
    scaling = HEAD_SIZE ** (-0.5)
    slice_rows, down_rows = gu_far_ref.shape[0], down_far_ref.shape[0]
    return_scratch, others = others[:5], others[5:]

    def load(number, src, dst):
        copy = pltpu.make_async_copy(src, dst, load_sems.at[number])
        copy.start()
        return copy

    def load_kv(block):
        return pltpu.make_async_copy(kv_ref.at[block], kv.at[block], kv_sems.at[block])

    def begin_load(block, carry):
        load_kv(block).start()
        return carry

    def end_load(block, carry):
        load_kv(block).wait()
        return carry

    gu_span, down_span = pl.ds(0, slice_rows), pl.ds(slice_rows, down_rows)

    def down_place(code):
        first = lax.rem(turned("context", code), 2) * down_rows
        return down_part_ref.at[code // 2, pl.ds(pl.multiple_of(first, 16), down_rows)]

    load_out = load(0, w_out_ref, w_dense)
    stage_loads = [
        load(2, gu_part_ref.at[2], stage_a.at[gu_span]),
        load(3, down_place(2), stage_a.at[down_span]),
        load(4, gu_far_ref, stage_b.at[gu_span]),
        load(5, down_far_ref, stage_b.at[down_span]),
    ]
    lax.fori_loop(0, me + 1, begin_load, 0)
    load_w_kv = load(1, w_qkv_ref.at[:, query_width:], w_kv)

    x, y, core = flip("dp", 1), flip("expert", 2), flip("expert", 1)
    near, far = flip("context", 1), flip("context", 2)
    greet([x, y, core] + [other("context", step) for step in range(1, contexts)])
    back = GroupReturn(y_ref, *return_scratch, rows)
    back.start()

    chunk = down_rows
    chunks = (slice_rows + down_rows) // chunk
    near_copies, far_copies, x_copies = [], [], []
    for index in range(chunks):
        span = pl.ds(index * chunk, chunk)
        source = down_place(1) if index == chunks - 1 else gu_part_ref.at[1, span]
        near_copies.append(
            remote(source, near_in.at[span], near_sems.at[0, index], near_sems.at[1, index], near)
        )
        far_copies.append(
            remote(
                stage_a.at[span], far_in.at[span], far_sems.at[0, index], far_sems.at[1, index], far
            )
        )

    grad_part, gain_grad = norm_pull(residual_ref[...], ffn_gain_ref[...], dh2_ref[...])
    gains_ref[...] = jnp.zeros_like(gains_ref)
    gains_ref[1:2] = gain_grad
    dres[...] = c_ref[...].astype(F32) + grad_part
    dbranch[...] = dres[...].astype(BF)
    for copy in stage_loads:
        copy.wait()
    for index in range(chunks):
        span = pl.ds(index * chunk, chunk)
        value = stage_a[span].astype(F32) + stage_b[span].astype(F32)
        stage_a[span] = value.astype(BF)
        if index == 0:
            far_copies[0].start()
    own_loads = [
        load(6, gu_part_ref.at[0], stage_b.at[gu_span]),
        load(7, down_place(0), stage_b.at[down_span]),
    ]
    load_out.wait()
    datt[...] = matmul(dbranch[...], w_dense[...], NT).astype(BF)
    load_w_q = load(8, w_qkv_ref.at[:, :query_width], w_dense)
    delta[...] = jnp.zeros_like(delta)
    for head in range(QUERY_HEADS):
        lanes = slice(head * HEAD_SIZE, (head + 1) * HEAD_SIZE)
        product = datt[:, lanes].astype(F32) * merged_ref[:, lanes].astype(F32)
        delta[head : head + 1] = jnp.sum(product.T, axis=0, keepdims=True)

    def dense_matmul(target, left, right):
        for index in range(contexts):
            lanes = slice(index * slice_rows, (index + 1) * slice_rows)
            target[index] = matmul(left[:, lanes], right, TN).astype(BF)

    middle = len(others) // 3
    streams = []
    for number, (part, target, lanes) in enumerate(
        (
            (dense, out_proj_ref, slice(0, D)),
            (dense, qkv_grad_ref, slice(0, query_width)),
            (dense_kv, qkv_grad_ref, slice(query_width, query_width + 2 * key_width)),
        )
    ):
        scratch = others[number * middle : (number + 1) * middle]
        streams.append(DenseReduce(part, *scratch[:-1], target, lanes, scratch[-1]))
    out_proj, queries, keys_values = streams
    dense_matmul(dense, merged_ref, dbranch[...])
    out_proj.start()

    back.far()

    lax.fori_loop(0, me + 1, end_load, 0)
    query_pos = me * rows + lax.broadcasted_iota(jnp.int32, (rows, rows), 1)
    dq[...] = jnp.zeros_like(dq)

    def pull(block):
        key_pos = block * rows + lax.broadcasted_iota(jnp.int32, (rows, rows), 0)
        allowed = (key_pos <= query_pos) & (key_pos >= begin_ref[...])
        bias[...] = jnp.where(allowed, 0.0, negative_huge)
        dkv_sum[...] = jnp.zeros_like(dkv_sum)
        for head in range(QUERY_HEADS):
            group = head // heads
            key_lanes = slice(group * HEAD_SIZE, (group + 1) * HEAD_SIZE)
            value_lanes = slice(key_width + group * HEAD_SIZE, key_width + (group + 1) * HEAD_SIZE)
            keys = kv[block, :, key_lanes]
            values = kv[block, :, value_lanes]
            upstream = datt[:, head * HEAD_SIZE : (head + 1) * HEAD_SIZE]
            scores = matmul(keys, q_ref[head], NT) * scaling + bias[...]
            probs = jnp.exp(scores - logsum_ref[head : head + 1])
            dprobs = matmul(values, upstream, NT)
            dscores = (probs * (dprobs - delta[head : head + 1])).astype(BF)
            dkv_sum[:, value_lanes] += matmul(probs.astype(BF), upstream)
            dkv_sum[:, key_lanes] += matmul(dscores, q_ref[head])
            dq[head] += matmul(keys, dscores, TN)

    def dkv_copy(step):
        return remote(
            dkv_out.at[step],
            dkv_in.at[step],
            dkv_sems.at[0, step],
            dkv_sems.at[1, step],
            {"context": lax.rem(me - step + contexts, contexts)},
        )

    def earlier(turn, carry):
        step = me - turn
        pull(turn)
        dkv_out[step] = dkv_sum[...].astype(BF)
        dkv_copy(step).start()
        return carry

    lax.fori_loop(0, me, earlier, 0)
    for index in range(chunks):
        near_copies[index].start()
        if index > 0:
            far_copies[index].start()
    pull(me)
    out_proj.after_core()
    out_proj.release()
    for head in range(QUERY_HEADS):
        lanes = slice(head * HEAD_SIZE, (head + 1) * HEAD_SIZE)
        dqkv[:, lanes] = unrotate(dq[head].T * scaling, cos_ref[...], sin_ref[...]).astype(BF)
    dense_matmul(dense, h1_ref, dqkv[:, :query_width])
    queries.start()
    back.middle()
    queries.after_core()

    def later(step, carry):
        dkv_copy(step).wait_recv()
        dkv_sum[...] += dkv_in[step].astype(F32)
        return carry

    lax.fori_loop(1, contexts - me, later, 0)
    for head in range(KEY_VALUE_HEADS):
        lanes = slice(head * HEAD_SIZE, (head + 1) * HEAD_SIZE)
        place = slice(query_width + head * HEAD_SIZE, query_width + (head + 1) * HEAD_SIZE)
        dqkv[:, place] = unrotate(
            dkv_sum[:, lanes] * scaling, cos_ref[...], sin_ref[...]
        ).astype(BF)
    dqkv[:, query_width + key_width :] = dkv_sum[:, key_width:].astype(BF)
    dense_matmul(dense_kv, h1_ref, dqkv[:, query_width:])
    keys_values.start()
    load_w_q.wait()
    load_w_kv.wait()
    dh1 = matmul(dqkv[:, :query_width], w_dense[...], NT)
    dh1 = dh1 + matmul(dqkv[:, query_width:], w_kv[...], NT)
    grad_part, gain_grad = norm_pull(x_ref[...].astype(F32), attn_gain_ref[...], dh1)
    gains_ref[0:1] = gain_grad
    packed_grad_ref[...] = dres[...] + grad_part

    exchange = [core, y, x, near, far]
    gain_copies = []

    def gain_start():
        step = len(gain_copies)
        copy = remote(
            gains_ref, gains_in.at[step], gain_sems.at[0, step], gain_sems.at[1, step], exchange[step]
        )
        copy.start()
        gain_copies.append(copy)

    def gain_add():
        gain_copies[-1].wait()
        gains_ref[...] += gains_in[len(gain_copies) - 1]

    gain_start()
    back.settle()
    for index in range(2):
        span = slice(index * half, (index + 1) * half)
        packed_out_ref[span] = (residual_ref[span] + back.total(index)).astype(BF)

    out_proj.after_y()
    keys_values.after_core()
    gain_add()
    gain_start()
    queries.after_y()
    out_proj.after_x()
    keys_values.after_y()
    gain_add()
    gain_start()
    queries.after_x()
    keys_values.after_x()
    gain_add()
    gain_start()

    outs = []
    for copy in own_loads:
        copy.wait()

    def weights_out(index):
        near_copies[index].wait_recv()
        far_copies[index].wait_recv()
        span = pl.ds(index * chunk, chunk)
        value = stage_b[span].astype(F32) + near_in[span].astype(F32)
        stage_b[span] = (value + far_in[span].astype(F32)).astype(BF)
        outs.append(load(9 + index, stage_b.at[span], weights_ref.at[dp, span]))
        copy = remote(
            stage_b.at[span],
            weights_ref.at[dp, span],
            x_sems.at[0, index],
            x_sems.at[1, index],
            x,
        )
        copy.start()
        x_copies.append(copy)

    weights_out(0)
    out_proj.after_near_z()
    queries.after_near_z()
    keys_values.after_near_z()
    gain_add()
    gain_start()
    out_proj.after_far_z()
    queries.after_far_z()
    keys_values.after_far_z()
    gain_add()
    weights_out(1)
    for stream in streams:
        stream.return_y()
    weights_out(2)
    for stream in streams:
        stream.return_core()
    for stream in streams:
        stream.finish()

    def sent(step, carry):
        dkv_copy(step).wait_send()
        return carry

    lax.fori_loop(1, me + 1, sent, 0)
    for copy in near_copies + far_copies:
        copy.wait_send()
    for copy in x_copies + outs:
        copy.wait()


def attention_backward(
    dh2,
    residual,
    cotangent,
    merged,
    logsum,
    query,
    h1,
    x,
    attn_gain,
    ffn_gain,
    begins,
    cosine,
    sine,
    kv,
    w_qkv,
    w_out,
    y,
    gu_part,
    down_part,
    gu_far,
    down_far,
):
    rows = x.shape[0]
    contexts = lax.axis_size("context")
    query_width = QUERY_HEADS * HEAD_SIZE
    kv_width = 2 * KEY_VALUE_HEADS * HEAD_SIZE
    slice_rows, down_rows = gu_far.shape[0], down_far.shape[0]
    total = slice_rows + down_rows
    shape = jax.ShapeDtypeStruct
    dma = pltpu.SemaphoreType.DMA
    return pl.pallas_call(
        backward_kernel,
        out_shape=[
            shape((rows, D), BF),
            shape((rows, D), F32),
            shape((8, D), F32),
            shape((slice_rows, D), BF),
            shape((slice_rows, query_width + kv_width), BF),
            shape((2, total, D), BF),
        ],
        in_specs=[VM] * 13 + [ANY] * 8,
        out_specs=[VM] * 5 + [ANY],
        scratch_shapes=[
            pltpu.VMEM(w_out.shape, BF),
            pltpu.VMEM((D, kv_width), BF),
            pltpu.VMEM(kv.shape, BF),
            pltpu.VMEM((rows, D), F32),
            pltpu.VMEM((rows, D), BF),
            pltpu.VMEM((rows, D), BF),
            pltpu.VMEM(logsum.shape, F32),
            pltpu.VMEM((rows, rows), F32),
            pltpu.VMEM((QUERY_HEADS, HEAD_SIZE, rows), F32),
            pltpu.VMEM((rows, kv_width), F32),
            pltpu.VMEM((contexts, rows, kv_width), BF),
            pltpu.VMEM((contexts, rows, kv_width), BF),
            pltpu.VMEM((rows, query_width + kv_width), BF),
            pltpu.VMEM((contexts, slice_rows, D), BF),
            pltpu.VMEM((contexts, slice_rows, kv_width), BF),
            pltpu.VMEM((total, D), BF),
            pltpu.VMEM((total, D), BF),
            pltpu.VMEM((total, D), BF),
            pltpu.VMEM((total, D), BF),
            pltpu.VMEM((5, 8, D), F32),
            dma((9 + total // down_rows,)),
            dma((contexts,)),
            dma((2, contexts)),
            dma((2, total // down_rows)),
            dma((2, total // down_rows)),
            dma((2, total // down_rows)),
            dma((2, 5)),
        ]
        + GroupReturn.scratch(rows)
        + DenseReduce.scratch(contexts, slice_rows, D)
        + DenseReduce.scratch(contexts, slice_rows, query_width)
        + DenseReduce.scratch(contexts, slice_rows, kv_width),
        compiler_params=pltpu.CompilerParams(
            collective_id=3, has_side_effects=True, vmem_limit_bytes=62 << 20
        ),
        cost_estimate=pl.CostEstimate(
            flops=2 * rows * D * 8000, bytes_accessed=40 << 20, transcendentals=rows * rows * 48
        ),
    )(
        dh2,
        residual,
        cotangent,
        merged,
        logsum,
        query,
        h1,
        x,
        attn_gain,
        ffn_gain,
        begins,
        cosine,
        sine,
        kv,
        w_qkv,
        w_out,
        y,
        gu_part,
        down_part,
        gu_far,
        down_far,
    )


def fast_body(
    packed_in,
    routes,
    gates,
    doc_starts,
    attn_gain,
    w_qkv,
    w_out,
    ffn_gain,
    expert_gate_up,
    expert_down,
    cotangent,
):
    x, c = packed_in[0], cotangent[0]
    rows = x.shape[0]
    contexts = lax.axis_size("context")
    expert_total = expert_gate_up.shape[0] * lax.axis_size("expert")
    attn_gain, ffn_gain = attn_gain[None], ffn_gain[None]
    begins, cosine, sine, share = prepare(routes, gates, doc_starts, rows, expert_total)
    h1, query, logsum, merged, residual, h2, kv, c_all, share_all = attention_forward(
        x, share, begins, cosine, sine, attn_gain, ffn_gain, c, w_qkv, w_out
    )
    h2_all, dgu, hidden, du = experts(h2, share_all, c_all, expert_gate_up, expert_down)
    dh2, gu_part, down_part, gu_far, down_far, y = expert_weights(
        h2_all, dgu, hidden, c_all, du, expert_down
    )
    packed_out, packed_grad, gains, out_proj, qkv_grad, weights = attention_backward(
        dh2,
        residual,
        c,
        merged,
        logsum,
        query,
        h1,
        x,
        attn_gain,
        ffn_gain,
        begins,
        cosine,
        sine,
        kv,
        w_qkv,
        w_out,
        y,
        gu_part,
        down_part,
        gu_far,
        down_far,
    )
    slice_rows = D // contexts
    gains = lax.dynamic_slice_in_dim(gains, lax.axis_index("context") * slice_rows, slice_rows, 1)
    return (
        packed_out[None],
        packed_grad[None],
        gains[0],
        qkv_grad.astype(F32),
        out_proj.astype(F32),
        gains[1],
        weights[:, :slice_rows].astype(F32),
        weights[:, slice_rows:].astype(F32),
    )


def fits(mesh):
    sizes = mesh.shape
    contexts = sizes["context"]
    return (
        sizes["dp"] == 2
        and sizes["expert"] == 4
        and contexts == 4
        and D % (contexts * 128) == 0
        and FF % (contexts * 64) == 0
    )


def solution(mesh):
    chosen_body = fast_body if fits(mesh) else body
    placed = (
        P(("dp", "expert"), "context", None),
        P(("dp", "expert"), "context", None),
        P(("dp", "expert"), "context", None),
        P(("dp", "expert"), None),
        P(),
        P(),
        P(),
        P(),
        P("expert", None, None),
        P("expert", None, None),
        P(("dp", "expert"), "context", None),
    )
    return jax.shard_map(
        chosen_body,
        mesh=mesh,
        in_specs=placed,
        out_specs=(
            P(("dp", "expert"), "context", None),
            P(("dp", "expert"), "context", None),
            P("context"),
            P("context", None),
            P("context", None),
            P("context"),
            P("expert", "context", None),
            P("expert", "context", None),
        ),
        check_vma=False,
    )
```

```python
import jax
import jax.numpy as jnp
import numpy as np
from jax import lax
from jax.experimental import pallas as pl
from jax.experimental.pallas import tpu as pltpu
from jax.sharding import PartitionSpec as P

D = 1536
QUERY_HEADS = 12
KEY_VALUE_HEADS = 2
HEAD_SIZE = 128
FF = 768
TOP = 4
CAP = 192


epsilon = 1e-06
rope_base = 10000.0
negative_huge = -1e30


def smooth_gate(preact):
    return jax.nn.gelu(preact, approximate=True)


def norm_rows(values, gain):
    inverse = lax.rsqrt(jnp.mean(values * values, axis=-1, keepdims=True) + epsilon)
    return (values * inverse * gain, inverse)


def norm_back(values, inverse, gain, upstream):
    scaled = upstream * gain
    inner = jnp.mean(scaled * values, axis=-1, keepdims=True)
    grad_in = inverse * scaled - values * inverse * inverse * inverse * inner
    grad_gain = jnp.sum(upstream * values * inverse, axis=0)
    return (grad_in, grad_gain)


def doc_begins(positions, starts):
    return jnp.max(jnp.where(starts[None, :] <= positions[:, None], starts[None, :], 0), axis=1)


def rope_tables(offsets, half_dim):
    frequency = rope_base ** (-(jnp.arange(half_dim, dtype=jnp.float32) * 2.0 / (2.0 * half_dim)))
    angles = offsets.astype(jnp.float32)[:, None] * frequency[None, :]
    return (jnp.cos(angles), jnp.sin(angles))


def apply_rotary(values, cosine_table, sine_values, forward):
    half_dim = cosine_table.shape[1]
    first = values[..., :half_dim]
    second = values[..., half_dim:]
    cosine_wide = cosine_table[:, None, :]
    sine_wide = sine_values[:, None, :]
    if forward:
        return jnp.concatenate(
            [first * cosine_wide - second * sine_wide, second * cosine_wide + first * sine_wide],
            axis=-1,
        )
    return jnp.concatenate(
        [first * cosine_wide + second * sine_wide, second * cosine_wide - first * sine_wide],
        axis=-1,
    )


def fold_keys(
    folded, key_matrix, value_matrix, key_start, query_matrix, positions, begins, scaling
):
    running_max, denominator, weighted = folded
    row_count = key_matrix.shape[0]
    key_pos = key_start + jnp.arange(row_count, dtype=jnp.int32)
    allowed = (key_pos[None, :] <= positions[:, None]) & (key_pos[None, :] >= begins[:, None])
    scores = (
        jnp.einsum("qgha,kga->ghqk", query_matrix, key_matrix, preferred_element_type=jnp.float32)
        * scaling
    )
    masked = jnp.where(allowed, scores, negative_huge)
    new_max = jnp.maximum(running_max, jnp.max(masked, axis=-1))
    weights = jnp.where(allowed, jnp.exp(scores - new_max[..., None]), 0.0)
    shrink = jnp.exp(running_max - new_max)
    denominator = denominator * shrink + jnp.sum(weights, axis=-1)
    weighted = weighted * shrink[..., None] + jnp.einsum(
        "ghqk,kga->ghqa",
        weights.astype(jnp.bfloat16),
        value_matrix,
        preferred_element_type=jnp.float32,
    )
    return (new_max, denominator, weighted)


def attend_back(
    query_matrix,
    output_gradient,
    logsum,
    delta,
    positions,
    begins,
    key_matrix,
    value_matrix,
    key_start,
    scaling,
):
    row_count = key_matrix.shape[0]
    key_pos = key_start + jnp.arange(row_count, dtype=jnp.int32)
    allowed = (key_pos[None, :] <= positions[:, None]) & (key_pos[None, :] >= begins[:, None])
    scores = (
        jnp.einsum("qgha,kga->ghqk", query_matrix, key_matrix, preferred_element_type=jnp.float32)
        * scaling
    )
    probs = jnp.where(allowed, jnp.exp(scores - logsum[..., None]), 0.0)
    grad_probs = jnp.einsum(
        "ghqa,kga->ghqk", output_gradient, value_matrix, preferred_element_type=jnp.float32
    )
    grad_scores = (probs * (grad_probs - delta[..., None])).astype(jnp.bfloat16)
    grad_query = (
        jnp.einsum("ghqk,kga->ghqa", grad_scores, key_matrix, preferred_element_type=jnp.float32)
        * scaling
    )
    grad_key = (
        jnp.einsum("ghqk,qgha->kga", grad_scores, query_matrix, preferred_element_type=jnp.float32)
        * scaling
    )
    grad_value = jnp.einsum(
        "ghqk,ghqa->kga",
        probs.astype(jnp.bfloat16),
        output_gradient,
        preferred_element_type=jnp.float32,
    )
    return (grad_query, grad_key, grad_value)


def body(
    packed_in,
    routes,
    gates,
    doc_starts,
    attn_gain,
    w_qkv,
    w_out,
    ffn_gain,
    expert_gate_up,
    expert_down,
    cotangent,
):
    tokens = packed_in[0].astype(jnp.float32)
    token_count = tokens.shape[0]
    query_groups = QUERY_HEADS // KEY_VALUE_HEADS
    query_width = QUERY_HEADS * HEAD_SIZE
    key_value_width = KEY_VALUE_HEADS * HEAD_SIZE
    scaling = HEAD_SIZE ** (-0.5)
    contexts = lax.axis_size("context")
    own_index = lax.axis_index("context")
    positions = own_index * token_count + jnp.arange(token_count, dtype=jnp.int32)
    last_pos = own_index * token_count + token_count - 1
    begins = doc_begins(positions, doc_starts[0])
    cosine_table, sine_values = rope_tables(positions - begins, HEAD_SIZE // 2)
    normed_a, inverse_a = norm_rows(tokens, attn_gain)
    normed_ab = normed_a.astype(jnp.bfloat16)
    projected_rows = jnp.dot(normed_ab, w_qkv, preferred_element_type=jnp.float32)
    query_matrix = apply_rotary(
        projected_rows[:, :query_width].reshape(token_count, QUERY_HEADS, HEAD_SIZE),
        cosine_table,
        sine_values,
        True,
    )
    query_matrix = query_matrix.astype(jnp.bfloat16).reshape(
        token_count, KEY_VALUE_HEADS, query_groups, HEAD_SIZE
    )
    key_matrix = apply_rotary(
        projected_rows[:, query_width : query_width + key_value_width].reshape(
            token_count, KEY_VALUE_HEADS, HEAD_SIZE
        ),
        cosine_table,
        sine_values,
        True,
    )
    key_matrix = key_matrix.astype(jnp.bfloat16)
    value_matrix = (
        projected_rows[:, query_width + key_value_width :]
        .reshape(token_count, KEY_VALUE_HEADS, HEAD_SIZE)
        .astype(jnp.bfloat16)
    )
    query_layout = (KEY_VALUE_HEADS, query_groups, token_count, HEAD_SIZE)
    start_state = (
        jnp.full((KEY_VALUE_HEADS, query_groups, token_count), negative_huge, jnp.float32),
        jnp.zeros((KEY_VALUE_HEADS, query_groups, token_count), jnp.float32),
        jnp.zeros(query_layout, jnp.float32),
    )
    part_keys = lax.all_gather(key_matrix, "context", axis=0, tiled=True)
    part_values = lax.all_gather(value_matrix, "context", axis=0, tiled=True)
    row_count = part_keys.shape[0]
    width = 512 if row_count > 1024 and row_count % 512 == 0 else row_count

    def inner_step(block_index, state_now):
        offset = block_index * width
        block_keys = lax.dynamic_slice_in_dim(part_keys, block_index * width, width, 0)
        block_values = lax.dynamic_slice_in_dim(part_values, block_index * width, width, 0)

        def update(state_in):
            return fold_keys(
                state_in, block_keys, block_values, offset, query_matrix, positions, begins, scaling
            )

        def unchanged(state_in):
            return state_in

        return lax.cond(offset <= last_pos, update, unchanged, state_now)

    running_max, denominator, weighted = lax.fori_loop(
        0, row_count // width, inner_step, start_state
    )
    attended = weighted / denominator[..., None]
    logsum = running_max + jnp.log(denominator)
    merged_b = (
        jnp.transpose(attended, (2, 0, 1, 3)).reshape(token_count, query_width).astype(jnp.bfloat16)
    )
    residual = tokens + jnp.dot(merged_b, w_out, preferred_element_type=jnp.float32)
    normed_f, inverse_f = norm_rows(residual, ffn_gain)
    normed_fb = normed_f.astype(jnp.bfloat16)
    local_experts = expert_gate_up.shape[0]
    expert_devices = lax.axis_size("expert")
    expert_total = local_experts * expert_devices
    chosen = routes[0].reshape(-1)
    onehot = (chosen[:, None] == jnp.arange(expert_total, dtype=jnp.int32)[None, :]).astype(
        jnp.int32
    )
    slots = jnp.sum((jnp.cumsum(onehot, axis=0) - onehot) * onehot, axis=1)
    repeated = jnp.repeat(normed_fb, TOP, axis=0)
    outgoing = jnp.zeros((expert_total, CAP, D), jnp.bfloat16).at[chosen, slots].set(repeated)
    outgoing = outgoing.reshape(expert_devices, local_experts, CAP, D)
    arrived_rows = lax.all_to_all(outgoing, "expert", split_axis=0, concat_axis=0, tiled=True)
    gate_up_rows = jnp.einsum(
        "sjcd,jdf->sjcf", arrived_rows, expert_gate_up, preferred_element_type=jnp.float32
    )
    hidden = (smooth_gate(gate_up_rows[..., :FF]) * gate_up_rows[..., FF:]).astype(jnp.bfloat16)
    produced = jnp.einsum("sjcf,jfd->sjcd", hidden, expert_down, preferred_element_type=jnp.float32)
    returned_rows = lax.all_to_all(
        produced.astype(jnp.bfloat16), "expert", split_axis=0, concat_axis=0, tiled=True
    )
    picked = (
        returned_rows.reshape(expert_total, CAP, D)[chosen, slots]
        .astype(jnp.float32)
        .reshape(token_count, TOP, D)
    )
    gate_values = gates[0]
    mixture = jnp.sum(gate_values[..., None] * picked, axis=1)
    packed_out = (residual + mixture).astype(jnp.bfloat16)
    upstream = cotangent[0].astype(jnp.float32)
    grad_mix = (
        (gate_values[..., None] * upstream[:, None, :])
        .astype(jnp.bfloat16)
        .reshape(token_count * TOP, D)
    )
    grad_send = jnp.zeros((expert_total, CAP, D), jnp.bfloat16).at[chosen, slots].set(grad_mix)
    grad_send = grad_send.reshape(expert_devices, local_experts, CAP, D)
    grad_arrived = lax.all_to_all(grad_send, "expert", split_axis=0, concat_axis=0, tiled=True)
    gate_part = gate_up_rows[..., :FF]
    up_part = gate_up_rows[..., FF:]
    activated, gelu_back = jax.vjp(smooth_gate, gate_part)
    hidden_b = (activated * up_part).astype(jnp.bfloat16)
    grad_hidden = jnp.einsum(
        "sjcd,jfd->sjcf", grad_arrived, expert_down, preferred_element_type=jnp.float32
    )
    down_grad = jnp.einsum(
        "sjcf,sjcd->jfd", hidden_b, grad_arrived, preferred_element_type=jnp.float32
    )
    grad_gate = gelu_back(grad_hidden * up_part)[0]
    grad_gu = jnp.concatenate([grad_gate, grad_hidden * activated], axis=-1).astype(jnp.bfloat16)
    gate_up_grad = jnp.einsum(
        "sjcd,sjcf->jdf", arrived_rows, grad_gu, preferred_element_type=jnp.float32
    )
    grad_rows = jnp.einsum(
        "sjcf,jdf->sjcd", grad_gu, expert_gate_up, preferred_element_type=jnp.float32
    )
    grad_back = lax.all_to_all(
        grad_rows.astype(jnp.bfloat16), "expert", split_axis=0, concat_axis=0, tiled=True
    )
    grad_picked = grad_back.reshape(expert_total, CAP, D)[chosen, slots].astype(jnp.float32)
    grad_normed_f = jnp.sum(grad_picked.reshape(token_count, TOP, D), axis=1)
    grad_resid_part, ffn_gain_grad = norm_back(residual, inverse_f, ffn_gain, grad_normed_f)
    grad_residual = upstream + grad_resid_part
    grad_branch = grad_residual.astype(jnp.bfloat16)
    out_proj_grad = jnp.einsum(
        "td,tf->df", merged_b, grad_branch, preferred_element_type=jnp.float32
    )
    merged_gradient = jnp.einsum(
        "tf,df->td", grad_branch, w_out, preferred_element_type=jnp.float32
    ).astype(jnp.bfloat16)
    output_gradient = jnp.transpose(
        merged_gradient.reshape(token_count, KEY_VALUE_HEADS, query_groups, HEAD_SIZE), (1, 2, 0, 3)
    )
    delta = jnp.sum(output_gradient.astype(jnp.float32) * attended, axis=-1)

    def block_back(part_keys, part_values, key_start):

        def compute(operands):
            return attend_back(
                query_matrix,
                output_gradient,
                logsum,
                delta,
                positions,
                begins,
                operands[0],
                operands[1],
                key_start,
                scaling,
            )

        def nothing(operands):
            return (
                jnp.zeros(query_layout, jnp.float32),
                jnp.zeros(operands[0].shape, jnp.float32),
                jnp.zeros(operands[1].shape, jnp.float32),
            )

        return lax.cond(key_start <= last_pos, compute, nothing, (part_keys, part_values))

    grad_query = jnp.zeros(query_layout, jnp.float32)
    complete_keys, whole_values = (
        lax.all_gather(key_matrix, "context", axis=0, tiled=True),
        lax.all_gather(value_matrix, "context", axis=0, tiled=True),
    )
    block_span = 2 * token_count

    def block_turn(turn_index, block_state):
        keys_grad_all, values_grad_all, query_sum = block_state
        offset = turn_index * block_span
        add_query, add_key, add_value = block_back(
            lax.dynamic_slice_in_dim(complete_keys, offset, block_span, 0),
            lax.dynamic_slice_in_dim(whole_values, offset, block_span, 0),
            offset,
        )
        keys_grad_all = lax.dynamic_update_slice_in_dim(keys_grad_all, add_key, offset, 0)
        values_grad_all = lax.dynamic_update_slice_in_dim(values_grad_all, add_value, offset, 0)
        return (keys_grad_all, values_grad_all, query_sum + add_query)

    zero_filled = jnp.zeros((complete_keys.shape[0], KEY_VALUE_HEADS, HEAD_SIZE), jnp.float32)
    finished = lax.fori_loop(0, contexts // 2, block_turn, (zero_filled, zero_filled, grad_query))
    grad_keys, grad_values = (
        lax.psum_scatter(
            finished[0].astype(jnp.bfloat16), "context", scatter_dimension=0, tiled=True
        ).astype(jnp.float32),
        lax.psum_scatter(
            finished[1].astype(jnp.bfloat16), "context", scatter_dimension=0, tiled=True
        ).astype(jnp.float32),
    )
    grad_query = finished[2]
    grad_q_rows = apply_rotary(
        jnp.transpose(grad_query, (2, 0, 1, 3)).reshape(token_count, QUERY_HEADS, HEAD_SIZE),
        cosine_table,
        sine_values,
        False,
    )
    grad_k_rows = apply_rotary(grad_keys, cosine_table, sine_values, False)
    grad_projected = jnp.concatenate(
        [
            grad_q_rows.reshape(token_count, query_width),
            grad_k_rows.reshape(token_count, key_value_width),
            grad_values.reshape(token_count, key_value_width),
        ],
        axis=-1,
    ).astype(jnp.bfloat16)
    qkv_grad = jnp.einsum(
        "td,tf->df", normed_ab, grad_projected, preferred_element_type=jnp.float32
    )
    grad_normed_a = jnp.einsum(
        "tf,df->td", grad_projected, w_qkv, preferred_element_type=jnp.float32
    )
    grad_in_part, attn_gain_grad = norm_back(tokens, inverse_a, attn_gain, grad_normed_a)
    packed_grad = grad_residual + grad_in_part
    summed = (
        lax.psum_scatter(
            attn_gain_grad.astype(jnp.bfloat16), "context", scatter_dimension=0, tiled=True
        ).astype(jnp.float32),
        lax.psum_scatter(
            qkv_grad.astype(jnp.bfloat16), "context", scatter_dimension=0, tiled=True
        ).astype(jnp.float32),
        lax.psum_scatter(
            out_proj_grad.astype(jnp.bfloat16), "context", scatter_dimension=0, tiled=True
        ).astype(jnp.float32),
        lax.psum_scatter(
            ffn_gain_grad.astype(jnp.bfloat16), "context", scatter_dimension=0, tiled=True
        ).astype(jnp.float32),
        lax.psum_scatter(
            gate_up_grad.astype(jnp.bfloat16), "context", scatter_dimension=1, tiled=True
        ).astype(jnp.float32),
        lax.psum_scatter(
            down_grad.astype(jnp.bfloat16), "context", scatter_dimension=1, tiled=True
        ).astype(jnp.float32),
    )
    dense_rows = (summed[0], summed[1], summed[2], summed[3])
    expert_sums = (
        lax.psum(summed[4].astype(jnp.bfloat16), "dp").astype(jnp.float32),
        lax.psum(summed[5].astype(jnp.bfloat16), "dp").astype(jnp.float32),
    )
    shared = (
        lax.psum(dense_rows[0].astype(jnp.bfloat16), ("dp", "expert")).astype(jnp.float32),
        lax.psum(dense_rows[1].astype(jnp.bfloat16), ("dp", "expert")).astype(jnp.float32),
        lax.psum(dense_rows[2].astype(jnp.bfloat16), ("dp", "expert")).astype(jnp.float32),
        lax.psum(dense_rows[3].astype(jnp.bfloat16), ("dp", "expert")).astype(jnp.float32),
    )
    return (
        packed_out[None],
        packed_grad[None],
        shared[0],
        shared[1],
        shared[2],
        shared[3],
        expert_sums[0],
        expert_sums[1],
    )


MESH = pl.DeviceIdType.MESH
BF = jnp.bfloat16
F32 = jnp.float32
NN = (((1,), (0,)), ((), ()))
NT = (((1,), (1,)), ((), ()))
TN = (((0,), (0,)), ((), ()))


def matmul(left, right, dims=NN):
    return lax.dot_general(left, right, dims, preferred_element_type=F32)


def flip(axis, bit):
    index = lax.axis_index(axis)
    return {axis: index + bit - 2 * bit * ((index // bit) % 2)}


def greet(peers):
    barrier = pltpu.get_barrier_semaphore()
    for peer in peers:
        pl.semaphore_signal(barrier, inc=1, device_id=peer, device_id_type=MESH)
    pl.semaphore_wait(barrier, len(peers))


def remote(src, dst, send_sem, recv_sem, peer):
    return pltpu.make_async_remote_copy(
        src_ref=src,
        dst_ref=dst,
        send_sem=send_sem,
        recv_sem=recv_sem,
        device_id=peer,
        device_id_type=MESH,
    )


def other(axis, distance):
    size = lax.axis_size(axis)
    return {axis: lax.rem(lax.axis_index(axis) + distance, size)}


def mate(code):
    expert = lax.axis_index("expert")
    for bit in (1, 2):
        if code & bit:
            expert = expert + bit - 2 * bit * ((expert // bit) % 2)
    return {**flip("dp", 1), "expert": expert} if code & 4 else {"expert": expert}


class GroupGather:
    def __init__(self, own, held, sems, rows):
        half = rows // 2
        self.x, self.y, self.core = flip("dp", 1), flip("expert", 2), flip("expert", 1)

        def part(which, index, amount=1):
            return held.at[pl.ds(which * 2 * rows + index * half, amount * half)]

        def link(number, src, dst, peer):
            return remote(src, dst, sems.at[0, number], sems.at[1, number], peer)

        first, second = own.at[pl.ds(0, half)], own.at[pl.ds(half, half)]
        self.links = [
            link(0, first, part(1, 0), self.x),
            link(1, second, part(1, 1), self.y),
            link(2, first, part(2, 0), self.y),
            link(3, second, part(2, 1), self.x),
            link(4, part(1, 0), part(3, 0), self.y),
            link(5, part(1, 1), part(3, 1), self.x),
        ]
        self.cores = [link(6, own, part(0, 2, 2), self.core)]
        for which in range(1, 4):
            self.cores.append(
                link(6 + which, part(which, 0, 2), part(which, 2, 2), self.core)
            )

    def start(self):
        for link in self.links[:4]:
            link.start()
        self.cores[0].start()

    def forward(self, which):
        for index in range(2 * which - 2, 2 * which):
            self.links[index].wait_recv()
            if which == 1:
                self.links[4 + index].start()
        self.cores[which].start()

    def arrived(self, which):
        self.cores[which].wait_recv()

    def finish(self):
        for link in self.links + self.cores:
            link.wait_send()


GATHER_SEMS = pltpu.SemaphoreType.DMA((2, 10))


def rotate(values, cosine, sine):
    return values * cosine + pltpu.roll(values, values.shape[1] // 2, 1) * sine


SLOT_CODES = ((0, 0, 1, 1), (4, 2, 5, 3), (2, 4, 3, 5), (6, 6, 7, 7))


def turned(axis, code):
    index = lax.axis_index(axis)
    bit = 1
    while bit <= code:
        if code & bit:
            index = index + bit - 2 * bit * ((index // bit) % 2)
        bit *= 2
    return index


def gelu_parts(gate):
    slope = 0.7978845608
    bend = 0.044715
    square = gate * gate
    tanh = jnp.tanh(slope * gate * (1.0 + bend * square))
    half = 0.5 * (1.0 + tanh)
    grad = half + 0.5 * slope * gate * (1.0 - tanh * tanh) * (1.0 + 3.0 * bend * square)
    return gate * half, grad


class GroupReturn:
    def __init__(self, source, near, second, third, sems, rows, whole=True):
        self.source, self.rows, self.half = source, rows, rows // 2
        self.near, self.second, self.third = near, second, third
        x, y, core = flip("dp", 1), flip("expert", 2), flip("expert", 1)

        def link(number, src, dst, peer):
            return remote(src, dst, sems.at[0, number], sems.at[1, number], peer)

        def part(which, index):
            return near.at[which, pl.ds(index * self.half, self.half)]

        self.cores = [
            link(6 + which, source.at[pl.ds((2 * which + 1) * rows, rows)], near.at[which], core)
            for which in range(4)
        ]
        self.finals = []
        if whole:
            self.finals = [
                link(0, part(1, 0), third.at[0], x),
                link(1, part(1, 1), third.at[1], y),
            ]
        self.links = [
            link(2, part(2, 0), third.at[2], y),
            link(3, part(2, 1), third.at[3], x),
            link(4, part(3, 0), second.at[0], y),
            link(5, part(3, 1), second.at[1], x),
        ]

    def fold(self, which, index):
        begin = 2 * which * self.rows + index * self.half
        value = self.source[begin : begin + self.half].astype(F32)
        span = slice(index * self.half, (index + 1) * self.half)
        return span, value + self.near[which, span].astype(F32)

    def side(self):
        self.cores[2].wait_recv()
        for index in range(2):
            span, value = self.fold(2, index)
            self.near[2, span] = value.astype(BF)
            self.links[index].start()

    def far(self):
        self.cores[3].wait_recv()
        for index in range(2):
            span, value = self.fold(3, index)
            self.near[3, span] = value.astype(BF)
            self.links[2 + index].start()

    def middle(self):
        self.cores[1].wait_recv()
        for index in range(2):
            self.links[2 + index].wait_recv()
            span, value = self.fold(1, index)
            self.near[1, span] = (value + self.second[index].astype(F32)).astype(BF)

    def last(self):
        for link in self.finals:
            link.start()

    def home(self, index):
        if index == 0:
            self.cores[0].wait_recv()
        self.links[index].wait_recv()
        span, value = self.fold(0, index)
        return span, value + self.third[2 + index].astype(F32)

    def sent(self):
        for copy in self.cores + self.links + self.finals:
            copy.wait_send()


def document_angles(starts_ref, frequency_ref, cosine, sine):
    rows = cosine.shape[0]
    offset = lax.axis_index("context") * rows
    positions = offset + lax.broadcasted_iota(jnp.int32, cosine.shape, 0)
    row_positions = offset + lax.broadcasted_iota(jnp.int32, (1, rows), 1)
    begins = jnp.zeros(cosine.shape, jnp.int32)
    begin_row = jnp.zeros((1, rows), jnp.int32)
    for document in range(starts_ref.shape[0]):
        start = starts_ref[document]
        begins = jnp.maximum(begins, jnp.where(positions >= start, start, 0))
        begin_row = jnp.maximum(begin_row, jnp.where(row_positions >= start, start, 0))
    angles = (positions - begins).astype(F32) * frequency_ref[...]
    cosine[...] = jnp.cos(angles)
    lane = lax.broadcasted_iota(jnp.int32, cosine.shape, 1)
    sine[...] = jnp.where(lane < HEAD_SIZE // 2, -1.0, 1.0) * jnp.sin(angles)
    return begin_row


def gain_row(gain_ref):
    return jnp.concatenate([gain_ref[index : index + 1] for index in range(D // 128)], axis=1)


def front_kernel(
    x_ref,
    routes_ref,
    gates_ref,
    starts_ref,
    frequency_ref,
    attn_gain_ref,
    ffn_gain_ref,
    c_ref,
    w_qkv_ref,
    w_out_ref,
    gate_up_ref,
    down_ref,
    h1_ref,
    q_ref,
    logsum_ref,
    merged_ref,
    residual_ref,
    kv_ref,
    dh2_ref,
    y_home_ref,
    y_side_ref,
    gu_near_ref,
    gu_far_ref,
    down_part_ref,
    gu_in_ref,
    down_in_ref,
    far_in_ref,
    w_gu,
    w_down,
    h2_all,
    c_all,
    dhid,
    gu,
    hidden,
    dgu,
    du,
    share,
    gu_part,
    down_part,
    near,
    second,
    third,
    gu_in,
    dh2,
    y_home,
    kv,
    top,
    total,
    bias,
    cosine,
    sine,
    share_own,
    share_all,
    load_sems,
    out_sems,
    kv_sems,
    keep_sems,
    share_sems,
    c_sems,
    h2_sems,
    z_sems,
    du_sems,
    y_sems,
    credits,
):
    contexts = lax.axis_size("context")
    me = lax.axis_index("context")
    dp = lax.axis_index("dp")
    rows = x_ref.shape[0]
    half = rows // 2
    two = 2 * rows
    slice_rows = gu_part.shape[1]
    first = gu_in.shape[0]
    down_rows = down_part.shape[1] // 2
    query_width = QUERY_HEADS * HEAD_SIZE
    key_width = KEY_VALUE_HEADS * HEAD_SIZE
    heads = QUERY_HEADS // KEY_VALUE_HEADS
    scaling = HEAD_SIZE ** (-0.5)

    w_q = du.at[pl.ds(0, D)]
    h1 = du.at[pl.ds(D, rows)]
    merged = du.at[pl.ds(D + rows, rows)]
    w_out = dgu.at[pl.ds(0, query_width)]
    query = dgu.at[pl.ds(query_width, rows)]
    w_kv = hidden.at[pl.ds(0, D), pl.ds(0, 2 * key_width)]
    residual = y_home

    def accumulated(head):
        across = gu.shape[1] // rows
        return gu.at[
            pl.ds(head // across * HEAD_SIZE, HEAD_SIZE), pl.ds(head % across * rows, rows)
        ]

    def load(number, src, dst):
        copy = pltpu.make_async_copy(src, dst, load_sems.at[number])
        copy.start()
        return copy

    load_kv = load(0, w_qkv_ref.at[:, query_width:], w_kv)
    load_q = load(1, w_qkv_ref.at[:, :query_width], w_q)
    load_c = load(2, c_ref, c_all.at[pl.ds(0, rows)])
    load_out = load(3, w_out_ref, w_out)
    load_down = load(4, down_ref.at[dp], w_down)
    load_gu = load(5, gate_up_ref.at[dp], w_gu)

    begin_row = document_angles(starts_ref, frequency_ref, cosine, sine)
    named = lax.broadcasted_iota(jnp.int32, share_own.shape, 0)
    gathered = jnp.zeros(share_own.shape, F32)
    for choice in range(TOP):
        chosen = routes_ref[choice : choice + 1] == named
        gathered = gathered + jnp.where(chosen, gates_ref[choice : choice + 1], 0.0)
    share_own[...] = gathered

    mates = [mate(code) for code in range(1, 8)]
    greet([other("context", step) for step in range(1, contexts)] + mates)

    c_gather = GroupGather(c_ref, c_all, c_sems, rows)
    c_gather.start()
    shares = [
        remote(
            share_own,
            share_all.at[1 + index],
            share_sems.at[0, index],
            share_sems.at[1, index],
            peer,
        )
        for index, peer in enumerate(mates)
    ]
    for copy in shares:
        copy.start()

    x = x_ref[...].astype(F32)
    inverse = lax.rsqrt(jnp.mean(x * x, axis=-1, keepdims=True) + epsilon)
    h1[...] = (x * inverse * gain_row(attn_gain_ref)).astype(BF)

    load_kv.wait()
    projected = matmul(h1[...], w_kv[...])
    for head in range(KEY_VALUE_HEADS):
        lanes = slice(head * HEAD_SIZE, (head + 1) * HEAD_SIZE)
        kv[me, :, lanes] = rotate(projected[:, lanes], cosine[...], sine[...]).astype(BF)
    kv[me, :, key_width:] = projected[:, key_width:].astype(BF)

    def kv_copy(block):
        return remote(
            kv.at[block],
            kv.at[block],
            kv_sems.at[0, block],
            kv_sems.at[1, block],
            {"context": lax.rem(me + 1, contexts)},
        )

    def pass_on(block):
        @pl.when(me + 1 < contexts)
        def _():
            kv_copy(block).start()

    pass_on(me)

    load_q.wait()
    span = 4 * HEAD_SIZE
    for offset in range(0, query_width, span):
        projected = matmul(h1[...], w_q[:, offset : offset + span])
        for head in range(span // HEAD_SIZE):
            lanes = slice(head * HEAD_SIZE, (head + 1) * HEAD_SIZE)
            place = slice(offset + head * HEAD_SIZE, offset + (head + 1) * HEAD_SIZE)
            query[:, place] = rotate(projected[:, lanes], cosine[...], sine[...]).astype(BF)

    outs = []

    def out(src, dst):
        copy = pltpu.make_async_copy(src, dst, out_sems.at[len(outs)])
        copy.start()
        outs.append(copy)

    out(h1, h1_ref)
    out(query, q_ref)
    top[...] = jnp.full_like(top, negative_huge)
    total[...] = jnp.zeros_like(total)
    gu[...] = jnp.zeros_like(gu)
    query_pos = me * rows + lax.broadcasted_iota(jnp.int32, (rows, rows), 1)

    def fold(block):
        key_pos = block * rows + lax.broadcasted_iota(jnp.int32, (rows, rows), 0)
        allowed = (key_pos <= query_pos) & (key_pos >= begin_row)
        bias[...] = jnp.where(allowed, 0.0, negative_huge)
        for head in range(QUERY_HEADS):
            group = head // heads
            keys = kv[block, :, group * HEAD_SIZE : (group + 1) * HEAD_SIZE]
            values = kv[
                block, :, key_width + group * HEAD_SIZE : key_width + (group + 1) * HEAD_SIZE
            ]
            queries = query[:, head * HEAD_SIZE : (head + 1) * HEAD_SIZE]
            scores = matmul(keys, queries, NT) * scaling + bias[...]
            old = top[head : head + 1]
            new = jnp.maximum(old, jnp.max(scores, axis=0, keepdims=True))
            weights = jnp.exp(scores - new)
            shrink = jnp.exp(old - new)
            top[head : head + 1] = new
            total[head : head + 1] = total[head : head + 1] * shrink + jnp.sum(
                weights, axis=0, keepdims=True
            )
            place = accumulated(head)
            place[...] = place[...] * shrink + matmul(values, weights.astype(BF), TN)

    fold(me)

    def backward_hidden(which):
        rows_of = slice(which * two, (which + 1) * two)
        dhid[which % 2] = matmul(c_all[rows_of], w_down[...], NT)

    for step in range(1, contexts):

        @pl.when(step <= me)
        def _():
            kv_copy(me - step).wait_recv()
            pass_on(me - step)
            fold(me - step)

        if step == 1:
            c_gather.forward(1)
            load_c.wait()
            load_down.wait()
            c_gather.arrived(0)
            backward_hidden(0)
    load_out.wait()
    for head in range(QUERY_HEADS):
        attended = accumulated(head)[...] / total[head : head + 1]
        merged[:, head * HEAD_SIZE : (head + 1) * HEAD_SIZE] = attended.T.astype(BF)
    top[...] = jnp.where(total[...] > 0, top[...] + jnp.log(total[...]), 0.0)
    out(merged, merged_ref)
    out(top, logsum_ref)
    value = x_ref[...].astype(F32) + matmul(merged[...], w_out[...])
    residual[...] = value
    out(residual, residual_ref)
    inverse = lax.rsqrt(jnp.mean(value * value, axis=-1, keepdims=True) + epsilon)
    h2_all[0:rows] = (value * inverse * gain_row(ffn_gain_ref)).astype(BF)

    gather = GroupGather(h2_all.at[pl.ds(0, rows)], h2_all, h2_sems, rows)
    gather.start()

    c_gather.forward(2)
    c_gather.arrived(1)
    backward_hidden(1)

    def keep_copy(block):
        return pltpu.make_async_copy(kv.at[block], kv_ref.at[block], keep_sems.at[block])

    def keep(block, carry):
        keep_copy(block).start()
        return carry

    lax.fori_loop(0, me + 1, keep, 0)
    share_all[0] = share_own[...]
    for copy in shares:
        copy.wait_recv()
    expert = lax.axis_index("expert") * lax.axis_size("dp") + dp
    columns = []
    for code in range(8):
        swapped = share_all[code].T
        mine = lax.broadcasted_iota(jnp.int32, swapped.shape, 1) == expert
        columns.append(jnp.sum(jnp.where(mine, swapped, 0.0), axis=1, keepdims=True))
    for which, codes in enumerate(SLOT_CODES):
        for index, code in enumerate(codes):
            part = (index % 2) * half
            share[pl.ds(which * two + index * half, half), :] = columns[code][part : part + half]

    def forward(which):
        gu[...] = matmul(h2_all[which * two : (which + 1) * two], w_gu[...])

    def activate(which):
        def body_of(step, carry):
            close = pl.ds(pl.multiple_of(step * half, half), half)
            place = pl.ds(pl.multiple_of(which * two + step * half, half), half)
            up = gu[close, FF:]
            activated, grad = gelu_parts(gu[close, :FF])
            scale = share[place, :]
            upstream = dhid[which % 2, close, :] * scale
            hidden[place, :] = (activated * up * scale).astype(BF)
            dgu[place, :FF] = (upstream * up * grad).astype(BF)
            dgu[place, FF:] = (upstream * activated).astype(BF)
            return carry

        lax.fori_loop(0, 4, body_of, 0)

    def backward(which):
        span = slice(which * two, (which + 1) * two)
        du[span] = matmul(dgu[span], w_gu[...], NT).astype(BF)
        back.cores[which].start()

    def gate_up_slice(code, begin, end):
        lane = turned("context", code) * slice_rows + begin
        lanes = pl.ds(pl.multiple_of(lane, 128), end - begin)
        gu_part[code, begin:end] = matmul(h2_all[:, lanes], dgu[...], TN).astype(BF)

    def down_pair(pair):
        first = turned("context", 2 * pair) // 2
        lanes = pl.ds(pl.multiple_of(first * 2 * down_rows, 128), 2 * down_rows)
        down_part[pair] = matmul(hidden[:, lanes], c_all[...], TN).astype(BF)

    back = GroupReturn(du, near, second, third, du_sems, rows)
    load_gu.wait()
    for copy in outs:
        copy.wait()
    gather.arrived(0)
    forward(0)
    activate(0)
    c_gather.arrived(2)
    backward_hidden(2)
    gather.forward(1)
    backward(0)
    gather.arrived(1)
    forward(1)
    activate(1)
    c_gather.forward(3)
    gather.forward(2)
    c_gather.arrived(3)
    backward_hidden(3)
    gather.arrived(2)
    forward(2)
    activate(2)
    gather.forward(3)
    backward(1)
    gather.arrived(3)
    forward(3)
    activate(3)
    z = flip("context", 1)
    sends = []

    def send(src, dst, peer):
        number = len(sends)
        copy = remote(src, dst, z_sems.at[0, number], z_sems.at[1, number], peer)
        copy.start()
        sends.append(copy)

    gate_up_slice(3, 0, first)
    send(gu_part.at[3, pl.ds(0, first)], gu_in, z)
    gate_up_slice(3, first, slice_rows)
    backward(3)
    backward(2)
    down_pair(1)
    back.far()
    back.side()
    gate_up_slice(2, 0, slice_rows)
    out(gu_part.at[2, pl.ds(first, slice_rows - first)], gu_far_ref)
    sends[0].wait_recv()
    send(gu_part.at[3, pl.ds(first, slice_rows - first)], gu_in_ref, z)
    place = pl.ds(
        pl.multiple_of(lax.rem(turned("context", 3), 2) * down_rows, 16), down_rows
    )
    send(down_part.at[1, place], down_in_ref, z)
    value = gu_part[2, :first].astype(F32) + gu_in[...].astype(F32)
    gu_part[2, :first] = value.astype(BF)
    send(gu_part.at[2, pl.ds(0, first)], far_in_ref, flip("context", 2))
    back.middle()
    back.last()
    gate_up_slice(1, 0, slice_rows)
    out(gu_part.at[1], gu_near_ref.at[0])
    down_pair(0)
    out(down_part, down_part_ref)
    gate_up_slice(0, 0, slice_rows)
    out(gu_part.at[0], gu_near_ref.at[1])
    gather.finish()
    for which in range(4):
        span = slice(which * two, (which + 1) * two)
        h2_all[span] = matmul(hidden[span], w_down[...]).astype(BF)
    for index in range(2):
        span, value = back.home(index)
        back.finals[index].wait_recv()
        dh2[span] = value + third[index].astype(F32)
    out(dh2, dh2_ref)
    back.sent()
    for number, mate_of in enumerate((flip("expert", 1), flip("dp", 1), flip("expert", 2))):
        pl.semaphore_signal(
            credits.at[number], inc=1, device_id=mate_of, device_id_type=MESH
        )
    for number in range(3):
        pl.semaphore_wait(credits.at[number], 1)
    back = GroupReturn(h2_all, near, second, third, y_sems, rows, False)
    for which in (3, 2, 1, 0):
        back.cores[which].start()
    back.far()
    back.side()
    back.middle()
    out(near.at[1], y_side_ref)
    for index in range(2):
        span, value = back.home(index)
        y_home[span] = value
    out(y_home, y_home_ref)
    back.sent()
    sends[0].wait_send()
    for copy in outs[5:] + sends[1:]:
        copy.wait()
    c_gather.finish()
    for copy in shares:
        copy.wait_send()

    def settle(block, carry):
        keep_copy(block).wait()

        @pl.when(me + 1 < contexts)
        def _():
            kv_copy(block).wait_send()

        return carry

    lax.fori_loop(0, me + 1, settle, 0)


VM = pl.BlockSpec(memory_space=pltpu.VMEM)
SM = pl.BlockSpec(memory_space=pltpu.SMEM)
ANY = pl.BlockSpec(memory_space=pl.ANY)


def front(
    x, routes, gates, starts, frequency, attn_gain, ffn_gain, cotangent, w_qkv, w_out, gate_up, down
):
    rows = x.shape[0]
    contexts = lax.axis_size("context")
    group = lax.axis_size("dp") * lax.axis_size("expert")
    expert_total = gate_up.shape[0] * lax.axis_size("expert")
    total = group * rows
    kv_width = 2 * KEY_VALUE_HEADS * HEAD_SIZE
    padded = -(-QUERY_HEADS // 8) * 8
    slice_rows, down_rows = D // contexts, FF // contexts
    first = 2 * slice_rows // 3
    gu_shape, down_shape = (contexts, slice_rows, 2 * FF), (contexts // 2, 2 * down_rows, D)
    shape = jax.ShapeDtypeStruct
    dma = pltpu.SemaphoreType.DMA
    return pl.pallas_call(
        front_kernel,
        out_shape=[
            shape((rows, D), BF),
            shape((rows, D), BF),
            shape((padded, rows), F32),
            shape((rows, D), BF),
            shape((rows, D), F32),
            shape((contexts, rows, kv_width), BF),
            shape((rows, D), F32),
            shape((rows, D), F32),
            shape((rows, D), BF),
            shape((2, slice_rows, D), BF),
            shape((slice_rows - first, D), BF),
            shape(down_shape, BF),
            shape((slice_rows - first, D), BF),
            shape((down_rows, D), BF),
            shape((first, D), BF),
        ],
        in_specs=[VM] * 3 + [SM] + [VM] * 3 + [ANY] * 5,
        out_specs=[ANY] * 15,
        scratch_shapes=[
            pltpu.VMEM(gate_up.shape[1:], BF),
            pltpu.VMEM(down.shape[1:], BF),
            pltpu.VMEM((total, D), BF),
            pltpu.VMEM((total, D), BF),
            pltpu.VMEM((2, 2 * rows, FF), F32),
            pltpu.VMEM((2 * rows, 2 * FF), F32),
            pltpu.VMEM((total, FF), BF),
            pltpu.VMEM((total, 2 * FF), BF),
            pltpu.VMEM((total, D), BF),
            pltpu.VMEM((total, 1), F32),
            pltpu.VMEM(gu_shape, BF),
            pltpu.VMEM(down_shape, BF),
            pltpu.VMEM((4, rows, D), BF),
            pltpu.VMEM((2, rows // 2, D), BF),
            pltpu.VMEM((4, rows // 2, D), BF),
            pltpu.VMEM((first, D), BF),
            pltpu.VMEM((rows, D), F32),
            pltpu.VMEM((rows, D), F32),
            pltpu.VMEM((contexts, rows, kv_width), BF),
            pltpu.VMEM((padded, rows), F32),
            pltpu.VMEM((padded, rows), F32),
            pltpu.VMEM((rows, rows), F32),
            pltpu.VMEM((rows, HEAD_SIZE), F32),
            pltpu.VMEM((rows, HEAD_SIZE), F32),
            pltpu.VMEM((expert_total, rows), F32),
            pltpu.VMEM((group, expert_total, rows), F32),
            dma((6,)),
            dma((12,)),
            dma((2, contexts)),
            dma((contexts,)),
            dma((2, group - 1)),
            GATHER_SEMS,
            GATHER_SEMS,
            dma((2, 4)),
            dma((2, 10)),
            dma((2, 10)),
            pltpu.SemaphoreType.REGULAR((3,)),
        ],
        compiler_params=pltpu.CompilerParams(
            collective_id=0, has_side_effects=True, vmem_limit_bytes=63 << 20
        ),
        cost_estimate=pl.CostEstimate(
            flops=2 * total * D * FF * 10, bytes_accessed=40 << 20, transcendentals=total * FF
        ),
    )(
        x,
        routes.T,
        gates.T,
        starts,
        frequency,
        attn_gain,
        ffn_gain,
        cotangent,
        w_qkv,
        w_out,
        gate_up,
        down,
    )


def bit_of(axis, bit):
    return lax.rem(lax.axis_index(axis) // bit, 2)


class DenseReduce:
    def __init__(self, part, near, first, second, third, fourth, sems, out, lanes, order):
        self.part, self.near, self.first, self.second = part, near, first, second
        self.third, self.fourth, self.out, self.lanes = third, fourth, out, lanes
        self.sems = sems
        self.rows = part.shape[1] // 8
        self.slices = part.shape[0]
        (axis, bit), (later_axis, later_bit) = order
        self.core, self.core_bit = flip("expert", 1), bit_of("expert", 1)
        self.one, self.one_bit = flip(axis, bit), bit_of(axis, bit)
        self.two, self.two_bit = flip(later_axis, later_bit), bit_of(later_axis, later_bit)
        self.pending = []
        self.released = 0

    def send(self, src, dst, peer, amount=1):
        number = len(self.pending)
        copy = remote(src, dst, self.sems.at[0, number], self.sems.at[1, number], peer)
        copy.start()
        self.pending.append(copy)
        self.waited = number + 1 - amount

    def wait(self):
        for copy in self.pending[self.waited :]:
            copy.wait_recv()

    def span(self, bit, size, base=0):
        return pl.ds(pl.multiple_of(base + bit * size, 16), size)

    def start(self):
        size = 4 * self.rows
        self.send(self.part.at[:, self.span(1 - self.core_bit, size)], self.near, self.core)

    def release(self):
        self.pending[0].wait_send()
        self.released = 1

    def after_core(self):
        self.wait()
        size = 4 * self.rows
        for index in range(self.slices):
            value = self.part[index, self.span(self.core_bit, size)].astype(F32)
            self.near[index] = (value + self.near[index].astype(F32)).astype(BF)
        size = 2 * self.rows
        self.send(self.near.at[:, self.span(1 - self.one_bit, size)], self.first, self.one)

    def after_one(self):
        self.wait()
        size = 2 * self.rows
        for index in range(self.slices):
            value = self.near[index, self.span(self.one_bit, size)].astype(F32)
            self.first[index] = (value + self.first[index].astype(F32)).astype(BF)
        self.send(self.first.at[:, self.span(1 - self.two_bit, self.rows)], self.second, self.two)

    def after_two(self):
        self.wait()
        for index in range(self.slices):
            value = self.first[index, self.span(self.two_bit, self.rows)].astype(F32)
            self.second[index] = (value + self.second[index].astype(F32)).astype(BF)
        bit = bit_of("context", 1)
        for index in range(2):
            source = self.second.at[2 * index + 1 - bit]
            self.send(source, self.third.at[index], flip("context", 1), index + 1)

    def after_near_z(self):
        self.wait()
        bit = bit_of("context", 1)
        for index in range(2):
            value = self.second[2 * index + bit].astype(F32) + self.third[index].astype(F32)
            self.third[index] = value.astype(BF)
        bit = bit_of("context", 2)
        self.send(self.third.at[1 - bit], self.fourth, flip("context", 2))

    def held(self, cuts):
        sizes = (1, 2, 4)
        base = self.core_bit * 4 * self.rows
        if cuts < 2:
            base = base + self.one_bit * 2 * self.rows
        if cuts < 1:
            base = base + self.two_bit * self.rows
        rows = pl.ds(pl.multiple_of(base, 16), sizes[cuts] * self.rows)
        return self.out.at[rows, self.lanes]

    def after_far_z(self):
        self.wait()
        value = self.third[bit_of("context", 2)].astype(F32) + self.fourth[...].astype(F32)
        place = self.held(0)
        place[...] = value.astype(BF)
        self.send(place, place, self.two)

    def return_one(self):
        self.wait()
        self.send(self.held(1), self.held(1), self.one)

    def return_core(self):
        self.wait()
        self.send(self.held(2), self.held(2), self.core)

    def finish(self):
        self.wait()
        for copy in self.pending[self.released :]:
            copy.wait_send()

    @staticmethod
    def scratch(contexts, rows, width):
        least = rows // 8
        return [
            pltpu.VMEM((contexts, 4 * least, width), BF),
            pltpu.VMEM((contexts, 2 * least, width), BF),
            pltpu.VMEM((contexts, least, width), BF),
            pltpu.VMEM((2, least, width), BF),
            pltpu.VMEM((least, width), BF),
            pltpu.SemaphoreType.DMA((2, 9)),
        ]


X_BIT, Y_BIT = ("dp", 1), ("expert", 2)


def unrotate(values, cosine, sine):
    return values * cosine - pltpu.roll(values, values.shape[1] // 2, 1) * sine


def norm_pull(values, gain, upstream):
    inverse = lax.rsqrt(jnp.mean(values * values, axis=-1, keepdims=True) + epsilon)
    scaled = upstream * gain
    inner = jnp.mean(scaled * values, axis=-1, keepdims=True)
    grad_in = inverse * scaled - values * (inverse * inverse * inverse * inner)
    return grad_in, jnp.sum(upstream * (values * inverse), axis=0, keepdims=True)


def backward_kernel(
    starts_ref,
    frequency_ref,
    attn_gain_ref,
    ffn_gain_ref,
    dh2_in,
    residual_in,
    c_in,
    merged_in,
    logsum_in,
    q_in,
    h1_in,
    x_in,
    y_home_in,
    kv_ref,
    w_qkv_ref,
    w_out_ref,
    y_side_ref,
    gu_near_ref,
    gu_far_ref,
    down_part_ref,
    gu_in_ref,
    down_in_ref,
    far_in_ref,
    packed_out_out,
    packed_grad_out,
    gains_ref,
    out_proj_ref,
    qkv_grad_ref,
    weights_ref,
    dh2_ref,
    residual_ref,
    c_ref,
    merged_ref,
    logsum_ref,
    q_ref,
    h1_ref,
    x_ref,
    y_home_ref,
    packed_out_ref,
    packed_grad_ref,
    cosine,
    sine,
    w_dense,
    w_kv,
    kv,
    dres,
    dbranch,
    datt,
    delta,
    bias,
    dq,
    dkv_sum,
    dkv_out,
    dkv_in,
    dqkv,
    dense,
    dense_kv,
    stage_a,
    stage_b,
    near_in,
    far_in,
    gains_in,
    y_in,
    load_sems,
    kv_sems,
    dkv_sems,
    near_sems,
    far_sems,
    x_sems,
    gain_sems,
    y_sems,
    *others,
):
    rows = x_ref.shape[0]
    half = rows // 2
    contexts = lax.axis_size("context")
    me = lax.axis_index("context")
    dp = lax.axis_index("dp")
    query_width = QUERY_HEADS * HEAD_SIZE
    key_width = KEY_VALUE_HEADS * HEAD_SIZE
    heads = QUERY_HEADS // KEY_VALUE_HEADS
    scaling = HEAD_SIZE ** (-0.5)
    slice_rows, down_rows = gu_near_ref.shape[1], down_in_ref.shape[0]
    first = far_in_ref.shape[0]
    spans = [
        pl.ds(0, first),
        pl.ds(first, slice_rows - first),
        pl.ds(slice_rows, down_rows),
    ]

    def load(number, src, dst):
        copy = pltpu.make_async_copy(src, dst, load_sems.at[number])
        copy.start()
        return copy

    def load_kv(block):
        return pltpu.make_async_copy(kv_ref.at[block], kv.at[block], kv_sems.at[block])

    def begin_load(block, carry):
        load_kv(block).start()
        return carry

    def end_load(block, carry):
        load_kv(block).wait()
        return carry

    def down_place(code):
        first = lax.rem(turned("context", code), 2) * down_rows
        return down_part_ref.at[code // 2, pl.ds(pl.multiple_of(first, 16), down_rows)]

    first_loads = [
        load(13, dh2_in, dh2_ref),
        load(14, residual_in, residual_ref),
        load(15, c_in, c_ref),
    ]
    load_out = load(0, w_out_ref, w_dense)
    later_loads = [
        load(16, merged_in, merged_ref),
        load(17, logsum_in, logsum_ref),
        load(18, q_in, q_ref),
        load(19, h1_in, h1_ref),
        load(20, x_in, x_ref),
        load(21, y_home_in, y_home_ref),
    ]
    stage_loads = [
        load(2, gu_far_ref, stage_a.at[spans[1]]),
        load(3, down_place(2), stage_a.at[spans[2]]),
        load(4, gu_in_ref, stage_b.at[spans[1]]),
        load(5, down_in_ref, stage_b.at[spans[2]]),
    ]
    lax.fori_loop(0, me + 1, begin_load, 0)
    load_w_kv = load(1, w_qkv_ref.at[:, query_width:], w_kv)

    begin_row = document_angles(starts_ref, frequency_ref, cosine, sine)
    x, y, core = flip("dp", 1), flip("expert", 2), flip("expert", 1)
    near, far = flip("context", 1), flip("context", 2)
    greet([x, y, core] + [other("context", step) for step in range(1, contexts)])
    y_copies = []
    for index, peer in enumerate((x, y)):
        span = pl.ds(index * half, half)
        copy = remote(
            y_side_ref.at[span], y_in.at[span], y_sems.at[0, index], y_sems.at[1, index], peer
        )
        copy.start()
        y_copies.append(copy)

    near_copies, far_copies, x_copies = [], [], []
    for index, span in enumerate(spans):
        source = down_place(1) if index == 2 else gu_near_ref.at[0, span]
        near_copies.append(
            remote(source, near_in.at[span], near_sems.at[0, index], near_sems.at[1, index], near)
        )
        if index > 0:
            far_copies.append(
                remote(
                    stage_a.at[span],
                    far_in.at[span],
                    far_sems.at[0, index],
                    far_sems.at[1, index],
                    far,
                )
            )
    near_copies[0].start()
    upward_near, upward_far = lax.rem(me, 2) == 0, me < contexts // 2

    @pl.when(upward_near)
    def _():
        for copy in near_copies[1:]:
            copy.start()

    for copy in first_loads:
        copy.wait()
    grad_part, gain_grad = norm_pull(residual_ref[...], gain_row(ffn_gain_ref), dh2_ref[...])
    gains_ref[...] = jnp.zeros_like(gains_ref)
    gains_ref[1:2] = gain_grad
    dres[...] = c_ref[...].astype(F32) + grad_part
    dbranch[...] = dres[...].astype(BF)
    for copy in stage_loads:
        copy.wait()
    for span in spans[1:]:
        value = stage_a[span].astype(F32) + stage_b[span].astype(F32)
        stage_a[span] = value.astype(BF)

    @pl.when(upward_far)
    def _():
        for copy in far_copies:
            copy.start()

    own_loads = [
        load(6, gu_near_ref.at[1], stage_b.at[pl.ds(0, slice_rows)]),
        load(7, down_place(0), stage_b.at[spans[2]]),
        load(8, far_in_ref, far_in.at[spans[0]]),
    ]
    load_out.wait()
    datt[...] = matmul(dbranch[...], w_dense[...], NT).astype(BF)
    load_w_q = load(9, w_qkv_ref.at[:, :query_width], w_dense)
    for copy in later_loads:
        copy.wait()
    delta[...] = jnp.zeros_like(delta)
    for head in range(QUERY_HEADS):
        lanes = slice(head * HEAD_SIZE, (head + 1) * HEAD_SIZE)
        product = datt[:, lanes].astype(F32) * merged_ref[:, lanes].astype(F32)
        delta[head : head + 1] = jnp.sum(product.T, axis=0, keepdims=True)

    def dense_matmul(target, left, right):
        for index in range(contexts):
            lanes = slice(index * slice_rows, (index + 1) * slice_rows)
            target[index] = matmul(left[:, lanes], right, TN).astype(BF)

    middle = len(others) // 3
    streams = []
    for number, (part, target, lanes, order) in enumerate(
        (
            (dense, out_proj_ref, slice(0, D), (Y_BIT, X_BIT)),
            (dense, qkv_grad_ref, slice(0, query_width), (X_BIT, Y_BIT)),
            (
                dense_kv,
                qkv_grad_ref,
                slice(query_width, query_width + 2 * key_width),
                (Y_BIT, X_BIT),
            ),
        )
    ):
        scratch = others[number * middle : (number + 1) * middle]
        streams.append(DenseReduce(part, *scratch, target, lanes, order))
    out_proj, query_grad, keys_values = streams
    dense_matmul(dense, merged_ref, dbranch[...])
    out_proj.start()

    lax.fori_loop(0, me + 1, end_load, 0)
    query_pos = me * rows + lax.broadcasted_iota(jnp.int32, (rows, rows), 1)
    dq[...] = jnp.zeros_like(dq)

    def pull(block):
        key_pos = block * rows + lax.broadcasted_iota(jnp.int32, (rows, rows), 0)
        allowed = (key_pos <= query_pos) & (key_pos >= begin_row)
        bias[...] = jnp.where(allowed, 0.0, negative_huge)
        dkv_sum[...] = jnp.zeros_like(dkv_sum)
        for head in range(QUERY_HEADS):
            group = head // heads
            key_lanes = slice(group * HEAD_SIZE, (group + 1) * HEAD_SIZE)
            value_lanes = slice(key_width + group * HEAD_SIZE, key_width + (group + 1) * HEAD_SIZE)
            keys = kv[block, :, key_lanes]
            values = kv[block, :, value_lanes]
            lanes = slice(head * HEAD_SIZE, (head + 1) * HEAD_SIZE)
            upstream, queries = datt[:, lanes], q_ref[:, lanes]
            scores = matmul(keys, queries, NT) * scaling + bias[...]
            probs = jnp.exp(scores - logsum_ref[head : head + 1])
            dprobs = matmul(values, upstream, NT)
            dscores = (probs * (dprobs - delta[head : head + 1])).astype(BF)
            dkv_sum[:, value_lanes] += matmul(probs.astype(BF), upstream)
            dkv_sum[:, key_lanes] += matmul(dscores, queries)
            dq[head] += matmul(keys, dscores, TN)

    def dkv_copy(block):
        return remote(
            dkv_out.at[block],
            dkv_in.at[block],
            dkv_sems.at[0, block],
            dkv_sems.at[1, block],
            {"context": lax.rem(me - 1 + contexts, contexts)},
        )

    def earlier(block, carry):
        pull(block)
        dkv_out[block] = dkv_sum[...].astype(BF)

        @pl.when(me + 1 == contexts)
        def _():
            dkv_copy(block).start()

        return carry

    lax.fori_loop(0, me, earlier, 0)
    pull(me)
    out_proj.after_core()
    out_proj.release()
    for head in range(QUERY_HEADS):
        lanes = slice(head * HEAD_SIZE, (head + 1) * HEAD_SIZE)
        dqkv[:, lanes] = unrotate(dq[head].T * scaling, cosine[...], sine[...]).astype(BF)
    dense_matmul(dense, h1_ref, dqkv[:, :query_width])
    query_grad.start()
    query_grad.after_core()

    def pass_back(block, carry):
        dkv_copy(block).wait_recv()
        value = dkv_out[block].astype(F32) + dkv_in[block].astype(F32)
        dkv_out[block] = value.astype(BF)
        dkv_copy(block).start()
        return carry

    @pl.when(me + 1 < contexts)
    def _():
        lax.fori_loop(0, me, pass_back, 0)
        dkv_copy(me).wait_recv()
        dkv_sum[...] += dkv_in[me].astype(F32)

    @pl.when(jnp.logical_not(upward_near))
    def _():
        for copy in near_copies[1:]:
            copy.start()

    for head in range(KEY_VALUE_HEADS):
        lanes = slice(head * HEAD_SIZE, (head + 1) * HEAD_SIZE)
        place = slice(query_width + head * HEAD_SIZE, query_width + (head + 1) * HEAD_SIZE)
        dqkv[:, place] = unrotate(
            dkv_sum[:, lanes] * scaling, cosine[...], sine[...]
        ).astype(BF)
    dqkv[:, query_width + key_width :] = dkv_sum[:, key_width:].astype(BF)
    dense_matmul(dense_kv, h1_ref, dqkv[:, query_width:])
    keys_values.start()
    load_w_q.wait()
    load_w_kv.wait()
    dh1 = matmul(dqkv[:, :query_width], w_dense[...], NT)
    dh1 = dh1 + matmul(dqkv[:, query_width:], w_kv[...], NT)
    grad_part, gain_grad = norm_pull(x_ref[...].astype(F32), gain_row(attn_gain_ref), dh1)
    gains_ref[0:1] = gain_grad
    packed_grad_ref[...] = dres[...] + grad_part
    outs = [load(22, packed_grad_ref, packed_grad_out)]

    exchange = [core, y, x, near, far]
    gain_copies = []

    def gain_start():
        step = len(gain_copies)
        copy = remote(
            gains_ref, gains_in.at[step], gain_sems.at[0, step], gain_sems.at[1, step], exchange[step]
        )
        copy.start()
        gain_copies.append(copy)

    def gain_add():
        gain_copies[-1].wait()
        gains_ref[...] += gains_in[len(gain_copies) - 1]

    gain_start()
    for copy in y_copies:
        copy.wait()
    mixture = y_home_ref[...] + y_in[...].astype(F32)
    packed_out_ref[...] = (residual_ref[...] + mixture).astype(BF)
    outs.append(load(23, packed_out_ref, packed_out_out))

    out_proj.after_one()

    @pl.when(jnp.logical_not(upward_far))
    def _():
        for copy in far_copies:
            copy.start()

    keys_values.after_core()
    gain_add()
    gain_start()
    query_grad.after_one()
    keys_values.after_one()
    gain_add()
    gain_start()
    out_proj.after_two()
    query_grad.after_two()
    keys_values.after_two()
    gain_add()
    gain_start()

    for copy in own_loads:
        copy.wait()

    def weights_out(index):
        near_copies[index].wait_recv()
        if index > 0:
            far_copies[index - 1].wait_recv()
        span = spans[index]
        value = stage_b[span].astype(F32) + near_in[span].astype(F32)
        stage_b[span] = (value + far_in[span].astype(F32)).astype(BF)
        outs.append(load(10 + index, stage_b.at[span], weights_ref.at[dp, span]))
        copy = remote(
            stage_b.at[span],
            weights_ref.at[dp, span],
            x_sems.at[0, index],
            x_sems.at[1, index],
            x,
        )
        copy.start()
        x_copies.append(copy)

    weights_out(0)
    out_proj.after_near_z()
    query_grad.after_near_z()
    keys_values.after_near_z()
    gain_add()
    gain_start()
    weights_out(1)
    weights_out(2)
    out_proj.after_far_z()
    query_grad.after_far_z()
    keys_values.after_far_z()
    gain_add()
    for stream in streams:
        stream.return_one()
    for stream in streams:
        stream.return_core()
    for stream in streams:
        stream.finish()

    def sent(block, carry):
        dkv_copy(block).wait_send()
        return carry

    lax.fori_loop(0, me, sent, 0)
    for copy in near_copies + far_copies:
        copy.wait_send()
    for copy in x_copies + outs:
        copy.wait()


def backward(starts, frequency, attn_gain, ffn_gain, *arrays):
    dh2, _, _, _, logsum, _, _, _, _, kv, w_qkv, w_out = arrays[:12]
    gu_near, _, _, _, down_in, _ = arrays[13:]
    rows = dh2.shape[0]
    contexts = lax.axis_size("context")
    query_width = QUERY_HEADS * HEAD_SIZE
    kv_width = 2 * KEY_VALUE_HEADS * HEAD_SIZE
    slice_rows, down_rows = gu_near.shape[1], down_in.shape[0]
    total = slice_rows + down_rows
    shape = jax.ShapeDtypeStruct
    dma = pltpu.SemaphoreType.DMA
    return pl.pallas_call(
        backward_kernel,
        out_shape=[
            shape((rows, D), BF),
            shape((rows, D), F32),
            shape((8, D), F32),
            shape((slice_rows, D), BF),
            shape((slice_rows, query_width + kv_width), BF),
            shape((2, total, D), BF),
        ],
        in_specs=[SM] + [VM] * 3 + [ANY] * 19,
        out_specs=[ANY] * 2 + [VM] * 3 + [ANY],
        scratch_shapes=[pltpu.VMEM(array.shape, array.dtype) for array in arrays[:9]]
        + [
            pltpu.VMEM((rows, D), BF),
            pltpu.VMEM((rows, D), F32),
            pltpu.VMEM((rows, HEAD_SIZE), F32),
            pltpu.VMEM((rows, HEAD_SIZE), F32),
            pltpu.VMEM(w_out.shape, BF),
            pltpu.VMEM((D, kv_width), BF),
            pltpu.VMEM(kv.shape, BF),
            pltpu.VMEM((rows, D), F32),
            pltpu.VMEM((rows, D), BF),
            pltpu.VMEM((rows, D), BF),
            pltpu.VMEM(logsum.shape, F32),
            pltpu.VMEM((rows, rows), F32),
            pltpu.VMEM((QUERY_HEADS, HEAD_SIZE, rows), F32),
            pltpu.VMEM((rows, kv_width), F32),
            pltpu.VMEM((contexts, rows, kv_width), BF),
            pltpu.VMEM((contexts, rows, kv_width), BF),
            pltpu.VMEM((rows, query_width + kv_width), BF),
            pltpu.VMEM((contexts, slice_rows, D), BF),
            pltpu.VMEM((contexts, slice_rows, kv_width), BF),
            pltpu.VMEM((total, D), BF),
            pltpu.VMEM((total, D), BF),
            pltpu.VMEM((total, D), BF),
            pltpu.VMEM((total, D), BF),
            pltpu.VMEM((5, 8, D), F32),
            pltpu.VMEM((rows, D), BF),
            dma((24,)),
            dma((contexts,)),
            dma((2, contexts)),
            dma((2, 3)),
            dma((2, 3)),
            dma((2, 3)),
            dma((2, 5)),
            dma((2, 2)),
        ]
        + DenseReduce.scratch(contexts, slice_rows, D)
        + DenseReduce.scratch(contexts, slice_rows, query_width)
        + DenseReduce.scratch(contexts, slice_rows, kv_width),
        compiler_params=pltpu.CompilerParams(
            collective_id=3, has_side_effects=True, vmem_limit_bytes=62 << 20
        ),
        cost_estimate=pl.CostEstimate(
            flops=2 * rows * D * 8000, bytes_accessed=40 << 20, transcendentals=rows * rows * 48
        ),
    )(starts, frequency, attn_gain, ffn_gain, *arrays)


def widen_kernel(
    packed_out_ref,
    packed_grad_ref,
    gains_ref,
    out_proj_ref,
    qkv_grad_ref,
    weights_ref,
    packed_out,
    packed_grad,
    attn_gain_grad,
    qkv_grad,
    out_proj,
    ffn_gain_grad,
    gate_up_grad,
    down_grad,
    *scratch,
):
    narrow, wide, held, sems = scratch[:6], scratch[6:12], scratch[12:14], scratch[14]
    slice_rows = out_proj_ref.shape[0]
    arrivals = [
        pltpu.make_async_copy(packed_out_ref, held[0], sems.at[0, 6]),
        pltpu.make_async_copy(packed_grad_ref, held[1], sems.at[0, 7]),
    ]
    moves = [
        pltpu.make_async_copy(held[0], packed_out, sems.at[1, 6]),
        pltpu.make_async_copy(held[1], packed_grad, sems.at[1, 7]),
    ]
    sources = [weights_ref.at[expert, pl.ds(0, slice_rows)] for expert in range(2)]
    sources += [
        weights_ref.at[expert, pl.ds(slice_rows, slice_rows // 2)] for expert in range(2)
    ]
    sources += [qkv_grad_ref, out_proj_ref]
    targets = [gate_up_grad.at[0], gate_up_grad.at[1], down_grad.at[0], down_grad.at[1]]
    targets += [qkv_grad, out_proj]
    loads, stores = [], []
    for index, source in enumerate(sources):
        loads.append(pltpu.make_async_copy(source, narrow[index], sems.at[0, index]))
        stores.append(pltpu.make_async_copy(wide[index], targets[index], sems.at[1, index]))
    for copy in loads + arrivals:
        copy.start()
    place = pl.ds(
        pl.multiple_of(lax.axis_index("context") * slice_rows, 128), slice_rows
    )
    attn_gain_grad[...] = gains_ref[0:1, place]
    ffn_gain_grad[...] = gains_ref[1:2, place]
    for index in range(6):
        loads[index].wait()
        wide[index][...] = narrow[index][...].astype(F32)
        stores[index].start()
    for arrival, move in zip(arrivals, moves):
        arrival.wait()
        move.start()
    for copy in stores + moves:
        copy.wait()


def widen(packed_out, packed_grad, gains, out_proj, qkv_grad, weights):
    slice_rows, total = out_proj.shape[0], weights.shape[1]
    parts = [(slice_rows, D)] * 2 + [(total - slice_rows, D)] * 2
    parts += [qkv_grad.shape, out_proj.shape]
    shape = jax.ShapeDtypeStruct
    return pl.pallas_call(
        widen_kernel,
        out_shape=[
            shape(packed_out.shape, BF),
            shape(packed_grad.shape, F32),
            shape((1, slice_rows), F32),
            shape(qkv_grad.shape, F32),
            shape(out_proj.shape, F32),
            shape((1, slice_rows), F32),
            shape((2, slice_rows, D), F32),
            shape((2, total - slice_rows, D), F32),
        ],
        in_specs=[ANY] * 2 + [VM] + [ANY] * 3,
        out_specs=[ANY] * 2 + [VM] + [ANY] * 2 + [VM] + [ANY] * 2,
        scratch_shapes=[pltpu.VMEM(part, BF) for part in parts]
        + [pltpu.VMEM(part, F32) for part in parts]
        + [pltpu.VMEM(packed_out.shape, BF), pltpu.VMEM(packed_grad.shape, F32)]
        + [pltpu.SemaphoreType.DMA((2, 8))],
        compiler_params=pltpu.CompilerParams(vmem_limit_bytes=62 << 20),
        cost_estimate=pl.CostEstimate(flops=0, bytes_accessed=24 << 20, transcendentals=0),
    )(packed_out, packed_grad, gains, out_proj, qkv_grad, weights)


def fast_body(
    packed_in,
    routes,
    gates,
    doc_starts,
    attn_gain,
    w_qkv,
    w_out,
    ffn_gain,
    expert_gate_up,
    expert_down,
    cotangent,
):
    x, c, starts = packed_in[0], cotangent[0], doc_starts[0]
    steps = np.arange(HEAD_SIZE) % (HEAD_SIZE // 2)
    frequency = jnp.asarray((rope_base ** (-2.0 * steps / HEAD_SIZE)).astype(np.float32)[None])
    attn_gain, ffn_gain = attn_gain.reshape(-1, 128), ffn_gain.reshape(-1, 128)
    h1, query, logsum, merged, residual, kv, dh2, y_home, y_side, *weight_parts = front(
        x,
        routes[0],
        gates[0],
        starts,
        frequency,
        attn_gain,
        ffn_gain,
        c,
        w_qkv,
        w_out,
        expert_gate_up,
        expert_down,
    )
    sums = backward(
        starts,
        frequency,
        attn_gain,
        ffn_gain,
        dh2,
        residual,
        c,
        merged,
        logsum,
        query,
        h1,
        x,
        y_home,
        kv,
        w_qkv,
        w_out,
        y_side,
        *weight_parts,
    )
    packed_out, packed_grad, attn_grad, qkv_grad, out_proj, ffn_grad, gate_up, down = widen(*sums)
    return (
        packed_out[None],
        packed_grad[None],
        attn_grad[0],
        qkv_grad,
        out_proj,
        ffn_grad[0],
        gate_up,
        down,
    )


def fits(mesh):
    sizes = mesh.shape
    contexts = sizes["context"]
    return (
        sizes["dp"] == 2
        and sizes["expert"] == 4
        and contexts == 4
        and D % (contexts * 384) == 0
        and FF % (contexts * 64) == 0
    )


def solution(mesh):
    chosen_body = fast_body if fits(mesh) else body
    placed = (
        P(("dp", "expert"), "context", None),
        P(("dp", "expert"), "context", None),
        P(("dp", "expert"), "context", None),
        P(("dp", "expert"), None),
        P(),
        P(),
        P(),
        P(),
        P("expert", None, None),
        P("expert", None, None),
        P(("dp", "expert"), "context", None),
    )
    return jax.shard_map(
        chosen_body,
        mesh=mesh,
        in_specs=placed,
        out_specs=(
            P(("dp", "expert"), "context", None),
            P(("dp", "expert"), "context", None),
            P("context"),
            P("context", None),
            P("context", None),
            P("context"),
            P("expert", "context", None),
            P("expert", "context", None),
        ),
        check_vma=False,
    )
```

```python
import jax
import jax.numpy as jnp
import numpy as np
from jax import lax
from jax.experimental import pallas as pl
from jax.experimental.pallas import tpu as pltpu
from jax.sharding import PartitionSpec as P

D = 1536
QUERY_HEADS = 12
KEY_VALUE_HEADS = 2
HEAD_SIZE = 128
FF = 768
TOP = 4
CAP = 192


epsilon = 1e-06
rope_base = 10000.0
negative_huge = -1e30


def smooth_gate(preact):
    return jax.nn.gelu(preact, approximate=True)


def norm_rows(values, gain):
    inverse = lax.rsqrt(jnp.mean(values * values, axis=-1, keepdims=True) + epsilon)
    return (values * inverse * gain, inverse)


def norm_back(values, inverse, gain, upstream):
    scaled = upstream * gain
    inner = jnp.mean(scaled * values, axis=-1, keepdims=True)
    grad_in = inverse * scaled - values * inverse * inverse * inverse * inner
    grad_gain = jnp.sum(upstream * values * inverse, axis=0)
    return (grad_in, grad_gain)


def doc_begins(positions, starts):
    return jnp.max(jnp.where(starts[None, :] <= positions[:, None], starts[None, :], 0), axis=1)


def rope_tables(offsets, half_dim):
    frequency = rope_base ** (-(jnp.arange(half_dim, dtype=jnp.float32) * 2.0 / (2.0 * half_dim)))
    angles = offsets.astype(jnp.float32)[:, None] * frequency[None, :]
    return (jnp.cos(angles), jnp.sin(angles))


def apply_rotary(values, cosine_table, sine_values, forward):
    half_dim = cosine_table.shape[1]
    first = values[..., :half_dim]
    second = values[..., half_dim:]
    cosine_wide = cosine_table[:, None, :]
    sine_wide = sine_values[:, None, :]
    if forward:
        return jnp.concatenate(
            [first * cosine_wide - second * sine_wide, second * cosine_wide + first * sine_wide],
            axis=-1,
        )
    return jnp.concatenate(
        [first * cosine_wide + second * sine_wide, second * cosine_wide - first * sine_wide],
        axis=-1,
    )


def fold_keys(
    folded, key_matrix, value_matrix, key_start, query_matrix, positions, begins, scaling
):
    running_max, denominator, weighted = folded
    row_count = key_matrix.shape[0]
    key_pos = key_start + jnp.arange(row_count, dtype=jnp.int32)
    allowed = (key_pos[None, :] <= positions[:, None]) & (key_pos[None, :] >= begins[:, None])
    scores = (
        jnp.einsum("qgha,kga->ghqk", query_matrix, key_matrix, preferred_element_type=jnp.float32)
        * scaling
    )
    masked = jnp.where(allowed, scores, negative_huge)
    new_max = jnp.maximum(running_max, jnp.max(masked, axis=-1))
    weights = jnp.where(allowed, jnp.exp(scores - new_max[..., None]), 0.0)
    shrink = jnp.exp(running_max - new_max)
    denominator = denominator * shrink + jnp.sum(weights, axis=-1)
    weighted = weighted * shrink[..., None] + jnp.einsum(
        "ghqk,kga->ghqa",
        weights.astype(jnp.bfloat16),
        value_matrix,
        preferred_element_type=jnp.float32,
    )
    return (new_max, denominator, weighted)


def attend_back(
    query_matrix,
    output_gradient,
    logsum,
    delta,
    positions,
    begins,
    key_matrix,
    value_matrix,
    key_start,
    scaling,
):
    row_count = key_matrix.shape[0]
    key_pos = key_start + jnp.arange(row_count, dtype=jnp.int32)
    allowed = (key_pos[None, :] <= positions[:, None]) & (key_pos[None, :] >= begins[:, None])
    scores = (
        jnp.einsum("qgha,kga->ghqk", query_matrix, key_matrix, preferred_element_type=jnp.float32)
        * scaling
    )
    probs = jnp.where(allowed, jnp.exp(scores - logsum[..., None]), 0.0)
    grad_probs = jnp.einsum(
        "ghqa,kga->ghqk", output_gradient, value_matrix, preferred_element_type=jnp.float32
    )
    grad_scores = (probs * (grad_probs - delta[..., None])).astype(jnp.bfloat16)
    grad_query = (
        jnp.einsum("ghqk,kga->ghqa", grad_scores, key_matrix, preferred_element_type=jnp.float32)
        * scaling
    )
    grad_key = (
        jnp.einsum("ghqk,qgha->kga", grad_scores, query_matrix, preferred_element_type=jnp.float32)
        * scaling
    )
    grad_value = jnp.einsum(
        "ghqk,ghqa->kga",
        probs.astype(jnp.bfloat16),
        output_gradient,
        preferred_element_type=jnp.float32,
    )
    return (grad_query, grad_key, grad_value)


def body(
    packed_in,
    routes,
    gates,
    doc_starts,
    attn_gain,
    w_qkv,
    w_out,
    ffn_gain,
    expert_gate_up,
    expert_down,
    cotangent,
):
    tokens = packed_in[0].astype(jnp.float32)
    token_count = tokens.shape[0]
    query_groups = QUERY_HEADS // KEY_VALUE_HEADS
    query_width = QUERY_HEADS * HEAD_SIZE
    key_value_width = KEY_VALUE_HEADS * HEAD_SIZE
    scaling = HEAD_SIZE ** (-0.5)
    contexts = lax.axis_size("context")
    own_index = lax.axis_index("context")
    positions = own_index * token_count + jnp.arange(token_count, dtype=jnp.int32)
    last_pos = own_index * token_count + token_count - 1
    begins = doc_begins(positions, doc_starts[0])
    cosine_table, sine_values = rope_tables(positions - begins, HEAD_SIZE // 2)
    normed_a, inverse_a = norm_rows(tokens, attn_gain)
    normed_ab = normed_a.astype(jnp.bfloat16)
    projected_rows = jnp.dot(normed_ab, w_qkv, preferred_element_type=jnp.float32)
    query_matrix = apply_rotary(
        projected_rows[:, :query_width].reshape(token_count, QUERY_HEADS, HEAD_SIZE),
        cosine_table,
        sine_values,
        True,
    )
    query_matrix = query_matrix.astype(jnp.bfloat16).reshape(
        token_count, KEY_VALUE_HEADS, query_groups, HEAD_SIZE
    )
    key_matrix = apply_rotary(
        projected_rows[:, query_width : query_width + key_value_width].reshape(
            token_count, KEY_VALUE_HEADS, HEAD_SIZE
        ),
        cosine_table,
        sine_values,
        True,
    )
    key_matrix = key_matrix.astype(jnp.bfloat16)
    value_matrix = (
        projected_rows[:, query_width + key_value_width :]
        .reshape(token_count, KEY_VALUE_HEADS, HEAD_SIZE)
        .astype(jnp.bfloat16)
    )
    query_layout = (KEY_VALUE_HEADS, query_groups, token_count, HEAD_SIZE)
    start_state = (
        jnp.full((KEY_VALUE_HEADS, query_groups, token_count), negative_huge, jnp.float32),
        jnp.zeros((KEY_VALUE_HEADS, query_groups, token_count), jnp.float32),
        jnp.zeros(query_layout, jnp.float32),
    )
    part_keys = lax.all_gather(key_matrix, "context", axis=0, tiled=True)
    part_values = lax.all_gather(value_matrix, "context", axis=0, tiled=True)
    row_count = part_keys.shape[0]
    width = 512 if row_count > 1024 and row_count % 512 == 0 else row_count

    def inner_step(block_index, state_now):
        offset = block_index * width
        block_keys = lax.dynamic_slice_in_dim(part_keys, block_index * width, width, 0)
        block_values = lax.dynamic_slice_in_dim(part_values, block_index * width, width, 0)

        def update(state_in):
            return fold_keys(
                state_in, block_keys, block_values, offset, query_matrix, positions, begins, scaling
            )

        def unchanged(state_in):
            return state_in

        return lax.cond(offset <= last_pos, update, unchanged, state_now)

    running_max, denominator, weighted = lax.fori_loop(
        0, row_count // width, inner_step, start_state
    )
    attended = weighted / denominator[..., None]
    logsum = running_max + jnp.log(denominator)
    merged_b = (
        jnp.transpose(attended, (2, 0, 1, 3)).reshape(token_count, query_width).astype(jnp.bfloat16)
    )
    residual = tokens + jnp.dot(merged_b, w_out, preferred_element_type=jnp.float32)
    normed_f, inverse_f = norm_rows(residual, ffn_gain)
    normed_fb = normed_f.astype(jnp.bfloat16)
    local_experts = expert_gate_up.shape[0]
    expert_devices = lax.axis_size("expert")
    expert_total = local_experts * expert_devices
    chosen = routes[0].reshape(-1)
    onehot = (chosen[:, None] == jnp.arange(expert_total, dtype=jnp.int32)[None, :]).astype(
        jnp.int32
    )
    slots = jnp.sum((jnp.cumsum(onehot, axis=0) - onehot) * onehot, axis=1)
    repeated = jnp.repeat(normed_fb, TOP, axis=0)
    outgoing = jnp.zeros((expert_total, CAP, D), jnp.bfloat16).at[chosen, slots].set(repeated)
    outgoing = outgoing.reshape(expert_devices, local_experts, CAP, D)
    arrived_rows = lax.all_to_all(outgoing, "expert", split_axis=0, concat_axis=0, tiled=True)
    gate_up_rows = jnp.einsum(
        "sjcd,jdf->sjcf", arrived_rows, expert_gate_up, preferred_element_type=jnp.float32
    )
    hidden = (smooth_gate(gate_up_rows[..., :FF]) * gate_up_rows[..., FF:]).astype(jnp.bfloat16)
    produced = jnp.einsum("sjcf,jfd->sjcd", hidden, expert_down, preferred_element_type=jnp.float32)
    returned_rows = lax.all_to_all(
        produced.astype(jnp.bfloat16), "expert", split_axis=0, concat_axis=0, tiled=True
    )
    picked = (
        returned_rows.reshape(expert_total, CAP, D)[chosen, slots]
        .astype(jnp.float32)
        .reshape(token_count, TOP, D)
    )
    gate_values = gates[0]
    mixture = jnp.sum(gate_values[..., None] * picked, axis=1)
    packed_out = (residual + mixture).astype(jnp.bfloat16)
    upstream = cotangent[0].astype(jnp.float32)
    grad_mix = (
        (gate_values[..., None] * upstream[:, None, :])
        .astype(jnp.bfloat16)
        .reshape(token_count * TOP, D)
    )
    grad_send = jnp.zeros((expert_total, CAP, D), jnp.bfloat16).at[chosen, slots].set(grad_mix)
    grad_send = grad_send.reshape(expert_devices, local_experts, CAP, D)
    grad_arrived = lax.all_to_all(grad_send, "expert", split_axis=0, concat_axis=0, tiled=True)
    gate_part = gate_up_rows[..., :FF]
    up_part = gate_up_rows[..., FF:]
    activated, gelu_back = jax.vjp(smooth_gate, gate_part)
    hidden_b = (activated * up_part).astype(jnp.bfloat16)
    grad_hidden = jnp.einsum(
        "sjcd,jfd->sjcf", grad_arrived, expert_down, preferred_element_type=jnp.float32
    )
    down_grad = jnp.einsum(
        "sjcf,sjcd->jfd", hidden_b, grad_arrived, preferred_element_type=jnp.float32
    )
    grad_gate = gelu_back(grad_hidden * up_part)[0]
    grad_gu = jnp.concatenate([grad_gate, grad_hidden * activated], axis=-1).astype(jnp.bfloat16)
    gate_up_grad = jnp.einsum(
        "sjcd,sjcf->jdf", arrived_rows, grad_gu, preferred_element_type=jnp.float32
    )
    grad_rows = jnp.einsum(
        "sjcf,jdf->sjcd", grad_gu, expert_gate_up, preferred_element_type=jnp.float32
    )
    grad_back = lax.all_to_all(
        grad_rows.astype(jnp.bfloat16), "expert", split_axis=0, concat_axis=0, tiled=True
    )
    grad_picked = grad_back.reshape(expert_total, CAP, D)[chosen, slots].astype(jnp.float32)
    grad_normed_f = jnp.sum(grad_picked.reshape(token_count, TOP, D), axis=1)
    grad_resid_part, ffn_gain_grad = norm_back(residual, inverse_f, ffn_gain, grad_normed_f)
    grad_residual = upstream + grad_resid_part
    grad_branch = grad_residual.astype(jnp.bfloat16)
    out_proj_grad = jnp.einsum(
        "td,tf->df", merged_b, grad_branch, preferred_element_type=jnp.float32
    )
    merged_gradient = jnp.einsum(
        "tf,df->td", grad_branch, w_out, preferred_element_type=jnp.float32
    ).astype(jnp.bfloat16)
    output_gradient = jnp.transpose(
        merged_gradient.reshape(token_count, KEY_VALUE_HEADS, query_groups, HEAD_SIZE), (1, 2, 0, 3)
    )
    delta = jnp.sum(output_gradient.astype(jnp.float32) * attended, axis=-1)

    def block_back(part_keys, part_values, key_start):

        def compute(operands):
            return attend_back(
                query_matrix,
                output_gradient,
                logsum,
                delta,
                positions,
                begins,
                operands[0],
                operands[1],
                key_start,
                scaling,
            )

        def nothing(operands):
            return (
                jnp.zeros(query_layout, jnp.float32),
                jnp.zeros(operands[0].shape, jnp.float32),
                jnp.zeros(operands[1].shape, jnp.float32),
            )

        return lax.cond(key_start <= last_pos, compute, nothing, (part_keys, part_values))

    grad_query = jnp.zeros(query_layout, jnp.float32)
    complete_keys, whole_values = (
        lax.all_gather(key_matrix, "context", axis=0, tiled=True),
        lax.all_gather(value_matrix, "context", axis=0, tiled=True),
    )
    block_span = 2 * token_count

    def block_turn(turn_index, block_state):
        keys_grad_all, values_grad_all, query_sum = block_state
        offset = turn_index * block_span
        add_query, add_key, add_value = block_back(
            lax.dynamic_slice_in_dim(complete_keys, offset, block_span, 0),
            lax.dynamic_slice_in_dim(whole_values, offset, block_span, 0),
            offset,
        )
        keys_grad_all = lax.dynamic_update_slice_in_dim(keys_grad_all, add_key, offset, 0)
        values_grad_all = lax.dynamic_update_slice_in_dim(values_grad_all, add_value, offset, 0)
        return (keys_grad_all, values_grad_all, query_sum + add_query)

    zero_filled = jnp.zeros((complete_keys.shape[0], KEY_VALUE_HEADS, HEAD_SIZE), jnp.float32)
    finished = lax.fori_loop(0, contexts // 2, block_turn, (zero_filled, zero_filled, grad_query))
    grad_keys, grad_values = (
        lax.psum_scatter(
            finished[0].astype(jnp.bfloat16), "context", scatter_dimension=0, tiled=True
        ).astype(jnp.float32),
        lax.psum_scatter(
            finished[1].astype(jnp.bfloat16), "context", scatter_dimension=0, tiled=True
        ).astype(jnp.float32),
    )
    grad_query = finished[2]
    grad_q_rows = apply_rotary(
        jnp.transpose(grad_query, (2, 0, 1, 3)).reshape(token_count, QUERY_HEADS, HEAD_SIZE),
        cosine_table,
        sine_values,
        False,
    )
    grad_k_rows = apply_rotary(grad_keys, cosine_table, sine_values, False)
    grad_projected = jnp.concatenate(
        [
            grad_q_rows.reshape(token_count, query_width),
            grad_k_rows.reshape(token_count, key_value_width),
            grad_values.reshape(token_count, key_value_width),
        ],
        axis=-1,
    ).astype(jnp.bfloat16)
    qkv_grad = jnp.einsum(
        "td,tf->df", normed_ab, grad_projected, preferred_element_type=jnp.float32
    )
    grad_normed_a = jnp.einsum(
        "tf,df->td", grad_projected, w_qkv, preferred_element_type=jnp.float32
    )
    grad_in_part, attn_gain_grad = norm_back(tokens, inverse_a, attn_gain, grad_normed_a)
    packed_grad = grad_residual + grad_in_part
    summed = (
        lax.psum_scatter(
            attn_gain_grad.astype(jnp.bfloat16), "context", scatter_dimension=0, tiled=True
        ).astype(jnp.float32),
        lax.psum_scatter(
            qkv_grad.astype(jnp.bfloat16), "context", scatter_dimension=0, tiled=True
        ).astype(jnp.float32),
        lax.psum_scatter(
            out_proj_grad.astype(jnp.bfloat16), "context", scatter_dimension=0, tiled=True
        ).astype(jnp.float32),
        lax.psum_scatter(
            ffn_gain_grad.astype(jnp.bfloat16), "context", scatter_dimension=0, tiled=True
        ).astype(jnp.float32),
        lax.psum_scatter(
            gate_up_grad.astype(jnp.bfloat16), "context", scatter_dimension=1, tiled=True
        ).astype(jnp.float32),
        lax.psum_scatter(
            down_grad.astype(jnp.bfloat16), "context", scatter_dimension=1, tiled=True
        ).astype(jnp.float32),
    )
    dense_rows = (summed[0], summed[1], summed[2], summed[3])
    expert_sums = (
        lax.psum(summed[4].astype(jnp.bfloat16), "dp").astype(jnp.float32),
        lax.psum(summed[5].astype(jnp.bfloat16), "dp").astype(jnp.float32),
    )
    shared = (
        lax.psum(dense_rows[0].astype(jnp.bfloat16), ("dp", "expert")).astype(jnp.float32),
        lax.psum(dense_rows[1].astype(jnp.bfloat16), ("dp", "expert")).astype(jnp.float32),
        lax.psum(dense_rows[2].astype(jnp.bfloat16), ("dp", "expert")).astype(jnp.float32),
        lax.psum(dense_rows[3].astype(jnp.bfloat16), ("dp", "expert")).astype(jnp.float32),
    )
    return (
        packed_out[None],
        packed_grad[None],
        shared[0],
        shared[1],
        shared[2],
        shared[3],
        expert_sums[0],
        expert_sums[1],
    )


MESH = pl.DeviceIdType.MESH
BF = jnp.bfloat16
F32 = jnp.float32
NN = (((1,), (0,)), ((), ()))
NT = (((1,), (1,)), ((), ()))
TN = (((0,), (0,)), ((), ()))


def matmul(left, right, dims=NN):
    return lax.dot_general(left, right, dims, preferred_element_type=F32)


def flip(axis, bit):
    index = lax.axis_index(axis)
    return {axis: index + bit - 2 * bit * ((index // bit) % 2)}


def greet(peers):
    barrier = pltpu.get_barrier_semaphore()
    for peer in peers:
        pl.semaphore_signal(barrier, inc=1, device_id=peer, device_id_type=MESH)
    pl.semaphore_wait(barrier, len(peers))


def remote(src, dst, send_sem, recv_sem, peer):
    return pltpu.make_async_remote_copy(
        src_ref=src,
        dst_ref=dst,
        send_sem=send_sem,
        recv_sem=recv_sem,
        device_id=peer,
        device_id_type=MESH,
    )


def other(axis, distance):
    size = lax.axis_size(axis)
    return {axis: lax.rem(lax.axis_index(axis) + distance, size)}


def mate(code):
    expert = lax.axis_index("expert")
    for bit in (1, 2):
        if code & bit:
            expert = expert + bit - 2 * bit * ((expert // bit) % 2)
    return {**flip("dp", 1), "expert": expert} if code & 4 else {"expert": expert}


class GroupGather:
    def __init__(self, own, held, sems, rows):
        half = rows // 2
        self.x, self.y, self.core = flip("dp", 1), flip("expert", 2), flip("expert", 1)

        def part(which, index, amount=1):
            return held.at[pl.ds(which * 2 * rows + index * half, amount * half)]

        def link(number, src, dst, peer):
            return remote(src, dst, sems.at[0, number], sems.at[1, number], peer)

        first, second = own.at[pl.ds(0, half)], own.at[pl.ds(half, half)]
        self.links = [
            link(0, first, part(1, 0), self.x),
            link(1, second, part(1, 1), self.y),
            link(2, first, part(2, 0), self.y),
            link(3, second, part(2, 1), self.x),
            link(4, part(1, 0), part(3, 0), self.y),
            link(5, part(1, 1), part(3, 1), self.x),
        ]
        self.cores = [link(6, own, part(0, 2, 2), self.core)]
        for which in range(1, 4):
            self.cores.append(
                link(6 + which, part(which, 0, 2), part(which, 2, 2), self.core)
            )

    def start(self):
        for link in self.links[:4]:
            link.start()
        self.cores[0].start()

    def forward(self, which):
        for index in range(2 * which - 2, 2 * which):
            self.links[index].wait_recv()
            if which == 1:
                self.links[4 + index].start()
        self.cores[which].start()

    def arrived(self, which):
        self.cores[which].wait_recv()

    def finish(self):
        for link in self.links + self.cores:
            link.wait_send()


GATHER_SEMS = pltpu.SemaphoreType.DMA((2, 10))


def rotate(values, cosine, sine):
    return values * cosine + pltpu.roll(values, values.shape[1] // 2, 1) * sine


SLOT_CODES = ((0, 0, 1, 1), (4, 2, 5, 3), (2, 4, 3, 5), (6, 6, 7, 7))


def turned(axis, code):
    index = lax.axis_index(axis)
    bit = 1
    while bit <= code:
        if code & bit:
            index = index + bit - 2 * bit * ((index // bit) % 2)
        bit *= 2
    return index


def gelu_parts(gate):
    slope = 0.7978845608
    bend = 0.044715
    square = gate * gate
    tanh = jnp.tanh(slope * gate * (1.0 + bend * square))
    half = 0.5 * (1.0 + tanh)
    grad = half + 0.5 * slope * gate * (1.0 - tanh * tanh) * (1.0 + 3.0 * bend * square)
    return gate * half, grad


class GroupReturn:
    def __init__(self, source, near, second, third, sems, rows, whole=True):
        self.source, self.rows, self.half = source, rows, rows // 2
        self.near, self.second, self.third = near, second, third
        x, y, core = flip("dp", 1), flip("expert", 2), flip("expert", 1)

        def link(number, src, dst, peer):
            return remote(src, dst, sems.at[0, number], sems.at[1, number], peer)

        def part(which, index):
            return near.at[which, pl.ds(index * self.half, self.half)]

        self.cores = [
            link(6 + which, source.at[pl.ds((2 * which + 1) * rows, rows)], near.at[which], core)
            for which in range(4)
        ]
        self.finals = []
        if whole:
            self.finals = [
                link(0, part(1, 0), third.at[0], x),
                link(1, part(1, 1), third.at[1], y),
            ]
        self.links = [
            link(2, part(2, 0), third.at[2], y),
            link(3, part(2, 1), third.at[3], x),
            link(4, part(3, 0), second.at[0], y),
            link(5, part(3, 1), second.at[1], x),
        ]

    def fold(self, which, index):
        begin = 2 * which * self.rows + index * self.half
        value = self.source[begin : begin + self.half].astype(F32)
        span = slice(index * self.half, (index + 1) * self.half)
        return span, value + self.near[which, span].astype(F32)

    def side(self):
        self.cores[2].wait_recv()
        for index in range(2):
            span, value = self.fold(2, index)
            self.near[2, span] = value.astype(BF)
            self.links[index].start()

    def far(self):
        self.cores[3].wait_recv()
        for index in range(2):
            span, value = self.fold(3, index)
            self.near[3, span] = value.astype(BF)
            self.links[2 + index].start()

    def middle(self):
        self.cores[1].wait_recv()
        for index in range(2):
            self.links[2 + index].wait_recv()
            span, value = self.fold(1, index)
            self.near[1, span] = (value + self.second[index].astype(F32)).astype(BF)

    def last(self):
        for link in self.finals:
            link.start()

    def home(self, index):
        if index == 0:
            self.cores[0].wait_recv()
        self.links[index].wait_recv()
        span, value = self.fold(0, index)
        return span, value + self.third[2 + index].astype(F32)

    def sent(self):
        for copy in self.cores + self.links + self.finals:
            copy.wait_send()


def document_angles(starts_ref, frequency_ref, cosine, sine):
    rows = cosine.shape[0]
    offset = lax.axis_index("context") * rows
    positions = offset + lax.broadcasted_iota(jnp.int32, cosine.shape, 0)
    row_positions = offset + lax.broadcasted_iota(jnp.int32, (1, rows), 1)
    begins = jnp.zeros(cosine.shape, jnp.int32)
    begin_row = jnp.zeros((1, rows), jnp.int32)
    for document in range(starts_ref.shape[0]):
        start = starts_ref[document]
        begins = jnp.maximum(begins, jnp.where(positions >= start, start, 0))
        begin_row = jnp.maximum(begin_row, jnp.where(row_positions >= start, start, 0))
    angles = (positions - begins).astype(F32) * frequency_ref[...]
    cosine[...] = jnp.cos(angles)
    lane = lax.broadcasted_iota(jnp.int32, cosine.shape, 1)
    sine[...] = jnp.where(lane < HEAD_SIZE // 2, -1.0, 1.0) * jnp.sin(angles)
    return begin_row


def gain_row(gain_ref):
    return jnp.concatenate([gain_ref[index : index + 1] for index in range(D // 128)], axis=1)


def front_kernel(
    x_ref,
    routes_ref,
    gates_ref,
    starts_ref,
    frequency_ref,
    attn_gain_ref,
    ffn_gain_ref,
    c_ref,
    w_qkv_ref,
    w_out_ref,
    gate_up_ref,
    down_ref,
    h1_ref,
    q_ref,
    logsum_ref,
    merged_ref,
    residual_ref,
    kv_ref,
    dh2_ref,
    y_home_ref,
    y_side_ref,
    gu_near_ref,
    gu_far_ref,
    down_part_ref,
    gu_in_ref,
    down_in_ref,
    far_in_ref,
    w_gu,
    w_down,
    h2_all,
    c_all,
    dhid,
    gu,
    hidden,
    dgu,
    du,
    share,
    gu_part,
    down_part,
    near,
    second,
    third,
    gu_in,
    dh2,
    y_home,
    kv,
    top,
    total,
    bias,
    cosine,
    sine,
    share_own,
    share_all,
    load_sems,
    out_sems,
    kv_sems,
    keep_sems,
    share_sems,
    c_sems,
    h2_sems,
    z_sems,
    du_sems,
    y_sems,
    credits,
):
    contexts = lax.axis_size("context")
    me = lax.axis_index("context")
    dp = lax.axis_index("dp")
    rows = x_ref.shape[0]
    half = rows // 2
    two = 2 * rows
    slice_rows = gu_part.shape[1]
    first = gu_in.shape[0]
    down_rows = down_part.shape[1] // 2
    query_width = QUERY_HEADS * HEAD_SIZE
    key_width = KEY_VALUE_HEADS * HEAD_SIZE
    heads = QUERY_HEADS // KEY_VALUE_HEADS
    scaling = HEAD_SIZE ** (-0.5)

    w_q = du.at[pl.ds(0, D)]
    h1 = du.at[pl.ds(D, rows)]
    merged = du.at[pl.ds(D + rows, rows)]
    w_out = dgu.at[pl.ds(0, query_width)]
    query = dgu.at[pl.ds(query_width, rows)]
    w_kv = hidden.at[pl.ds(0, D), pl.ds(0, 2 * key_width)]
    residual = y_home

    def accumulated(head):
        across = gu.shape[1] // rows
        return gu.at[
            pl.ds(head // across * HEAD_SIZE, HEAD_SIZE), pl.ds(head % across * rows, rows)
        ]

    def load(number, src, dst):
        copy = pltpu.make_async_copy(src, dst, load_sems.at[number])
        copy.start()
        return copy

    load_kv = load(0, w_qkv_ref.at[:, query_width:], w_kv)
    load_q = load(1, w_qkv_ref.at[:, :query_width], w_q)
    load_c = load(2, c_ref, c_all.at[pl.ds(0, rows)])
    load_out = load(3, w_out_ref, w_out)
    load_down = load(4, down_ref.at[dp], w_down)
    load_gu = load(5, gate_up_ref.at[dp], w_gu)

    begin_row = document_angles(starts_ref, frequency_ref, cosine, sine)
    named = lax.broadcasted_iota(jnp.int32, share_own.shape, 0)
    gathered = jnp.zeros(share_own.shape, F32)
    for choice in range(TOP):
        chosen = routes_ref[choice : choice + 1] == named
        gathered = gathered + jnp.where(chosen, gates_ref[choice : choice + 1], 0.0)
    share_own[...] = gathered

    mates = [mate(code) for code in range(1, 8)]
    greet([other("context", step) for step in range(1, contexts)] + mates)

    c_gather = GroupGather(c_ref, c_all, c_sems, rows)
    c_gather.start()
    shares = [
        remote(
            share_own,
            share_all.at[1 + index],
            share_sems.at[0, index],
            share_sems.at[1, index],
            peer,
        )
        for index, peer in enumerate(mates)
    ]
    for copy in shares:
        copy.start()

    x = x_ref[...].astype(F32)
    inverse = lax.rsqrt(jnp.mean(x * x, axis=-1, keepdims=True) + epsilon)
    h1[...] = (x * inverse * gain_row(attn_gain_ref)).astype(BF)

    load_kv.wait()
    projected = matmul(h1[...], w_kv[...])
    for head in range(KEY_VALUE_HEADS):
        lanes = slice(head * HEAD_SIZE, (head + 1) * HEAD_SIZE)
        kv[me, :, lanes] = rotate(projected[:, lanes], cosine[...], sine[...]).astype(BF)
    kv[me, :, key_width:] = projected[:, key_width:].astype(BF)

    def kv_copy(block):
        return remote(
            kv.at[block],
            kv.at[block],
            kv_sems.at[0, block],
            kv_sems.at[1, block],
            {"context": lax.rem(me + 1, contexts)},
        )

    def pass_on(block):
        @pl.when(me + 1 < contexts)
        def _():
            kv_copy(block).start()

    pass_on(me)

    load_q.wait()
    span = 4 * HEAD_SIZE
    for offset in range(0, query_width, span):
        projected = matmul(h1[...], w_q[:, offset : offset + span])
        for head in range(span // HEAD_SIZE):
            lanes = slice(head * HEAD_SIZE, (head + 1) * HEAD_SIZE)
            place = slice(offset + head * HEAD_SIZE, offset + (head + 1) * HEAD_SIZE)
            query[:, place] = rotate(projected[:, lanes], cosine[...], sine[...]).astype(BF)

    outs = []

    def out(src, dst):
        copy = pltpu.make_async_copy(src, dst, out_sems.at[len(outs)])
        copy.start()
        outs.append(copy)

    out(h1, h1_ref)
    out(query, q_ref)
    top[...] = jnp.full_like(top, negative_huge)
    total[...] = jnp.zeros_like(total)
    gu[...] = jnp.zeros_like(gu)
    query_pos = me * rows + lax.broadcasted_iota(jnp.int32, (rows, rows), 1)

    def fold(block):
        key_pos = block * rows + lax.broadcasted_iota(jnp.int32, (rows, rows), 0)
        allowed = (key_pos <= query_pos) & (key_pos >= begin_row)
        bias[...] = jnp.where(allowed, 0.0, negative_huge)
        for head in range(QUERY_HEADS):
            group = head // heads
            keys = kv[block, :, group * HEAD_SIZE : (group + 1) * HEAD_SIZE]
            values = kv[
                block, :, key_width + group * HEAD_SIZE : key_width + (group + 1) * HEAD_SIZE
            ]
            queries = query[:, head * HEAD_SIZE : (head + 1) * HEAD_SIZE]
            scores = matmul(keys, queries, NT) * scaling + bias[...]
            old = top[head : head + 1]
            new = jnp.maximum(old, jnp.max(scores, axis=0, keepdims=True))
            weights = jnp.exp(scores - new)
            shrink = jnp.exp(old - new)
            top[head : head + 1] = new
            total[head : head + 1] = total[head : head + 1] * shrink + jnp.sum(
                weights, axis=0, keepdims=True
            )
            place = accumulated(head)
            place[...] = place[...] * shrink + matmul(values, weights.astype(BF), TN)

    fold(me)

    def backward_hidden(which):
        rows_of = slice(which * two, (which + 1) * two)
        dhid[which % 2] = matmul(c_all[rows_of], w_down[...], NT)

    for step in range(1, contexts):

        @pl.when(step <= me)
        def _():
            kv_copy(me - step).wait_recv()
            pass_on(me - step)
            fold(me - step)

        if step == 1:
            c_gather.forward(1)
            load_c.wait()
            load_down.wait()
            c_gather.arrived(0)
            backward_hidden(0)
    load_out.wait()
    for head in range(QUERY_HEADS):
        attended = accumulated(head)[...] / total[head : head + 1]
        merged[:, head * HEAD_SIZE : (head + 1) * HEAD_SIZE] = attended.T.astype(BF)
    top[...] = jnp.where(total[...] > 0, top[...] + jnp.log(total[...]), 0.0)
    out(merged, merged_ref)
    out(top, logsum_ref)
    value = x_ref[...].astype(F32) + matmul(merged[...], w_out[...])
    residual[...] = value
    out(residual, residual_ref)
    inverse = lax.rsqrt(jnp.mean(value * value, axis=-1, keepdims=True) + epsilon)
    h2_all[0:rows] = (value * inverse * gain_row(ffn_gain_ref)).astype(BF)

    gather = GroupGather(h2_all.at[pl.ds(0, rows)], h2_all, h2_sems, rows)
    gather.start()

    c_gather.forward(2)
    c_gather.arrived(1)
    backward_hidden(1)

    def keep_copy(block):
        return pltpu.make_async_copy(kv.at[block], kv_ref.at[block], keep_sems.at[block])

    def keep(block, carry):
        keep_copy(block).start()
        return carry

    lax.fori_loop(0, me + 1, keep, 0)
    share_all[0] = share_own[...]
    for copy in shares:
        copy.wait_recv()
    expert = lax.axis_index("expert") * lax.axis_size("dp") + dp
    columns = []
    for code in range(8):
        swapped = share_all[code].T
        mine = lax.broadcasted_iota(jnp.int32, swapped.shape, 1) == expert
        columns.append(jnp.sum(jnp.where(mine, swapped, 0.0), axis=1, keepdims=True))
    for which, codes in enumerate(SLOT_CODES):
        for index, code in enumerate(codes):
            part = (index % 2) * half
            share[pl.ds(which * two + index * half, half), :] = columns[code][part : part + half]

    def forward(which):
        gu[...] = matmul(h2_all[which * two : (which + 1) * two], w_gu[...])

    def activate(which):
        def body_of(step, carry):
            close = pl.ds(pl.multiple_of(step * half, half), half)
            place = pl.ds(pl.multiple_of(which * two + step * half, half), half)
            up = gu[close, FF:]
            activated, grad = gelu_parts(gu[close, :FF])
            scale = share[place, :]
            upstream = dhid[which % 2, close, :] * scale
            hidden[place, :] = (activated * up * scale).astype(BF)
            dgu[place, :FF] = (upstream * up * grad).astype(BF)
            dgu[place, FF:] = (upstream * activated).astype(BF)
            return carry

        lax.fori_loop(0, 4, body_of, 0)

    def backward(which):
        span = slice(which * two, (which + 1) * two)
        du[span] = matmul(dgu[span], w_gu[...], NT).astype(BF)
        back.cores[which].start()

    def gate_up_slice(code, begin, end):
        lane = turned("context", code) * slice_rows + begin
        lanes = pl.ds(pl.multiple_of(lane, 128), end - begin)
        gu_part[code, begin:end] = matmul(h2_all[:, lanes], dgu[...], TN).astype(BF)

    def down_pair(pair):
        first = turned("context", 2 * pair) // 2
        lanes = pl.ds(pl.multiple_of(first * 2 * down_rows, 128), 2 * down_rows)
        down_part[pair] = matmul(hidden[:, lanes], c_all[...], TN).astype(BF)

    back = GroupReturn(du, near, second, third, du_sems, rows)
    load_gu.wait()
    for copy in outs:
        copy.wait()
    gather.arrived(0)
    forward(0)
    activate(0)
    c_gather.arrived(2)
    backward_hidden(2)
    gather.forward(1)
    backward(0)
    gather.arrived(1)
    forward(1)
    activate(1)
    c_gather.forward(3)
    gather.forward(2)
    c_gather.arrived(3)
    backward_hidden(3)
    gather.arrived(2)
    forward(2)
    activate(2)
    gather.forward(3)
    backward(2)
    gather.arrived(3)
    forward(3)
    activate(3)
    z = flip("context", 1)
    sends = []

    def send(src, dst, peer):
        number = len(sends)
        copy = remote(src, dst, z_sems.at[0, number], z_sems.at[1, number], peer)
        copy.start()
        sends.append(copy)

    gate_up_slice(3, 0, first)
    early = [pl.ds(index * first // 2, first // 2) for index in range(2)]
    for span in early:
        send(gu_part.at[3, span], gu_in.at[span], z)
    gate_up_slice(3, first, slice_rows)
    back.side()
    backward(3)
    down_pair(1)
    back.far()
    backward(1)
    gate_up_slice(2, 0, slice_rows)
    out(gu_part.at[2, pl.ds(first, slice_rows - first)], gu_far_ref)

    def far_early(index):
        span = early[index]
        sends[index].wait_recv()
        value = gu_part[2, span].astype(F32) + gu_in[span].astype(F32)
        gu_part[2, span] = value.astype(BF)
        send(gu_part.at[2, span], far_in_ref.at[span], flip("context", 2))

    far_early(0)
    send(gu_part.at[3, pl.ds(first, slice_rows - first)], gu_in_ref, z)
    down_pair(0)
    out(down_part, down_part_ref)
    back.middle()
    back.last()
    far_early(1)
    place = pl.ds(
        pl.multiple_of(lax.rem(turned("context", 3), 2) * down_rows, 16), down_rows
    )
    send(down_part.at[1, place], down_in_ref, z)
    c_gather.finish()
    for which in range(4):
        span = slice(which * two, (which + 1) * two)
        c_all[span] = matmul(hidden[span], w_down[...]).astype(BF)
    for index in range(2):
        span, value = back.home(index)
        back.finals[index].wait_recv()
        dh2[span] = value + third[index].astype(F32)
    out(dh2, dh2_ref)
    back.sent()
    for number, mate_of in enumerate((flip("expert", 1), flip("dp", 1), flip("expert", 2))):
        pl.semaphore_signal(
            credits.at[number], inc=1, device_id=mate_of, device_id_type=MESH
        )
    for number in range(3):
        pl.semaphore_wait(credits.at[number], 1)
    back = GroupReturn(c_all, near, second, third, y_sems, rows, False)
    for which in (3, 2, 1, 0):
        back.cores[which].start()
    back.far()
    back.side()
    gate_up_slice(1, 0, slice_rows)
    out(gu_part.at[1], gu_near_ref.at[0])
    gate_up_slice(0, 0, slice_rows)
    out(gu_part.at[0], gu_near_ref.at[1])
    back.middle()
    out(near.at[1], y_side_ref)
    for index in range(2):
        span, value = back.home(index)
        y_home[span] = value
    out(y_home, y_home_ref)
    back.sent()
    for copy in sends[:2]:
        copy.wait_send()
    for copy in outs[5:] + sends[2:]:
        copy.wait()
    gather.finish()
    for copy in shares:
        copy.wait_send()

    def settle(block, carry):
        keep_copy(block).wait()

        @pl.when(me + 1 < contexts)
        def _():
            kv_copy(block).wait_send()

        return carry

    lax.fori_loop(0, me + 1, settle, 0)


VM = pl.BlockSpec(memory_space=pltpu.VMEM)
SM = pl.BlockSpec(memory_space=pltpu.SMEM)
ANY = pl.BlockSpec(memory_space=pl.ANY)


def front(
    x, routes, gates, starts, frequency, attn_gain, ffn_gain, cotangent, w_qkv, w_out, gate_up, down
):
    rows = x.shape[0]
    contexts = lax.axis_size("context")
    group = lax.axis_size("dp") * lax.axis_size("expert")
    expert_total = gate_up.shape[0] * lax.axis_size("expert")
    total = group * rows
    kv_width = 2 * KEY_VALUE_HEADS * HEAD_SIZE
    padded = -(-QUERY_HEADS // 8) * 8
    slice_rows, down_rows = D // contexts, FF // contexts
    first = 2 * slice_rows // 3
    gu_shape, down_shape = (contexts, slice_rows, 2 * FF), (contexts // 2, 2 * down_rows, D)
    shape = jax.ShapeDtypeStruct
    dma = pltpu.SemaphoreType.DMA
    return pl.pallas_call(
        front_kernel,
        out_shape=[
            shape((rows, D), BF),
            shape((rows, D), BF),
            shape((padded, rows), F32),
            shape((rows, D), BF),
            shape((rows, D), F32),
            shape((contexts, rows, kv_width), BF),
            shape((rows, D), F32),
            shape((rows, D), F32),
            shape((rows, D), BF),
            shape((2, slice_rows, D), BF),
            shape((slice_rows - first, D), BF),
            shape(down_shape, BF),
            shape((slice_rows - first, D), BF),
            shape((down_rows, D), BF),
            shape((first, D), BF),
        ],
        in_specs=[VM] * 3 + [SM] + [VM] * 3 + [ANY] * 5,
        out_specs=[ANY] * 15,
        scratch_shapes=[
            pltpu.VMEM(gate_up.shape[1:], BF),
            pltpu.VMEM(down.shape[1:], BF),
            pltpu.VMEM((total, D), BF),
            pltpu.VMEM((total, D), BF),
            pltpu.VMEM((2, 2 * rows, FF), F32),
            pltpu.VMEM((2 * rows, 2 * FF), F32),
            pltpu.VMEM((total, FF), BF),
            pltpu.VMEM((total, 2 * FF), BF),
            pltpu.VMEM((total, D), BF),
            pltpu.VMEM((total, 1), F32),
            pltpu.VMEM(gu_shape, BF),
            pltpu.VMEM(down_shape, BF),
            pltpu.VMEM((4, rows, D), BF),
            pltpu.VMEM((2, rows // 2, D), BF),
            pltpu.VMEM((4, rows // 2, D), BF),
            pltpu.VMEM((first, D), BF),
            pltpu.VMEM((rows, D), F32),
            pltpu.VMEM((rows, D), F32),
            pltpu.VMEM((contexts, rows, kv_width), BF),
            pltpu.VMEM((padded, rows), F32),
            pltpu.VMEM((padded, rows), F32),
            pltpu.VMEM((rows, rows), F32),
            pltpu.VMEM((rows, HEAD_SIZE), F32),
            pltpu.VMEM((rows, HEAD_SIZE), F32),
            pltpu.VMEM((expert_total, rows), F32),
            pltpu.VMEM((group, expert_total, rows), F32),
            dma((6,)),
            dma((12,)),
            dma((2, contexts)),
            dma((contexts,)),
            dma((2, group - 1)),
            GATHER_SEMS,
            GATHER_SEMS,
            dma((2, 6)),
            dma((2, 10)),
            dma((2, 10)),
            pltpu.SemaphoreType.REGULAR((3,)),
        ],
        compiler_params=pltpu.CompilerParams(
            collective_id=0, has_side_effects=True, vmem_limit_bytes=63 << 20
        ),
        cost_estimate=pl.CostEstimate(
            flops=2 * total * D * FF * 10, bytes_accessed=40 << 20, transcendentals=total * FF
        ),
    )(
        x,
        routes.T,
        gates.T,
        starts,
        frequency,
        attn_gain,
        ffn_gain,
        cotangent,
        w_qkv,
        w_out,
        gate_up,
        down,
    )


def bit_of(axis, bit):
    return lax.rem(lax.axis_index(axis) // bit, 2)


class DenseReduce:
    def __init__(self, part, near, first, second, third, fourth, sems, out, lanes, order):
        self.part, self.near, self.first, self.second = part, near, first, second
        self.third, self.fourth, self.out, self.lanes = third, fourth, out, lanes
        self.sems = sems
        self.rows = part.shape[1] // 8
        self.slices = part.shape[0]
        (axis, bit), (later_axis, later_bit) = order
        self.core, self.core_bit = flip("expert", 1), bit_of("expert", 1)
        self.one, self.one_bit = flip(axis, bit), bit_of(axis, bit)
        self.two, self.two_bit = flip(later_axis, later_bit), bit_of(later_axis, later_bit)
        self.pending = []
        self.released = 0

    def send(self, src, dst, peer, amount=1):
        number = len(self.pending)
        copy = remote(src, dst, self.sems.at[0, number], self.sems.at[1, number], peer)
        copy.start()
        self.pending.append(copy)
        self.waited = number + 1 - amount

    def wait(self):
        for copy in self.pending[self.waited :]:
            copy.wait_recv()

    def span(self, bit, size, base=0):
        return pl.ds(pl.multiple_of(base + bit * size, 16), size)

    def start(self):
        size = 4 * self.rows
        self.send(self.part.at[:, self.span(1 - self.core_bit, size)], self.near, self.core)

    def release(self):
        self.pending[0].wait_send()
        self.released = 1

    def after_core(self):
        self.wait()
        size = 4 * self.rows
        for index in range(self.slices):
            value = self.part[index, self.span(self.core_bit, size)].astype(F32)
            self.near[index] = (value + self.near[index].astype(F32)).astype(BF)
        size = 2 * self.rows
        self.send(self.near.at[:, self.span(1 - self.one_bit, size)], self.first, self.one)

    def after_one(self):
        self.wait()
        size = 2 * self.rows
        for index in range(self.slices):
            value = self.near[index, self.span(self.one_bit, size)].astype(F32)
            self.first[index] = (value + self.first[index].astype(F32)).astype(BF)
        self.send(self.first.at[:, self.span(1 - self.two_bit, self.rows)], self.second, self.two)

    def after_two(self):
        self.wait()
        for index in range(self.slices):
            value = self.first[index, self.span(self.two_bit, self.rows)].astype(F32)
            self.second[index] = (value + self.second[index].astype(F32)).astype(BF)
        bit = bit_of("context", 1)
        for index in range(2):
            source = self.second.at[2 * index + 1 - bit]
            self.send(source, self.third.at[index], flip("context", 1), index + 1)

    def after_near_z(self):
        self.wait()
        bit = bit_of("context", 1)
        for index in range(2):
            value = self.second[2 * index + bit].astype(F32) + self.third[index].astype(F32)
            self.third[index] = value.astype(BF)
        bit = bit_of("context", 2)
        self.send(self.third.at[1 - bit], self.fourth, flip("context", 2))

    def held(self, cuts):
        sizes = (1, 2, 4)
        base = self.core_bit * 4 * self.rows
        if cuts < 2:
            base = base + self.one_bit * 2 * self.rows
        if cuts < 1:
            base = base + self.two_bit * self.rows
        rows = pl.ds(pl.multiple_of(base, 16), sizes[cuts] * self.rows)
        return self.out.at[rows, self.lanes]

    def after_far_z(self):
        self.wait()
        value = self.third[bit_of("context", 2)].astype(F32) + self.fourth[...].astype(F32)
        place = self.held(0)
        place[...] = value.astype(BF)
        self.send(place, place, self.two)

    def return_one(self):
        self.wait()
        self.send(self.held(1), self.held(1), self.one)

    def return_core(self):
        self.wait()
        self.send(self.held(2), self.held(2), self.core)

    def finish(self):
        self.wait()
        for copy in self.pending[self.released :]:
            copy.wait_send()

    @staticmethod
    def scratch(contexts, rows, width):
        least = rows // 8
        return [
            pltpu.VMEM((contexts, 4 * least, width), BF),
            pltpu.VMEM((contexts, 2 * least, width), BF),
            pltpu.VMEM((contexts, least, width), BF),
            pltpu.VMEM((2, least, width), BF),
            pltpu.VMEM((least, width), BF),
            pltpu.SemaphoreType.DMA((2, 9)),
        ]


X_BIT, Y_BIT = ("dp", 1), ("expert", 2)


def unrotate(values, cosine, sine):
    return values * cosine - pltpu.roll(values, values.shape[1] // 2, 1) * sine


def norm_pull(values, gain, upstream):
    inverse = lax.rsqrt(jnp.mean(values * values, axis=-1, keepdims=True) + epsilon)
    scaled = upstream * gain
    inner = jnp.mean(scaled * values, axis=-1, keepdims=True)
    grad_in = inverse * scaled - values * (inverse * inverse * inverse * inner)
    return grad_in, jnp.sum(upstream * (values * inverse), axis=0, keepdims=True)


def backward_kernel(
    starts_ref,
    frequency_ref,
    attn_gain_ref,
    ffn_gain_ref,
    dh2_in,
    residual_in,
    c_in,
    merged_in,
    logsum_in,
    q_in,
    h1_in,
    x_in,
    y_home_in,
    kv_ref,
    w_qkv_ref,
    w_out_ref,
    y_side_ref,
    gu_near_ref,
    gu_far_ref,
    down_part_ref,
    gu_in_ref,
    down_in_ref,
    far_in_ref,
    packed_out_out,
    packed_grad_out,
    gains_ref,
    out_proj_ref,
    qkv_grad_ref,
    weights_ref,
    dh2_ref,
    residual_ref,
    c_ref,
    merged_ref,
    logsum_ref,
    q_ref,
    h1_ref,
    x_ref,
    y_home_ref,
    packed_out_ref,
    packed_grad_ref,
    cosine,
    sine,
    w_dense,
    w_kv,
    kv,
    dres,
    dbranch,
    datt,
    delta,
    bias,
    dq,
    dkv_sum,
    dkv_out,
    dkv_in,
    dqkv,
    dense,
    dense_kv,
    stage_a,
    stage_b,
    near_in,
    far_in,
    gains_in,
    y_in,
    load_sems,
    kv_sems,
    dkv_sems,
    near_sems,
    far_sems,
    x_sems,
    gain_sems,
    y_sems,
    *others,
):
    rows = x_ref.shape[0]
    half = rows // 2
    contexts = lax.axis_size("context")
    me = lax.axis_index("context")
    dp = lax.axis_index("dp")
    query_width = QUERY_HEADS * HEAD_SIZE
    key_width = KEY_VALUE_HEADS * HEAD_SIZE
    heads = QUERY_HEADS // KEY_VALUE_HEADS
    scaling = HEAD_SIZE ** (-0.5)
    slice_rows, down_rows = gu_near_ref.shape[1], down_in_ref.shape[0]
    first = far_in_ref.shape[0]
    cuts = [0, first, slice_rows, slice_rows + 2 * down_rows // 3, slice_rows + down_rows]
    spans = [pl.ds(begin, end - begin) for begin, end in zip(cuts, cuts[1:])]
    down_span = pl.ds(slice_rows, down_rows)

    def load(number, src, dst):
        copy = pltpu.make_async_copy(src, dst, load_sems.at[number])
        copy.start()
        return copy

    def load_kv(block):
        return pltpu.make_async_copy(kv_ref.at[block], kv.at[block], kv_sems.at[block])

    def begin_load(block, carry):
        load_kv(block).start()
        return carry

    def end_load(block, carry):
        load_kv(block).wait()
        return carry

    def down_place(code, begin=0, end=down_rows):
        base = lax.rem(turned("context", code), 2) * down_rows + begin
        return down_part_ref.at[code // 2, pl.ds(pl.multiple_of(base, 16), end - begin)]

    first_loads = [
        load(13, dh2_in, dh2_ref),
        load(14, residual_in, residual_ref),
        load(15, c_in, c_ref),
    ]
    load_out = load(0, w_out_ref, w_dense)
    later_loads = [
        load(16, merged_in, merged_ref),
        load(17, logsum_in, logsum_ref),
        load(18, q_in, q_ref),
        load(19, h1_in, h1_ref),
        load(20, x_in, x_ref),
        load(21, y_home_in, y_home_ref),
    ]
    stage_loads = [
        load(2, gu_far_ref, stage_a.at[spans[1]]),
        load(3, down_place(2), stage_a.at[down_span]),
        load(4, gu_in_ref, stage_b.at[spans[1]]),
        load(5, down_in_ref, stage_b.at[down_span]),
    ]
    lax.fori_loop(0, me + 1, begin_load, 0)
    load_w_kv = load(1, w_qkv_ref.at[:, query_width:], w_kv)

    begin_row = document_angles(starts_ref, frequency_ref, cosine, sine)
    x, y, core = flip("dp", 1), flip("expert", 2), flip("expert", 1)
    near, far = flip("context", 1), flip("context", 2)
    greet([x, y, core] + [other("context", step) for step in range(1, contexts)])
    y_copies = []
    for index, peer in enumerate((x, y)):
        span = pl.ds(index * half, half)
        copy = remote(
            y_side_ref.at[span], y_in.at[span], y_sems.at[0, index], y_sems.at[1, index], peer
        )
        copy.start()
        y_copies.append(copy)

    near_copies, far_copies, x_copies = [], [], []
    for index, span in enumerate(spans):
        if index < 2:
            source = gu_near_ref.at[0, span]
        else:
            source = down_place(1, cuts[index] - slice_rows, cuts[index + 1] - slice_rows)
        near_copies.append(
            remote(source, near_in.at[span], near_sems.at[0, index], near_sems.at[1, index], near)
        )
        if index > 0:
            far_copies.append(
                remote(
                    stage_a.at[span],
                    far_in.at[span],
                    far_sems.at[0, index],
                    far_sems.at[1, index],
                    far,
                )
            )
    last, upper = me + 1 == contexts, me >= contexts // 2
    downward = lax.rem(me, 2) == 1

    @pl.when(jnp.logical_not(last))
    def _():
        for copy in near_copies[:2]:
            copy.start()

    @pl.when(jnp.logical_not(downward))
    def _():
        for copy in near_copies[2:]:
            copy.start()

    for copy in first_loads:
        copy.wait()
    grad_part, gain_grad = norm_pull(residual_ref[...], gain_row(ffn_gain_ref), dh2_ref[...])
    gains_ref[...] = jnp.zeros_like(gains_ref)
    gains_ref[1:2] = gain_grad
    dres[...] = c_ref[...].astype(F32) + grad_part
    dbranch[...] = dres[...].astype(BF)
    for copy in stage_loads:
        copy.wait()
    for span in spans[1:]:
        value = stage_a[span].astype(F32) + stage_b[span].astype(F32)
        stage_a[span] = value.astype(BF)
    far_copies[0].start()

    @pl.when(jnp.logical_not(upper))
    def _():
        for copy in far_copies[1:]:
            copy.start()

    own_loads = [
        load(6, gu_near_ref.at[1], stage_b.at[pl.ds(0, slice_rows)]),
        load(7, down_place(0), stage_b.at[down_span]),
        load(8, far_in_ref, far_in.at[spans[0]]),
    ]
    load_out.wait()
    datt[...] = matmul(dbranch[...], w_dense[...], NT).astype(BF)
    load_w_q = load(9, w_qkv_ref.at[:, :query_width], w_dense)
    for copy in later_loads:
        copy.wait()
    delta[...] = jnp.zeros_like(delta)
    for head in range(QUERY_HEADS):
        lanes = slice(head * HEAD_SIZE, (head + 1) * HEAD_SIZE)
        product = datt[:, lanes].astype(F32) * merged_ref[:, lanes].astype(F32)
        delta[head : head + 1] = jnp.sum(product.T, axis=0, keepdims=True)

    def dense_matmul(target, left, right):
        for index in range(contexts):
            lanes = slice(index * slice_rows, (index + 1) * slice_rows)
            target[index] = matmul(left[:, lanes], right, TN).astype(BF)

    def streams_of(scratch, part, target, base, width):
        found = []
        for number, order in enumerate(((Y_BIT, X_BIT), (X_BIT, Y_BIT))):
            begin = number * width // 2
            found.append(
                DenseReduce(
                    part.at[:, :, pl.ds(begin, width // 2)],
                    *scratch[6 * number : 6 * number + 6],
                    target,
                    slice(base + begin, base + begin + width // 2),
                    order,
                )
            )
        return found

    out_proj = streams_of(others[:12], dense, out_proj_ref, 0, D)
    query_grad = streams_of(others[12:24], dense, qkv_grad_ref, 0, query_width)
    keys_values = streams_of(others[24:], dense_kv, qkv_grad_ref, query_width, 2 * key_width)
    streams = out_proj + query_grad + keys_values

    def each(group, step):
        for stream in group:
            getattr(stream, step)()

    dense_matmul(dense, merged_ref, dbranch[...])
    each(out_proj, "start")

    lax.fori_loop(0, me + 1, end_load, 0)
    query_pos = me * rows + lax.broadcasted_iota(jnp.int32, (rows, rows), 1)
    dq[...] = jnp.zeros_like(dq)

    def pull(block):
        key_pos = block * rows + lax.broadcasted_iota(jnp.int32, (rows, rows), 0)
        allowed = (key_pos <= query_pos) & (key_pos >= begin_row)
        bias[...] = jnp.where(allowed, 0.0, negative_huge)
        dkv_sum[...] = jnp.zeros_like(dkv_sum)
        for head in range(QUERY_HEADS):
            group = head // heads
            key_lanes = slice(group * HEAD_SIZE, (group + 1) * HEAD_SIZE)
            value_lanes = slice(key_width + group * HEAD_SIZE, key_width + (group + 1) * HEAD_SIZE)
            keys = kv[block, :, key_lanes]
            values = kv[block, :, value_lanes]
            lanes = slice(head * HEAD_SIZE, (head + 1) * HEAD_SIZE)
            upstream, queries = datt[:, lanes], q_ref[:, lanes]
            scores = matmul(keys, queries, NT) * scaling + bias[...]
            probs = jnp.exp(scores - logsum_ref[head : head + 1])
            dprobs = matmul(values, upstream, NT)
            dscores = (probs * (dprobs - delta[head : head + 1])).astype(BF)
            dkv_sum[:, value_lanes] += matmul(probs.astype(BF), upstream)
            dkv_sum[:, key_lanes] += matmul(dscores, queries)
            dq[head] += matmul(keys, dscores, TN)

    def dkv_copy(block):
        return remote(
            dkv_out.at[block],
            dkv_in.at[block],
            dkv_sems.at[0, block],
            dkv_sems.at[1, block],
            {"context": lax.rem(me - 1 + contexts, contexts)},
        )

    def earlier(block, carry):
        pull(block)
        dkv_out[block] = dkv_sum[...].astype(BF)

        @pl.when(me + 1 == contexts)
        def _():
            dkv_copy(block).start()

        return carry

    lax.fori_loop(0, me, earlier, 0)
    pull(me)
    each(out_proj, "after_core")
    each(out_proj, "release")
    for head in range(QUERY_HEADS):
        lanes = slice(head * HEAD_SIZE, (head + 1) * HEAD_SIZE)
        dqkv[:, lanes] = unrotate(dq[head].T * scaling, cosine[...], sine[...]).astype(BF)
    dense_matmul(dense, h1_ref, dqkv[:, :query_width])
    each(query_grad, "start")
    each(query_grad, "after_core")

    @pl.when(last)
    def _():
        for copy in near_copies[:2]:
            copy.start()


    def pass_back(block, carry):
        dkv_copy(block).wait_recv()
        value = dkv_out[block].astype(F32) + dkv_in[block].astype(F32)
        dkv_out[block] = value.astype(BF)
        dkv_copy(block).start()
        return carry

    @pl.when(me + 1 < contexts)
    def _():
        lax.fori_loop(0, me, pass_back, 0)

    @pl.when(jnp.logical_and(downward, jnp.logical_not(last)))
    def _():
        for copy in near_copies[2:]:
            copy.start()

    @pl.when(upper)
    def _():
        for copy in far_copies[1:]:
            copy.start()

    for copy in y_copies:
        copy.wait()
    mixture = y_home_ref[...] + y_in[...].astype(F32)
    packed_out_ref[...] = (residual_ref[...] + mixture).astype(BF)
    outs = [load(23, packed_out_ref, packed_out_out)]

    each(out_proj, "after_one")
    each(query_grad, "after_one")
    each(out_proj, "after_two")

    @pl.when(me + 1 < contexts)
    def _():
        dkv_copy(me).wait_recv()
        dkv_sum[...] += dkv_in[me].astype(F32)

    for head in range(KEY_VALUE_HEADS):
        lanes = slice(head * HEAD_SIZE, (head + 1) * HEAD_SIZE)
        place = slice(query_width + head * HEAD_SIZE, query_width + (head + 1) * HEAD_SIZE)
        dqkv[:, place] = unrotate(
            dkv_sum[:, lanes] * scaling, cosine[...], sine[...]
        ).astype(BF)
    dqkv[:, query_width + key_width :] = dkv_sum[:, key_width:].astype(BF)
    dense_matmul(dense_kv, h1_ref, dqkv[:, query_width:])
    each(keys_values, "start")
    load_w_q.wait()
    load_w_kv.wait()
    dh1 = matmul(dqkv[:, :query_width], w_dense[...], NT)
    dh1 = dh1 + matmul(dqkv[:, query_width:], w_kv[...], NT)
    grad_part, gain_grad = norm_pull(x_ref[...].astype(F32), gain_row(attn_gain_ref), dh1)
    gains_ref[0:1] = gain_grad
    packed_grad_ref[...] = dres[...] + grad_part
    outs.append(load(22, packed_grad_ref, packed_grad_out))

    exchange = [core, y, x, near, far]
    gain_copies = []

    def gain_start():
        step = len(gain_copies)
        copy = remote(
            gains_ref, gains_in.at[step], gain_sems.at[0, step], gain_sems.at[1, step], exchange[step]
        )
        copy.start()
        gain_copies.append(copy)

    def gain_add():
        gain_copies[-1].wait()
        gains_ref[...] += gains_in[len(gain_copies) - 1]

    gain_start()
    each(query_grad, "after_two")
    each(keys_values, "after_core")
    gain_add()
    gain_start()
    each(keys_values, "after_one")
    gain_add()
    gain_start()
    each(keys_values, "after_two")
    gain_add()
    gain_start()

    @pl.when(last)
    def _():
        for copy in near_copies[2:]:
            copy.start()

    for copy in own_loads:
        copy.wait()

    def weights_out(index):
        near_copies[index].wait_recv()
        if index > 0:
            far_copies[index - 1].wait_recv()
        span = spans[index]
        value = stage_b[span].astype(F32) + near_in[span].astype(F32)
        stage_b[span] = (value + far_in[span].astype(F32)).astype(BF)
        outs.append(load((10, 11, 12, 24)[index], stage_b.at[span], weights_ref.at[dp, span]))
        copy = remote(
            stage_b.at[span],
            weights_ref.at[dp, span],
            x_sems.at[0, index],
            x_sems.at[1, index],
            x,
        )
        copy.start()
        x_copies.append(copy)

    weights_out(0)
    weights_out(1)
    each(out_proj, "after_near_z")
    each(query_grad, "after_near_z")
    each(keys_values, "after_near_z")
    gain_add()
    gain_start()
    weights_out(2)
    each(out_proj, "after_far_z")
    each(query_grad, "after_far_z")
    each(keys_values, "after_far_z")
    gain_add()
    each(streams, "return_one")
    each(streams, "return_core")
    weights_out(3)
    each(streams, "finish")

    def sent(block, carry):
        dkv_copy(block).wait_send()
        return carry

    lax.fori_loop(0, me, sent, 0)
    for copy in near_copies + far_copies:
        copy.wait_send()
    for copy in x_copies + outs:
        copy.wait()


def backward(starts, frequency, attn_gain, ffn_gain, *arrays):
    dh2, _, _, _, logsum, _, _, _, _, kv, w_qkv, w_out = arrays[:12]
    gu_near, _, _, _, down_in, _ = arrays[13:]
    rows = dh2.shape[0]
    contexts = lax.axis_size("context")
    query_width = QUERY_HEADS * HEAD_SIZE
    kv_width = 2 * KEY_VALUE_HEADS * HEAD_SIZE
    slice_rows, down_rows = gu_near.shape[1], down_in.shape[0]
    total = slice_rows + down_rows
    shape = jax.ShapeDtypeStruct
    dma = pltpu.SemaphoreType.DMA
    return pl.pallas_call(
        backward_kernel,
        out_shape=[
            shape((rows, D), BF),
            shape((rows, D), F32),
            shape((8, D), F32),
            shape((slice_rows, D), BF),
            shape((slice_rows, query_width + kv_width), BF),
            shape((2, total, D), BF),
        ],
        in_specs=[SM] + [VM] * 3 + [ANY] * 19,
        out_specs=[ANY] * 2 + [VM] * 3 + [ANY],
        scratch_shapes=[pltpu.VMEM(array.shape, array.dtype) for array in arrays[:9]]
        + [
            pltpu.VMEM((rows, D), BF),
            pltpu.VMEM((rows, D), F32),
            pltpu.VMEM((rows, HEAD_SIZE), F32),
            pltpu.VMEM((rows, HEAD_SIZE), F32),
            pltpu.VMEM(w_out.shape, BF),
            pltpu.VMEM((D, kv_width), BF),
            pltpu.VMEM(kv.shape, BF),
            pltpu.VMEM((rows, D), F32),
            pltpu.VMEM((rows, D), BF),
            pltpu.VMEM((rows, D), BF),
            pltpu.VMEM(logsum.shape, F32),
            pltpu.VMEM((rows, rows), F32),
            pltpu.VMEM((QUERY_HEADS, HEAD_SIZE, rows), F32),
            pltpu.VMEM((rows, kv_width), F32),
            pltpu.VMEM((contexts, rows, kv_width), BF),
            pltpu.VMEM((contexts, rows, kv_width), BF),
            pltpu.VMEM((rows, query_width + kv_width), BF),
            pltpu.VMEM((contexts, slice_rows, D), BF),
            pltpu.VMEM((contexts, slice_rows, kv_width), BF),
            pltpu.VMEM((total, D), BF),
            pltpu.VMEM((total, D), BF),
            pltpu.VMEM((total, D), BF),
            pltpu.VMEM((total, D), BF),
            pltpu.VMEM((5, 8, D), F32),
            pltpu.VMEM((rows, D), BF),
            dma((25,)),
            dma((contexts,)),
            dma((2, contexts)),
            dma((2, 4)),
            dma((2, 4)),
            dma((2, 4)),
            dma((2, 5)),
            dma((2, 2)),
        ]
        + DenseReduce.scratch(contexts, slice_rows, D // 2) * 2
        + DenseReduce.scratch(contexts, slice_rows, query_width // 2) * 2
        + DenseReduce.scratch(contexts, slice_rows, kv_width // 2) * 2,
        compiler_params=pltpu.CompilerParams(
            collective_id=3, has_side_effects=True, vmem_limit_bytes=62 << 20
        ),
        cost_estimate=pl.CostEstimate(
            flops=2 * rows * D * 8000, bytes_accessed=40 << 20, transcendentals=rows * rows * 48
        ),
    )(starts, frequency, attn_gain, ffn_gain, *arrays)


def widen_kernel(
    packed_out_ref,
    packed_grad_ref,
    gains_ref,
    out_proj_ref,
    qkv_grad_ref,
    weights_ref,
    packed_out,
    packed_grad,
    attn_gain_grad,
    qkv_grad,
    out_proj,
    ffn_gain_grad,
    gate_up_grad,
    down_grad,
    *scratch,
):
    narrow, wide, held, sems = scratch[:6], scratch[6:12], scratch[12:14], scratch[14]
    slice_rows = out_proj_ref.shape[0]
    arrivals = [
        pltpu.make_async_copy(packed_out_ref, held[0], sems.at[0, 6]),
        pltpu.make_async_copy(packed_grad_ref, held[1], sems.at[0, 7]),
    ]
    moves = [
        pltpu.make_async_copy(held[0], packed_out, sems.at[1, 6]),
        pltpu.make_async_copy(held[1], packed_grad, sems.at[1, 7]),
    ]
    sources = [weights_ref.at[expert, pl.ds(0, slice_rows)] for expert in range(2)]
    sources += [
        weights_ref.at[expert, pl.ds(slice_rows, slice_rows // 2)] for expert in range(2)
    ]
    sources += [qkv_grad_ref, out_proj_ref]
    targets = [gate_up_grad.at[0], gate_up_grad.at[1], down_grad.at[0], down_grad.at[1]]
    targets += [qkv_grad, out_proj]
    loads, stores = [], []
    for index, source in enumerate(sources):
        loads.append(pltpu.make_async_copy(source, narrow[index], sems.at[0, index]))
        stores.append(pltpu.make_async_copy(wide[index], targets[index], sems.at[1, index]))
    for copy in loads + arrivals:
        copy.start()
    place = pl.ds(
        pl.multiple_of(lax.axis_index("context") * slice_rows, 128), slice_rows
    )
    attn_gain_grad[...] = gains_ref[0:1, place].reshape(slice_rows)
    ffn_gain_grad[...] = gains_ref[1:2, place].reshape(slice_rows)
    for index in range(6):
        loads[index].wait()
        wide[index][...] = narrow[index][...].astype(F32)
        stores[index].start()
    for arrival, move in zip(arrivals, moves):
        arrival.wait()
        move.start()
    for copy in stores + moves:
        copy.wait()


def widen(packed_out, packed_grad, gains, out_proj, qkv_grad, weights):
    slice_rows, total = out_proj.shape[0], weights.shape[1]
    parts = [(slice_rows, D)] * 2 + [(total - slice_rows, D)] * 2
    parts += [qkv_grad.shape, out_proj.shape]
    shape = jax.ShapeDtypeStruct
    return pl.pallas_call(
        widen_kernel,
        out_shape=[
            shape(packed_out.shape, BF),
            shape(packed_grad.shape, F32),
            shape((slice_rows,), F32),
            shape(qkv_grad.shape, F32),
            shape(out_proj.shape, F32),
            shape((slice_rows,), F32),
            shape((2, slice_rows, D), F32),
            shape((2, total - slice_rows, D), F32),
        ],
        in_specs=[ANY] * 2 + [VM] + [ANY] * 3,
        out_specs=[ANY] * 2 + [VM] + [ANY] * 2 + [VM] + [ANY] * 2,
        scratch_shapes=[pltpu.VMEM(part, BF) for part in parts]
        + [pltpu.VMEM(part, F32) for part in parts]
        + [pltpu.VMEM(packed_out.shape, BF), pltpu.VMEM(packed_grad.shape, F32)]
        + [pltpu.SemaphoreType.DMA((2, 8))],
        compiler_params=pltpu.CompilerParams(vmem_limit_bytes=62 << 20),
        cost_estimate=pl.CostEstimate(flops=0, bytes_accessed=24 << 20, transcendentals=0),
    )(packed_out, packed_grad, gains, out_proj, qkv_grad, weights)


def fast_body(
    packed_in,
    routes,
    gates,
    doc_starts,
    attn_gain,
    w_qkv,
    w_out,
    ffn_gain,
    expert_gate_up,
    expert_down,
    cotangent,
):
    x, c, starts = packed_in[0], cotangent[0], doc_starts[0]
    steps = np.arange(HEAD_SIZE) % (HEAD_SIZE // 2)
    frequency = jnp.asarray((rope_base ** (-2.0 * steps / HEAD_SIZE)).astype(np.float32)[None])
    attn_gain, ffn_gain = attn_gain.reshape(-1, 128), ffn_gain.reshape(-1, 128)
    h1, query, logsum, merged, residual, kv, dh2, y_home, y_side, *weight_parts = front(
        x,
        routes[0],
        gates[0],
        starts,
        frequency,
        attn_gain,
        ffn_gain,
        c,
        w_qkv,
        w_out,
        expert_gate_up,
        expert_down,
    )
    sums = backward(
        starts,
        frequency,
        attn_gain,
        ffn_gain,
        dh2,
        residual,
        c,
        merged,
        logsum,
        query,
        h1,
        x,
        y_home,
        kv,
        w_qkv,
        w_out,
        y_side,
        *weight_parts,
    )
    packed_out, packed_grad, attn_grad, qkv_grad, out_proj, ffn_grad, gate_up, down = widen(*sums)
    return (
        packed_out[None],
        packed_grad[None],
        attn_grad,
        qkv_grad,
        out_proj,
        ffn_grad,
        gate_up,
        down,
    )


def fits(mesh):
    sizes = mesh.shape
    contexts = sizes["context"]
    return (
        sizes["dp"] == 2
        and sizes["expert"] == 4
        and contexts == 4
        and D % (contexts * 384) == 0
        and FF % (contexts * 64) == 0
    )


def solution(mesh):
    chosen_body = fast_body if fits(mesh) else body
    placed = (
        P(("dp", "expert"), "context", None),
        P(("dp", "expert"), "context", None),
        P(("dp", "expert"), "context", None),
        P(("dp", "expert"), None),
        P(),
        P(),
        P(),
        P(),
        P("expert", None, None),
        P("expert", None, None),
        P(("dp", "expert"), "context", None),
    )
    return jax.shard_map(
        chosen_body,
        mesh=mesh,
        in_specs=placed,
        out_specs=(
            P(("dp", "expert"), "context", None),
            P(("dp", "expert"), "context", None),
            P("context"),
            P("context", None),
            P("context", None),
            P("context"),
            P("expert", "context", None),
            P("expert", "context", None),
        ),
        check_vma=False,
    )
```

```python
import jax
import jax.numpy as jnp
import numpy as np
from jax import lax
from jax.experimental import pallas as pl
from jax.experimental.pallas import tpu as pltpu
from jax.sharding import PartitionSpec as P

D = 1536
QUERY_HEADS = 12
KEY_VALUE_HEADS = 2
HEAD_SIZE = 128
FF = 768
TOP = 4
CAP = 192


epsilon = 1e-06
rope_base = 10000.0
negative_huge = -1e30


def smooth_gate(preact):
    return jax.nn.gelu(preact, approximate=True)


def norm_rows(values, gain):
    inverse = lax.rsqrt(jnp.mean(values * values, axis=-1, keepdims=True) + epsilon)
    return (values * inverse * gain, inverse)


def norm_back(values, inverse, gain, upstream):
    scaled = upstream * gain
    inner = jnp.mean(scaled * values, axis=-1, keepdims=True)
    grad_in = inverse * scaled - values * inverse * inverse * inverse * inner
    grad_gain = jnp.sum(upstream * values * inverse, axis=0)
    return (grad_in, grad_gain)


def doc_begins(positions, starts):
    return jnp.max(jnp.where(starts[None, :] <= positions[:, None], starts[None, :], 0), axis=1)


def rope_tables(offsets, half_dim):
    frequency = rope_base ** (-(jnp.arange(half_dim, dtype=jnp.float32) * 2.0 / (2.0 * half_dim)))
    angles = offsets.astype(jnp.float32)[:, None] * frequency[None, :]
    return (jnp.cos(angles), jnp.sin(angles))


def apply_rotary(values, cosine_table, sine_values, forward):
    half_dim = cosine_table.shape[1]
    first = values[..., :half_dim]
    second = values[..., half_dim:]
    cosine_wide = cosine_table[:, None, :]
    sine_wide = sine_values[:, None, :]
    if forward:
        return jnp.concatenate(
            [first * cosine_wide - second * sine_wide, second * cosine_wide + first * sine_wide],
            axis=-1,
        )
    return jnp.concatenate(
        [first * cosine_wide + second * sine_wide, second * cosine_wide - first * sine_wide],
        axis=-1,
    )


def fold_keys(
    folded, key_matrix, value_matrix, key_start, query_matrix, positions, begins, scaling
):
    running_max, denominator, weighted = folded
    row_count = key_matrix.shape[0]
    key_pos = key_start + jnp.arange(row_count, dtype=jnp.int32)
    allowed = (key_pos[None, :] <= positions[:, None]) & (key_pos[None, :] >= begins[:, None])
    scores = (
        jnp.einsum("qgha,kga->ghqk", query_matrix, key_matrix, preferred_element_type=jnp.float32)
        * scaling
    )
    masked = jnp.where(allowed, scores, negative_huge)
    new_max = jnp.maximum(running_max, jnp.max(masked, axis=-1))
    weights = jnp.where(allowed, jnp.exp(scores - new_max[..., None]), 0.0)
    shrink = jnp.exp(running_max - new_max)
    denominator = denominator * shrink + jnp.sum(weights, axis=-1)
    weighted = weighted * shrink[..., None] + jnp.einsum(
        "ghqk,kga->ghqa",
        weights.astype(jnp.bfloat16),
        value_matrix,
        preferred_element_type=jnp.float32,
    )
    return (new_max, denominator, weighted)


def attend_back(
    query_matrix,
    output_gradient,
    logsum,
    delta,
    positions,
    begins,
    key_matrix,
    value_matrix,
    key_start,
    scaling,
):
    row_count = key_matrix.shape[0]
    key_pos = key_start + jnp.arange(row_count, dtype=jnp.int32)
    allowed = (key_pos[None, :] <= positions[:, None]) & (key_pos[None, :] >= begins[:, None])
    scores = (
        jnp.einsum("qgha,kga->ghqk", query_matrix, key_matrix, preferred_element_type=jnp.float32)
        * scaling
    )
    probs = jnp.where(allowed, jnp.exp(scores - logsum[..., None]), 0.0)
    grad_probs = jnp.einsum(
        "ghqa,kga->ghqk", output_gradient, value_matrix, preferred_element_type=jnp.float32
    )
    grad_scores = (probs * (grad_probs - delta[..., None])).astype(jnp.bfloat16)
    grad_query = (
        jnp.einsum("ghqk,kga->ghqa", grad_scores, key_matrix, preferred_element_type=jnp.float32)
        * scaling
    )
    grad_key = (
        jnp.einsum("ghqk,qgha->kga", grad_scores, query_matrix, preferred_element_type=jnp.float32)
        * scaling
    )
    grad_value = jnp.einsum(
        "ghqk,ghqa->kga",
        probs.astype(jnp.bfloat16),
        output_gradient,
        preferred_element_type=jnp.float32,
    )
    return (grad_query, grad_key, grad_value)


def body(
    packed_in,
    routes,
    gates,
    doc_starts,
    attn_gain,
    w_qkv,
    w_out,
    ffn_gain,
    expert_gate_up,
    expert_down,
    cotangent,
):
    tokens = packed_in[0].astype(jnp.float32)
    token_count = tokens.shape[0]
    query_groups = QUERY_HEADS // KEY_VALUE_HEADS
    query_width = QUERY_HEADS * HEAD_SIZE
    key_value_width = KEY_VALUE_HEADS * HEAD_SIZE
    scaling = HEAD_SIZE ** (-0.5)
    contexts = lax.axis_size("context")
    own_index = lax.axis_index("context")
    positions = own_index * token_count + jnp.arange(token_count, dtype=jnp.int32)
    last_pos = own_index * token_count + token_count - 1
    begins = doc_begins(positions, doc_starts[0])
    cosine_table, sine_values = rope_tables(positions - begins, HEAD_SIZE // 2)
    normed_a, inverse_a = norm_rows(tokens, attn_gain)
    normed_ab = normed_a.astype(jnp.bfloat16)
    projected_rows = jnp.dot(normed_ab, w_qkv, preferred_element_type=jnp.float32)
    query_matrix = apply_rotary(
        projected_rows[:, :query_width].reshape(token_count, QUERY_HEADS, HEAD_SIZE),
        cosine_table,
        sine_values,
        True,
    )
    query_matrix = query_matrix.astype(jnp.bfloat16).reshape(
        token_count, KEY_VALUE_HEADS, query_groups, HEAD_SIZE
    )
    key_matrix = apply_rotary(
        projected_rows[:, query_width : query_width + key_value_width].reshape(
            token_count, KEY_VALUE_HEADS, HEAD_SIZE
        ),
        cosine_table,
        sine_values,
        True,
    )
    key_matrix = key_matrix.astype(jnp.bfloat16)
    value_matrix = (
        projected_rows[:, query_width + key_value_width :]
        .reshape(token_count, KEY_VALUE_HEADS, HEAD_SIZE)
        .astype(jnp.bfloat16)
    )
    query_layout = (KEY_VALUE_HEADS, query_groups, token_count, HEAD_SIZE)
    start_state = (
        jnp.full((KEY_VALUE_HEADS, query_groups, token_count), negative_huge, jnp.float32),
        jnp.zeros((KEY_VALUE_HEADS, query_groups, token_count), jnp.float32),
        jnp.zeros(query_layout, jnp.float32),
    )
    part_keys = lax.all_gather(key_matrix, "context", axis=0, tiled=True)
    part_values = lax.all_gather(value_matrix, "context", axis=0, tiled=True)
    row_count = part_keys.shape[0]
    width = 512 if row_count > 1024 and row_count % 512 == 0 else row_count

    def inner_step(block_index, state_now):
        offset = block_index * width
        block_keys = lax.dynamic_slice_in_dim(part_keys, block_index * width, width, 0)
        block_values = lax.dynamic_slice_in_dim(part_values, block_index * width, width, 0)

        def update(state_in):
            return fold_keys(
                state_in, block_keys, block_values, offset, query_matrix, positions, begins, scaling
            )

        def unchanged(state_in):
            return state_in

        return lax.cond(offset <= last_pos, update, unchanged, state_now)

    running_max, denominator, weighted = lax.fori_loop(
        0, row_count // width, inner_step, start_state
    )
    attended = weighted / denominator[..., None]
    logsum = running_max + jnp.log(denominator)
    merged_b = (
        jnp.transpose(attended, (2, 0, 1, 3)).reshape(token_count, query_width).astype(jnp.bfloat16)
    )
    residual = tokens + jnp.dot(merged_b, w_out, preferred_element_type=jnp.float32)
    normed_f, inverse_f = norm_rows(residual, ffn_gain)
    normed_fb = normed_f.astype(jnp.bfloat16)
    local_experts = expert_gate_up.shape[0]
    expert_devices = lax.axis_size("expert")
    expert_total = local_experts * expert_devices
    chosen = routes[0].reshape(-1)
    onehot = (chosen[:, None] == jnp.arange(expert_total, dtype=jnp.int32)[None, :]).astype(
        jnp.int32
    )
    slots = jnp.sum((jnp.cumsum(onehot, axis=0) - onehot) * onehot, axis=1)
    repeated = jnp.repeat(normed_fb, TOP, axis=0)
    outgoing = jnp.zeros((expert_total, CAP, D), jnp.bfloat16).at[chosen, slots].set(repeated)
    outgoing = outgoing.reshape(expert_devices, local_experts, CAP, D)
    arrived_rows = lax.all_to_all(outgoing, "expert", split_axis=0, concat_axis=0, tiled=True)
    gate_up_rows = jnp.einsum(
        "sjcd,jdf->sjcf", arrived_rows, expert_gate_up, preferred_element_type=jnp.float32
    )
    hidden = (smooth_gate(gate_up_rows[..., :FF]) * gate_up_rows[..., FF:]).astype(jnp.bfloat16)
    produced = jnp.einsum("sjcf,jfd->sjcd", hidden, expert_down, preferred_element_type=jnp.float32)
    returned_rows = lax.all_to_all(
        produced.astype(jnp.bfloat16), "expert", split_axis=0, concat_axis=0, tiled=True
    )
    picked = (
        returned_rows.reshape(expert_total, CAP, D)[chosen, slots]
        .astype(jnp.float32)
        .reshape(token_count, TOP, D)
    )
    gate_values = gates[0]
    mixture = jnp.sum(gate_values[..., None] * picked, axis=1)
    packed_out = (residual + mixture).astype(jnp.bfloat16)
    upstream = cotangent[0].astype(jnp.float32)
    grad_mix = (
        (gate_values[..., None] * upstream[:, None, :])
        .astype(jnp.bfloat16)
        .reshape(token_count * TOP, D)
    )
    grad_send = jnp.zeros((expert_total, CAP, D), jnp.bfloat16).at[chosen, slots].set(grad_mix)
    grad_send = grad_send.reshape(expert_devices, local_experts, CAP, D)
    grad_arrived = lax.all_to_all(grad_send, "expert", split_axis=0, concat_axis=0, tiled=True)
    gate_part = gate_up_rows[..., :FF]
    up_part = gate_up_rows[..., FF:]
    activated, gelu_back = jax.vjp(smooth_gate, gate_part)
    hidden_b = (activated * up_part).astype(jnp.bfloat16)
    grad_hidden = jnp.einsum(
        "sjcd,jfd->sjcf", grad_arrived, expert_down, preferred_element_type=jnp.float32
    )
    down_grad = jnp.einsum(
        "sjcf,sjcd->jfd", hidden_b, grad_arrived, preferred_element_type=jnp.float32
    )
    grad_gate = gelu_back(grad_hidden * up_part)[0]
    grad_gu = jnp.concatenate([grad_gate, grad_hidden * activated], axis=-1).astype(jnp.bfloat16)
    gate_up_grad = jnp.einsum(
        "sjcd,sjcf->jdf", arrived_rows, grad_gu, preferred_element_type=jnp.float32
    )
    grad_rows = jnp.einsum(
        "sjcf,jdf->sjcd", grad_gu, expert_gate_up, preferred_element_type=jnp.float32
    )
    grad_back = lax.all_to_all(
        grad_rows.astype(jnp.bfloat16), "expert", split_axis=0, concat_axis=0, tiled=True
    )
    grad_picked = grad_back.reshape(expert_total, CAP, D)[chosen, slots].astype(jnp.float32)
    grad_normed_f = jnp.sum(grad_picked.reshape(token_count, TOP, D), axis=1)
    grad_resid_part, ffn_gain_grad = norm_back(residual, inverse_f, ffn_gain, grad_normed_f)
    grad_residual = upstream + grad_resid_part
    grad_branch = grad_residual.astype(jnp.bfloat16)
    out_proj_grad = jnp.einsum(
        "td,tf->df", merged_b, grad_branch, preferred_element_type=jnp.float32
    )
    merged_gradient = jnp.einsum(
        "tf,df->td", grad_branch, w_out, preferred_element_type=jnp.float32
    ).astype(jnp.bfloat16)
    output_gradient = jnp.transpose(
        merged_gradient.reshape(token_count, KEY_VALUE_HEADS, query_groups, HEAD_SIZE), (1, 2, 0, 3)
    )
    delta = jnp.sum(output_gradient.astype(jnp.float32) * attended, axis=-1)

    def block_back(part_keys, part_values, key_start):

        def compute(operands):
            return attend_back(
                query_matrix,
                output_gradient,
                logsum,
                delta,
                positions,
                begins,
                operands[0],
                operands[1],
                key_start,
                scaling,
            )

        def nothing(operands):
            return (
                jnp.zeros(query_layout, jnp.float32),
                jnp.zeros(operands[0].shape, jnp.float32),
                jnp.zeros(operands[1].shape, jnp.float32),
            )

        return lax.cond(key_start <= last_pos, compute, nothing, (part_keys, part_values))

    grad_query = jnp.zeros(query_layout, jnp.float32)
    complete_keys, whole_values = (
        lax.all_gather(key_matrix, "context", axis=0, tiled=True),
        lax.all_gather(value_matrix, "context", axis=0, tiled=True),
    )
    block_span = 2 * token_count

    def block_turn(turn_index, block_state):
        keys_grad_all, values_grad_all, query_sum = block_state
        offset = turn_index * block_span
        add_query, add_key, add_value = block_back(
            lax.dynamic_slice_in_dim(complete_keys, offset, block_span, 0),
            lax.dynamic_slice_in_dim(whole_values, offset, block_span, 0),
            offset,
        )
        keys_grad_all = lax.dynamic_update_slice_in_dim(keys_grad_all, add_key, offset, 0)
        values_grad_all = lax.dynamic_update_slice_in_dim(values_grad_all, add_value, offset, 0)
        return (keys_grad_all, values_grad_all, query_sum + add_query)

    zero_filled = jnp.zeros((complete_keys.shape[0], KEY_VALUE_HEADS, HEAD_SIZE), jnp.float32)
    finished = lax.fori_loop(0, contexts // 2, block_turn, (zero_filled, zero_filled, grad_query))
    grad_keys, grad_values = (
        lax.psum_scatter(
            finished[0].astype(jnp.bfloat16), "context", scatter_dimension=0, tiled=True
        ).astype(jnp.float32),
        lax.psum_scatter(
            finished[1].astype(jnp.bfloat16), "context", scatter_dimension=0, tiled=True
        ).astype(jnp.float32),
    )
    grad_query = finished[2]
    grad_q_rows = apply_rotary(
        jnp.transpose(grad_query, (2, 0, 1, 3)).reshape(token_count, QUERY_HEADS, HEAD_SIZE),
        cosine_table,
        sine_values,
        False,
    )
    grad_k_rows = apply_rotary(grad_keys, cosine_table, sine_values, False)
    grad_projected = jnp.concatenate(
        [
            grad_q_rows.reshape(token_count, query_width),
            grad_k_rows.reshape(token_count, key_value_width),
            grad_values.reshape(token_count, key_value_width),
        ],
        axis=-1,
    ).astype(jnp.bfloat16)
    qkv_grad = jnp.einsum(
        "td,tf->df", normed_ab, grad_projected, preferred_element_type=jnp.float32
    )
    grad_normed_a = jnp.einsum(
        "tf,df->td", grad_projected, w_qkv, preferred_element_type=jnp.float32
    )
    grad_in_part, attn_gain_grad = norm_back(tokens, inverse_a, attn_gain, grad_normed_a)
    packed_grad = grad_residual + grad_in_part
    summed = (
        lax.psum_scatter(
            attn_gain_grad.astype(jnp.bfloat16), "context", scatter_dimension=0, tiled=True
        ).astype(jnp.float32),
        lax.psum_scatter(
            qkv_grad.astype(jnp.bfloat16), "context", scatter_dimension=0, tiled=True
        ).astype(jnp.float32),
        lax.psum_scatter(
            out_proj_grad.astype(jnp.bfloat16), "context", scatter_dimension=0, tiled=True
        ).astype(jnp.float32),
        lax.psum_scatter(
            ffn_gain_grad.astype(jnp.bfloat16), "context", scatter_dimension=0, tiled=True
        ).astype(jnp.float32),
        lax.psum_scatter(
            gate_up_grad.astype(jnp.bfloat16), "context", scatter_dimension=1, tiled=True
        ).astype(jnp.float32),
        lax.psum_scatter(
            down_grad.astype(jnp.bfloat16), "context", scatter_dimension=1, tiled=True
        ).astype(jnp.float32),
    )
    dense_rows = (summed[0], summed[1], summed[2], summed[3])
    expert_sums = (
        lax.psum(summed[4].astype(jnp.bfloat16), "dp").astype(jnp.float32),
        lax.psum(summed[5].astype(jnp.bfloat16), "dp").astype(jnp.float32),
    )
    shared = (
        lax.psum(dense_rows[0].astype(jnp.bfloat16), ("dp", "expert")).astype(jnp.float32),
        lax.psum(dense_rows[1].astype(jnp.bfloat16), ("dp", "expert")).astype(jnp.float32),
        lax.psum(dense_rows[2].astype(jnp.bfloat16), ("dp", "expert")).astype(jnp.float32),
        lax.psum(dense_rows[3].astype(jnp.bfloat16), ("dp", "expert")).astype(jnp.float32),
    )
    return (
        packed_out[None],
        packed_grad[None],
        shared[0],
        shared[1],
        shared[2],
        shared[3],
        expert_sums[0],
        expert_sums[1],
    )


MESH = pl.DeviceIdType.MESH
BF = jnp.bfloat16
F32 = jnp.float32
NN = (((1,), (0,)), ((), ()))
NT = (((1,), (1,)), ((), ()))
TN = (((0,), (0,)), ((), ()))


def matmul(left, right, dims=NN):
    return lax.dot_general(left, right, dims, preferred_element_type=F32)


def flip(axis, bit):
    index = lax.axis_index(axis)
    return {axis: index + bit - 2 * bit * ((index // bit) % 2)}


def greet(peers):
    barrier = pltpu.get_barrier_semaphore()
    for peer in peers:
        pl.semaphore_signal(barrier, inc=1, device_id=peer, device_id_type=MESH)
    pl.semaphore_wait(barrier, len(peers))


def remote(src, dst, send_sem, recv_sem, peer):
    return pltpu.make_async_remote_copy(
        src_ref=src,
        dst_ref=dst,
        send_sem=send_sem,
        recv_sem=recv_sem,
        device_id=peer,
        device_id_type=MESH,
    )


def other(axis, distance):
    size = lax.axis_size(axis)
    return {axis: lax.rem(lax.axis_index(axis) + distance, size)}


def mate(code):
    expert = lax.axis_index("expert")
    for bit in (1, 2):
        if code & bit:
            expert = expert + bit - 2 * bit * ((expert // bit) % 2)
    return {**flip("dp", 1), "expert": expert} if code & 4 else {"expert": expert}


class GroupGather:
    def __init__(self, own, held, sems, rows):
        half = rows // 2
        self.x, self.y, self.core = flip("dp", 1), flip("expert", 2), flip("expert", 1)

        def part(which, index, amount=1):
            return held.at[pl.ds(which * 2 * rows + index * half, amount * half)]

        def link(number, src, dst, peer):
            return remote(src, dst, sems.at[0, number], sems.at[1, number], peer)

        first, second = own.at[pl.ds(0, half)], own.at[pl.ds(half, half)]
        self.links = [
            link(0, first, part(1, 0), self.x),
            link(1, second, part(1, 1), self.y),
            link(2, first, part(2, 0), self.y),
            link(3, second, part(2, 1), self.x),
            link(4, part(1, 0), part(3, 0), self.y),
            link(5, part(1, 1), part(3, 1), self.x),
        ]
        self.cores = [link(6, own, part(0, 2, 2), self.core)]
        for which in range(1, 4):
            self.cores.append(
                link(6 + which, part(which, 0, 2), part(which, 2, 2), self.core)
            )

    def start(self):
        for link in self.links[:4]:
            link.start()
        self.cores[0].start()

    def forward(self, which):
        for index in range(2 * which - 2, 2 * which):
            self.links[index].wait_recv()
            if which == 1:
                self.links[4 + index].start()
        self.cores[which].start()

    def arrived(self, which):
        self.cores[which].wait_recv()

    def finish(self):
        for link in self.links + self.cores:
            link.wait_send()


GATHER_SEMS = pltpu.SemaphoreType.DMA((2, 10))


def rotate(values, cosine, sine):
    return values * cosine + pltpu.roll(values, values.shape[1] // 2, 1) * sine


SLOT_CODES = ((0, 0, 1, 1), (4, 2, 5, 3), (2, 4, 3, 5), (6, 6, 7, 7))


def turned(axis, code):
    index = lax.axis_index(axis)
    bit = 1
    while bit <= code:
        if code & bit:
            index = index + bit - 2 * bit * ((index // bit) % 2)
        bit *= 2
    return index


def gelu_parts(gate):
    slope = 0.7978845608
    bend = 0.044715
    square = gate * gate
    tanh = jnp.tanh(slope * gate * (1.0 + bend * square))
    half = 0.5 * (1.0 + tanh)
    grad = half + 0.5 * slope * gate * (1.0 - tanh * tanh) * (1.0 + 3.0 * bend * square)
    return gate * half, grad


class GroupReturn:
    def __init__(self, source, near, second, third, sems, rows, whole=True):
        self.source, self.rows, self.half = source, rows, rows // 2
        self.near, self.second, self.third = near, second, third
        x, y, core = flip("dp", 1), flip("expert", 2), flip("expert", 1)

        def link(number, src, dst, peer):
            return remote(src, dst, sems.at[0, number], sems.at[1, number], peer)

        def part(which, index):
            return near.at[which, pl.ds(index * self.half, self.half)]

        self.cores = [
            link(6 + which, source.at[pl.ds((2 * which + 1) * rows, rows)], near.at[which], core)
            for which in range(4)
        ]
        self.finals = []
        if whole:
            self.finals = [
                link(0, part(1, 0), third.at[0], x),
                link(1, part(1, 1), third.at[1], y),
            ]
        self.links = [
            link(2, part(2, 0), third.at[2], y),
            link(3, part(2, 1), third.at[3], x),
            link(4, part(3, 0), second.at[0], y),
            link(5, part(3, 1), second.at[1], x),
        ]

    def fold(self, which, index):
        begin = 2 * which * self.rows + index * self.half
        value = self.source[begin : begin + self.half].astype(F32)
        span = slice(index * self.half, (index + 1) * self.half)
        return span, value + self.near[which, span].astype(F32)

    def side(self):
        self.cores[2].wait_recv()
        for index in range(2):
            span, value = self.fold(2, index)
            self.near[2, span] = value.astype(BF)
            self.links[index].start()

    def far(self):
        self.cores[3].wait_recv()
        for index in range(2):
            span, value = self.fold(3, index)
            self.near[3, span] = value.astype(BF)
            self.links[2 + index].start()

    def middle(self):
        self.cores[1].wait_recv()
        for index in range(2):
            self.links[2 + index].wait_recv()
            span, value = self.fold(1, index)
            self.near[1, span] = (value + self.second[index].astype(F32)).astype(BF)

    def last(self):
        for link in self.finals:
            link.start()

    def home(self, index):
        if index == 0:
            self.cores[0].wait_recv()
        self.links[index].wait_recv()
        span, value = self.fold(0, index)
        return span, value + self.third[2 + index].astype(F32)

    def sent(self):
        for copy in self.cores + self.links + self.finals:
            copy.wait_send()


def document_angles(starts_ref, frequency_ref, cosine, sine):
    rows = cosine.shape[0]
    offset = lax.axis_index("context") * rows
    positions = offset + lax.broadcasted_iota(jnp.int32, cosine.shape, 0)
    row_positions = offset + lax.broadcasted_iota(jnp.int32, (1, rows), 1)
    begins = jnp.zeros(cosine.shape, jnp.int32)
    begin_row = jnp.zeros((1, rows), jnp.int32)
    for document in range(starts_ref.shape[0]):
        start = starts_ref[document]
        begins = jnp.maximum(begins, jnp.where(positions >= start, start, 0))
        begin_row = jnp.maximum(begin_row, jnp.where(row_positions >= start, start, 0))
    angles = (positions - begins).astype(F32) * frequency_ref[...]
    cosine[...] = jnp.cos(angles)
    lane = lax.broadcasted_iota(jnp.int32, cosine.shape, 1)
    sine[...] = jnp.where(lane < HEAD_SIZE // 2, -1.0, 1.0) * jnp.sin(angles)
    return begin_row


def gain_row(gain_ref):
    return jnp.concatenate([gain_ref[index : index + 1] for index in range(D // 128)], axis=1)


def front_kernel(
    x_ref,
    routes_ref,
    gates_ref,
    starts_ref,
    frequency_ref,
    attn_gain_ref,
    ffn_gain_ref,
    c_ref,
    w_qkv_ref,
    w_out_ref,
    gate_up_ref,
    down_ref,
    h1_ref,
    q_ref,
    logsum_ref,
    merged_ref,
    residual_ref,
    kv_ref,
    dh2_ref,
    y_home_ref,
    y_side_ref,
    gu_near_ref,
    gu_far_ref,
    down_part_ref,
    gu_in_ref,
    down_in_ref,
    far_in_ref,
    w_gu,
    w_down,
    h2_all,
    c_all,
    dhid,
    gu,
    hidden,
    dgu,
    du,
    share,
    gu_part,
    down_part,
    near,
    second,
    third,
    gu_in,
    kv,
    top,
    total,
    bias,
    cosine,
    sine,
    share_own,
    share_all,
    load_sems,
    out_sems,
    kv_sems,
    keep_sems,
    share_sems,
    c_sems,
    h2_sems,
    z_sems,
    du_sems,
    y_sems,
    credits,
):
    contexts = lax.axis_size("context")
    me = lax.axis_index("context")
    dp = lax.axis_index("dp")
    rows = x_ref.shape[0]
    half = rows // 2
    two = 2 * rows
    slice_rows = gu_part.shape[1]
    first = gu_in.shape[0]
    down_rows = down_part.shape[1] // 2
    query_width = QUERY_HEADS * HEAD_SIZE
    key_width = KEY_VALUE_HEADS * HEAD_SIZE
    heads = QUERY_HEADS // KEY_VALUE_HEADS
    scaling = HEAD_SIZE ** (-0.5)

    w_q = du.at[pl.ds(0, D)]
    h1 = du.at[pl.ds(D, rows)]
    merged = du.at[pl.ds(D + rows, rows)]
    w_out = dgu.at[pl.ds(0, query_width)]
    query = dgu.at[pl.ds(query_width, rows)]
    w_kv = hidden.at[pl.ds(0, D), pl.ds(0, 2 * key_width)]
    residual = gu.at[pl.ds(0, rows)]
    dh2, y_home = gu.at[pl.ds(0, rows)], gu.at[pl.ds(rows, rows)]

    def accumulated(head):
        across = gu.shape[1] // rows
        return gu.at[
            pl.ds(head // across * HEAD_SIZE, HEAD_SIZE), pl.ds(head % across * rows, rows)
        ]

    def load(number, src, dst):
        copy = pltpu.make_async_copy(src, dst, load_sems.at[number])
        copy.start()
        return copy

    load_kv = load(0, w_qkv_ref.at[:, query_width:], w_kv)
    load_q = load(1, w_qkv_ref.at[:, :query_width], w_q)
    load_c = load(2, c_ref, c_all.at[pl.ds(0, rows)])
    load_out = load(3, w_out_ref, w_out)
    load_down = load(4, down_ref.at[dp], w_down)
    load_gu = load(5, gate_up_ref.at[dp], w_gu)

    begin_row = document_angles(starts_ref, frequency_ref, cosine, sine)
    named = lax.broadcasted_iota(jnp.int32, share_own.shape, 0)
    gathered = jnp.zeros(share_own.shape, F32)
    for choice in range(TOP):
        chosen = routes_ref[choice : choice + 1] == named
        gathered = gathered + jnp.where(chosen, gates_ref[choice : choice + 1], 0.0)
    share_own[...] = gathered

    mates = [mate(code) for code in range(1, 8)]
    greet([other("context", step) for step in range(1, contexts)] + mates)

    c_gather = GroupGather(c_ref, c_all, c_sems, rows)
    c_gather.start()
    shares = [
        remote(
            share_own,
            share_all.at[1 + index],
            share_sems.at[0, index],
            share_sems.at[1, index],
            peer,
        )
        for index, peer in enumerate(mates)
    ]
    for copy in shares:
        copy.start()

    x = x_ref[...].astype(F32)
    inverse = lax.rsqrt(jnp.mean(x * x, axis=-1, keepdims=True) + epsilon)
    h1[...] = (x * inverse * gain_row(attn_gain_ref)).astype(BF)

    load_kv.wait()
    projected = matmul(h1[...], w_kv[...])
    for head in range(KEY_VALUE_HEADS):
        lanes = slice(head * HEAD_SIZE, (head + 1) * HEAD_SIZE)
        kv[me, :, lanes] = rotate(projected[:, lanes], cosine[...], sine[...]).astype(BF)
    kv[me, :, key_width:] = projected[:, key_width:].astype(BF)

    def kv_copy(block):
        return remote(
            kv.at[block],
            kv.at[block],
            kv_sems.at[0, block],
            kv_sems.at[1, block],
            {"context": lax.rem(me + 1, contexts)},
        )

    def pass_on(block):
        @pl.when(me + 1 < contexts)
        def _():
            kv_copy(block).start()

    pass_on(me)

    load_q.wait()
    span = 4 * HEAD_SIZE
    for offset in range(0, query_width, span):
        projected = matmul(h1[...], w_q[:, offset : offset + span])
        for head in range(span // HEAD_SIZE):
            lanes = slice(head * HEAD_SIZE, (head + 1) * HEAD_SIZE)
            place = slice(offset + head * HEAD_SIZE, offset + (head + 1) * HEAD_SIZE)
            query[:, place] = rotate(projected[:, lanes], cosine[...], sine[...]).astype(BF)

    outs = []

    def out(src, dst):
        copy = pltpu.make_async_copy(src, dst, out_sems.at[len(outs)])
        copy.start()
        outs.append(copy)

    out(h1, h1_ref)
    out(query, q_ref)
    top[...] = jnp.full_like(top, negative_huge)
    total[...] = jnp.zeros_like(total)
    gu[...] = jnp.zeros_like(gu)
    query_pos = me * rows + lax.broadcasted_iota(jnp.int32, (rows, rows), 1)

    def fold(block):
        key_pos = block * rows + lax.broadcasted_iota(jnp.int32, (rows, rows), 0)
        allowed = (key_pos <= query_pos) & (key_pos >= begin_row)
        bias[...] = jnp.where(allowed, 0.0, negative_huge)
        for head in range(QUERY_HEADS):
            group = head // heads
            keys = kv[block, :, group * HEAD_SIZE : (group + 1) * HEAD_SIZE]
            values = kv[
                block, :, key_width + group * HEAD_SIZE : key_width + (group + 1) * HEAD_SIZE
            ]
            queries = query[:, head * HEAD_SIZE : (head + 1) * HEAD_SIZE]
            scores = matmul(keys, queries, NT) * scaling + bias[...]
            old = top[head : head + 1]
            new = jnp.maximum(old, jnp.max(scores, axis=0, keepdims=True))
            weights = jnp.exp(scores - new)
            shrink = jnp.exp(old - new)
            top[head : head + 1] = new
            total[head : head + 1] = total[head : head + 1] * shrink + jnp.sum(
                weights, axis=0, keepdims=True
            )
            place = accumulated(head)
            place[...] = place[...] * shrink + matmul(values, weights.astype(BF), TN)

    def backward_hidden(which):
        rows_of = slice(which * two, (which + 1) * two)
        dhid[which % 3] = matmul(c_all[rows_of], w_down[...], NT)

    def earlier(step, carry):
        @pl.when(step > 0)
        def _():
            kv_copy(me - step).wait_recv()
            pass_on(me - step)

        fold(me - step)

        @pl.when(step == jnp.minimum(me, 1))
        def _():
            c_gather.forward(1)
            load_c.wait()
            load_down.wait()
            c_gather.arrived(0)
            backward_hidden(0)

        return carry

    lax.fori_loop(0, me + 1, earlier, 0)
    load_out.wait()
    for head in range(QUERY_HEADS):
        attended = accumulated(head)[...] / total[head : head + 1]
        merged[:, head * HEAD_SIZE : (head + 1) * HEAD_SIZE] = attended.T.astype(BF)
    top[...] = jnp.where(total[...] > 0, top[...] + jnp.log(total[...]), 0.0)
    out(merged, merged_ref)
    out(top, logsum_ref)
    value = x_ref[...].astype(F32) + matmul(merged[...], w_out[...])
    residual[...] = value
    out(residual, residual_ref)
    inverse = lax.rsqrt(jnp.mean(value * value, axis=-1, keepdims=True) + epsilon)
    h2_all[0:rows] = (value * inverse * gain_row(ffn_gain_ref)).astype(BF)

    gather = GroupGather(h2_all.at[pl.ds(0, rows)], h2_all, h2_sems, rows)
    gather.start()

    c_gather.forward(2)
    c_gather.arrived(1)
    backward_hidden(1)

    def keep_copy(block):
        return pltpu.make_async_copy(kv.at[block], kv_ref.at[block], keep_sems.at[block])

    def keep(block, carry):
        keep_copy(block).start()
        return carry

    lax.fori_loop(0, me + 1, keep, 0)
    share_all[0] = share_own[...]
    for copy in shares:
        copy.wait_recv()
    expert = lax.axis_index("expert") * lax.axis_size("dp") + dp
    columns = []
    for code in range(8):
        swapped = share_all[code].T
        mine = lax.broadcasted_iota(jnp.int32, swapped.shape, 1) == expert
        columns.append(jnp.sum(jnp.where(mine, swapped, 0.0), axis=1, keepdims=True))
    for which, codes in enumerate(SLOT_CODES):
        for index, code in enumerate(codes):
            part = (index % 2) * half
            share[pl.ds(which * two + index * half, half), :] = columns[code][part : part + half]

    def forward(which):
        gu[...] = matmul(h2_all[which * two : (which + 1) * two], w_gu[...])

    def activate(which):
        def body_of(step, carry):
            close = pl.ds(pl.multiple_of(step * half, half), half)
            place = pl.ds(pl.multiple_of(which * two + step * half, half), half)
            up = gu[close, FF:]
            activated, grad = gelu_parts(gu[close, :FF])
            scale = share[place, :]
            upstream = dhid[which % 3, close, :] * scale
            hidden[place, :] = (activated * up * scale).astype(BF)
            dgu[place, :FF] = (upstream * up * grad).astype(BF)
            dgu[place, FF:] = (upstream * activated).astype(BF)
            return carry

        lax.fori_loop(0, 4, body_of, 0)

    def backward(which):
        span = slice(which * two, (which + 1) * two)
        du[span] = matmul(dgu[span], w_gu[...], NT).astype(BF)
        back.cores[which].start()

    def gate_up_slice(code, begin, end):
        lane = turned("context", code) * slice_rows + begin
        lanes = pl.ds(pl.multiple_of(lane, 128), end - begin)
        gu_part[code, begin:end] = matmul(h2_all[:, lanes], dgu[...], TN).astype(BF)

    def down_pair(pair):
        first = turned("context", 2 * pair) // 2
        lanes = pl.ds(pl.multiple_of(first * 2 * down_rows, 128), 2 * down_rows)
        down_part[pair] = matmul(hidden[:, lanes], c_all[...], TN).astype(BF)

    back = GroupReturn(du, near, second, third, du_sems, rows)
    load_gu.wait()
    for copy in outs:
        copy.wait()
    gather.arrived(0)
    forward(0)
    activate(0)
    c_gather.arrived(2)
    backward_hidden(2)
    gather.forward(1)
    backward(0)
    gather.arrived(1)
    forward(1)
    activate(1)
    c_gather.forward(3)
    gather.forward(2)
    c_gather.arrived(3)
    backward_hidden(3)
    gather.arrived(2)
    forward(2)
    activate(2)
    gather.forward(3)
    backward(2)
    gather.arrived(3)
    forward(3)
    activate(3)
    z = flip("context", 1)
    sends = []

    def send(src, dst, peer):
        number = len(sends)
        copy = remote(src, dst, z_sems.at[0, number], z_sems.at[1, number], peer)
        copy.start()
        sends.append(copy)

    gate_up_slice(3, 0, first)
    early = [pl.ds(index * first // 2, first // 2) for index in range(2)]
    for span in early:
        send(gu_part.at[3, span], gu_in.at[span], z)
    gate_up_slice(3, first, slice_rows)
    back.side()
    backward(3)
    down_pair(1)
    back.far()
    backward(1)
    gate_up_slice(2, 0, slice_rows)
    out(gu_part.at[2, pl.ds(first, slice_rows - first)], gu_far_ref)

    def far_early(index):
        span = early[index]
        sends[index].wait_recv()
        value = gu_part[2, span].astype(F32) + gu_in[span].astype(F32)
        gu_part[2, span] = value.astype(BF)
        send(gu_part.at[2, span], far_in_ref.at[span], flip("context", 2))

    far_early(0)
    send(gu_part.at[3, pl.ds(first, slice_rows - first)], gu_in_ref, z)
    down_pair(0)
    out(down_part, down_part_ref)
    back.middle()
    back.last()
    far_early(1)
    place = pl.ds(
        pl.multiple_of(lax.rem(turned("context", 3), 2) * down_rows, 16), down_rows
    )
    send(down_part.at[1, place], down_in_ref, z)
    c_gather.finish()
    for which in range(4):
        span = slice(which * two, (which + 1) * two)
        c_all[span] = matmul(hidden[span], w_down[...]).astype(BF)
    for index in range(2):
        span, value = back.home(index)
        back.finals[index].wait_recv()
        dh2[span] = value + third[index].astype(F32)
    out(dh2, dh2_ref)
    back.sent()
    for number, mate_of in enumerate((flip("expert", 1), flip("dp", 1), flip("expert", 2))):
        pl.semaphore_signal(
            credits.at[number], inc=1, device_id=mate_of, device_id_type=MESH
        )
    for number in range(3):
        pl.semaphore_wait(credits.at[number], 1)
    back = GroupReturn(c_all, near, second, third, y_sems, rows, False)
    for which in (3, 2, 1, 0):
        back.cores[which].start()
    back.far()
    back.side()
    gate_up_slice(1, 0, slice_rows)
    out(gu_part.at[1], gu_near_ref.at[0])
    gate_up_slice(0, 0, slice_rows)
    out(gu_part.at[0], gu_near_ref.at[1])
    back.middle()
    out(near.at[1], y_side_ref)
    for index in range(2):
        span, value = back.home(index)
        y_home[span] = value
    out(y_home, y_home_ref)
    back.sent()
    for copy in sends[:2]:
        copy.wait_send()
    for copy in outs[5:] + sends[2:]:
        copy.wait()
    gather.finish()
    for copy in shares:
        copy.wait_send()

    def settle(block, carry):
        keep_copy(block).wait()

        @pl.when(me + 1 < contexts)
        def _():
            kv_copy(block).wait_send()

        return carry

    lax.fori_loop(0, me + 1, settle, 0)


VM = pl.BlockSpec(memory_space=pltpu.VMEM)
SM = pl.BlockSpec(memory_space=pltpu.SMEM)
ANY = pl.BlockSpec(memory_space=pl.ANY)


def front(
    x, routes, gates, starts, frequency, attn_gain, ffn_gain, cotangent, w_qkv, w_out, gate_up, down
):
    rows = x.shape[0]
    contexts = lax.axis_size("context")
    group = lax.axis_size("dp") * lax.axis_size("expert")
    expert_total = gate_up.shape[0] * lax.axis_size("expert")
    total = group * rows
    kv_width = 2 * KEY_VALUE_HEADS * HEAD_SIZE
    padded = -(-QUERY_HEADS // 8) * 8
    slice_rows, down_rows = D // contexts, FF // contexts
    first = 2 * slice_rows // 3
    gu_shape, down_shape = (contexts, slice_rows, 2 * FF), (contexts // 2, 2 * down_rows, D)
    shape = jax.ShapeDtypeStruct
    dma = pltpu.SemaphoreType.DMA
    return pl.pallas_call(
        front_kernel,
        out_shape=[
            shape((rows, D), BF),
            shape((rows, D), BF),
            shape((padded, rows), F32),
            shape((rows, D), BF),
            shape((rows, D), F32),
            shape((contexts, rows, kv_width), BF),
            shape((rows, D), F32),
            shape((rows, D), F32),
            shape((rows, D), BF),
            shape((2, slice_rows, D), BF),
            shape((slice_rows - first, D), BF),
            shape(down_shape, BF),
            shape((slice_rows - first, D), BF),
            shape((down_rows, D), BF),
            shape((first, D), BF),
        ],
        in_specs=[VM] * 3 + [SM] + [VM] * 3 + [ANY] * 5,
        out_specs=[ANY] * 15,
        scratch_shapes=[
            pltpu.VMEM(gate_up.shape[1:], BF),
            pltpu.VMEM(down.shape[1:], BF),
            pltpu.VMEM((total, D), BF),
            pltpu.VMEM((total, D), BF),
            pltpu.VMEM((3, 2 * rows, FF), F32),
            pltpu.VMEM((2 * rows, 2 * FF), F32),
            pltpu.VMEM((total, FF), BF),
            pltpu.VMEM((total, 2 * FF), BF),
            pltpu.VMEM((total, D), BF),
            pltpu.VMEM((total, 1), F32),
            pltpu.VMEM(gu_shape, BF),
            pltpu.VMEM(down_shape, BF),
            pltpu.VMEM((4, rows, D), BF),
            pltpu.VMEM((2, rows // 2, D), BF),
            pltpu.VMEM((4, rows // 2, D), BF),
            pltpu.VMEM((first, D), BF),
            pltpu.VMEM((contexts, rows, kv_width), BF),
            pltpu.VMEM((padded, rows), F32),
            pltpu.VMEM((padded, rows), F32),
            pltpu.VMEM((rows, rows), F32),
            pltpu.VMEM((rows, HEAD_SIZE), F32),
            pltpu.VMEM((rows, HEAD_SIZE), F32),
            pltpu.VMEM((expert_total, rows), F32),
            pltpu.VMEM((group, expert_total, rows), F32),
            dma((6,)),
            dma((12,)),
            dma((2, contexts)),
            dma((contexts,)),
            dma((2, group - 1)),
            GATHER_SEMS,
            GATHER_SEMS,
            dma((2, 6)),
            dma((2, 10)),
            dma((2, 10)),
            pltpu.SemaphoreType.REGULAR((3,)),
        ],
        compiler_params=pltpu.CompilerParams(
            collective_id=0, has_side_effects=True, vmem_limit_bytes=63 << 20
        ),
        cost_estimate=pl.CostEstimate(
            flops=2 * total * D * FF * 10, bytes_accessed=40 << 20, transcendentals=total * FF
        ),
    )(
        x,
        routes.T,
        gates.T,
        starts,
        frequency,
        attn_gain,
        ffn_gain,
        cotangent,
        w_qkv,
        w_out,
        gate_up,
        down,
    )


def bit_of(axis, bit):
    return lax.rem(lax.axis_index(axis) // bit, 2)


class DenseReduce:
    def __init__(self, part, near, first, second, third, fourth, sems, out, lanes, order):
        self.part, self.near, self.first, self.second = part, near, first, second
        self.third, self.fourth, self.out, self.lanes = third, fourth, out, lanes
        self.sems = sems
        self.rows = part.shape[1] // 8
        self.slices = part.shape[0]
        (axis, bit), (later_axis, later_bit) = order
        self.core, self.core_bit = flip("expert", 1), bit_of("expert", 1)
        self.one, self.one_bit = flip(axis, bit), bit_of(axis, bit)
        self.two, self.two_bit = flip(later_axis, later_bit), bit_of(later_axis, later_bit)
        self.pending = []
        self.released = 0

    def send(self, src, dst, peer, amount=1):
        number = len(self.pending)
        copy = remote(src, dst, self.sems.at[0, number], self.sems.at[1, number], peer)
        copy.start()
        self.pending.append(copy)
        self.waited = number + 1 - amount

    def wait(self):
        for copy in self.pending[self.waited :]:
            copy.wait_recv()

    def span(self, bit, size, base=0):
        return pl.ds(pl.multiple_of(base + bit * size, 16), size)

    def start(self):
        size = 4 * self.rows
        self.send(self.part.at[:, self.span(1 - self.core_bit, size)], self.near, self.core)

    def release(self):
        self.pending[0].wait_send()
        self.released = 1

    def after_core(self):
        self.wait()
        size = 4 * self.rows
        for index in range(self.slices):
            value = self.part[index, self.span(self.core_bit, size)].astype(F32)
            self.near[index] = (value + self.near[index].astype(F32)).astype(BF)
        size = 2 * self.rows
        self.send(self.near.at[:, self.span(1 - self.one_bit, size)], self.first, self.one)

    def after_one(self):
        self.wait()
        size = 2 * self.rows
        for index in range(self.slices):
            value = self.near[index, self.span(self.one_bit, size)].astype(F32)
            self.first[index] = (value + self.first[index].astype(F32)).astype(BF)
        self.send(self.first.at[:, self.span(1 - self.two_bit, self.rows)], self.second, self.two)

    def after_two(self):
        self.wait()
        for index in range(self.slices):
            value = self.first[index, self.span(self.two_bit, self.rows)].astype(F32)
            self.second[index] = (value + self.second[index].astype(F32)).astype(BF)
        bit = bit_of("context", 1)
        for index in range(2):
            source = self.second.at[2 * index + 1 - bit]
            self.send(source, self.third.at[index], flip("context", 1), index + 1)

    def after_near_z(self):
        self.wait()
        bit = bit_of("context", 1)
        for index in range(2):
            value = self.second[2 * index + bit].astype(F32) + self.third[index].astype(F32)
            self.third[index] = value.astype(BF)
        bit = bit_of("context", 2)
        self.send(self.third.at[1 - bit], self.fourth, flip("context", 2))

    def held(self, cuts):
        sizes = (1, 2, 4)
        base = self.core_bit * 4 * self.rows
        if cuts < 2:
            base = base + self.one_bit * 2 * self.rows
        if cuts < 1:
            base = base + self.two_bit * self.rows
        rows = pl.ds(pl.multiple_of(base, 16), sizes[cuts] * self.rows)
        return self.out.at[rows, self.lanes]

    def after_far_z(self):
        self.wait()
        value = self.third[bit_of("context", 2)].astype(F32) + self.fourth[...].astype(F32)
        place = self.held(0)
        place[...] = value.astype(BF)
        self.send(place, place, self.two)

    def return_one(self):
        self.wait()
        self.send(self.held(1), self.held(1), self.one)

    def return_core(self):
        self.wait()
        self.send(self.held(2), self.held(2), self.core)

    def finish(self):
        self.wait()
        for copy in self.pending[self.released :]:
            copy.wait_send()

    @staticmethod
    def scratch(contexts, rows, width):
        least = rows // 8
        return [
            pltpu.VMEM((contexts, 4 * least, width), BF),
            pltpu.VMEM((contexts, 2 * least, width), BF),
            pltpu.VMEM((contexts, least, width), BF),
            pltpu.VMEM((2, least, width), BF),
            pltpu.VMEM((least, width), BF),
            pltpu.SemaphoreType.DMA((2, 9)),
        ]


X_BIT, Y_BIT = ("dp", 1), ("expert", 2)


def unrotate(values, cosine, sine):
    return values * cosine - pltpu.roll(values, values.shape[1] // 2, 1) * sine


def norm_pull(values, gain, upstream):
    inverse = lax.rsqrt(jnp.mean(values * values, axis=-1, keepdims=True) + epsilon)
    scaled = upstream * gain
    inner = jnp.mean(scaled * values, axis=-1, keepdims=True)
    grad_in = inverse * scaled - values * (inverse * inverse * inverse * inner)
    return grad_in, jnp.sum(upstream * (values * inverse), axis=0, keepdims=True)


def backward_kernel(
    starts_ref,
    frequency_ref,
    attn_gain_ref,
    ffn_gain_ref,
    dh2_in,
    residual_in,
    c_in,
    merged_in,
    logsum_in,
    q_in,
    h1_in,
    x_in,
    y_home_in,
    kv_ref,
    w_qkv_ref,
    w_out_ref,
    y_side_ref,
    gu_near_ref,
    gu_far_ref,
    down_part_ref,
    gu_in_ref,
    down_in_ref,
    far_in_ref,
    packed_out_out,
    packed_grad_out,
    gains_ref,
    out_proj_ref,
    qkv_grad_ref,
    weights_ref,
    dh2_ref,
    residual_ref,
    c_ref,
    merged_ref,
    logsum_ref,
    q_ref,
    h1_ref,
    x_ref,
    y_home_ref,
    packed_out_ref,
    packed_grad_ref,
    cosine,
    sine,
    w_dense,
    w_kv,
    kv,
    dres,
    dbranch,
    datt,
    delta,
    bias,
    dq,
    dkv_sum,
    dkv_out,
    dkv_in,
    dqkv,
    dense,
    dense_kv,
    stage_a,
    stage_b,
    near_in,
    far_in,
    gains_in,
    y_in,
    load_sems,
    kv_sems,
    dkv_sems,
    near_sems,
    far_sems,
    x_sems,
    gain_sems,
    y_sems,
    *others,
):
    rows = x_ref.shape[0]
    half = rows // 2
    contexts = lax.axis_size("context")
    me = lax.axis_index("context")
    dp = lax.axis_index("dp")
    query_width = QUERY_HEADS * HEAD_SIZE
    key_width = KEY_VALUE_HEADS * HEAD_SIZE
    heads = QUERY_HEADS // KEY_VALUE_HEADS
    scaling = HEAD_SIZE ** (-0.5)
    slice_rows, down_rows = gu_near_ref.shape[1], down_in_ref.shape[0]
    first = far_in_ref.shape[0]
    cuts = [0, first // 2, first, slice_rows]
    cuts += [slice_rows + 2 * down_rows // 3, slice_rows + down_rows]
    spans = [pl.ds(begin, end - begin) for begin, end in zip(cuts, cuts[1:])]
    down_span = pl.ds(slice_rows, down_rows)

    def load(number, src, dst):
        copy = pltpu.make_async_copy(src, dst, load_sems.at[number])
        copy.start()
        return copy

    def load_kv(block):
        return pltpu.make_async_copy(kv_ref.at[block], kv.at[block], kv_sems.at[block])

    def begin_load(block, carry):
        load_kv(block).start()
        return carry

    def end_load(block, carry):
        load_kv(block).wait()
        return carry

    def down_place(code, begin=0, end=down_rows):
        base = lax.rem(turned("context", code), 2) * down_rows + begin
        return down_part_ref.at[code // 2, pl.ds(pl.multiple_of(base, 16), end - begin)]

    first_loads = [
        load(13, dh2_in, dh2_ref),
        load(14, residual_in, residual_ref),
        load(15, c_in, c_ref),
    ]
    load_out = load(0, w_out_ref, w_dense)
    later_loads = [
        load(16, merged_in, merged_ref),
        load(17, logsum_in, logsum_ref),
        load(18, q_in, q_ref),
        load(19, h1_in, h1_ref),
        load(20, x_in, x_ref),
        load(21, y_home_in, y_home_ref),
    ]
    stage_loads = [
        load(2, gu_far_ref, stage_a.at[spans[2]]),
        load(3, down_place(2), stage_a.at[down_span]),
        load(4, gu_in_ref, stage_b.at[spans[2]]),
        load(5, down_in_ref, stage_b.at[down_span]),
    ]
    lax.fori_loop(0, me + 1, begin_load, 0)
    load_w_kv = load(1, w_qkv_ref.at[:, query_width:], w_kv)

    begin_row = document_angles(starts_ref, frequency_ref, cosine, sine)
    x, y, core = flip("dp", 1), flip("expert", 2), flip("expert", 1)
    near, far = flip("context", 1), flip("context", 2)
    greet([x, y, core] + [other("context", step) for step in range(1, contexts)])
    y_copies = []
    for index, peer in enumerate((x, y)):
        span = pl.ds(index * half, half)
        copy = remote(
            y_side_ref.at[span], y_in.at[span], y_sems.at[0, index], y_sems.at[1, index], peer
        )
        copy.start()
        y_copies.append(copy)

    near_copies, far_copies, x_copies = [], [], []
    for index, span in enumerate(spans):
        if index < 3:
            source = gu_near_ref.at[0, span]
        else:
            source = down_place(1, cuts[index] - slice_rows, cuts[index + 1] - slice_rows)
        near_copies.append(
            remote(source, near_in.at[span], near_sems.at[0, index], near_sems.at[1, index], near)
        )
        if index > 1:
            far_copies.append(
                remote(
                    stage_a.at[span],
                    far_in.at[span],
                    far_sems.at[0, index],
                    far_sems.at[1, index],
                    far,
                )
            )
    last, upper = me + 1 == contexts, me >= contexts // 2

    near_copies[0].start()

    @pl.when(jnp.logical_not(last))
    def _():
        for copy in near_copies[1:3]:
            copy.start()

    for copy in first_loads:
        copy.wait()
    grad_part, gain_grad = norm_pull(residual_ref[...], gain_row(ffn_gain_ref), dh2_ref[...])
    gains_ref[...] = jnp.zeros_like(gains_ref)
    gains_ref[1:2] = gain_grad
    dres[...] = c_ref[...].astype(F32) + grad_part
    dbranch[...] = dres[...].astype(BF)
    for copy in later_loads:
        copy.wait()
    def dense_matmul(target, left, right):
        for index in range(contexts):
            lanes = slice(index * slice_rows, (index + 1) * slice_rows)
            target[index] = matmul(left[:, lanes], right, TN).astype(BF)

    def streams_of(scratch, part, target, base, width):
        found = []
        for number, order in enumerate(((Y_BIT, X_BIT), (X_BIT, Y_BIT))):
            begin = number * width // 2
            found.append(
                DenseReduce(
                    part.at[:, :, pl.ds(begin, width // 2)],
                    *scratch[6 * number : 6 * number + 6],
                    target,
                    slice(base + begin, base + begin + width // 2),
                    order,
                )
            )
        return found

    out_proj = streams_of(others[:12], dense, out_proj_ref, 0, D)
    query_grad = streams_of(others[12:24], dense, qkv_grad_ref, 0, query_width)
    keys_values = streams_of(others[24:], dense_kv, qkv_grad_ref, query_width, 2 * key_width)
    streams = out_proj + query_grad + keys_values

    def each(group, step):
        for stream in group:
            getattr(stream, step)()

    dense_matmul(dense, merged_ref, dbranch[...])
    each(out_proj, "start")

    for copy in stage_loads:
        copy.wait()
    for span in spans[2:]:
        value = stage_a[span].astype(F32) + stage_b[span].astype(F32)
        stage_a[span] = value.astype(BF)
    far_copies[0].start()

    @pl.when(jnp.logical_not(upper))
    def _():
        for copy in far_copies[1:]:
            copy.start()

    own_loads = [
        load(6, gu_near_ref.at[1], stage_b.at[pl.ds(0, slice_rows)]),
        load(7, down_place(0), stage_b.at[down_span]),
        load(8, far_in_ref, far_in.at[pl.ds(0, first)]),
    ]
    load_out.wait()
    datt[...] = matmul(dbranch[...], w_dense[...], NT).astype(BF)
    load_w_q = load(9, w_qkv_ref.at[:, :query_width], w_dense)
    delta[...] = jnp.zeros_like(delta)
    for head in range(QUERY_HEADS):
        lanes = slice(head * HEAD_SIZE, (head + 1) * HEAD_SIZE)
        product = datt[:, lanes].astype(F32) * merged_ref[:, lanes].astype(F32)
        delta[head : head + 1] = jnp.sum(product.T, axis=0, keepdims=True)

    each(out_proj, "after_core")
    lax.fori_loop(0, me + 1, end_load, 0)
    query_pos = me * rows + lax.broadcasted_iota(jnp.int32, (rows, rows), 1)
    dq[...] = jnp.zeros_like(dq)

    def pull(block):
        key_pos = block * rows + lax.broadcasted_iota(jnp.int32, (rows, rows), 0)
        allowed = (key_pos <= query_pos) & (key_pos >= begin_row)
        bias[...] = jnp.where(allowed, 0.0, negative_huge)
        dkv_sum[...] = jnp.zeros_like(dkv_sum)
        for head in range(QUERY_HEADS):
            group = head // heads
            key_lanes = slice(group * HEAD_SIZE, (group + 1) * HEAD_SIZE)
            value_lanes = slice(key_width + group * HEAD_SIZE, key_width + (group + 1) * HEAD_SIZE)
            keys = kv[block, :, key_lanes]
            values = kv[block, :, value_lanes]
            lanes = slice(head * HEAD_SIZE, (head + 1) * HEAD_SIZE)
            upstream, queries = datt[:, lanes], q_ref[:, lanes]
            scores = matmul(keys, queries, NT) * scaling + bias[...]
            probs = jnp.exp(scores - logsum_ref[head : head + 1])
            dprobs = matmul(values, upstream, NT)
            dscores = (probs * (dprobs - delta[head : head + 1])).astype(BF)
            dkv_sum[:, value_lanes] += matmul(probs.astype(BF), upstream)
            dkv_sum[:, key_lanes] += matmul(dscores, queries)
            dq[head] += matmul(keys, dscores, TN)

    def dkv_copy(block):
        return remote(
            dkv_out.at[block],
            dkv_in.at[block],
            dkv_sems.at[0, block],
            dkv_sems.at[1, block],
            {"context": lax.rem(me - 1 + contexts, contexts)},
        )

    def earlier(block, carry):
        pull(block)
        dkv_out[block] = dkv_sum[...].astype(BF)

        @pl.when(me + 1 == contexts)
        def _():
            dkv_copy(block).start()

        return carry

    lax.fori_loop(0, me, earlier, 0)
    pull(me)
    each(out_proj, "release")
    for head in range(QUERY_HEADS):
        lanes = slice(head * HEAD_SIZE, (head + 1) * HEAD_SIZE)
        dqkv[:, lanes] = unrotate(dq[head].T * scaling, cosine[...], sine[...]).astype(BF)
    dense_matmul(dense, h1_ref, dqkv[:, :query_width])
    each(query_grad, "start")
    each(query_grad, "after_core")

    @pl.when(last)
    def _():
        for copy in near_copies[1:3]:
            copy.start()


    def pass_back(block, carry):
        dkv_copy(block).wait_recv()
        value = dkv_out[block].astype(F32) + dkv_in[block].astype(F32)
        dkv_out[block] = value.astype(BF)
        dkv_copy(block).start()
        return carry

    @pl.when(me + 1 < contexts)
    def _():
        lax.fori_loop(0, me, pass_back, 0)

    for copy in y_copies:
        copy.wait()
    mixture = y_home_ref[...] + y_in[...].astype(F32)
    packed_out_ref[...] = (residual_ref[...] + mixture).astype(BF)
    outs = [load(23, packed_out_ref, packed_out_out)]

    each(out_proj, "after_one")
    each(query_grad, "after_one")

    @pl.when(upper)
    def _():
        for copy in far_copies[1:]:
            copy.start()

    each(out_proj, "after_two")

    @pl.when(me + 1 < contexts)
    def _():
        dkv_copy(me).wait_recv()
        dkv_sum[...] += dkv_in[me].astype(F32)

    for head in range(KEY_VALUE_HEADS):
        lanes = slice(head * HEAD_SIZE, (head + 1) * HEAD_SIZE)
        place = slice(query_width + head * HEAD_SIZE, query_width + (head + 1) * HEAD_SIZE)
        dqkv[:, place] = unrotate(
            dkv_sum[:, lanes] * scaling, cosine[...], sine[...]
        ).astype(BF)
    dqkv[:, query_width + key_width :] = dkv_sum[:, key_width:].astype(BF)
    dense_matmul(dense_kv, h1_ref, dqkv[:, query_width:])
    each(keys_values, "start")
    load_w_q.wait()
    load_w_kv.wait()
    dh1 = matmul(dqkv[:, :query_width], w_dense[...], NT)
    dh1 = dh1 + matmul(dqkv[:, query_width:], w_kv[...], NT)
    grad_part, gain_grad = norm_pull(x_ref[...].astype(F32), gain_row(attn_gain_ref), dh1)
    gains_ref[0:1] = gain_grad
    packed_grad_ref[...] = dres[...] + grad_part
    outs.append(load(22, packed_grad_ref, packed_grad_out))

    exchange = [core, y, x, near, far]
    gain_copies = []

    def gain_start():
        step = len(gain_copies)
        copy = remote(
            gains_ref, gains_in.at[step], gain_sems.at[0, step], gain_sems.at[1, step], exchange[step]
        )
        copy.start()
        gain_copies.append(copy)

    def gain_add():
        gain_copies[-1].wait()
        gains_ref[...] += gains_in[len(gain_copies) - 1]

    gain_start()
    each(query_grad, "after_two")
    for copy in own_loads:
        copy.wait()

    def weights_out(index):
        near_copies[index].wait_recv()
        if index > 1:
            far_copies[index - 2].wait_recv()
        span = spans[index]
        value = stage_b[span].astype(F32) + near_in[span].astype(F32)
        stage_b[span] = (value + far_in[span].astype(F32)).astype(BF)
        outs.append(load(24 + index, stage_b.at[span], weights_ref.at[dp, span]))
        copy = remote(
            stage_b.at[span],
            weights_ref.at[dp, span],
            x_sems.at[0, index],
            x_sems.at[1, index],
            x,
        )
        copy.start()
        x_copies.append(copy)

    each(keys_values, "after_core")
    weights_out(0)
    gain_add()
    gain_start()
    each(keys_values, "after_one")
    gain_add()
    gain_start()
    each(keys_values, "after_two")
    gain_add()
    gain_start()
    near_copies[3].start()

    weights_out(1)
    weights_out(2)
    each(out_proj, "after_near_z")
    each(query_grad, "after_near_z")
    each(keys_values, "after_near_z")
    gain_add()
    gain_start()
    near_copies[4].start()

    weights_out(3)
    each(out_proj, "after_far_z")
    each(query_grad, "after_far_z")
    each(keys_values, "after_far_z")
    gain_add()
    each(streams, "return_one")
    weights_out(4)
    each(streams, "return_core")
    each(streams, "finish")

    def sent(block, carry):
        dkv_copy(block).wait_send()
        return carry

    lax.fori_loop(0, me, sent, 0)
    for copy in near_copies + far_copies:
        copy.wait_send()
    for copy in x_copies + outs:
        copy.wait()


def backward(starts, frequency, attn_gain, ffn_gain, *arrays):
    dh2, _, _, _, logsum, _, _, _, _, kv, w_qkv, w_out = arrays[:12]
    gu_near, _, _, _, down_in, _ = arrays[13:]
    rows = dh2.shape[0]
    contexts = lax.axis_size("context")
    query_width = QUERY_HEADS * HEAD_SIZE
    kv_width = 2 * KEY_VALUE_HEADS * HEAD_SIZE
    slice_rows, down_rows = gu_near.shape[1], down_in.shape[0]
    total = slice_rows + down_rows
    shape = jax.ShapeDtypeStruct
    dma = pltpu.SemaphoreType.DMA
    return pl.pallas_call(
        backward_kernel,
        out_shape=[
            shape((rows, D), BF),
            shape((rows, D), F32),
            shape((8, D), F32),
            shape((slice_rows, D), BF),
            shape((slice_rows, query_width + kv_width), BF),
            shape((2, total, D), BF),
        ],
        in_specs=[SM] + [VM] * 3 + [ANY] * 19,
        out_specs=[ANY] * 2 + [VM] * 3 + [ANY],
        scratch_shapes=[pltpu.VMEM(array.shape, array.dtype) for array in arrays[:9]]
        + [
            pltpu.VMEM((rows, D), BF),
            pltpu.VMEM((rows, D), F32),
            pltpu.VMEM((rows, HEAD_SIZE), F32),
            pltpu.VMEM((rows, HEAD_SIZE), F32),
            pltpu.VMEM(w_out.shape, BF),
            pltpu.VMEM((D, kv_width), BF),
            pltpu.VMEM(kv.shape, BF),
            pltpu.VMEM((rows, D), F32),
            pltpu.VMEM((rows, D), BF),
            pltpu.VMEM((rows, D), BF),
            pltpu.VMEM(logsum.shape, F32),
            pltpu.VMEM((rows, rows), F32),
            pltpu.VMEM((QUERY_HEADS, HEAD_SIZE, rows), F32),
            pltpu.VMEM((rows, kv_width), F32),
            pltpu.VMEM((contexts, rows, kv_width), BF),
            pltpu.VMEM((contexts, rows, kv_width), BF),
            pltpu.VMEM((rows, query_width + kv_width), BF),
            pltpu.VMEM((contexts, slice_rows, D), BF),
            pltpu.VMEM((contexts, slice_rows, kv_width), BF),
            pltpu.VMEM((total, D), BF),
            pltpu.VMEM((total, D), BF),
            pltpu.VMEM((total, D), BF),
            pltpu.VMEM((total, D), BF),
            pltpu.VMEM((5, 8, D), F32),
            pltpu.VMEM((rows, D), BF),
            dma((29,)),
            dma((contexts,)),
            dma((2, contexts)),
            dma((2, 5)),
            dma((2, 5)),
            dma((2, 5)),
            dma((2, 5)),
            dma((2, 2)),
        ]
        + DenseReduce.scratch(contexts, slice_rows, D // 2) * 2
        + DenseReduce.scratch(contexts, slice_rows, query_width // 2) * 2
        + DenseReduce.scratch(contexts, slice_rows, kv_width // 2) * 2,
        compiler_params=pltpu.CompilerParams(
            collective_id=3, has_side_effects=True, vmem_limit_bytes=62 << 20
        ),
        cost_estimate=pl.CostEstimate(
            flops=2 * rows * D * 8000, bytes_accessed=40 << 20, transcendentals=rows * rows * 48
        ),
    )(starts, frequency, attn_gain, ffn_gain, *arrays)


def widen_kernel(
    packed_out_ref,
    packed_grad_ref,
    gains_ref,
    out_proj_ref,
    qkv_grad_ref,
    weights_ref,
    packed_out,
    packed_grad,
    attn_gain_grad,
    qkv_grad,
    out_proj,
    ffn_gain_grad,
    gate_up_grad,
    down_grad,
    *scratch,
):
    narrow, wide, held, sems = scratch[:6], scratch[6:12], scratch[12:14], scratch[14]
    slice_rows = out_proj_ref.shape[0]
    arrivals = [
        pltpu.make_async_copy(packed_out_ref, held[0], sems.at[0, 6]),
        pltpu.make_async_copy(packed_grad_ref, held[1], sems.at[0, 7]),
    ]
    moves = [
        pltpu.make_async_copy(held[0], packed_out, sems.at[1, 6]),
        pltpu.make_async_copy(held[1], packed_grad, sems.at[1, 7]),
    ]
    sources = [weights_ref.at[expert, pl.ds(0, slice_rows)] for expert in range(2)]
    sources += [
        weights_ref.at[expert, pl.ds(slice_rows, slice_rows // 2)] for expert in range(2)
    ]
    sources += [qkv_grad_ref, out_proj_ref]
    targets = [gate_up_grad.at[0], gate_up_grad.at[1], down_grad.at[0], down_grad.at[1]]
    targets += [qkv_grad, out_proj]
    loads, stores = [], []
    for index, source in enumerate(sources):
        loads.append(pltpu.make_async_copy(source, narrow[index], sems.at[0, index]))
        stores.append(pltpu.make_async_copy(wide[index], targets[index], sems.at[1, index]))
    for copy in loads + arrivals:
        copy.start()
    place = pl.ds(
        pl.multiple_of(lax.axis_index("context") * slice_rows, 128), slice_rows
    )
    attn_gain_grad[...] = gains_ref[0:1, place].reshape(slice_rows)
    ffn_gain_grad[...] = gains_ref[1:2, place].reshape(slice_rows)
    for index in range(6):
        loads[index].wait()
        wide[index][...] = narrow[index][...].astype(F32)
        stores[index].start()
    for arrival, move in zip(arrivals, moves):
        arrival.wait()
        move.start()
    for copy in stores + moves:
        copy.wait()


def widen(packed_out, packed_grad, gains, out_proj, qkv_grad, weights):
    slice_rows, total = out_proj.shape[0], weights.shape[1]
    parts = [(slice_rows, D)] * 2 + [(total - slice_rows, D)] * 2
    parts += [qkv_grad.shape, out_proj.shape]
    shape = jax.ShapeDtypeStruct
    return pl.pallas_call(
        widen_kernel,
        out_shape=[
            shape(packed_out.shape, BF),
            shape(packed_grad.shape, F32),
            shape((slice_rows,), F32),
            shape(qkv_grad.shape, F32),
            shape(out_proj.shape, F32),
            shape((slice_rows,), F32),
            shape((2, slice_rows, D), F32),
            shape((2, total - slice_rows, D), F32),
        ],
        in_specs=[ANY] * 2 + [VM] + [ANY] * 3,
        out_specs=[ANY] * 2 + [VM] + [ANY] * 2 + [VM] + [ANY] * 2,
        scratch_shapes=[pltpu.VMEM(part, BF) for part in parts]
        + [pltpu.VMEM(part, F32) for part in parts]
        + [pltpu.VMEM(packed_out.shape, BF), pltpu.VMEM(packed_grad.shape, F32)]
        + [pltpu.SemaphoreType.DMA((2, 8))],
        compiler_params=pltpu.CompilerParams(vmem_limit_bytes=62 << 20),
        cost_estimate=pl.CostEstimate(flops=0, bytes_accessed=24 << 20, transcendentals=0),
    )(packed_out, packed_grad, gains, out_proj, qkv_grad, weights)


def fast_body(
    packed_in,
    routes,
    gates,
    doc_starts,
    attn_gain,
    w_qkv,
    w_out,
    ffn_gain,
    expert_gate_up,
    expert_down,
    cotangent,
):
    x, c, starts = packed_in[0], cotangent[0], doc_starts[0]
    steps = np.arange(HEAD_SIZE) % (HEAD_SIZE // 2)
    frequency = jnp.asarray((rope_base ** (-2.0 * steps / HEAD_SIZE)).astype(np.float32)[None])
    attn_gain, ffn_gain = attn_gain.reshape(-1, 128), ffn_gain.reshape(-1, 128)
    h1, query, logsum, merged, residual, kv, dh2, y_home, y_side, *weight_parts = front(
        x,
        routes[0],
        gates[0],
        starts,
        frequency,
        attn_gain,
        ffn_gain,
        c,
        w_qkv,
        w_out,
        expert_gate_up,
        expert_down,
    )
    sums = backward(
        starts,
        frequency,
        attn_gain,
        ffn_gain,
        dh2,
        residual,
        c,
        merged,
        logsum,
        query,
        h1,
        x,
        y_home,
        kv,
        w_qkv,
        w_out,
        y_side,
        *weight_parts,
    )
    packed_out, packed_grad, attn_grad, qkv_grad, out_proj, ffn_grad, gate_up, down = widen(*sums)
    return (
        packed_out[None],
        packed_grad[None],
        attn_grad,
        qkv_grad,
        out_proj,
        ffn_grad,
        gate_up,
        down,
    )


def fits(mesh):
    sizes = mesh.shape
    contexts = sizes["context"]
    return (
        sizes["dp"] == 2
        and sizes["expert"] == 4
        and contexts == 4
        and D % (contexts * 384) == 0
        and FF % (contexts * 64) == 0
    )


def solution(mesh):
    chosen_body = fast_body if fits(mesh) else body
    placed = (
        P(("dp", "expert"), "context", None),
        P(("dp", "expert"), "context", None),
        P(("dp", "expert"), "context", None),
        P(("dp", "expert"), None),
        P(),
        P(),
        P(),
        P(),
        P("expert", None, None),
        P("expert", None, None),
        P(("dp", "expert"), "context", None),
    )
    return jax.shard_map(
        chosen_body,
        mesh=mesh,
        in_specs=placed,
        out_specs=(
            P(("dp", "expert"), "context", None),
            P(("dp", "expert"), "context", None),
            P("context"),
            P("context", None),
            P("context", None),
            P("context"),
            P("expert", "context", None),
            P("expert", "context", None),
        ),
        check_vma=False,
    )
```
